32 devices in a mesh: group: 8 (over z, y), tensor: 4 (over x, core).
Axes of the slice: x: 2, y: 2, z: 4, core: 2. Of those that a mesh axis runs over, the one named last changes fastest.
Arguments:
- hidden: bfloat16 [4096, 8192], P('group'), may hold values from -1000 to 1000
- norm_gain: float32 [8192], replicated, may hold values from 0.1 to 1.9
- q_weight: bfloat16 [8192, 8192], P('group', 'tensor'), may hold values from -0.0625 to 0.0625
- q_bias: float32 [8192], P('tensor'), may hold values from -3 to 3
- kv_weight: bfloat16 [8192, 2, 1024], P('group'), may hold values from -0.0625 to 0.0625
- kv_bias: float32 [2, 1024], replicated, may hold values from -200 to 200
- prefix_lens: int32 [32], replicated, may hold values from 1 to 256, as said below
- assignment: int32 [32], replicated, may hold values from 0 to 7, as said below
Outputs:
- context: bfloat16 [4096, 8192], P('group', 'tensor')
- kv_cache: bfloat16 [4096, 2, 1024], P('group', None, 'tensor')
The draws below stay inside these ranges and needn't reach their ends.
Inputs may be any that keep to these rules, and one draw needn't show every extreme that they name: `prefix_lens`: the rollouts of one group have lengths summing to exactly 512; in every group one rollout has exactly 256. `assignment`: every group receives exactly 4 rollouts.
All inputs are finite; a program needn't handle non-finite values.
Results may differ from the reference program's by a relative error of at most 0.004.
The reference program's roundings to bfloat16 on the way count: a program that leaves them out, or rounds other values in their place, can miss the bound.
Values may be sent and summed in bfloat16 or wider, within the bound.
No kernel may reach another device: no remote copies, remote signals or barrier semaphores. Data moves between devices by JAX's collectives and lax.ppermute only.
A program may use at most 256 MiB of HBM per device.

```python
import math
import jax
import jax.numpy as jnp
from jax import lax

D = 8192
HQ = 64
KVH = 8
HD = 128
GTOK = 512
ROLL_GROUP = 4
MAXLEN = 256
ROLLOUTS = 32
TOKENS = 4096
N_GROUP = 8


def rollout_plan(key):
    groups = ROLLOUTS // ROLL_GROUP
    remainder = GTOK - MAXLEN

    def one_group(group_key):
        cut_key, slot_key = jax.random.split(group_key)
        cut_points = jnp.sort(jax.random.permutation(cut_key, remainder - 1)[:ROLL_GROUP - 2] + 1).astype(jnp.int32)
        boundary = jnp.concatenate([jnp.zeros((1,), jnp.int32), cut_points, jnp.full((1,), remainder, jnp.int32)])
        pieces = boundary[1:] - boundary[:-1]
        lengths_row = jnp.concatenate([jnp.full((1,), MAXLEN, jnp.int32), pieces])
        rotation = jax.random.randint(slot_key, (), 0, ROLL_GROUP)
        return jnp.roll(lengths_row, rotation)
    per_group = jax.vmap(one_group)(jax.random.split(key, groups))
    shuffle = jax.random.permutation(jax.random.fold_in(key, 7), ROLLOUTS)
    lengths = jnp.zeros((ROLLOUTS,), jnp.int32).at[shuffle].set(per_group.reshape(-1).astype(jnp.int32))
    owners = jnp.zeros((ROLLOUTS,), jnp.int32).at[shuffle].set(jnp.repeat(jnp.arange(groups, dtype=jnp.int32), ROLL_GROUP))
    return (lengths, owners)


def draw_prefix_lens(key, part):
    return rollout_plan(key)[0]


def draw_assignment(key, part):
    return rollout_plan(key)[1]


def draw_hidden(key, part):
    key = jax.random.fold_in(key, 11)
    noise_key, row_key, col_key = jax.random.split(key, 3)
    col_scale = jnp.exp(jax.random.uniform(col_key, (1, D), jnp.float32, 0.0, math.log(10.0)))
    row_scale = jnp.exp(jax.random.uniform(row_key, (TOKENS, 1), jnp.float32, 0.0, math.log(10.0)))
    noise = jnp.clip(jax.random.normal(noise_key, (TOKENS, D), jnp.float32), -6.0, 6.0)
    values = noise * row_scale * col_scale
    return values.astype(jnp.bfloat16)


def draw_kv_bias(key, part):
    key = jax.random.fold_in(key, 23)
    key_seed, value_seed = jax.random.split(key)
    value_part = 0.5 * jnp.clip(jax.random.normal(value_seed, (1, KVH * HD), jnp.float32), -6.0, 6.0)
    key_part = jnp.clip(jax.random.normal(key_seed, (1, KVH * HD), jnp.float32), -6.0, 6.0)
    return jnp.concatenate([key_part, value_part], axis=0)


def level_of(stream_key, shape, cuts, least, top_value):
    gain = 1.0
    for position, shards_of in cuts:
        heights = jax.random.uniform(jax.random.fold_in(jax.random.fold_in(stream_key, 6), position), (shards_of,), jnp.float32, least / len(cuts), top_value / len(cuts))
        gain = gain * jnp.repeat(jnp.exp(heights), shape[position] // shards_of).reshape((-1,) + (1,) * (len(shape) - 1 - position))
    return gain


def scatter_about(own_key, shape, scale, limit, shards=(), kind=jnp.bfloat16):
    result = jax.random.normal(own_key, shape, jnp.float32) * scale
    if len(shards) > 0:
        result = level_of(own_key, shape, shards, -0.22, 0.18) * result
    return jnp.clip(result, min=-limit, max=limit).astype(kind)


def setup_inputs(seed: int = 0) -> dict:
    seeds = jax.random.split(jax.random.key(seed), 9)
    return {
        "hidden": draw_hidden(jax.random.fold_in(seeds[8], 71), 0),
        "norm_gain": jnp.clip(1.0 + 0.18 * jax.random.normal(seeds[1], (D,), jnp.float32), 0.1, 1.9),
        "q_weight": scatter_about(seeds[2], (D, HQ * HD), D ** -0.5, 0.0625, ((0, 8), (1, 4))),
        "q_bias": scatter_about(seeds[3], (HQ * HD,), 0.5, 3.0, ((0, 4),), jnp.float32),
        "kv_weight": scatter_about(seeds[4], (D, 2, KVH * HD), D ** -0.5, 0.0625, ((0, 8),)),
        "kv_bias": draw_kv_bias(jax.random.fold_in(seeds[8], 71), 0),
        "prefix_lens": draw_prefix_lens(jax.random.fold_in(seeds[8], 71), 0),
        "assignment": draw_assignment(jax.random.fold_in(seeds[8], 71), 0),
    }


EPS = 1e-06
THETA = 1000000.0

def settle(values):
    return lax.optimization_barrier(values.astype(jnp.bfloat16))

def token_layout(prefix_lens, assignment, group_id, tok_rows):
    rollouts = prefix_lens.shape[0]
    member = assignment == group_id
    own_lens = jnp.where(member, prefix_lens, 0).astype(jnp.int32)
    starts = (jnp.cumsum(own_lens) - own_lens).astype(jnp.int32)
    places = jnp.arange(tok_rows, dtype=jnp.int32)
    inside = member[None, :] & (places[:, None] >= starts[None, :]) & (places[:, None] < (starts + own_lens)[None, :])
    owner_id = lax.optimization_barrier(jnp.sum(jnp.where(inside, jnp.arange(rollouts, dtype=jnp.int32)[None, :], 0), axis=1)).astype(jnp.int32)
    offset = (places - lax.optimization_barrier(jnp.sum(jnp.where(inside, starts[None, :], 0), axis=1))).astype(jnp.int32)
    return (owner_id, offset, places)

def rotate(values, offset):
    half_dim = values.shape[-1] // 2
    inverse_freq = THETA ** (-2.0 * jnp.arange(half_dim, dtype=jnp.float32) / values.shape[-1])
    angles = offset.astype(jnp.float32)[:, None] * inverse_freq[None, :]
    cosine = jnp.cos(angles)[:, None, :]
    sine_part = jnp.sin(angles)[:, None, :]
    first_half = values[..., :half_dim]
    second_half = values[..., half_dim:]
    return jnp.concatenate([first_half * cosine - second_half * sine_part, second_half * cosine + first_half * sine_part], axis=-1)

def attend(grouped, rotated_keys, value_heads, visible):
    scores = jnp.einsum('qgph,kgh->gpqk', grouped.astype(jnp.float32), rotated_keys.astype(jnp.float32)) / math.sqrt(HD)
    scores = jnp.where(visible[None, None], scores, -jnp.inf)
    row_max = lax.optimization_barrier(jnp.max(scores, axis=-1, keepdims=True))
    exponent = jnp.exp(scores - row_max)
    weights_bf = settle(exponent / lax.optimization_barrier(jnp.sum(exponent, axis=-1, keepdims=True)))
    return jnp.einsum('gpqk,kgh->qgph', weights_bf.astype(jnp.float32), value_heads.astype(jnp.float32))

def reference(hidden, norm_gain, q_weight, q_bias, kv_weight, kv_bias, prefix_lens, assignment):
    repeats = HQ // KVH

    def one_group(inputs):
        group_rows, group_id = inputs
        widened = group_rows.astype(jnp.float32)
        normed = (widened * lax.rsqrt(lax.optimization_barrier(jnp.mean(widened * widened, axis=-1, keepdims=True)) + EPS) * norm_gain).astype(jnp.bfloat16)
        queries = jnp.dot(normed, q_weight, preferred_element_type=jnp.float32) + q_bias
        projected = jnp.dot(normed, kv_weight.reshape(D, 2 * KVH * HD), preferred_element_type=jnp.float32).reshape(GTOK, 2, KVH * HD) + kv_bias
        owner_id, offset, places = token_layout(prefix_lens, assignment, group_id, GTOK)
        rotated_queries = settle(rotate(queries.reshape(GTOK, HQ, HD), offset))
        rotated_keys = settle(rotate(projected[:, 0].reshape(GTOK, KVH, HD), offset))
        value_heads = settle(projected[:, 1].reshape(GTOK, KVH, HD))
        visible = (owner_id[:, None] == owner_id[None, :]) & (places[None, :] <= places[:, None])
        context = attend(rotated_queries.reshape(GTOK, KVH, repeats, HD), rotated_keys, value_heads, visible)
        kv_cache = jnp.stack([rotated_keys.reshape(GTOK, KVH * HD), value_heads.reshape(GTOK, KVH * HD)], axis=1)
        return (context.reshape(GTOK, HQ * HD).astype(jnp.bfloat16), kv_cache)
    stacked = hidden.reshape(N_GROUP, GTOK, D)
    context, kv_cache = lax.map(one_group, (stacked, jnp.arange(N_GROUP, dtype=jnp.int32)))
    return (context.reshape(TOKENS, HQ * HD), kv_cache.reshape(TOKENS, 2, KVH * HD))
```

```python
import functools
import math

import jax
import jax.numpy as jnp
from jax import lax
from jax.experimental import pallas as pl
from jax.experimental.pallas import tpu as pltpu
from jax.sharding import PartitionSpec as P

HD = 128


EPS = 1e-06
THETA = 1000000.0
QROWS = 128
MAXLEN = 256


def token_layout(prefix_lens, assignment, group_id, tok_rows):
    rollouts = prefix_lens.shape[0]
    member = assignment == group_id
    own_lens = jnp.where(member, prefix_lens, 0)
    starts = jnp.cumsum(own_lens) - own_lens
    places = jnp.arange(tok_rows, dtype=jnp.int32)
    inside = (
        member[None, :]
        & (places[:, None] >= starts[None, :])
        & (places[:, None] < (starts + own_lens)[None, :])
    )
    owner_id = jnp.sum(jnp.where(inside, jnp.arange(rollouts, dtype=jnp.int32)[None, :], 0), axis=1)
    offset = places - jnp.sum(jnp.where(inside, starts[None, :], 0), axis=1)
    return (owner_id, offset, places)


def rotate(values, offset):
    half_dim = values.shape[-1] // 2
    inverse_freq = THETA ** (-2.0 * jnp.arange(half_dim, dtype=jnp.float32) / values.shape[-1])
    angles = offset.astype(jnp.float32)[:, None] * inverse_freq[None, :]
    cosine = jnp.cos(angles)[:, None, :]
    sine_part = jnp.sin(angles)[:, None, :]
    first_half = values[..., :half_dim]
    second_half = values[..., half_dim:]
    return jnp.concatenate(
        [
            first_half * cosine - second_half * sine_part,
            second_half * cosine + first_half * sine_part,
        ],
        axis=-1,
    )


def add_product(normed, portion):
    return jnp.dot(normed, portion, preferred_element_type=jnp.float32)


def normalise(hidden, norm_gain):
    widened = hidden.astype(jnp.float32)
    return (
        widened * lax.rsqrt(jnp.mean(widened * widened, axis=-1, keepdims=True) + EPS) * norm_gain
    ).astype(jnp.bfloat16)


def gathered_form(
    hidden, norm_gain, q_weight, q_bias, kv_weight, kv_bias, prefix_lens, assignment
):
    tok_rows, features = hidden.shape
    slice_rows = kv_weight.shape[0]
    q_cols = q_weight.shape[1]
    kv_total = kv_weight.shape[2]
    heads_here = q_cols // HD
    tensor_pos = lax.axis_index("tensor")
    kv_cols = kv_total // lax.axis_size("tensor")
    normed = normalise(hidden, norm_gain)
    queries = add_product(normed, lax.all_gather(q_weight, "group", axis=0, tiled=True)) + q_bias
    head_span = max(kv_cols, HD)
    head_base = tensor_pos * kv_cols // head_span * head_span
    local_start = tensor_pos * kv_cols - head_base
    head_rows = lax.dynamic_slice_in_dim(kv_weight, head_base, head_span, 2).reshape(
        slice_rows, 2 * head_span
    )
    projected = add_product(normed, lax.all_gather(head_rows, "group", axis=0, tiled=True))
    projected = projected.reshape(tok_rows, 2, head_span) + lax.dynamic_slice_in_dim(
        kv_bias, head_base, head_span, 1
    )
    kv_here = head_span // HD
    group_size = heads_here // kv_here
    owner_id, offset, places = token_layout(
        prefix_lens, assignment, lax.axis_index("group"), tok_rows
    )
    rotated_queries = rotate(queries.reshape(tok_rows, heads_here, HD), offset).astype(jnp.bfloat16)
    rotated_keys = rotate(projected[:, 0].reshape(tok_rows, kv_here, HD), offset).astype(
        jnp.bfloat16
    )
    value_heads = projected[:, 1].reshape(tok_rows, kv_here, HD).astype(jnp.bfloat16)
    visible = (owner_id[:, None] == owner_id[None, :]) & (places[None, :] <= places[:, None])
    grouped = rotated_queries.reshape(tok_rows, kv_here, group_size, HD)
    scores = jnp.einsum(
        "qgph,kgh->gpqk", grouped, rotated_keys, preferred_element_type=jnp.float32
    ) / math.sqrt(HD)
    scores = jnp.where(visible[None, None], scores, -jnp.inf)
    row_max = jnp.max(scores, axis=-1, keepdims=True)
    exponent = jnp.exp(scores - row_max)
    weights_bf = (exponent / jnp.sum(exponent, axis=-1, keepdims=True)).astype(jnp.bfloat16)
    context = jnp.einsum(
        "gpqk,kgh->qgph", weights_bf, value_heads, preferred_element_type=jnp.float32
    )
    context = context.astype(jnp.bfloat16).reshape(tok_rows, q_cols)
    stacked = jnp.stack(
        [rotated_keys.reshape(tok_rows, head_span), value_heads.reshape(tok_rows, head_span)],
        axis=1,
    )
    kv_cache = lax.dynamic_slice_in_dim(stacked, local_start, kv_cols, 2)
    return (context, kv_cache)


def attention_kernel(q_ref, bias_ref, cos_ref, sin_ref, k_ref, v_ref, first_ref, out_ref):
    rows = q_ref.shape[0]
    queries = q_ref[...] + bias_ref[...]
    turned = queries * cos_ref[...] + pltpu.roll(queries, HD // 2, 1) * sin_ref[...]
    turned = turned.astype(jnp.bfloat16)
    for block in range(rows // QROWS):
        top = block * QROWS
        low = max(0, top - MAXLEN)
        end = top + QROWS
        scores = lax.dot_general(
            turned[top:end],
            k_ref[low:end],
            (((1,), (1,)), ((), ())),
            preferred_element_type=jnp.float32,
        ) * (1.0 / math.sqrt(HD))
        row = lax.broadcasted_iota(jnp.int32, scores.shape, 0) + top
        col = lax.broadcasted_iota(jnp.int32, scores.shape, 1) + low
        visible = (col <= row) & (col >= first_ref[top:end])
        scores = jnp.where(visible, scores, -jnp.inf)
        exponent = jnp.exp(scores - jnp.max(scores, axis=-1, keepdims=True))
        weights = (exponent / jnp.sum(exponent, axis=-1, keepdims=True)).astype(jnp.bfloat16)
        out_ref[top:end] = jnp.dot(
            weights, v_ref[low:end], preferred_element_type=jnp.float32
        ).astype(jnp.bfloat16)


def attend(queries, skip, bias, cosine, sine, keys_values, first):
    rows, cols = queries.shape
    heads = cols // HD - skip
    flops = 4 * heads * rows * 3 * QROWS * HD
    return pl.pallas_call(
        attention_kernel,
        grid=(heads,),
        in_specs=[
            pl.BlockSpec((rows, HD), lambda h: (0, h + skip)),
            pl.BlockSpec((1, HD), lambda h: (0, h)),
            pl.BlockSpec((rows, HD), lambda h: (0, 0)),
            pl.BlockSpec((rows, HD), lambda h: (0, 0)),
            pl.BlockSpec((rows, HD), lambda h: (0, 0)),
            pl.BlockSpec((rows, HD), lambda h: (0, 1)),
            pl.BlockSpec((rows, 1), lambda h: (0, 0)),
        ],
        out_specs=pl.BlockSpec((rows, HD), lambda h: (0, h)),
        out_shape=jax.ShapeDtypeStruct((rows, heads * HD), jnp.bfloat16),
        compiler_params=pltpu.CompilerParams(vmem_limit_bytes=32 * 2**20),
        cost_estimate=pl.CostEstimate(
            flops=flops,
            bytes_accessed=rows * heads * HD * 6 + rows * HD * 12,
            transcendentals=heads * rows * 3 * QROWS,
        ),
    )(queries, bias, cosine, sine, keys_values, keys_values, first)


CODES = (0, 1, 6, 7, 2, 3, 4, 5)


def pairs_from(sources, code):
    return [(s, s ^ code) for s in sources]


MIDDLE = (2, 3, 4, 5)
ENDS = (0, 1, 6, 7)


def middle_form(hidden, norm_gain, q_weight, q_bias, kv_weight, kv_bias, prefix_lens, assignment):
    tok_rows, features = hidden.shape
    slice_rows, q_cols = q_weight.shape
    half_cols = q_cols // 2
    group = lax.axis_index("group")
    tensor = lax.axis_index("tensor")
    y = group & 1
    is_middle = (group >= 2) & (group < 6)
    blocks = features // slice_rows

    def over_group(value, sources, code):
        return lax.ppermute(value, "group", pairs_from(sources, code))

    def over_tensor(value, code):
        return lax.ppermute(value, "tensor", pairs_from(range(4), code))

    widths = (2 * HD, half_cols // 2, half_cols // 4)

    def columns(half):
        head = (2 * tensor + half) * HD
        kv_part = lax.dynamic_slice_in_dim(kv_weight, head, HD, 2).reshape(slice_rows, 2 * HD)
        taken, place = [], half * half_cols
        for chunk, width in enumerate(widths):
            part = lax.dynamic_slice_in_dim(q_weight, place, width, 1)
            taken.append(jnp.concatenate([kv_part, part], axis=1) if chunk == 0 else part)
            place = place + width
        return taken

    own = columns(y)
    other = columns(1 - y)

    normed = normalise(hidden, norm_gain)
    normed = normed.reshape(tok_rows, blocks, slice_rows).transpose(1, 0, 2)

    core = tensor & 1
    half = lax.dynamic_slice_in_dim(normed, core * (blocks // 2), blocks // 2, 0)
    quarter = lax.dynamic_slice_in_dim(normed, tensor * 2, 2, 0)

    def placed(parts):
        whole = jnp.zeros_like(normed)
        for part, at in parts:
            whole = lax.dynamic_update_slice_in_dim(whole, part, at, 0)
        return whole

    def from_half(got):
        twin = over_tensor(got, 1)
        return placed([(got, core * (blocks // 2)), (twin, (1 - core) * (blocks // 2))])

    def from_quarter(got):
        across = over_tensor(got, 2)
        return placed(
            [
                (got, tensor * 2),
                (across, (tensor ^ 2) * 2),
                (over_tensor(got, 1), (tensor ^ 1) * 2),
                (over_tensor(across, 1), (tensor ^ 3) * 2),
            ]
        )

    rows_of = [
        normed,
        from_half(over_group(half, MIDDLE, 1)),
        from_quarter(over_group(quarter, ENDS, 2)),
        from_quarter(over_group(quarter, ENDS, 3)),
    ]

    pieces = []
    for mine, its in zip(own, other):
        end_own = over_group(mine, ENDS, 2)
        end_swap = over_group(its, ENDS, 3)
        pieces.append(
            {
                0: mine,
                1: over_group(its, MIDDLE, 1),
                6: over_group(mine, MIDDLE, 6),
                7: over_group(its, MIDDLE, 7),
                2: end_own,
                3: end_swap,
                4: over_group(end_own, MIDDLE, 6),
                5: over_group(end_swap, MIDDLE, 6),
            }
        )

    bias = lax.dynamic_slice_in_dim(q_bias, y * half_cols, half_cols, 0)[None, :]
    kv_bias_here = lax.dynamic_slice_in_dim(kv_bias, (2 * tensor + y) * HD, HD, 1)
    inverse_freq = THETA ** (-2.0 * jnp.arange(HD // 2, dtype=jnp.float32) / HD)

    results = []
    for code in range(4):
        _, offset, places = token_layout(prefix_lens, assignment, group ^ code, tok_rows)
        angles = offset.astype(jnp.float32)[:, None] * inverse_freq[None, :]
        cosine, sine = jnp.cos(angles), jnp.sin(angles)
        cosine = jnp.concatenate([cosine, cosine], axis=1)
        sine = jnp.concatenate([-sine, sine], axis=1)
        first = (places - offset)[:, None]
        place = 0
        outs = []
        for chunk, width in enumerate(widths):
            total = None
            for piece in CODES:
                block = lax.dynamic_index_in_dim(rows_of[code], group ^ piece, 0, keepdims=False)
                term = add_product(block, pieces[chunk][piece])
                total = term if total is None else total + term
            if chunk == 0:
                keys = total[:, :HD] + kv_bias_here[0]
                swapped = jnp.concatenate([keys[:, HD // 2 :], keys[:, : HD // 2]], axis=1)
                keys = keys * cosine + swapped * sine
                values = total[:, HD : 2 * HD] + kv_bias_here[1]
                keys_values = jnp.concatenate([keys, values], axis=1).astype(jnp.bfloat16)
            out = attend(
                total,
                2 if chunk == 0 else 0,
                bias[:, place : place + width],
                cosine,
                sine,
                keys_values,
                first,
            )
            place += width
            outs.append(jnp.concatenate([keys_values, out], axis=1) if chunk == 0 else out)
        results.append(outs)

    mine, its = [], []
    for chunk in range(len(widths)):
        back_own = over_group(results[2][chunk], MIDDLE, 2)
        back_other = over_group(results[3][chunk], MIDDLE, 3)
        beside = over_group(results[1][chunk], MIDDLE, 1)
        mine.append(jnp.where(is_middle, results[0][chunk], back_own))
        its.append(jnp.where(is_middle, beside, back_other))

    def in_order(a, b):
        return jnp.where(y == 0, jnp.concatenate([a, b], axis=-1), jnp.concatenate([b, a], axis=-1))

    context = in_order(
        jnp.concatenate([mine[0][:, 2 * HD :]] + mine[1:], axis=1),
        jnp.concatenate([its[0][:, 2 * HD :]] + its[1:], axis=1),
    )
    kv_cache = in_order(
        mine[0][:, : 2 * HD].reshape(tok_rows, 2, HD), its[0][:, : 2 * HD].reshape(tok_rows, 2, HD)
    )
    return (context, kv_cache)


def solution(mesh):
    placed = (
        P("group", None),
        P(),
        P("group", "tensor"),
        P("tensor"),
        P("group", None, None),
        P(),
        P(),
        P(),
    )
    fits = mesh.shape["group"] == 8 and mesh.shape["tensor"] == 4
    return jax.shard_map(
        middle_form if fits else gathered_form,
        mesh=mesh,
        in_specs=placed,
        out_specs=(P("group", "tensor"), P("group", None, "tensor")),
        check_vma=False,
    )
```

```python
import functools
import math

import jax
import jax.numpy as jnp
from jax import lax
from jax.experimental import pallas as pl
from jax.experimental.pallas import tpu as pltpu
from jax.sharding import PartitionSpec as P

HD = 128


EPS = 1e-06
THETA = 1000000.0
QROWS = 128
MAXLEN = 256


def token_layout(prefix_lens, assignment, group_id, tok_rows):
    rollouts = prefix_lens.shape[0]
    member = assignment == group_id
    own_lens = jnp.where(member, prefix_lens, 0)
    starts = jnp.cumsum(own_lens) - own_lens
    places = jnp.arange(tok_rows, dtype=jnp.int32)
    inside = (
        member[None, :]
        & (places[:, None] >= starts[None, :])
        & (places[:, None] < (starts + own_lens)[None, :])
    )
    owner_id = jnp.sum(jnp.where(inside, jnp.arange(rollouts, dtype=jnp.int32)[None, :], 0), axis=1)
    offset = places - jnp.sum(jnp.where(inside, starts[None, :], 0), axis=1)
    return (owner_id, offset, places)


def rotate(values, offset):
    half_dim = values.shape[-1] // 2
    inverse_freq = THETA ** (-2.0 * jnp.arange(half_dim, dtype=jnp.float32) / values.shape[-1])
    angles = offset.astype(jnp.float32)[:, None] * inverse_freq[None, :]
    cosine = jnp.cos(angles)[:, None, :]
    sine_part = jnp.sin(angles)[:, None, :]
    first_half = values[..., :half_dim]
    second_half = values[..., half_dim:]
    return jnp.concatenate(
        [
            first_half * cosine - second_half * sine_part,
            second_half * cosine + first_half * sine_part,
        ],
        axis=-1,
    )


def add_product(normed, portion):
    return jnp.dot(normed, portion, preferred_element_type=jnp.float32)


def normalise(hidden, norm_gain):
    widened = hidden.astype(jnp.float32)
    return (
        widened * lax.rsqrt(jnp.mean(widened * widened, axis=-1, keepdims=True) + EPS) * norm_gain
    ).astype(jnp.bfloat16)


def gathered_form(
    hidden, norm_gain, q_weight, q_bias, kv_weight, kv_bias, prefix_lens, assignment
):
    tok_rows, features = hidden.shape
    slice_rows = kv_weight.shape[0]
    q_cols = q_weight.shape[1]
    kv_total = kv_weight.shape[2]
    heads_here = q_cols // HD
    tensor_pos = lax.axis_index("tensor")
    kv_cols = kv_total // lax.axis_size("tensor")
    normed = normalise(hidden, norm_gain)
    queries = add_product(normed, lax.all_gather(q_weight, "group", axis=0, tiled=True)) + q_bias
    head_span = max(kv_cols, HD)
    head_base = tensor_pos * kv_cols // head_span * head_span
    local_start = tensor_pos * kv_cols - head_base
    head_rows = lax.dynamic_slice_in_dim(kv_weight, head_base, head_span, 2).reshape(
        slice_rows, 2 * head_span
    )
    projected = add_product(normed, lax.all_gather(head_rows, "group", axis=0, tiled=True))
    projected = projected.reshape(tok_rows, 2, head_span) + lax.dynamic_slice_in_dim(
        kv_bias, head_base, head_span, 1
    )
    kv_here = head_span // HD
    group_size = heads_here // kv_here
    owner_id, offset, places = token_layout(
        prefix_lens, assignment, lax.axis_index("group"), tok_rows
    )
    rotated_queries = rotate(queries.reshape(tok_rows, heads_here, HD), offset).astype(jnp.bfloat16)
    rotated_keys = rotate(projected[:, 0].reshape(tok_rows, kv_here, HD), offset).astype(
        jnp.bfloat16
    )
    value_heads = projected[:, 1].reshape(tok_rows, kv_here, HD).astype(jnp.bfloat16)
    visible = (owner_id[:, None] == owner_id[None, :]) & (places[None, :] <= places[:, None])
    grouped = rotated_queries.reshape(tok_rows, kv_here, group_size, HD)
    scores = jnp.einsum(
        "qgph,kgh->gpqk", grouped, rotated_keys, preferred_element_type=jnp.float32
    ) / math.sqrt(HD)
    scores = jnp.where(visible[None, None], scores, -jnp.inf)
    row_max = jnp.max(scores, axis=-1, keepdims=True)
    exponent = jnp.exp(scores - row_max)
    weights_bf = (exponent / jnp.sum(exponent, axis=-1, keepdims=True)).astype(jnp.bfloat16)
    context = jnp.einsum(
        "gpqk,kgh->qgph", weights_bf, value_heads, preferred_element_type=jnp.float32
    )
    context = context.astype(jnp.bfloat16).reshape(tok_rows, q_cols)
    stacked = jnp.stack(
        [rotated_keys.reshape(tok_rows, head_span), value_heads.reshape(tok_rows, head_span)],
        axis=1,
    )
    kv_cache = lax.dynamic_slice_in_dim(stacked, local_start, kv_cols, 2)
    return (context, kv_cache)


def attention_kernel(q_ref, bias_ref, cos_ref, sin_ref, k_ref, v_ref, first_ref, out_ref):
    rows, cols = out_ref.shape
    heads = cols // HD
    skip = q_ref.shape[1] - cols
    cosine, sine = cos_ref[...], sin_ref[...]
    turned = []
    for head in range(heads):
        at = head * HD
        query = q_ref[:, skip + at : skip + at + HD] + bias_ref[:, at : at + HD]
        query = query * cosine + pltpu.roll(query, HD // 2, 1) * sine
        turned.append(query.astype(jnp.bfloat16))
    for block in range(rows // QROWS):
        top = block * QROWS
        low = max(0, top - MAXLEN)
        end = top + QROWS
        span = end - low
        stacked = jnp.concatenate([query[top:end] for query in turned], axis=0)
        scores = lax.dot_general(
            stacked, k_ref[low:end], (((1,), (1,)), ((), ())), preferred_element_type=jnp.float32
        ) * (1.0 / math.sqrt(HD))
        row = lax.broadcasted_iota(jnp.int32, (QROWS, span), 0) + top
        col = lax.broadcasted_iota(jnp.int32, (QROWS, span), 1) + low
        visible = (col <= row) & (col >= first_ref[top:end])
        scores = jnp.where(visible[None], scores.reshape(heads, QROWS, span), -jnp.inf)
        exponent = jnp.exp(scores - jnp.max(scores, axis=-1, keepdims=True))
        weights = (exponent / jnp.sum(exponent, axis=-1, keepdims=True)).astype(jnp.bfloat16)
        context = jnp.dot(
            weights.reshape(heads * QROWS, span), v_ref[low:end], preferred_element_type=jnp.float32
        ).astype(jnp.bfloat16)
        for head in range(heads):
            out_ref[top:end, head * HD : (head + 1) * HD] = context[
                head * QROWS : (head + 1) * QROWS
            ]


def attend(queries, heads, bias, cosine, sine, keys, values, first):
    rows = queries.shape[0]
    return pl.pallas_call(
        attention_kernel,
        out_shape=jax.ShapeDtypeStruct((rows, heads * HD), jnp.bfloat16),
        compiler_params=pltpu.CompilerParams(vmem_limit_bytes=40 * 2**20),
        cost_estimate=pl.CostEstimate(
            flops=4 * heads * rows * 3 * QROWS * HD,
            bytes_accessed=rows * heads * HD * 6 + rows * HD * 12,
            transcendentals=heads * rows * 3 * QROWS,
        ),
    )(queries, bias, cosine, sine, keys, values, first)


def project_kernel(count, at_ref, *refs):
    blocks, pieces = refs[:count], refs[count : 2 * count]
    out_ref = refs[-1]
    total = None if len(refs) == 2 * count + 1 else refs[2 * count][...]
    for block, piece in zip(blocks, pieces):
        weight = piece[...].reshape(piece.shape[-2:])
        term = jnp.dot(block[0], weight, preferred_element_type=jnp.float32)
        total = term if total is None else total + term
    out_ref[...] = total


def project(rows, at, pieces, width, total=None):
    count = len(pieces)
    tokens, depth = rows.shape[1], pieces[0][0].shape[-2]
    tile = 2 * HD
    in_specs = [
        pl.BlockSpec((1, tokens, depth), functools.partial(lambda p, j, at: (at[0, p], 0, at[1, p]), p))
        for p in range(count)
    ]
    for array, lead, skip in pieces:
        if array.ndim == 3:
            in_specs.append(
                pl.BlockSpec(
                    (1, depth, tile),
                    functools.partial(lambda l, s, j, at: (l, 0, j + s), lead, skip // tile),
                )
            )
        else:
            in_specs.append(
                pl.BlockSpec(
                    (depth, tile), functools.partial(lambda s, j, at: (0, j + s), skip // tile)
                )
            )
    operands = [rows] * count + [array for array, _, _ in pieces]
    if total is not None:
        in_specs.append(pl.BlockSpec((tokens, tile), lambda j, at: (0, j)))
        operands.append(total)
    return pl.pallas_call(
        functools.partial(project_kernel, count),
        grid_spec=pltpu.PrefetchScalarGridSpec(
            num_scalar_prefetch=1,
            grid=(width // tile,),
            in_specs=in_specs,
            out_specs=pl.BlockSpec((tokens, tile), lambda j, at: (0, j)),
        ),
        out_shape=jax.ShapeDtypeStruct((tokens, width), jnp.float32),
        compiler_params=pltpu.CompilerParams(vmem_limit_bytes=48 * 2**20),
        cost_estimate=pl.CostEstimate(
            flops=2 * count * tokens * depth * width,
            bytes_accessed=2 * count * depth * (tokens + width) + 8 * tokens * width,
            transcendentals=0,
        ),
    )(at, *operands)


MIDDLE = (2, 3, 4, 5)
ENDS = (0, 1, 6, 7)
FIRST_CODES = (0, 1, 6, 7)
LAST_CODES = (2, 3, 4, 5)


def pairs_from(sources, code):
    return [(s, s ^ code) for s in sources]


def after(value, *others):
    return lax.optimization_barrier((value,) + others)[0]


def middle_form(hidden, norm_gain, q_weight, q_bias, kv_weight, kv_bias, prefix_lens, assignment):
    tok_rows, features = hidden.shape
    slice_rows, q_cols = q_weight.shape
    half_cols = q_cols // 2
    group = lax.axis_index("group")
    tensor = lax.axis_index("tensor")
    core = tensor & 1
    y = group & 1
    is_middle = (group >= 2) & (group < 6)

    def over_group(value, sources, code):
        return lax.ppermute(value, "group", pairs_from(sources, code))

    def over_y(value):
        return over_group(value, range(8), 1)

    def to_middle(value):
        return over_group(value, ENDS, 2)

    def across_middle(value):
        return over_group(value, MIDDLE, 6)

    def over_x(value):
        return lax.ppermute(value, "tensor", pairs_from(range(4), 2))

    def over_core(value):
        return lax.ppermute(value, "tensor", pairs_from(range(4), 1))

    heads = (2, 4, 2)
    cut = heads[0] * HD

    def columns(half):
        head = (2 * tensor + half) * HD
        kv_part = lax.dynamic_slice_in_dim(kv_weight, head, HD, 2).reshape(slice_rows, 2 * HD)
        early = lax.dynamic_slice_in_dim(q_weight, half * half_cols, cut, 1)
        late = lax.dynamic_slice_in_dim(q_weight, half * half_cols + cut, half_cols - cut, 1)
        return jnp.concatenate([kv_part, early], axis=1), late

    own0, own12 = columns(y)
    other0, other12 = columns(1 - y)
    mid_cols = heads[1] * HD

    m_own0 = across_middle(own0)
    swap0 = over_y(other0)
    normed = normalise(hidden, norm_gain)
    quarter = lax.dynamic_slice_in_dim(normed, tensor * (features // 4), features // 4, 1)
    half = lax.dynamic_slice_in_dim(normed, core * (features // 2), features // 2, 1)
    end2 = to_middle(quarter)
    m_swap0 = across_middle(swap0)
    swap12 = over_y(after(other12, swap0, m_own0))
    m_own12 = across_middle(after(own12, m_own0))
    e0 = to_middle(after(jnp.stack([own0, swap0]), end2))
    across2 = over_x(end2)
    m_swap12 = across_middle(after(swap12, m_swap0))
    end3 = over_group(after(end2, swap12), MIDDLE, 1)

    def whole(near, across):
        both = jnp.stack([near, across])
        return jnp.concatenate([both, over_core(both)])

    rows0 = normed[None]
    rows2 = whole(end2, across2)

    def spots(codes, places):
        block = jnp.stack([group ^ code for code in codes])
        if places == 1:
            return jnp.stack([block * 0, block])
        if places == 2:
            return jnp.stack([(block >> 2) ^ core, block & 3])
        apart = (block >> 1) ^ tensor
        return jnp.stack([(apart >> 1) | ((apart & 1) << 1), block & 1])

    places_of = (1, 2, 4, 4)
    first_at = [spots(FIRST_CODES, n) for n in places_of]
    last_at = [spots(LAST_CODES, n) for n in places_of]

    first0 = [(own0, 0, 0), (swap0, 0, 0), (m_own0, 0, 0), (m_swap0, 0, 0)]
    first1 = [(own12, 0, 0), (swap12, 0, 0), (m_own12, 0, 0), (m_swap12, 0, 0)]
    first2 = [(array, 0, mid_cols) for array, _, _ in first1]
    firsts = (first0, first1, first2)
    widths = (2 * HD + cut, mid_cols, heads[2] * HD)

    def first_part(code, rows, chunk):
        return project(rows, first_at[code], firsts[chunk], widths[chunk])

    sums = {}
    sums[0, 0] = first_part(0, rows0, 0)
    m_e0 = across_middle(after(e0, m_own12, sums[0, 0]))
    late = jnp.stack([own12, swap12])
    e1 = to_middle(after(late[:, :, :mid_cols], e0))
    across3 = over_x(after(end3, across2))
    beside_half = over_group(after(half, end3), MIDDLE, 1)
    for chunk in (1, 2):
        sums[0, chunk] = first_part(0, rows0, chunk)
    for chunk in range(3):
        sums[2, chunk] = first_part(2, rows2, chunk)
    rows3 = whole(end3, across3)
    m_e1 = across_middle(after(e1, m_swap12, *[sums[0, c] for c in (1, 2)], *[sums[2, c] for c in range(3)]))
    e2 = to_middle(after(late[:, :, mid_cols:], e1))
    for chunk in range(3):
        sums[3, chunk] = first_part(3, rows3, chunk)

    bias = lax.dynamic_slice_in_dim(q_bias, y * half_cols, half_cols, 0)[None, :]
    kv_bias_here = lax.dynamic_slice_in_dim(kv_bias, (2 * tensor + y) * HD, HD, 1)
    inverse_freq = THETA ** (-2.0 * jnp.arange(HD // 2, dtype=jnp.float32) / HD)
    tables = []
    for code in range(4):
        _, offset, places = token_layout(prefix_lens, assignment, group ^ code, tok_rows)
        angles = offset.astype(jnp.float32)[:, None] * inverse_freq[None, :]
        cosine, sine = jnp.cos(angles), jnp.sin(angles)
        cosine = jnp.concatenate([cosine, cosine], axis=1)
        sine = jnp.concatenate([-sine, sine], axis=1)
        tables.append((cosine, sine, (places - offset)[:, None]))

    last0 = [(e0, 0, 0), (e0, 1, 0), (m_e0, 0, 0), (m_e0, 1, 0)]
    keys_values, outs = {}, {}

    def finish(code, rows, chunk, lasts, total, place):
        total = project(rows, last_at[code], lasts, widths[chunk], total)
        cosine, sine, first = tables[code]
        if chunk == 0:
            keys = total[:, :HD] + kv_bias_here[0]
            swapped = jnp.concatenate([keys[:, HD // 2 :], keys[:, : HD // 2]], axis=1)
            keys = (keys * cosine + swapped * sine).astype(jnp.bfloat16)
            values = (total[:, HD : 2 * HD] + kv_bias_here[1]).astype(jnp.bfloat16)
            keys_values[code] = (keys, values)
        keys, values = keys_values[code]
        out = attend(
            total,
            heads[chunk],
            bias[:, place : place + heads[chunk] * HD],
            cosine,
            sine,
            keys,
            values,
            first,
        )
        outs[code, chunk] = jnp.concatenate([keys, values, out], axis=1) if chunk == 0 else out

    def send_back(chunk):
        return (
            over_group(outs[1, chunk], MIDDLE, 1),
            over_group(outs[2, chunk], MIDDLE, 2),
            over_group(outs[3, chunk], MIDDLE, 3),
        )

    for code, rows in ((0, rows0), (2, rows2), (3, rows3)):
        finish(code, rows, 0, last0, sums[code, 0], 0)
    m_e2 = across_middle(after(e2, m_e0, *[outs[c, 0] for c in (0, 2, 3)]))
    rows1 = jnp.stack([beside_half, over_core(beside_half)])
    for chunk in range(3):
        sums[1, chunk] = first_part(1, rows1, chunk)
    finish(1, rows1, 0, last0, sums[1, 0], 0)
    all_rows = (rows0, rows1, rows2, rows3)
    back = [send_back(0)]
    last1 = [(e1, 0, 0), (e1, 1, 0), (m_e1, 0, 0), (m_e1, 1, 0)]
    last2 = [(e2, 0, 0), (e2, 1, 0), (m_e2, 0, 0), (m_e2, 1, 0)]
    for chunk, lasts, place in ((1, last1, cut), (2, last2, cut + mid_cols)):
        for code in (2, 3, 1, 0):
            finish(code, all_rows[code], chunk, lasts, sums[code, chunk], place)
        back.append(send_back(chunk))

    mine, its = [], []
    for chunk in range(3):
        beside, back_own, back_other = back[chunk]
        mine.append(jnp.where(is_middle, outs[0, chunk], back_own))
        its.append(jnp.where(is_middle, beside, back_other))

    def in_order(a, b):
        return jnp.where(y == 0, jnp.concatenate([a, b], axis=-1), jnp.concatenate([b, a], axis=-1))

    context = in_order(
        jnp.concatenate([mine[0][:, 2 * HD :]] + mine[1:], axis=1),
        jnp.concatenate([its[0][:, 2 * HD :]] + its[1:], axis=1),
    )
    kv_cache = in_order(
        mine[0][:, : 2 * HD].reshape(tok_rows, 2, HD), its[0][:, : 2 * HD].reshape(tok_rows, 2, HD)
    )
    return (context, kv_cache)


def solution(mesh):
    placed = (
        P("group", None),
        P(),
        P("group", "tensor"),
        P("tensor"),
        P("group", None, None),
        P(),
        P(),
        P(),
    )
    fits = mesh.shape["group"] == 8 and mesh.shape["tensor"] == 4
    return jax.shard_map(
        middle_form if fits else gathered_form,
        mesh=mesh,
        in_specs=placed,
        out_specs=(P("group", "tensor"), P("group", None, "tensor")),
        check_vma=False,
    )
```

```python
import functools
import math

import jax
import jax.numpy as jnp
from jax import lax
from jax.experimental import pallas as pl
from jax.experimental.pallas import tpu as pltpu
from jax.sharding import PartitionSpec as P

HD = 128


EPS = 1e-06
THETA = 1000000.0
QROWS = 128
MAXLEN = 256


def token_layout(prefix_lens, assignment, group_id, tok_rows):
    rollouts = prefix_lens.shape[0]
    member = assignment == group_id
    own_lens = jnp.where(member, prefix_lens, 0)
    starts = jnp.cumsum(own_lens) - own_lens
    places = jnp.arange(tok_rows, dtype=jnp.int32)
    inside = (
        member[None, :]
        & (places[:, None] >= starts[None, :])
        & (places[:, None] < (starts + own_lens)[None, :])
    )
    owner_id = jnp.sum(jnp.where(inside, jnp.arange(rollouts, dtype=jnp.int32)[None, :], 0), axis=1)
    offset = places - jnp.sum(jnp.where(inside, starts[None, :], 0), axis=1)
    return (owner_id, offset, places)


def rotate(values, offset):
    half_dim = values.shape[-1] // 2
    inverse_freq = THETA ** (-2.0 * jnp.arange(half_dim, dtype=jnp.float32) / values.shape[-1])
    angles = offset.astype(jnp.float32)[:, None] * inverse_freq[None, :]
    cosine = jnp.cos(angles)[:, None, :]
    sine_part = jnp.sin(angles)[:, None, :]
    first_half = values[..., :half_dim]
    second_half = values[..., half_dim:]
    return jnp.concatenate(
        [
            first_half * cosine - second_half * sine_part,
            second_half * cosine + first_half * sine_part,
        ],
        axis=-1,
    )


def add_product(normed, portion):
    return jnp.dot(normed, portion, preferred_element_type=jnp.float32)


def normalise(hidden, norm_gain):
    widened = hidden.astype(jnp.float32)
    return (
        widened * lax.rsqrt(jnp.mean(widened * widened, axis=-1, keepdims=True) + EPS) * norm_gain
    ).astype(jnp.bfloat16)


def gathered_form(
    hidden, norm_gain, q_weight, q_bias, kv_weight, kv_bias, prefix_lens, assignment
):
    tok_rows, features = hidden.shape
    slice_rows = kv_weight.shape[0]
    q_cols = q_weight.shape[1]
    kv_total = kv_weight.shape[2]
    heads_here = q_cols // HD
    tensor_pos = lax.axis_index("tensor")
    kv_cols = kv_total // lax.axis_size("tensor")
    normed = normalise(hidden, norm_gain)
    queries = add_product(normed, lax.all_gather(q_weight, "group", axis=0, tiled=True)) + q_bias
    head_span = max(kv_cols, HD)
    head_base = tensor_pos * kv_cols // head_span * head_span
    local_start = tensor_pos * kv_cols - head_base
    head_rows = lax.dynamic_slice_in_dim(kv_weight, head_base, head_span, 2).reshape(
        slice_rows, 2 * head_span
    )
    projected = add_product(normed, lax.all_gather(head_rows, "group", axis=0, tiled=True))
    projected = projected.reshape(tok_rows, 2, head_span) + lax.dynamic_slice_in_dim(
        kv_bias, head_base, head_span, 1
    )
    kv_here = head_span // HD
    group_size = heads_here // kv_here
    owner_id, offset, places = token_layout(
        prefix_lens, assignment, lax.axis_index("group"), tok_rows
    )
    rotated_queries = rotate(queries.reshape(tok_rows, heads_here, HD), offset).astype(jnp.bfloat16)
    rotated_keys = rotate(projected[:, 0].reshape(tok_rows, kv_here, HD), offset).astype(
        jnp.bfloat16
    )
    value_heads = projected[:, 1].reshape(tok_rows, kv_here, HD).astype(jnp.bfloat16)
    visible = (owner_id[:, None] == owner_id[None, :]) & (places[None, :] <= places[:, None])
    grouped = rotated_queries.reshape(tok_rows, kv_here, group_size, HD)
    scores = jnp.einsum(
        "qgph,kgh->gpqk", grouped, rotated_keys, preferred_element_type=jnp.float32
    ) / math.sqrt(HD)
    scores = jnp.where(visible[None, None], scores, -jnp.inf)
    row_max = jnp.max(scores, axis=-1, keepdims=True)
    exponent = jnp.exp(scores - row_max)
    weights_bf = (exponent / jnp.sum(exponent, axis=-1, keepdims=True)).astype(jnp.bfloat16)
    context = jnp.einsum(
        "gpqk,kgh->qgph", weights_bf, value_heads, preferred_element_type=jnp.float32
    )
    context = context.astype(jnp.bfloat16).reshape(tok_rows, q_cols)
    stacked = jnp.stack(
        [rotated_keys.reshape(tok_rows, head_span), value_heads.reshape(tok_rows, head_span)],
        axis=1,
    )
    kv_cache = lax.dynamic_slice_in_dim(stacked, local_start, kv_cols, 2)
    return (context, kv_cache)


def attention_kernel(q_ref, bias_ref, cos_ref, sin_ref, k_ref, v_ref, first_ref, out_ref):
    rows, cols = out_ref.shape
    heads = cols // HD
    skip = q_ref.shape[1] - cols
    cosine, sine = cos_ref[...], sin_ref[...]
    turned = []
    for head in range(heads):
        at = head * HD
        query = q_ref[:, skip + at : skip + at + HD] + bias_ref[:, at : at + HD]
        query = query * cosine + pltpu.roll(query, HD // 2, 1) * sine
        turned.append(query.astype(jnp.bfloat16))
    for block in range(rows // QROWS):
        top = block * QROWS
        low = max(0, top - MAXLEN)
        end = top + QROWS
        span = end - low
        stacked = jnp.concatenate([query[top:end] for query in turned], axis=0)
        scores = lax.dot_general(
            stacked, k_ref[low:end], (((1,), (1,)), ((), ())), preferred_element_type=jnp.float32
        ) * (1.0 / math.sqrt(HD))
        row = lax.broadcasted_iota(jnp.int32, (QROWS, span), 0) + top
        col = lax.broadcasted_iota(jnp.int32, (QROWS, span), 1) + low
        visible = (col <= row) & (col >= first_ref[top:end])
        scores = jnp.where(visible[None], scores.reshape(heads, QROWS, span), -jnp.inf)
        exponent = jnp.exp(scores - jnp.max(scores, axis=-1, keepdims=True))
        weights = (exponent / jnp.sum(exponent, axis=-1, keepdims=True)).astype(jnp.bfloat16)
        context = jnp.dot(
            weights.reshape(heads * QROWS, span), v_ref[low:end], preferred_element_type=jnp.float32
        ).astype(jnp.bfloat16)
        for head in range(heads):
            out_ref[top:end, head * HD : (head + 1) * HD] = context[
                head * QROWS : (head + 1) * QROWS
            ]


def attend(queries, heads, bias, cosine, sine, keys, values, first):
    rows = queries.shape[0]
    return pl.pallas_call(
        attention_kernel,
        out_shape=jax.ShapeDtypeStruct((rows, heads * HD), jnp.bfloat16),
        compiler_params=pltpu.CompilerParams(vmem_limit_bytes=40 * 2**20),
        cost_estimate=pl.CostEstimate(
            flops=4 * heads * rows * 3 * QROWS * HD,
            bytes_accessed=rows * heads * HD * 6 + rows * HD * 12,
            transcendentals=heads * rows * 3 * QROWS,
        ),
    )(queries, bias, cosine, sine, keys, values, first)


def norm_kernel(part_ref, hidden_ref, gain_ref, out_ref, part_out_ref):
    widened = hidden_ref[...].astype(jnp.float32)
    scale = lax.rsqrt(jnp.mean(widened * widened, axis=-1, keepdims=True) + EPS)
    out_ref[...] = (widened * scale * gain_ref[...]).astype(jnp.bfloat16)
    width = part_out_ref.shape[1]
    part_out_ref[...] = out_ref[:, pl.ds(pl.multiple_of(part_ref[0] * width, width), width)]


def norm(hidden, norm_gain, part, width):
    rows, features = hidden.shape
    step = 64
    return pl.pallas_call(
        norm_kernel,
        grid_spec=pltpu.PrefetchScalarGridSpec(
            num_scalar_prefetch=1,
            grid=(rows // step,),
            in_specs=[
                pl.BlockSpec((step, features), lambda i, part: (i, 0)),
                pl.BlockSpec((1, features), lambda i, part: (0, 0)),
            ],
            out_specs=[
                pl.BlockSpec((step, features), lambda i, part: (i, 0)),
                pl.BlockSpec((step, width), lambda i, part: (i, 0)),
            ],
        ),
        out_shape=[
            jax.ShapeDtypeStruct((rows, features), jnp.bfloat16),
            jax.ShapeDtypeStruct((rows, width), jnp.bfloat16),
        ],
        compiler_params=pltpu.CompilerParams(vmem_limit_bytes=32 * 2**20),
        cost_estimate=pl.CostEstimate(
            flops=4 * rows * features, bytes_accessed=5 * rows * features, transcendentals=rows
        ),
    )(part[None], hidden, norm_gain[None])


def project_kernel(sources, leads, first_col, width, with_totals, pick_ref, *refs):
    sets, count = len(sources), len(leads)
    refs = list(refs)

    def take(number):
        taken = refs[:number]
        del refs[:number]
        return taken

    row_refs = [take(number) for number in sources]
    weight_refs = take(count)
    totals = take(sets) if with_totals else [None] * sets
    outs = take(sets)
    row_buf, weight_buf, row_sem, weight_sem = refs
    depth = weight_buf.shape[1]

    def weight_copy(piece):
        ref, lead = weight_refs[piece], leads[piece]
        ref = ref if lead is None else ref.at[lead]
        skip = first_col if ref.shape[1] > width else 0
        return pltpu.make_async_copy(
            ref.at[:, skip : skip + width], weight_buf.at[piece], weight_sem.at[piece]
        )

    def row_copy(which, piece, source):
        at = pl.multiple_of(pick_ref[which, 1, piece] * depth, depth)
        return pltpu.make_async_copy(
            row_refs[which][source].at[:, pl.ds(at, depth)],
            row_buf.at[which, piece],
            row_sem.at[which, piece],
        )

    for piece in range(count):
        weight_copy(piece).start()
        for which in range(sets):
            if sources[which] == 1:
                row_copy(which, piece, 0).start()
            else:
                for source in range(sources[which]):

                    @pl.when(pick_ref[which, 0, piece] == source)
                    def _():
                        row_copy(which, piece, source).start()

    for piece in range(count):
        weight_copy(piece).wait()
        for which in range(sets):
            row_copy(which, piece, 0).wait()
            term = jnp.dot(
                row_buf[which, piece], weight_buf[piece], preferred_element_type=jnp.float32
            )
            if piece > 0:
                outs[which][...] += term
            elif totals[which] is None:
                outs[which][...] = term
            else:
                outs[which][...] = totals[which][...] + term


def project(row_sets, picks, pieces, first_col, width, totals=None):
    sets, count = len(row_sets), len(pieces)
    sources = tuple(len(rows) for rows in row_sets)
    leads = tuple(lead for _, lead in pieces)
    tokens, depth = row_sets[0][0].shape[0], pieces[0][0].shape[-2]
    operands = [array for rows in row_sets for array in rows] + [array for array, _ in pieces]
    in_specs = [pl.BlockSpec(memory_space=pl.ANY)] * len(operands)
    if totals is not None:
        for total in totals:
            at = first_col // width if total.shape[1] > width else 0
            in_specs.append(
                pl.BlockSpec((tokens, width), functools.partial(lambda at, i, pick: (0, at), at))
            )
            operands.append(total)
    out = pl.BlockSpec((tokens, width), lambda i, pick: (0, 0))
    return pl.pallas_call(
        functools.partial(
            project_kernel, sources, leads, first_col, width, totals is not None
        ),
        grid_spec=pltpu.PrefetchScalarGridSpec(
            num_scalar_prefetch=1,
            grid=(1,),
            in_specs=in_specs,
            out_specs=[out] * sets,
            scratch_shapes=[
                pltpu.VMEM((sets, count, tokens, depth), jnp.bfloat16),
                pltpu.VMEM((count, depth, width), jnp.bfloat16),
                pltpu.SemaphoreType.DMA((sets, count)),
                pltpu.SemaphoreType.DMA((count,)),
            ],
        ),
        out_shape=[jax.ShapeDtypeStruct((tokens, width), jnp.float32)] * sets,
        compiler_params=pltpu.CompilerParams(vmem_limit_bytes=52 * 2**20),
        cost_estimate=pl.CostEstimate(
            flops=2 * sets * count * tokens * depth * width,
            bytes_accessed=2 * count * depth * (sets * tokens + width) + 8 * sets * tokens * width,
            transcendentals=0,
        ),
    )(jnp.stack(picks), *operands)


MIDDLE = (2, 3, 4, 5)
ENDS = (0, 1, 6, 7)


def pairs_from(sources, code):
    return [(s, s ^ code) for s in sources]


def middle_form(hidden, norm_gain, q_weight, q_bias, kv_weight, kv_bias, prefix_lens, assignment):
    tok_rows, features = hidden.shape
    slice_rows, q_cols = q_weight.shape
    half_cols = q_cols // 2
    group = lax.axis_index("group")
    tensor = lax.axis_index("tensor")
    y = group & 1
    is_middle = (group >= 2) & (group < 6)
    barrier = lax.optimization_barrier

    def over_group(value, sources, code):
        return lax.ppermute(value, "group", pairs_from(sources, code))

    def to_middle(value):
        return over_group(value, ENDS, 2)

    def across_middle(value):
        return over_group(value, MIDDLE, 6)

    def over_x(value):
        return lax.ppermute(value, "tensor", pairs_from(range(4), 2))

    def over_core(value):
        return lax.ppermute(value, "tensor", pairs_from(range(4), 1))

    heads = (2, 4, 2)
    widths = (2 * HD + heads[0] * HD, heads[1] * HD, heads[2] * HD)
    begin = (0, widths[0], widths[0] + widths[1])
    every = sum(widths)

    def columns(half):
        head = (2 * tensor + half) * HD
        kv_part = lax.dynamic_slice_in_dim(kv_weight, head, HD, 2).reshape(slice_rows, 2 * HD)
        q_part = lax.dynamic_slice_in_dim(q_weight, half * half_cols, half_cols, 1)
        return jnp.concatenate([kv_part, q_part], axis=1)

    def both(one, two, chunk):
        low, high = begin[chunk], begin[chunk] + widths[chunk]
        return jnp.stack([one[:, low:high], two[:, low:high]])

    def pick(code_of_rows, codes):
        block = jnp.stack([group ^ code for code in codes])
        if code_of_rows == 0:
            return jnp.stack([block * 0, block])
        return jnp.stack([(block >> 1) ^ tensor, block & 1])

    def projected(sets, codes, pieces, chunk, totals=None):
        first, width = (0, every) if chunk is None else (begin[chunk], widths[chunk])
        return project(
            [rows_of[c] for c in sets],
            [pick(c, codes) for c in sets],
            [pieces[code] for code in codes],
            first,
            width,
            totals,
        )

    own = columns(y)
    other = columns(1 - y)
    m_own = across_middle(own)
    swap = over_group(other, range(8), 1)
    normed, quarter = norm(hidden, norm_gain, tensor, features // 4)
    end2 = to_middle(quarter)

    bias = lax.dynamic_slice_in_dim(q_bias, y * half_cols, half_cols, 0)[None, :]
    kv_bias_here = lax.dynamic_slice_in_dim(kv_bias, (2 * tensor + y) * HD, HD, 1)
    inverse_freq = THETA ** (-2.0 * jnp.arange(HD // 2, dtype=jnp.float32) / HD)
    own, swap, m_own, normed, quarter, end2 = barrier((own, swap, m_own, normed, quarter, end2))

    rows_of = {0: [normed]}
    m_swap = across_middle(swap[:, : begin[2]])
    e0 = to_middle(both(own, swap, 0))
    end3 = over_group(end2, MIDDLE, 1)
    across2 = over_x(end2)
    twin2 = over_core(end2)
    early = {0: (own, None), 1: (swap, None), 6: (m_own, None)}
    sums = {0: projected([0], (0, 1, 6), early, None)[0]}
    tables = []
    for code in range(4):
        _, offset, places = token_layout(prefix_lens, assignment, group ^ code, tok_rows)
        angles = offset.astype(jnp.float32)[:, None] * inverse_freq[None, :]
        cosine, sine = jnp.cos(angles), jnp.sin(angles)
        cosine = jnp.concatenate([cosine, cosine], axis=1)
        sine = jnp.concatenate([-sine, sine], axis=1)
        tables.append((cosine, sine, (places - offset)[:, None]))
    (own, swap, m_swap, e0, end2, end3, across2, twin2, sums[0], tables, quarter) = barrier(
        (own, swap, m_swap, e0, end2, end3, across2, twin2, sums[0], tables, quarter)
    )

    m_e0 = across_middle(e0)
    e1 = to_middle(both(own, swap, 1))
    end1 = over_group(quarter, MIDDLE, 1)
    across3 = over_x(end3)
    far2 = over_core(across2)
    rows_of[2] = [end2, twin2, across2, far2]
    sums[2] = projected([2], (0, 1, 6), early, None)[0]
    (own, swap, m_e0, e0, e1, end1, end3, across3, far2, sums[2]) = barrier(
        (own, swap, m_e0, e0, e1, end1, end3, across3, far2, sums[2])
    )
    rows_of[2] = [end2, twin2, across2, far2]

    m_e1 = across_middle(e1)
    e2 = to_middle(both(own, swap, 2))
    across1 = over_x(end1)
    twin3 = over_core(end3)
    far3 = over_core(across3)
    rows_of[3] = [end3, twin3, across3, far3]
    sums[3] = projected([3], (0, 1, 6), early, None)[0]

    keys_values, outs = {}, {}

    def attended(code, chunk, total):
        cosine, sine, first = tables[code]
        if chunk == 0:
            keys = total[:, :HD] + kv_bias_here[0]
            swapped = jnp.concatenate([keys[:, HD // 2 :], keys[:, : HD // 2]], axis=1)
            keys = (keys * cosine + swapped * sine).astype(jnp.bfloat16)
            values = (total[:, HD : 2 * HD] + kv_bias_here[1]).astype(jnp.bfloat16)
            keys_values[code] = (keys, values)
        keys, values = keys_values[code]
        place = sum(heads[:chunk]) * HD
        out = attend(
            total,
            heads[chunk],
            bias[:, place : place + heads[chunk] * HD],
            cosine,
            sine,
            keys,
            values,
            first,
        )
        outs[code, chunk] = jnp.concatenate([keys, values, out], axis=1) if chunk == 0 else out

    def send_back(code, chunk):
        return over_group(outs[code, chunk], MIDDLE, code)

    late = (7, 2, 3, 4, 5)
    late0 = {7: (m_swap, None), 2: (e0, 0), 3: (e0, 1), 4: (m_e0, 0), 5: (m_e0, 1)}
    three = (2, 3, 0)
    totals = projected(three, late, late0, 0, [sums[c] for c in three])
    for code, total in zip(three, totals):
        attended(code, 0, total)
    back = {(code, 0): send_back(code, 0) for code in (2, 3)}
    (swap, m_e1, e1, e2, end1, across1, back[2, 0], back[3, 0], outs[0, 0], sums[3]) = barrier(
        (swap, m_e1, e1, e2, end1, across1, back[2, 0], back[3, 0], outs[0, 0], sums[3])
    )

    last = jnp.concatenate([swap[None, :, begin[2] :], e2])
    m_last = across_middle(last)
    twin1 = over_core(end1)
    far1 = over_core(across1)
    rows_of[1] = [end1, twin1, across1, far1]
    late1 = {7: (m_swap, None), 2: (e1, 0), 3: (e1, 1), 4: (m_e1, 0), 5: (m_e1, 1)}
    totals = projected(three, late, late1, 1, [sums[c] for c in three])
    for code, total in zip(three, totals):
        attended(code, 1, total)
    sums[1] = projected([1], (0, 1, 6), early, None)[0]
    for chunk, pieces in ((0, late0), (1, late1)):
        attended(1, chunk, projected([1], late, pieces, chunk, [sums[1]])[0])
    back[1, 0] = send_back(1, 0)
    for code in (2, 3, 1):
        back[code, 1] = send_back(code, 1)
    (m_last, *ready) = barrier((m_last, *[outs[c, 1] for c in range(4)]))
    for code in range(4):
        outs[code, 1] = ready[code]

    late2 = {7: (m_last, 0), 2: (e2, 0), 3: (e2, 1), 4: (m_last, 1), 5: (m_last, 2)}
    order = (3, 2, 1, 0)
    totals = projected(order, late, late2, 2, [sums[c] for c in order])
    for code, total in zip(order, totals):
        attended(code, 2, total)
        if code > 0:
            back[code, 2] = send_back(code, 2)

    mine, its = [], []
    for chunk in range(3):
        beside, back_own, back_other = (back[code, chunk] for code in (1, 2, 3))
        mine.append(jnp.where(is_middle, outs[0, chunk], back_own))
        its.append(jnp.where(is_middle, beside, back_other))

    def in_order(a, b):
        return jnp.where(y == 0, jnp.concatenate([a, b], axis=-1), jnp.concatenate([b, a], axis=-1))

    context = in_order(
        jnp.concatenate([mine[0][:, 2 * HD :]] + mine[1:], axis=1),
        jnp.concatenate([its[0][:, 2 * HD :]] + its[1:], axis=1),
    )
    kv_cache = in_order(
        mine[0][:, : 2 * HD].reshape(tok_rows, 2, HD), its[0][:, : 2 * HD].reshape(tok_rows, 2, HD)
    )
    return (context, kv_cache)


def solution(mesh):
    placed = (
        P("group", None),
        P(),
        P("group", "tensor"),
        P("tensor"),
        P("group", None, None),
        P(),
        P(),
        P(),
    )
    fits = mesh.shape["group"] == 8 and mesh.shape["tensor"] == 4
    return jax.shard_map(
        middle_form if fits else gathered_form,
        mesh=mesh,
        in_specs=placed,
        out_specs=(P("group", "tensor"), P("group", None, "tensor")),
        check_vma=False,
    )
```

```python
import functools
import math

import jax
import jax.numpy as jnp
from jax import lax
from jax.experimental import pallas as pl
from jax.experimental.pallas import tpu as pltpu
from jax.sharding import PartitionSpec as P

HD = 128


EPS = 1e-06
THETA = 1000000.0
QROWS = 128
MAXLEN = 256


def token_layout(prefix_lens, assignment, group_id, tok_rows):
    rollouts = prefix_lens.shape[0]
    member = assignment == group_id
    own_lens = jnp.where(member, prefix_lens, 0)
    starts = jnp.cumsum(own_lens) - own_lens
    places = jnp.arange(tok_rows, dtype=jnp.int32)
    inside = (
        member[None, :]
        & (places[:, None] >= starts[None, :])
        & (places[:, None] < (starts + own_lens)[None, :])
    )
    owner_id = jnp.sum(jnp.where(inside, jnp.arange(rollouts, dtype=jnp.int32)[None, :], 0), axis=1)
    offset = places - jnp.sum(jnp.where(inside, starts[None, :], 0), axis=1)
    return (owner_id, offset, places)


def rotate(values, offset):
    half_dim = values.shape[-1] // 2
    inverse_freq = THETA ** (-2.0 * jnp.arange(half_dim, dtype=jnp.float32) / values.shape[-1])
    angles = offset.astype(jnp.float32)[:, None] * inverse_freq[None, :]
    cosine = jnp.cos(angles)[:, None, :]
    sine_part = jnp.sin(angles)[:, None, :]
    first_half = values[..., :half_dim]
    second_half = values[..., half_dim:]
    return jnp.concatenate(
        [
            first_half * cosine - second_half * sine_part,
            second_half * cosine + first_half * sine_part,
        ],
        axis=-1,
    )


def add_product(normed, portion):
    return jnp.dot(normed, portion, preferred_element_type=jnp.float32)


def normalise(hidden, norm_gain):
    widened = hidden.astype(jnp.float32)
    return (
        widened * lax.rsqrt(jnp.mean(widened * widened, axis=-1, keepdims=True) + EPS) * norm_gain
    ).astype(jnp.bfloat16)


def gathered_form(
    hidden, norm_gain, q_weight, q_bias, kv_weight, kv_bias, prefix_lens, assignment
):
    tok_rows, features = hidden.shape
    slice_rows = kv_weight.shape[0]
    q_cols = q_weight.shape[1]
    kv_total = kv_weight.shape[2]
    heads_here = q_cols // HD
    tensor_pos = lax.axis_index("tensor")
    kv_cols = kv_total // lax.axis_size("tensor")
    normed = normalise(hidden, norm_gain)
    queries = add_product(normed, lax.all_gather(q_weight, "group", axis=0, tiled=True)) + q_bias
    head_span = max(kv_cols, HD)
    head_base = tensor_pos * kv_cols // head_span * head_span
    local_start = tensor_pos * kv_cols - head_base
    head_rows = lax.dynamic_slice_in_dim(kv_weight, head_base, head_span, 2).reshape(
        slice_rows, 2 * head_span
    )
    projected = add_product(normed, lax.all_gather(head_rows, "group", axis=0, tiled=True))
    projected = projected.reshape(tok_rows, 2, head_span) + lax.dynamic_slice_in_dim(
        kv_bias, head_base, head_span, 1
    )
    kv_here = head_span // HD
    group_size = heads_here // kv_here
    owner_id, offset, places = token_layout(
        prefix_lens, assignment, lax.axis_index("group"), tok_rows
    )
    rotated_queries = rotate(queries.reshape(tok_rows, heads_here, HD), offset).astype(jnp.bfloat16)
    rotated_keys = rotate(projected[:, 0].reshape(tok_rows, kv_here, HD), offset).astype(
        jnp.bfloat16
    )
    value_heads = projected[:, 1].reshape(tok_rows, kv_here, HD).astype(jnp.bfloat16)
    visible = (owner_id[:, None] == owner_id[None, :]) & (places[None, :] <= places[:, None])
    grouped = rotated_queries.reshape(tok_rows, kv_here, group_size, HD)
    scores = jnp.einsum(
        "qgph,kgh->gpqk", grouped, rotated_keys, preferred_element_type=jnp.float32
    ) / math.sqrt(HD)
    scores = jnp.where(visible[None, None], scores, -jnp.inf)
    row_max = jnp.max(scores, axis=-1, keepdims=True)
    exponent = jnp.exp(scores - row_max)
    weights_bf = (exponent / jnp.sum(exponent, axis=-1, keepdims=True)).astype(jnp.bfloat16)
    context = jnp.einsum(
        "gpqk,kgh->qgph", weights_bf, value_heads, preferred_element_type=jnp.float32
    )
    context = context.astype(jnp.bfloat16).reshape(tok_rows, q_cols)
    stacked = jnp.stack(
        [rotated_keys.reshape(tok_rows, head_span), value_heads.reshape(tok_rows, head_span)],
        axis=1,
    )
    kv_cache = lax.dynamic_slice_in_dim(stacked, local_start, kv_cols, 2)
    return (context, kv_cache)


def attention_kernel(q_ref, bias_ref, cos_ref, sin_ref, k_ref, v_ref, first_ref, out_ref):
    rows, cols = out_ref.shape
    heads = cols // HD
    skip = q_ref.shape[1] - cols
    cosine, sine = cos_ref[...], sin_ref[...]
    turned = []
    for head in range(heads):
        at = head * HD
        query = q_ref[:, skip + at : skip + at + HD] + bias_ref[:, at : at + HD]
        query = query * cosine + pltpu.roll(query, HD // 2, 1) * sine
        turned.append(query.astype(jnp.bfloat16))
    for block in range(rows // QROWS):
        top = block * QROWS
        low = max(0, top - MAXLEN)
        end = top + QROWS
        span = end - low
        stacked = jnp.concatenate([query[top:end] for query in turned], axis=0)
        scores = lax.dot_general(
            stacked, k_ref[low:end], (((1,), (1,)), ((), ())), preferred_element_type=jnp.float32
        ) * (1.0 / math.sqrt(HD))
        row = lax.broadcasted_iota(jnp.int32, (QROWS, span), 0) + top
        col = lax.broadcasted_iota(jnp.int32, (QROWS, span), 1) + low
        visible = (col <= row) & (col >= first_ref[top:end])
        scores = jnp.where(visible[None], scores.reshape(heads, QROWS, span), -jnp.inf)
        exponent = jnp.exp(scores - jnp.max(scores, axis=-1, keepdims=True))
        weights = (exponent / jnp.sum(exponent, axis=-1, keepdims=True)).astype(jnp.bfloat16)
        context = jnp.dot(
            weights.reshape(heads * QROWS, span), v_ref[low:end], preferred_element_type=jnp.float32
        ).astype(jnp.bfloat16)
        for head in range(heads):
            out_ref[top:end, head * HD : (head + 1) * HD] = context[
                head * QROWS : (head + 1) * QROWS
            ]


def attend(queries, heads, bias, cosine, sine, keys, values, first):
    rows = queries.shape[0]
    return pl.pallas_call(
        attention_kernel,
        out_shape=jax.ShapeDtypeStruct((rows, heads * HD), jnp.bfloat16),
        compiler_params=pltpu.CompilerParams(vmem_limit_bytes=40 * 2**20),
        cost_estimate=pl.CostEstimate(
            flops=4 * heads * rows * 3 * QROWS * HD,
            bytes_accessed=rows * heads * HD * 6 + rows * HD * 12,
            transcendentals=heads * rows * 3 * QROWS,
        ),
    )(queries, bias, cosine, sine, keys, values, first)


def norm_kernel(part_ref, hidden_ref, gain_ref, out_ref, part_out_ref):
    widened = hidden_ref[...].astype(jnp.float32)
    scale = lax.rsqrt(jnp.mean(widened * widened, axis=-1, keepdims=True) + EPS)
    out_ref[...] = (widened * scale * gain_ref[...]).astype(jnp.bfloat16)
    width = part_out_ref.shape[1]
    part_out_ref[...] = out_ref[:, pl.ds(pl.multiple_of(part_ref[0] * width, width), width)]


def norm(hidden, norm_gain, part, width):
    rows, features = hidden.shape
    step = 64
    return pl.pallas_call(
        norm_kernel,
        grid_spec=pltpu.PrefetchScalarGridSpec(
            num_scalar_prefetch=1,
            grid=(rows // step,),
            in_specs=[
                pl.BlockSpec((step, features), lambda i, part: (i, 0)),
                pl.BlockSpec((1, features), lambda i, part: (0, 0)),
            ],
            out_specs=[
                pl.BlockSpec((step, features), lambda i, part: (i, 0)),
                pl.BlockSpec((step, width), lambda i, part: (i, 0)),
            ],
        ),
        out_shape=[
            jax.ShapeDtypeStruct((rows, features), jnp.bfloat16),
            jax.ShapeDtypeStruct((rows, width), jnp.bfloat16),
        ],
        compiler_params=pltpu.CompilerParams(vmem_limit_bytes=32 * 2**20),
        cost_estimate=pl.CostEstimate(
            flops=4 * rows * features, bytes_accessed=5 * rows * features, transcendentals=rows
        ),
    )(part[None], hidden, norm_gain[None])


def project_kernel(sources, leads, first_col, width, with_totals, pick_ref, *refs):
    sets, count = len(sources), len(leads)
    refs = list(refs)

    def take(number):
        taken = refs[:number]
        del refs[:number]
        return taken

    row_refs = [take(number) for number in sources]
    weight_refs = take(count)
    totals = take(sets) if with_totals else [None] * sets
    outs = take(sets)
    row_buf, weight_buf, row_sem, weight_sem = refs
    depth = weight_buf.shape[0] // count
    tokens = row_buf.shape[0] // sets

    def weight_copy(piece):
        ref, lead = weight_refs[piece], leads[piece]
        ref = ref if lead is None else ref.at[lead]
        skip = first_col if ref.shape[1] > width else 0
        return pltpu.make_async_copy(
            ref.at[:, skip : skip + width],
            weight_buf.at[piece * depth : (piece + 1) * depth],
            weight_sem.at[piece],
        )

    def row_copy(which, piece, source):
        at = pl.multiple_of(pick_ref[which, 1, piece] * depth, depth)
        return pltpu.make_async_copy(
            row_refs[which][source].at[:, pl.ds(at, depth)],
            row_buf.at[
                which * tokens : (which + 1) * tokens, piece * depth : (piece + 1) * depth
            ],
            row_sem.at[which, piece],
        )

    for piece in range(count):
        weight_copy(piece).start()
        for which in range(sets):
            if sources[which] == 1:
                row_copy(which, piece, 0).start()
            else:
                for source in range(sources[which]):

                    @pl.when(pick_ref[which, 0, piece] == source)
                    def _():
                        row_copy(which, piece, source).start()

    done = 0
    for ready in (count // 2, count):
        for piece in range(done, ready):
            weight_copy(piece).wait()
            for which in range(sets):
                row_copy(which, piece, 0).wait()
        low, high = done * depth, ready * depth
        for which in range(sets):
            for col in range(0, width, 2 * HD):
                cols = slice(col, col + 2 * HD)
                term = jnp.dot(
                    row_buf[which * tokens : (which + 1) * tokens, low:high],
                    weight_buf[low:high, cols],
                    preferred_element_type=jnp.float32,
                )
                if done > 0:
                    outs[which][:, cols] += term
                elif totals[which] is None:
                    outs[which][:, cols] = term
                else:
                    outs[which][:, cols] = totals[which][:, cols] + term
        done = ready


def project(row_sets, picks, pieces, first_col, width, totals=None):
    sets, count = len(row_sets), len(pieces)
    sources = tuple(len(rows) for rows in row_sets)
    leads = tuple(lead for _, lead in pieces)
    tokens, depth = row_sets[0][0].shape[0], pieces[0][0].shape[-2]
    operands = [array for rows in row_sets for array in rows] + [array for array, _ in pieces]
    in_specs = [pl.BlockSpec(memory_space=pl.ANY)] * len(operands)
    if totals is not None:
        for total in totals:
            at = first_col // width if total.shape[1] > width else 0
            in_specs.append(
                pl.BlockSpec((tokens, width), functools.partial(lambda at, i, pick: (0, at), at))
            )
            operands.append(total)
    out = pl.BlockSpec((tokens, width), lambda i, pick: (0, 0))
    return pl.pallas_call(
        functools.partial(
            project_kernel, sources, leads, first_col, width, totals is not None
        ),
        grid_spec=pltpu.PrefetchScalarGridSpec(
            num_scalar_prefetch=1,
            grid=(1,),
            in_specs=in_specs,
            out_specs=[out] * sets,
            scratch_shapes=[
                pltpu.VMEM((sets * tokens, count * depth), jnp.bfloat16),
                pltpu.VMEM((count * depth, width), jnp.bfloat16),
                pltpu.SemaphoreType.DMA((sets, count)),
                pltpu.SemaphoreType.DMA((count,)),
            ],
        ),
        out_shape=[jax.ShapeDtypeStruct((tokens, width), jnp.float32)] * sets,
        compiler_params=pltpu.CompilerParams(vmem_limit_bytes=52 * 2**20),
        cost_estimate=pl.CostEstimate(
            flops=2 * sets * count * tokens * depth * width,
            bytes_accessed=2 * count * depth * (sets * tokens + width) + 8 * sets * tokens * width,
            transcendentals=0,
        ),
    )(jnp.stack(picks), *operands)


MIDDLE = (2, 3, 4, 5)
ENDS = (0, 1, 6, 7)


def after(value, *others):
    return lax.optimization_barrier((value,) + others)[0]


def pairs_from(sources, code):
    return [(s, s ^ code) for s in sources]


def middle_form(hidden, norm_gain, q_weight, q_bias, kv_weight, kv_bias, prefix_lens, assignment):
    tok_rows, features = hidden.shape
    slice_rows, q_cols = q_weight.shape
    half_cols = q_cols // 2
    group = lax.axis_index("group")
    tensor = lax.axis_index("tensor")
    y = group & 1
    is_middle = (group >= 2) & (group < 6)
    barrier = lax.optimization_barrier

    def over_group(value, sources, code):
        return lax.ppermute(value, "group", pairs_from(sources, code))

    def to_middle(value):
        return over_group(value, ENDS, 2)

    def across_middle(value):
        return over_group(value, MIDDLE, 6)

    def over_x(value):
        return lax.ppermute(value, "tensor", pairs_from(range(4), 2))

    def over_core(value):
        return lax.ppermute(value, "tensor", pairs_from(range(4), 1))

    heads = (2, 4, 2)
    widths = (2 * HD + heads[0] * HD, heads[1] * HD, heads[2] * HD)
    begin = (0, widths[0], widths[0] + widths[1])
    every = sum(widths)

    def columns(half):
        head = (2 * tensor + half) * HD
        kv_part = lax.dynamic_slice_in_dim(kv_weight, head, HD, 2).reshape(slice_rows, 2 * HD)
        q_part = lax.dynamic_slice_in_dim(q_weight, half * half_cols, half_cols, 1)
        return jnp.concatenate([kv_part, q_part], axis=1)

    def both(one, two, chunk):
        low, high = begin[chunk], begin[chunk] + widths[chunk]
        return jnp.stack([one[:, low:high], two[:, low:high]])

    def pick(code_of_rows, codes):
        block = jnp.stack([group ^ code for code in codes])
        if code_of_rows == 0:
            return jnp.stack([block * 0, block])
        return jnp.stack([(block >> 1) ^ tensor, block & 1])

    def projected(sets, codes, pieces, chunk, totals=None):
        first, width = (0, every) if chunk is None else (begin[chunk], widths[chunk])
        return project(
            [rows_of[c] for c in sets],
            [pick(c, codes) for c in sets],
            [pieces[code] for code in codes],
            first,
            width,
            totals,
        )

    own = columns(y)
    other = columns(1 - y)
    m_own = across_middle(own)
    swap = over_group(other, range(8), 1)
    normed, quarter = norm(hidden, norm_gain, tensor, features // 4)
    end2 = to_middle(quarter)

    bias = lax.dynamic_slice_in_dim(q_bias, y * half_cols, half_cols, 0)[None, :]
    kv_bias_here = lax.dynamic_slice_in_dim(kv_bias, (2 * tensor + y) * HD, HD, 1)
    inverse_freq = THETA ** (-2.0 * jnp.arange(HD // 2, dtype=jnp.float32) / HD)
    m_swap = across_middle(after(swap, m_own))
    own, swap, m_own, normed, quarter, end2 = barrier((own, swap, m_own, normed, quarter, end2))

    rows_of = {0: [normed]}
    e0 = to_middle(both(own, swap, 0))
    next1, next2 = both(own, swap, 1), both(own, swap, 2)
    end3 = over_group(end2, MIDDLE, 1)
    across2 = over_x(end2)
    twin2 = over_core(end2)
    early = {0: (own, None), 1: (swap, None), 6: (m_own, None)}
    sums = {0: projected([0], (0, 1, 6), early, None)[0]}
    tables = []
    for code in range(4):
        _, offset, places = token_layout(prefix_lens, assignment, group ^ code, tok_rows)
        angles = offset.astype(jnp.float32)[:, None] * inverse_freq[None, :]
        cosine, sine = jnp.cos(angles), jnp.sin(angles)
        cosine = jnp.concatenate([cosine, cosine], axis=1)
        sine = jnp.concatenate([-sine, sine], axis=1)
        tables.append((cosine, sine, (places - offset)[:, None]))
    m_e0 = across_middle(after(e0, m_swap))
    (next1, next2, m_swap, e0, end2, end3, across2, twin2, sums[0], tables, quarter) = barrier(
        (next1, next2, m_swap, e0, end2, end3, across2, twin2, sums[0], tables, quarter)
    )

    e1 = to_middle(next1)
    end1 = over_group(quarter, MIDDLE, 1)
    across3 = over_x(end3)
    far2 = over_core(across2)
    rows_of[2] = [end2, twin2, across2, far2]
    sums[2] = projected([2], (0, 1, 6), early, None)[0]
    m_e1 = across_middle(after(e1, m_e0))
    (next2, m_e0, e0, e1, end1, end3, across3, far2, sums[2]) = barrier(
        (next2, m_e0, e0, e1, end1, end3, across3, far2, sums[2])
    )
    rows_of[2] = [end2, twin2, across2, far2]

    e2 = to_middle(next2)
    across1 = over_x(end1)
    twin3 = over_core(end3)
    far3 = over_core(across3)
    rows_of[3] = [end3, twin3, across3, far3]
    sums[3] = projected([3], (0, 1, 6), early, None)[0]

    keys_values, outs = {}, {}

    def attended(code, chunk, total):
        cosine, sine, first = tables[code]
        if chunk == 0:
            keys = total[:, :HD] + kv_bias_here[0]
            swapped = jnp.concatenate([keys[:, HD // 2 :], keys[:, : HD // 2]], axis=1)
            keys = (keys * cosine + swapped * sine).astype(jnp.bfloat16)
            values = (total[:, HD : 2 * HD] + kv_bias_here[1]).astype(jnp.bfloat16)
            keys_values[code] = (keys, values)
        keys, values = keys_values[code]
        place = sum(heads[:chunk]) * HD
        out = attend(
            total,
            heads[chunk],
            bias[:, place : place + heads[chunk] * HD],
            cosine,
            sine,
            keys,
            values,
            first,
        )
        outs[code, chunk] = jnp.concatenate([keys, values, out], axis=1) if chunk == 0 else out

    def send_back(code, chunk):
        return over_group(outs[code, chunk], MIDDLE, code)

    late = (7, 2, 3, 4, 5)
    late0 = {7: (m_swap, None), 2: (e0, 0), 3: (e0, 1), 4: (m_e0, 0), 5: (m_e0, 1)}
    late1 = {7: (m_swap, None), 2: (e1, 0), 3: (e1, 1)}
    three = (2, 3, 0)
    totals = projected(three, late, late0, 0, [sums[c] for c in three])
    for code, total in zip(three, totals):
        attended(code, 0, total)
    back = {(code, 0): send_back(code, 0) for code in (2, 3)}
    part1 = projected(three, late[:3], late1, 1, [sums[c] for c in three])
    m_e2 = across_middle(after(e2, m_e1))
    (m_e1, e2, end1, across1, outs[0, 0], part1, sums[3]) = barrier(
        (m_e1, e2, end1, across1, outs[0, 0], part1, sums[3])
    )

    twin1 = over_core(end1)
    far1 = over_core(across1)
    rows_of[1] = [end1, twin1, across1, far1]
    late1 = {**late1, 4: (m_e1, 0), 5: (m_e1, 1)}
    totals = projected(three, late[3:], late1, 1, part1)
    for code, total in zip(three, totals):
        attended(code, 1, total)
    for code in (2, 3):
        back[code, 1] = send_back(code, 1)
    sums[1] = projected([1], (0, 1, 6), early, None)[0]
    for chunk, pieces in ((0, late0), (1, late1)):
        attended(1, chunk, projected([1], late, pieces, chunk, [sums[1]])[0])
        back[1, chunk] = send_back(1, chunk)
    (m_e2, *ready) = barrier((m_e2, *[outs[c, 1] for c in range(4)]))
    for code in range(4):
        outs[code, 1] = ready[code]

    late2 = {7: (m_swap, None), 2: (e2, 0), 3: (e2, 1), 4: (m_e2, 0), 5: (m_e2, 1)}
    order = (3, 2, 1, 0)
    totals = projected(order, late, late2, 2, [sums[c] for c in order])
    for code, total in zip(order, totals):
        attended(code, 2, total)
        if code > 0:
            back[code, 2] = send_back(code, 2)

    mine, its = [], []
    for chunk in range(3):
        beside, back_own, back_other = (back[code, chunk] for code in (1, 2, 3))
        mine.append(jnp.where(is_middle, outs[0, chunk], back_own))
        its.append(jnp.where(is_middle, beside, back_other))

    def in_order(a, b):
        return jnp.where(y == 0, jnp.concatenate([a, b], axis=-1), jnp.concatenate([b, a], axis=-1))

    context = in_order(
        jnp.concatenate([mine[0][:, 2 * HD :]] + mine[1:], axis=1),
        jnp.concatenate([its[0][:, 2 * HD :]] + its[1:], axis=1),
    )
    kv_cache = in_order(
        mine[0][:, : 2 * HD].reshape(tok_rows, 2, HD), its[0][:, : 2 * HD].reshape(tok_rows, 2, HD)
    )
    return (context, kv_cache)


def solution(mesh):
    placed = (
        P("group", None),
        P(),
        P("group", "tensor"),
        P("tensor"),
        P("group", None, None),
        P(),
        P(),
        P(),
    )
    fits = mesh.shape["group"] == 8 and mesh.shape["tensor"] == 4
    return jax.shard_map(
        middle_form if fits else gathered_form,
        mesh=mesh,
        in_specs=placed,
        out_specs=(P("group", "tensor"), P("group", None, "tensor")),
        check_vma=False,
    )
```

```python
import functools
import math

import jax
import jax.numpy as jnp
from jax import lax
from jax.experimental import pallas as pl
from jax.experimental.pallas import tpu as pltpu
from jax.sharding import PartitionSpec as P

HD = 128


EPS = 1e-06
THETA = 1000000.0
QROWS = 128
MAXLEN = 256


def token_layout(prefix_lens, assignment, group_id, tok_rows):
    rollouts = prefix_lens.shape[0]
    member = assignment == group_id
    own_lens = jnp.where(member, prefix_lens, 0)
    starts = jnp.cumsum(own_lens) - own_lens
    places = jnp.arange(tok_rows, dtype=jnp.int32)
    inside = (
        member[None, :]
        & (places[:, None] >= starts[None, :])
        & (places[:, None] < (starts + own_lens)[None, :])
    )
    owner_id = jnp.sum(jnp.where(inside, jnp.arange(rollouts, dtype=jnp.int32)[None, :], 0), axis=1)
    offset = places - jnp.sum(jnp.where(inside, starts[None, :], 0), axis=1)
    return (owner_id, offset, places)


def rotate(values, offset):
    half_dim = values.shape[-1] // 2
    inverse_freq = THETA ** (-2.0 * jnp.arange(half_dim, dtype=jnp.float32) / values.shape[-1])
    angles = offset.astype(jnp.float32)[:, None] * inverse_freq[None, :]
    cosine = jnp.cos(angles)[:, None, :]
    sine_part = jnp.sin(angles)[:, None, :]
    first_half = values[..., :half_dim]
    second_half = values[..., half_dim:]
    return jnp.concatenate(
        [
            first_half * cosine - second_half * sine_part,
            second_half * cosine + first_half * sine_part,
        ],
        axis=-1,
    )


def add_product(normed, portion):
    return jnp.dot(normed, portion, preferred_element_type=jnp.float32)


def normalise(hidden, norm_gain):
    widened = hidden.astype(jnp.float32)
    return (
        widened * lax.rsqrt(jnp.mean(widened * widened, axis=-1, keepdims=True) + EPS) * norm_gain
    ).astype(jnp.bfloat16)


def gathered_form(
    hidden, norm_gain, q_weight, q_bias, kv_weight, kv_bias, prefix_lens, assignment
):
    tok_rows, features = hidden.shape
    slice_rows = kv_weight.shape[0]
    q_cols = q_weight.shape[1]
    kv_total = kv_weight.shape[2]
    heads_here = q_cols // HD
    tensor_pos = lax.axis_index("tensor")
    kv_cols = kv_total // lax.axis_size("tensor")
    normed = normalise(hidden, norm_gain)
    queries = add_product(normed, lax.all_gather(q_weight, "group", axis=0, tiled=True)) + q_bias
    head_span = max(kv_cols, HD)
    head_base = tensor_pos * kv_cols // head_span * head_span
    local_start = tensor_pos * kv_cols - head_base
    head_rows = lax.dynamic_slice_in_dim(kv_weight, head_base, head_span, 2).reshape(
        slice_rows, 2 * head_span
    )
    projected = add_product(normed, lax.all_gather(head_rows, "group", axis=0, tiled=True))
    projected = projected.reshape(tok_rows, 2, head_span) + lax.dynamic_slice_in_dim(
        kv_bias, head_base, head_span, 1
    )
    kv_here = head_span // HD
    group_size = heads_here // kv_here
    owner_id, offset, places = token_layout(
        prefix_lens, assignment, lax.axis_index("group"), tok_rows
    )
    rotated_queries = rotate(queries.reshape(tok_rows, heads_here, HD), offset).astype(jnp.bfloat16)
    rotated_keys = rotate(projected[:, 0].reshape(tok_rows, kv_here, HD), offset).astype(
        jnp.bfloat16
    )
    value_heads = projected[:, 1].reshape(tok_rows, kv_here, HD).astype(jnp.bfloat16)
    visible = (owner_id[:, None] == owner_id[None, :]) & (places[None, :] <= places[:, None])
    grouped = rotated_queries.reshape(tok_rows, kv_here, group_size, HD)
    scores = jnp.einsum(
        "qgph,kgh->gpqk", grouped, rotated_keys, preferred_element_type=jnp.float32
    ) / math.sqrt(HD)
    scores = jnp.where(visible[None, None], scores, -jnp.inf)
    row_max = jnp.max(scores, axis=-1, keepdims=True)
    exponent = jnp.exp(scores - row_max)
    weights_bf = (exponent / jnp.sum(exponent, axis=-1, keepdims=True)).astype(jnp.bfloat16)
    context = jnp.einsum(
        "gpqk,kgh->qgph", weights_bf, value_heads, preferred_element_type=jnp.float32
    )
    context = context.astype(jnp.bfloat16).reshape(tok_rows, q_cols)
    stacked = jnp.stack(
        [rotated_keys.reshape(tok_rows, head_span), value_heads.reshape(tok_rows, head_span)],
        axis=1,
    )
    kv_cache = lax.dynamic_slice_in_dim(stacked, local_start, kv_cols, 2)
    return (context, kv_cache)


def norm_kernel(part_ref, hidden_ref, gain_ref, out_ref, part_out_ref):
    widened = hidden_ref[...].astype(jnp.float32)
    scale = lax.rsqrt(jnp.mean(widened * widened, axis=-1, keepdims=True) + EPS)
    normed = (widened * scale * gain_ref[...]).astype(jnp.bfloat16)
    depth = out_ref.shape[2]
    for block in range(out_ref.shape[0]):
        out_ref[block] = normed[:, block * depth : (block + 1) * depth]
    count = part_out_ref.shape[0]
    part_out_ref[...] = out_ref[pl.ds(part_ref[0] * count, count)]


def norm(hidden, norm_gain, part, depth, count):
    rows, features = hidden.shape
    blocks = features // depth
    step = 64
    return pl.pallas_call(
        norm_kernel,
        grid_spec=pltpu.PrefetchScalarGridSpec(
            num_scalar_prefetch=1,
            grid=(rows // step,),
            in_specs=[
                pl.BlockSpec((step, features), lambda i, part: (i, 0)),
                pl.BlockSpec((1, features), lambda i, part: (0, 0)),
            ],
            out_specs=[
                pl.BlockSpec((blocks, step, depth), lambda i, part: (0, i, 0)),
                pl.BlockSpec((count, step, depth), lambda i, part: (0, i, 0)),
            ],
        ),
        out_shape=[
            jax.ShapeDtypeStruct((blocks, rows, depth), jnp.bfloat16),
            jax.ShapeDtypeStruct((count, rows, depth), jnp.bfloat16),
        ],
        compiler_params=pltpu.CompilerParams(vmem_limit_bytes=32 * 2**20),
        cost_estimate=pl.CostEstimate(
            flops=4 * rows * features, bytes_accessed=5 * rows * features, transcendentals=rows
        ),
    )(part[None], hidden, norm_gain[None])


TILE = 2 * HD


def turn(value, cosine, sine):
    return (value * cosine + pltpu.roll(value, HD // 2, 1) * sine).astype(jnp.bfloat16)


def attention(queries, keys, values, first_ref, out_ref, skip):
    heads = len(queries)
    rows = out_ref.shape[0]
    for block in range(rows // QROWS):
        top = block * QROWS
        low = max(0, top - MAXLEN)
        end = top + QROWS
        span = end - low
        stacked = jnp.concatenate([query[top:end] for query in queries], axis=0)
        scores = lax.dot_general(
            stacked, keys[low:end], (((1,), (1,)), ((), ())), preferred_element_type=jnp.float32
        ) * (1.0 / math.sqrt(HD))
        row = lax.broadcasted_iota(jnp.int32, (QROWS, span), 0) + top
        col = lax.broadcasted_iota(jnp.int32, (QROWS, span), 1) + low
        visible = (col <= row) & (col >= first_ref[top:end])
        scores = jnp.where(visible[None], scores.reshape(heads, QROWS, span), -jnp.inf)
        exponent = jnp.exp(scores - jnp.max(scores, axis=-1, keepdims=True))
        weights = (exponent / jnp.sum(exponent, axis=-1, keepdims=True)).astype(jnp.bfloat16)
        context = jnp.dot(
            weights.reshape(heads * QROWS, span), values[low:end], preferred_element_type=jnp.float32
        ).astype(jnp.bfloat16)
        for head in range(heads):
            out_ref[top:end, skip + head * HD : skip + (head + 1) * HD] = context[
                head * QROWS : (head + 1) * QROWS
            ]


def heads_kernel(plan, pick_ref, *refs):
    sources, places, tiles, with_totals, finish, with_keys = plan
    sets, count = len(sources), len(places)
    refs = list(refs)

    def take(number):
        taken = refs[:number]
        del refs[:number]
        return taken

    row_refs = [take(number) for number in sources]
    weight_refs = take(count)
    totals = take(sets) if with_totals else [None] * sets
    if finish:
        (bias_ref,) = take(1)
        tables = [take(3) for _ in range(sets)]
        caches = [None] * sets if with_keys else take(sets)
    outs = take(sets)
    row_buf, weight_buf, *rest = refs
    acc = rest.pop(0) if finish else None
    row_sem, weight_sem = rest

    def weight_copy(piece):
        return pltpu.make_async_copy(
            weight_refs[piece].at[pl.ds(places[piece], tiles)],
            weight_buf.at[piece],
            weight_sem.at[piece],
        )

    def row_copy(which, piece, source):
        return pltpu.make_async_copy(
            row_refs[which][source].at[pick_ref[which, 1, piece]],
            row_buf.at[which, piece],
            row_sem.at[which, piece],
        )

    for piece in range(count):
        weight_copy(piece).start()
        for which in range(sets):
            if sources[which] == 1:
                row_copy(which, piece, 0).start()
            else:
                for source in range(sources[which]):

                    @pl.when(pick_ref[which, 0, piece] == source)
                    def _():
                        row_copy(which, piece, source).start()

    done = 0
    while done < count:
        ready = min(count, done + (1 if done < 2 else 2))
        for piece in range(done, ready):
            weight_copy(piece).wait()
        for which in range(sets):
            for piece in range(done, ready):
                row_copy(which, piece, 0).wait()
            total_ref = acc.at[which] if finish else outs[which]
            for tile in range(tiles):
                cols = slice(tile * TILE, (tile + 1) * TILE)
                term = None
                if done > 0:
                    term = total_ref[:, cols]
                elif totals[which] is not None:
                    term = totals[which][:, cols]
                for piece in range(done, ready):
                    product = jnp.dot(
                        row_buf[which, piece],
                        weight_buf[piece, tile],
                        preferred_element_type=jnp.float32,
                    )
                    term = product if term is None else term + product
                total_ref[:, cols] = term
        done = ready
    if not finish:
        return

    for which in range(sets):
        cos_ref, sin_ref, first_ref = tables[which]
        cosine, sine = cos_ref[...], sin_ref[...]
        out_ref = outs[which]
        skip = TILE if with_keys else 0
        if with_keys:
            out_ref[:, :HD] = turn(acc[which, :, :HD] + bias_ref[:, :HD], cosine, sine)
            out_ref[:, HD:TILE] = (acc[which, :, HD:TILE] + bias_ref[:, HD:TILE]).astype(jnp.bfloat16)
        cache = out_ref if with_keys else caches[which]
        queries = []
        for col in range(skip, out_ref.shape[1], HD):
            cols = slice(col, col + HD)
            queries.append(turn(acc[which, :, cols] + bias_ref[:, cols], cosine, sine))
        attention(queries, cache.at[:, :HD], cache.at[:, HD:TILE], first_ref, out_ref, skip)


def heads_of(row_sets, picks, pieces, tiles, totals=None, finish=None):
    sets, count = len(row_sets), len(pieces)
    sources = tuple(len(rows) for rows in row_sets)
    tokens, depth = row_sets[0][0].shape[1:]
    width = tiles * TILE
    operands = [array for rows in row_sets for array in rows] + [array for array, _ in pieces]
    in_specs = [pl.BlockSpec(memory_space=pl.ANY)] * len(operands)

    def block(shape, column=0):
        return pl.BlockSpec(shape, functools.partial(lambda at, i, pick: (0, at), column))

    if totals is not None:
        for total, column in totals:
            in_specs.append(block((tokens, width), column))
            operands.append(total)
    with_keys = False
    scratch = [
        pltpu.VMEM((sets, count, tokens, depth), jnp.bfloat16),
        pltpu.VMEM((count, tiles, depth, TILE), jnp.bfloat16),
    ]
    kind = jnp.float32
    if finish is not None:
        bias, tables, caches = finish
        kind = jnp.bfloat16
        in_specs.append(block((1, width)))
        operands.append(bias)
        for table in tables:
            for array in table:
                in_specs.append(block(array.shape))
                operands.append(array)
        with_keys = caches is None
        if not with_keys:
            for cache in caches:
                in_specs.append(block((tokens, TILE)))
                operands.append(cache)
        scratch.append(pltpu.VMEM((sets, tokens, width), jnp.float32))
    scratch += [pltpu.SemaphoreType.DMA((sets, count)), pltpu.SemaphoreType.DMA((count,))]
    plan = (
        sources,
        tuple(place for _, place in pieces),
        tiles,
        totals is not None,
        finish is not None,
        with_keys,
    )
    return pl.pallas_call(
        functools.partial(heads_kernel, plan),
        grid_spec=pltpu.PrefetchScalarGridSpec(
            num_scalar_prefetch=1,
            grid=(1,),
            in_specs=in_specs,
            out_specs=[block((tokens, width))] * sets,
            scratch_shapes=scratch,
        ),
        out_shape=[jax.ShapeDtypeStruct((tokens, width), kind)] * sets,
        compiler_params=pltpu.CompilerParams(vmem_limit_bytes=56 * 2**20),
        cost_estimate=pl.CostEstimate(
            flops=2 * sets * count * tokens * depth * width,
            bytes_accessed=2 * count * depth * (sets * tokens + width) + 8 * sets * tokens * width,
            transcendentals=0,
        ),
    )(jnp.stack(picks), *operands)


def gather_kernel(parts, flag_ref, *refs):
    near, beside, back, other = (refs[i * parts : (i + 1) * parts] for i in range(4))
    out_ref, sem = refs[-2:]
    half = out_ref.shape[1] // 2
    y, middle = flag_ref[0], flag_ref[1]

    def copies(sources, side, start):
        place = 0
        for part, source in enumerate(sources):
            skip = TILE if part == 0 else 0
            width = source.shape[1] - skip
            at = pl.multiple_of(side * half + place, TILE)
            copy = pltpu.make_async_copy(
                source.at[:, skip : skip + width],
                out_ref.at[:, pl.ds(at, width)],
                sem.at[start + part],
            )
            copy.start()
            place += width

    def waits(sources, start):
        for part, source in enumerate(sources):
            skip = TILE if part == 0 else 0
            width = source.shape[1] - skip
            pltpu.make_async_copy(
                source.at[:, skip : skip + width], out_ref.at[:, :width], sem.at[start + part]
            ).wait()

    @pl.when(middle == 1)
    def _():
        copies(near, y, 0)
        copies(beside, 1 - y, parts)

    @pl.when(middle == 0)
    def _():
        copies(back, y, 0)
        copies(other, 1 - y, parts)

    waits(near, 0)
    waits(beside, parts)


def gather_context(flags, near, beside, back, other, rows, cols):
    parts = len(near)
    operands = [*near, *beside, *back, *other]
    return pl.pallas_call(
        functools.partial(gather_kernel, parts),
        grid_spec=pltpu.PrefetchScalarGridSpec(
            num_scalar_prefetch=1,
            grid=(1,),
            in_specs=[pl.BlockSpec(memory_space=pl.ANY)] * len(operands),
            out_specs=pl.BlockSpec(memory_space=pl.ANY),
            scratch_shapes=[pltpu.SemaphoreType.DMA((2 * parts,))],
        ),
        out_shape=jax.ShapeDtypeStruct((rows, cols), jnp.bfloat16),
        cost_estimate=pl.CostEstimate(flops=0, bytes_accessed=4 * rows * cols, transcendentals=0),
    )(flags, *operands)


MIDDLE = (2, 3, 4, 5)
ENDS = (0, 1, 6, 7)


def after(value, *others):
    return lax.optimization_barrier((value,) + others)[0]


def pairs_from(sources, code):
    return [(s, s ^ code) for s in sources]


def middle_form(hidden, norm_gain, q_weight, q_bias, kv_weight, kv_bias, prefix_lens, assignment):
    tok_rows, features = hidden.shape
    slice_rows, q_cols = q_weight.shape
    half_cols = q_cols // 2
    group = lax.axis_index("group")
    tensor = lax.axis_index("tensor")
    y = group & 1
    is_middle = (group >= 2) & (group < 6)
    barrier = lax.optimization_barrier

    def over_group(value, sources, code):
        return lax.ppermute(value, "group", pairs_from(sources, code))

    def to_middle(value):
        return over_group(value, ENDS, 2)

    def across_middle(value):
        return over_group(value, MIDDLE, 6)

    def over_x(value):
        return lax.ppermute(value, "tensor", pairs_from(range(4), 2))

    def over_core(value):
        return lax.ppermute(value, "tensor", pairs_from(range(4), 1))

    tiles = (2, 2, 1)
    begin = (0, 2, 4)

    def columns(half):
        head = (2 * tensor + half) * HD
        kv_part = lax.dynamic_slice_in_dim(kv_weight, head, HD, 2).reshape(slice_rows, TILE)
        return jnp.stack(
            [kv_part]
            + [
                lax.dynamic_slice_in_dim(q_weight, half * half_cols + at, TILE, 1)
                for at in range(0, half_cols, TILE)
            ]
        )

    def both(one, two, chunk):
        low, high = begin[chunk], begin[chunk] + tiles[chunk]
        return jnp.concatenate([one[low:high], two[low:high]])

    def pick(code_of_rows, codes):
        block = jnp.stack([group ^ code for code in codes])
        if code_of_rows == 0:
            return jnp.stack([block * 0, block])
        return jnp.stack([(block >> 1) ^ tensor, block & 1])

    def rows_and_picks(sets, codes):
        return [rows_of[c] for c in sets], [pick(c, codes) for c in sets]

    own = columns(y)
    other = columns(1 - y)
    m_own = across_middle(own)
    swap = over_group(other, range(8), 1)
    normed, quarter = norm(hidden, norm_gain, tensor, slice_rows, 2)
    end2 = to_middle(quarter)

    bias = lax.dynamic_slice_in_dim(q_bias, y * half_cols, half_cols, 0)
    kv_bias_here = lax.dynamic_slice_in_dim(kv_bias, (2 * tensor + y) * HD, HD, 1)
    bias = jnp.concatenate([kv_bias_here[0], kv_bias_here[1], bias])[None, :]
    inverse_freq = THETA ** (-2.0 * jnp.arange(HD // 2, dtype=jnp.float32) / HD)
    m_swap = across_middle(after(swap, m_own))
    own, swap, m_own, normed, quarter, end2 = barrier((own, swap, m_own, normed, quarter, end2))

    rows_of = {0: [normed]}
    e0 = to_middle(both(own, swap, 0))
    next1, next2 = both(own, swap, 1), both(own, swap, 2)
    end3 = over_group(end2, MIDDLE, 1)
    across2 = over_x(end2)
    twin2 = over_core(end2)
    tables = []
    for code in range(4):
        _, offset, places = token_layout(prefix_lens, assignment, group ^ code, tok_rows)
        angles = offset.astype(jnp.float32)[:, None] * inverse_freq[None, :]
        cosine, sine = jnp.cos(angles), jnp.sin(angles)
        cosine = jnp.concatenate([cosine, cosine], axis=1)
        sine = jnp.concatenate([-sine, sine], axis=1)
        tables.append((cosine, sine, (places - offset)[:, None]))
    m_e0 = across_middle(after(e0, m_swap))
    (next1, next2, m_swap, e0, end2, end3, across2, twin2, tables, quarter) = barrier(
        (next1, next2, m_swap, e0, end2, end3, across2, twin2, tables, quarter)
    )

    first_codes, last_codes = (0, 1, 6, 7), (2, 3, 4, 5)
    first_pieces = {0: own, 1: swap, 6: m_own, 7: m_swap}

    def first_sums(sets):
        rows, picks = rows_and_picks(sets, first_codes)
        return heads_of(rows, picks, [(first_pieces[c], begin[1]) for c in first_codes], 3)

    outs = {}

    def finished(sets, chunk, last_pieces, totals=None):
        codes = last_codes if totals is not None else first_codes + last_codes
        rows, picks = rows_and_picks(sets, codes)
        width = tiles[chunk]
        places = {2: 0, 3: width, 4: 0, 5: width}
        pieces = [
            (first_pieces[c], begin[chunk]) if c in first_codes else (last_pieces[c], places[c])
            for c in codes
        ]
        if totals is not None:
            totals = [(total, (begin[chunk] - begin[1]) // width) for total in totals]
        made = heads_of(
            rows,
            picks,
            pieces,
            width,
            totals,
            (
                bias[:, begin[chunk] * TILE : (begin[chunk] + width) * TILE],
                [tables[c] for c in sets],
                None if chunk == 0 else [outs[c, 0] for c in sets],
            ),
        )
        for code, out in zip(sets, made):
            outs[code, chunk] = out

    e1 = to_middle(next1)
    end1 = over_group(quarter, MIDDLE, 1)
    across3 = over_x(end3)
    far2 = over_core(across2)
    rows_of[2] = [end2, twin2, across2, far2]
    sums = dict(zip((0, 2), first_sums((0, 2))))
    m_e1 = across_middle(after(e1, m_e0))
    (next2, m_e0, e0, e1, end1, end3, across3, far2, sums) = barrier(
        (next2, m_e0, e0, e1, end1, end3, across3, far2, sums)
    )
    rows_of[2] = [end2, twin2, across2, far2]

    e2 = to_middle(next2)
    across1 = over_x(end1)
    twin3 = over_core(end3)
    far3 = over_core(across3)
    rows_of[3] = [end3, twin3, across3, far3]

    def send_back(code, chunk):
        return over_group(outs[code, chunk], MIDDLE, code)

    pieces0 = {2: e0, 3: e0, 4: m_e0, 5: m_e0}
    finished((2, 3, 0), 0, pieces0)
    back = {(code, 0): send_back(code, 0) for code in (2, 3)}
    (sums[3],) = first_sums((3,))
    m_e2 = across_middle(after(e2, m_e1))
    (m_e1, e2, end1, across1, outs[0, 0], outs[2, 0], outs[3, 0], sums) = barrier(
        (m_e1, e2, end1, across1, outs[0, 0], outs[2, 0], outs[3, 0], sums)
    )

    twin1 = over_core(end1)
    far1 = over_core(across1)
    rows_of[1] = [end1, twin1, across1, far1]
    pieces1 = {2: e1, 3: e1, 4: m_e1, 5: m_e1}
    three = (2, 3, 0)
    finished(three, 1, pieces1, [sums[c] for c in three])
    for code in (2, 3):
        back[code, 1] = send_back(code, 1)
    finished((1,), 0, pieces0)
    back[1, 0] = send_back(1, 0)
    (sums[1],) = first_sums((1,))
    finished((1,), 1, pieces1, [after(sums[1], m_e2)])
    back[1, 1] = send_back(1, 1)
    (m_e2, sums, *ready) = barrier((m_e2, sums, *[outs[c, 1] for c in range(4)]))
    for code in range(4):
        outs[code, 1] = ready[code]

    pieces2 = {2: e2, 3: e2, 4: m_e2, 5: m_e2}
    order = (3, 2, 1, 0)
    finished(order, 2, pieces2, [sums[c] for c in order])
    for code in (3, 2, 1):
        back[code, 2] = send_back(code, 2)

    parts = range(3)
    context = gather_context(
        jnp.stack([y, is_middle.astype(jnp.int32)]),
        [outs[0, part] for part in parts],
        [back[1, part] for part in parts],
        [back[2, part] for part in parts],
        [back[3, part] for part in parts],
        tok_rows,
        q_cols,
    )

    def cache(part):
        return part[:, :TILE].reshape(tok_rows, 2, HD)

    mine = jnp.where(is_middle, cache(outs[0, 0]), cache(back[2, 0]))
    its = jnp.where(is_middle, cache(back[1, 0]), cache(back[3, 0]))
    kv_cache = jnp.where(
        y == 0,
        jnp.concatenate([mine, its], axis=-1),
        jnp.concatenate([its, mine], axis=-1),
    )
    return (context, kv_cache)


def solution(mesh):
    placed = (
        P("group", None),
        P(),
        P("group", "tensor"),
        P("tensor"),
        P("group", None, None),
        P(),
        P(),
        P(),
    )
    fits = mesh.shape["group"] == 8 and mesh.shape["tensor"] == 4
    return jax.shard_map(
        middle_form if fits else gathered_form,
        mesh=mesh,
        in_specs=placed,
        out_specs=(P("group", "tensor"), P("group", None, "tensor")),
        check_vma=False,
    )
```

```python
import functools
import math

import jax
import jax.numpy as jnp
from jax import lax
from jax.experimental import pallas as pl
from jax.experimental.pallas import tpu as pltpu
from jax.sharding import PartitionSpec as P

HD = 128


EPS = 1e-06
THETA = 1000000.0
QROWS = 128
MAXLEN = 256


def token_layout(prefix_lens, assignment, group_id, tok_rows):
    rollouts = prefix_lens.shape[0]
    member = assignment == group_id
    own_lens = jnp.where(member, prefix_lens, 0)
    starts = jnp.cumsum(own_lens) - own_lens
    places = jnp.arange(tok_rows, dtype=jnp.int32)
    inside = (
        member[None, :]
        & (places[:, None] >= starts[None, :])
        & (places[:, None] < (starts + own_lens)[None, :])
    )
    owner_id = jnp.sum(jnp.where(inside, jnp.arange(rollouts, dtype=jnp.int32)[None, :], 0), axis=1)
    offset = places - jnp.sum(jnp.where(inside, starts[None, :], 0), axis=1)
    return (owner_id, offset, places)


def rotate(values, offset):
    half_dim = values.shape[-1] // 2
    inverse_freq = THETA ** (-2.0 * jnp.arange(half_dim, dtype=jnp.float32) / values.shape[-1])
    angles = offset.astype(jnp.float32)[:, None] * inverse_freq[None, :]
    cosine = jnp.cos(angles)[:, None, :]
    sine_part = jnp.sin(angles)[:, None, :]
    first_half = values[..., :half_dim]
    second_half = values[..., half_dim:]
    return jnp.concatenate(
        [
            first_half * cosine - second_half * sine_part,
            second_half * cosine + first_half * sine_part,
        ],
        axis=-1,
    )


def add_product(normed, portion):
    return jnp.dot(normed, portion, preferred_element_type=jnp.float32)


def normalise(hidden, norm_gain):
    widened = hidden.astype(jnp.float32)
    return (
        widened * lax.rsqrt(jnp.mean(widened * widened, axis=-1, keepdims=True) + EPS) * norm_gain
    ).astype(jnp.bfloat16)


def gathered_form(
    hidden, norm_gain, q_weight, q_bias, kv_weight, kv_bias, prefix_lens, assignment
):
    tok_rows, features = hidden.shape
    slice_rows = kv_weight.shape[0]
    q_cols = q_weight.shape[1]
    kv_total = kv_weight.shape[2]
    heads_here = q_cols // HD
    tensor_pos = lax.axis_index("tensor")
    kv_cols = kv_total // lax.axis_size("tensor")
    normed = normalise(hidden, norm_gain)
    queries = add_product(normed, lax.all_gather(q_weight, "group", axis=0, tiled=True)) + q_bias
    head_span = max(kv_cols, HD)
    head_base = tensor_pos * kv_cols // head_span * head_span
    local_start = tensor_pos * kv_cols - head_base
    head_rows = lax.dynamic_slice_in_dim(kv_weight, head_base, head_span, 2).reshape(
        slice_rows, 2 * head_span
    )
    projected = add_product(normed, lax.all_gather(head_rows, "group", axis=0, tiled=True))
    projected = projected.reshape(tok_rows, 2, head_span) + lax.dynamic_slice_in_dim(
        kv_bias, head_base, head_span, 1
    )
    kv_here = head_span // HD
    group_size = heads_here // kv_here
    owner_id, offset, places = token_layout(
        prefix_lens, assignment, lax.axis_index("group"), tok_rows
    )
    rotated_queries = rotate(queries.reshape(tok_rows, heads_here, HD), offset).astype(jnp.bfloat16)
    rotated_keys = rotate(projected[:, 0].reshape(tok_rows, kv_here, HD), offset).astype(
        jnp.bfloat16
    )
    value_heads = projected[:, 1].reshape(tok_rows, kv_here, HD).astype(jnp.bfloat16)
    visible = (owner_id[:, None] == owner_id[None, :]) & (places[None, :] <= places[:, None])
    grouped = rotated_queries.reshape(tok_rows, kv_here, group_size, HD)
    scores = jnp.einsum(
        "qgph,kgh->gpqk", grouped, rotated_keys, preferred_element_type=jnp.float32
    ) / math.sqrt(HD)
    scores = jnp.where(visible[None, None], scores, -jnp.inf)
    row_max = jnp.max(scores, axis=-1, keepdims=True)
    exponent = jnp.exp(scores - row_max)
    weights_bf = (exponent / jnp.sum(exponent, axis=-1, keepdims=True)).astype(jnp.bfloat16)
    context = jnp.einsum(
        "gpqk,kgh->qgph", weights_bf, value_heads, preferred_element_type=jnp.float32
    )
    context = context.astype(jnp.bfloat16).reshape(tok_rows, q_cols)
    stacked = jnp.stack(
        [rotated_keys.reshape(tok_rows, head_span), value_heads.reshape(tok_rows, head_span)],
        axis=1,
    )
    kv_cache = lax.dynamic_slice_in_dim(stacked, local_start, kv_cols, 2)
    return (context, kv_cache)


def norm_kernel(part_ref, hidden_ref, gain_ref, out_ref, part_out_ref):
    widened = hidden_ref[...].astype(jnp.float32)
    scale = lax.rsqrt(jnp.mean(widened * widened, axis=-1, keepdims=True) + EPS)
    normed = (widened * scale * gain_ref[...]).astype(jnp.bfloat16)
    depth = out_ref.shape[2]
    for block in range(out_ref.shape[0]):
        out_ref[block] = normed[:, block * depth : (block + 1) * depth]
    count = part_out_ref.shape[0]
    part_out_ref[...] = out_ref[pl.ds(part_ref[0] * count, count)]


def norm(hidden, norm_gain, part, depth, count):
    rows, features = hidden.shape
    blocks = features // depth
    step = 64
    return pl.pallas_call(
        norm_kernel,
        grid_spec=pltpu.PrefetchScalarGridSpec(
            num_scalar_prefetch=1,
            grid=(rows // step,),
            in_specs=[
                pl.BlockSpec((step, features), lambda i, part: (i, 0)),
                pl.BlockSpec((1, features), lambda i, part: (0, 0)),
            ],
            out_specs=[
                pl.BlockSpec((blocks, step, depth), lambda i, part: (0, i, 0)),
                pl.BlockSpec((count, step, depth), lambda i, part: (0, i, 0)),
            ],
        ),
        out_shape=[
            jax.ShapeDtypeStruct((blocks, rows, depth), jnp.bfloat16),
            jax.ShapeDtypeStruct((count, rows, depth), jnp.bfloat16),
        ],
        compiler_params=pltpu.CompilerParams(vmem_limit_bytes=32 * 2**20),
        cost_estimate=pl.CostEstimate(
            flops=4 * rows * features, bytes_accessed=5 * rows * features, transcendentals=rows
        ),
    )(part[None], hidden, norm_gain[None])


TILE = 2 * HD


def turn(value, cosine, sine):
    return (value * cosine + pltpu.roll(value, HD // 2, 1) * sine).astype(jnp.bfloat16)


def attention(queries, keys, values, first_ref, out_ref, skip):
    heads = len(queries)
    rows = out_ref.shape[0]
    spans = [(max(0, top - MAXLEN), top, top + QROWS) for top in range(0, rows, QROWS)]
    shares = []
    for low, top, end in spans:
        stacked = jnp.concatenate([query[top:end] for query in queries], axis=0)
        shares.append(
            lax.dot_general(
                stacked,
                keys[low:end],
                (((1,), (1,)), ((), ())),
                preferred_element_type=jnp.float32,
            )
            * (1.0 / math.sqrt(HD))
        )
    for block, (low, top, end) in enumerate(spans):
        shape = (QROWS, end - low)
        row = lax.broadcasted_iota(jnp.int32, shape, 0) + top
        col = lax.broadcasted_iota(jnp.int32, shape, 1) + low
        visible = (col <= row) & (col >= first_ref[top:end])
        scores = jnp.where(visible[None], shares[block].reshape(heads, *shape), -jnp.inf)
        exponent = jnp.exp(scores - jnp.max(scores, axis=-1, keepdims=True))
        weights = (exponent / jnp.sum(exponent, axis=-1, keepdims=True)).astype(jnp.bfloat16)
        shares[block] = weights.reshape(heads * QROWS, end - low)
    for block, (low, top, end) in enumerate(spans):
        shares[block] = jnp.dot(
            shares[block], values[low:end], preferred_element_type=jnp.float32
        ).astype(jnp.bfloat16)
    for block, (low, top, end) in enumerate(spans):
        for head in range(heads):
            out_ref[top:end, skip + head * HD : skip + (head + 1) * HD] = shares[block][
                head * QROWS : (head + 1) * QROWS
            ]


def heads_kernel(plan, pick_ref, *refs):
    sources, places, width, with_totals, finish, with_keys = plan
    sets, count = len(sources), len(places)
    refs = list(refs)

    def take(number):
        taken = refs[:number]
        del refs[:number]
        return taken

    row_refs = [take(number) for number in sources]
    weight_refs = take(count)
    totals = take(sets) if with_totals else [None] * sets
    if finish:
        (bias_ref,) = take(1)
        tables = [take(3) for _ in range(sets)]
        caches = [None] * sets if with_keys else take(sets)
    outs = take(sets)
    row_buf, weight_buf, *rest = refs
    acc = rest.pop(0) if finish else None
    row_sem, weight_sem = rest

    depth = row_buf.shape[2] // count

    def weight_copy(piece):
        lead, skip = places[piece]
        ref = weight_refs[piece] if lead is None else weight_refs[piece].at[lead]
        return pltpu.make_async_copy(
            ref.at[:, skip : skip + width],
            weight_buf.at[piece * depth : (piece + 1) * depth],
            weight_sem.at[piece],
        )

    def row_copy(which, piece, source):
        return pltpu.make_async_copy(
            row_refs[which][source].at[pick_ref[which, 1, piece]],
            row_buf.at[which, :, piece * depth : (piece + 1) * depth],
            row_sem.at[which, piece],
        )

    half = count // 2
    stages = [(0, 0, half), (0, half, count)] + [(which, 0, count) for which in range(1, sets)]

    def start(stage):
        which, low, high = stages[stage]
        for piece in range(low, high):
            if which == 0:
                weight_copy(piece).start()
            if sources[which] == 1:
                row_copy(which, piece, 0).start()
            else:
                for source in range(sources[which]):

                    @pl.when(pick_ref[which, 0, piece] == source)
                    def _():
                        row_copy(which, piece, source).start()

    start(0)
    for stage, (which, low, high) in enumerate(stages):
        for piece in range(low, high):
            if which == 0:
                weight_copy(piece).wait()
            row_copy(which, piece, 0).wait()
        if stage + 1 < len(stages):
            start(stage + 1)
        total_ref = acc.at[which] if finish else outs[which]
        for at in range(0, width, TILE):
            cols = slice(at, at + TILE)
            term = jnp.dot(
                row_buf[which, :, low * depth : high * depth],
                weight_buf[low * depth : high * depth, cols],
                preferred_element_type=jnp.float32,
            )
            if low > 0:
                term = total_ref[:, cols] + term
            elif totals[which] is not None:
                term = totals[which][:, cols] + term
            total_ref[:, cols] = term
    if not finish:
        return

    for which in range(sets):
        cos_ref, sin_ref, first_ref = tables[which]
        cosine, sine = cos_ref[...], sin_ref[...]
        out_ref = outs[which]
        skip = TILE if with_keys else 0
        if with_keys:
            out_ref[:, :HD] = turn(acc[which, :, :HD] + bias_ref[:, :HD], cosine, sine)
            out_ref[:, HD:TILE] = (acc[which, :, HD:TILE] + bias_ref[:, HD:TILE]).astype(jnp.bfloat16)
        cache = out_ref if with_keys else caches[which]
        queries = []
        for col in range(skip, out_ref.shape[1], HD):
            cols = slice(col, col + HD)
            queries.append(turn(acc[which, :, cols] + bias_ref[:, cols], cosine, sine))
        attention(queries, cache.at[:, :HD], cache.at[:, HD:TILE], first_ref, out_ref, skip)


def heads_of(row_sets, picks, pieces, width, totals=None, finish=None):
    sets, count = len(row_sets), len(pieces)
    sources = tuple(len(rows) for rows in row_sets)
    tokens, depth = row_sets[0][0].shape[1:]
    operands = [array for rows in row_sets for array in rows] + [array for array, _ in pieces]
    in_specs = [pl.BlockSpec(memory_space=pl.ANY)] * len(operands)

    def block(shape, column=0):
        return pl.BlockSpec(shape, functools.partial(lambda at, i, pick: (0, at), column))

    if totals is not None:
        for total, column in totals:
            in_specs.append(block((tokens, width), column))
            operands.append(total)
    with_keys = False
    scratch = [
        pltpu.VMEM((sets, tokens, count * depth), jnp.bfloat16),
        pltpu.VMEM((count * depth, width), jnp.bfloat16),
    ]
    kind = jnp.float32
    if finish is not None:
        bias, tables, caches = finish
        kind = jnp.bfloat16
        in_specs.append(block((1, width)))
        operands.append(bias)
        for table in tables:
            for array in table:
                in_specs.append(block(array.shape))
                operands.append(array)
        with_keys = caches is None
        if not with_keys:
            for cache in caches:
                in_specs.append(block((tokens, TILE)))
                operands.append(cache)
        scratch.append(pltpu.VMEM((sets, tokens, width), jnp.float32))
    scratch += [pltpu.SemaphoreType.DMA((sets, count)), pltpu.SemaphoreType.DMA((count,))]
    plan = (
        sources,
        tuple(place for _, place in pieces),
        width,
        totals is not None,
        finish is not None,
        with_keys,
    )
    return pl.pallas_call(
        functools.partial(heads_kernel, plan),
        grid_spec=pltpu.PrefetchScalarGridSpec(
            num_scalar_prefetch=1,
            grid=(1,),
            in_specs=in_specs,
            out_specs=[block((tokens, width))] * sets,
            scratch_shapes=scratch,
        ),
        out_shape=[jax.ShapeDtypeStruct((tokens, width), kind)] * sets,
        compiler_params=pltpu.CompilerParams(vmem_limit_bytes=56 * 2**20),
        cost_estimate=pl.CostEstimate(
            flops=2 * sets * count * tokens * depth * width,
            bytes_accessed=2 * count * depth * (sets * tokens + width) + 8 * sets * tokens * width,
            transcendentals=0,
        ),
    )(jnp.stack(picks), *operands)


def gather_kernel(parts, flag_ref, *refs):
    near, beside, back, other = (refs[i * parts : (i + 1) * parts] for i in range(4))
    out_ref = refs[-1]
    half = out_ref.shape[1] // 2

    def put(sources, side):
        place = side * half
        for part, source in enumerate(sources):
            value = source[:, TILE if part == 0 else 0 :]
            out_ref[:, place : place + value.shape[1]] = value
            place += value.shape[1]

    for middle, mine, its in ((1, near, beside), (0, back, other)):
        for side in range(2):

            @pl.when((flag_ref[0] == side) & (flag_ref[1] == middle))
            def _():
                put(mine, side)
                put(its, 1 - side)


def gather_context(flags, near, beside, back, other, cols):
    operands = [*near, *beside, *back, *other]
    rows, step = near[0].shape[0], QROWS
    return pl.pallas_call(
        functools.partial(gather_kernel, len(near)),
        grid_spec=pltpu.PrefetchScalarGridSpec(
            num_scalar_prefetch=1,
            grid=(rows // step,),
            in_specs=[
                pl.BlockSpec((step, operand.shape[1]), lambda i, flags: (i, 0))
                for operand in operands
            ],
            out_specs=pl.BlockSpec((step, cols), lambda i, flags: (i, 0)),
        ),
        out_shape=jax.ShapeDtypeStruct((rows, cols), jnp.bfloat16),
        compiler_params=pltpu.CompilerParams(vmem_limit_bytes=24 * 2**20),
        cost_estimate=pl.CostEstimate(flops=0, bytes_accessed=6 * rows * cols, transcendentals=0),
    )(flags, *operands)


MIDDLE = (2, 3, 4, 5)
ENDS = (0, 1, 6, 7)


def after(value, *others):
    return lax.optimization_barrier((value,) + others)[0]


def pairs_from(sources, code):
    return [(s, s ^ code) for s in sources]


def middle_form(hidden, norm_gain, q_weight, q_bias, kv_weight, kv_bias, prefix_lens, assignment):
    tok_rows, features = hidden.shape
    slice_rows, q_cols = q_weight.shape
    half_cols = q_cols // 2
    group = lax.axis_index("group")
    tensor = lax.axis_index("tensor")
    y = group & 1
    is_middle = (group >= 2) & (group < 6)
    barrier = lax.optimization_barrier

    def over_group(value, sources, code):
        return lax.ppermute(value, "group", pairs_from(sources, code))

    def to_middle(value):
        return over_group(value, ENDS, 2)

    def across_middle(value):
        return over_group(value, MIDDLE, 6)

    def over_x(value):
        return lax.ppermute(value, "tensor", pairs_from(range(4), 2))

    def over_core(value):
        return lax.ppermute(value, "tensor", pairs_from(range(4), 1))

    begin, widths = (0, 2 * TILE, 4 * TILE), (2 * TILE, 2 * TILE, TILE)

    def columns(half):
        head = (2 * tensor + half) * HD
        kv_part = lax.dynamic_slice_in_dim(kv_weight, head, HD, 2).reshape(slice_rows, TILE)
        q_part = lax.dynamic_slice_in_dim(q_weight, half * half_cols, half_cols, 1)
        return jnp.concatenate([kv_part, q_part], axis=1)

    def both(one, two, chunk):
        low, high = begin[chunk], begin[chunk] + widths[chunk]
        return jnp.stack([one[:, low:high], two[:, low:high]])

    def pick(code_of_rows, codes):
        block = jnp.stack([group ^ code for code in codes])
        if code_of_rows == 0:
            return jnp.stack([block * 0, block])
        return jnp.stack([(block >> 1) ^ tensor, block & 1])

    def rows_and_picks(sets, codes):
        return [rows_of[c] for c in sets], [pick(c, codes) for c in sets]

    own = columns(y)
    other = columns(1 - y)
    m_own = across_middle(own)
    swap = over_group(other, range(8), 1)
    normed, quarter = norm(hidden, norm_gain, tensor, slice_rows, 2)
    end2 = to_middle(quarter)

    bias = lax.dynamic_slice_in_dim(q_bias, y * half_cols, half_cols, 0)
    kv_bias_here = lax.dynamic_slice_in_dim(kv_bias, (2 * tensor + y) * HD, HD, 1)
    bias = jnp.concatenate([kv_bias_here[0], kv_bias_here[1], bias])[None, :]
    inverse_freq = THETA ** (-2.0 * jnp.arange(HD // 2, dtype=jnp.float32) / HD)
    m_swap = across_middle(after(swap, m_own))
    own, swap, m_own, normed, quarter, end2 = barrier((own, swap, m_own, normed, quarter, end2))

    rows_of = {0: [normed]}
    e0 = to_middle(both(own, swap, 0))
    next1, next2 = both(own, swap, 1), both(own, swap, 2)
    end3 = over_group(end2, MIDDLE, 1)
    across2 = over_x(end2)
    twin2 = over_core(end2)
    tables = []
    for code in range(4):
        _, offset, places = token_layout(prefix_lens, assignment, group ^ code, tok_rows)
        angles = offset.astype(jnp.float32)[:, None] * inverse_freq[None, :]
        cosine, sine = jnp.cos(angles), jnp.sin(angles)
        cosine = jnp.concatenate([cosine, cosine], axis=1)
        sine = jnp.concatenate([-sine, sine], axis=1)
        tables.append((cosine, sine, (places - offset)[:, None]))
    m_e0 = across_middle(after(e0, m_swap))
    (next1, next2, m_swap, e0, end2, end3, across2, twin2, tables, quarter) = barrier(
        (next1, next2, m_swap, e0, end2, end3, across2, twin2, tables, quarter)
    )

    first_codes, last_codes = (0, 1, 6, 7), (2, 3, 4, 5)
    first_pieces = {0: own, 1: swap, 6: m_own, 7: m_swap}

    def first_sums(sets):
        rows, picks = rows_and_picks(sets, first_codes)
        pieces = [(first_pieces[c], (None, begin[1])) for c in first_codes]
        return heads_of(rows, picks, pieces, sum(widths[1:]))

    outs = {}

    def finished(sets, chunk, last_pieces, totals=None):
        codes = last_codes if totals is not None else first_codes + last_codes
        rows, picks = rows_and_picks(sets, codes)
        width = widths[chunk]
        pieces = [
            (first_pieces[c], (None, begin[chunk]))
            if c in first_codes
            else (last_pieces[c], (c & 1, 0))
            for c in codes
        ]
        if totals is not None:
            totals = [(total, (begin[chunk] - begin[1]) // width) for total in totals]
        made = heads_of(
            rows,
            picks,
            pieces,
            width,
            totals,
            (
                bias[:, begin[chunk] : begin[chunk] + width],
                [tables[c] for c in sets],
                None if chunk == 0 else [outs[c, 0] for c in sets],
            ),
        )
        for code, out in zip(sets, made):
            outs[code, chunk] = out

    e1 = to_middle(next1)
    end1 = over_group(quarter, MIDDLE, 1)
    across3 = over_x(end3)
    far2 = over_core(across2)
    rows_of[2] = [end2, twin2, across2, far2]
    sums = dict(zip((0, 2), first_sums((0, 2))))
    m_e1 = across_middle(after(e1, m_e0))
    (next2, m_e0, e0, e1, end1, end3, across3, far2, sums) = barrier(
        (next2, m_e0, e0, e1, end1, end3, across3, far2, sums)
    )
    rows_of[2] = [end2, twin2, across2, far2]

    e2 = to_middle(next2)
    across1 = over_x(end1)
    twin3 = over_core(end3)
    far3 = over_core(across3)
    rows_of[3] = [end3, twin3, across3, far3]

    def send_back(code, chunk):
        return over_group(outs[code, chunk], MIDDLE, code)

    pieces0 = {2: e0, 3: e0, 4: m_e0, 5: m_e0}
    finished((2, 3, 0), 0, pieces0)
    back = {(code, 0): send_back(code, 0) for code in (2, 3)}
    (sums[3],) = first_sums((3,))
    m_e2 = across_middle(after(e2, m_e1))
    (m_e1, e2, end1, across1, outs[0, 0], outs[2, 0], outs[3, 0], sums) = barrier(
        (m_e1, e2, end1, across1, outs[0, 0], outs[2, 0], outs[3, 0], sums)
    )

    twin1 = over_core(end1)
    far1 = over_core(across1)
    rows_of[1] = [end1, twin1, across1, far1]
    pieces1 = {2: e1, 3: e1, 4: m_e1, 5: m_e1}
    three = (2, 3, 0)
    finished(three, 1, pieces1, [sums[c] for c in three])
    for code in (2, 3):
        back[code, 1] = send_back(code, 1)
    finished((1,), 0, pieces0)
    back[1, 0] = send_back(1, 0)
    (sums[1],) = first_sums((1,))
    finished((1,), 1, pieces1, [after(sums[1], m_e2)])
    back[1, 1] = send_back(1, 1)
    (m_e2, sums, *ready) = barrier((m_e2, sums, *[outs[c, 1] for c in range(4)]))
    for code in range(4):
        outs[code, 1] = ready[code]

    pieces2 = {2: e2, 3: e2, 4: m_e2, 5: m_e2}
    order = (3, 2, 1, 0)
    finished(order, 2, pieces2, [sums[c] for c in order])
    for code in (3, 2, 1):
        back[code, 2] = send_back(code, 2)

    parts = range(3)
    context = gather_context(
        jnp.stack([y, is_middle.astype(jnp.int32)]),
        [outs[0, part] for part in parts],
        [back[1, part] for part in parts],
        [back[2, part] for part in parts],
        [back[3, part] for part in parts],
        q_cols,
    )

    def cache(part):
        return part[:, :TILE].reshape(tok_rows, 2, HD)

    mine = jnp.where(is_middle, cache(outs[0, 0]), cache(back[2, 0]))
    its = jnp.where(is_middle, cache(back[1, 0]), cache(back[3, 0]))
    kv_cache = jnp.where(
        y == 0,
        jnp.concatenate([mine, its], axis=-1),
        jnp.concatenate([its, mine], axis=-1),
    )
    return (context, kv_cache)


def solution(mesh):
    placed = (
        P("group", None),
        P(),
        P("group", "tensor"),
        P("tensor"),
        P("group", None, None),
        P(),
        P(),
        P(),
    )
    fits = mesh.shape["group"] == 8 and mesh.shape["tensor"] == 4
    return jax.shard_map(
        middle_form if fits else gathered_form,
        mesh=mesh,
        in_specs=placed,
        out_specs=(P("group", "tensor"), P("group", None, "tensor")),
        check_vma=False,
    )
```

```python
import functools
import math

import jax
import jax.numpy as jnp
from jax import lax
from jax.experimental import pallas as pl
from jax.experimental.pallas import tpu as pltpu
from jax.sharding import PartitionSpec as P

HD = 128


EPS = 1e-06
THETA = 1000000.0
QROWS = 128
MAXLEN = 256


def token_layout(prefix_lens, assignment, group_id, tok_rows):
    rollouts = prefix_lens.shape[0]
    member = assignment == group_id
    own_lens = jnp.where(member, prefix_lens, 0)
    starts = jnp.cumsum(own_lens) - own_lens
    places = jnp.arange(tok_rows, dtype=jnp.int32)
    inside = (
        member[None, :]
        & (places[:, None] >= starts[None, :])
        & (places[:, None] < (starts + own_lens)[None, :])
    )
    owner_id = jnp.sum(jnp.where(inside, jnp.arange(rollouts, dtype=jnp.int32)[None, :], 0), axis=1)
    offset = places - jnp.sum(jnp.where(inside, starts[None, :], 0), axis=1)
    return (owner_id, offset, places)


def rotate(values, offset):
    half_dim = values.shape[-1] // 2
    inverse_freq = THETA ** (-2.0 * jnp.arange(half_dim, dtype=jnp.float32) / values.shape[-1])
    angles = offset.astype(jnp.float32)[:, None] * inverse_freq[None, :]
    cosine = jnp.cos(angles)[:, None, :]
    sine_part = jnp.sin(angles)[:, None, :]
    first_half = values[..., :half_dim]
    second_half = values[..., half_dim:]
    return jnp.concatenate(
        [
            first_half * cosine - second_half * sine_part,
            second_half * cosine + first_half * sine_part,
        ],
        axis=-1,
    )


def add_product(normed, portion):
    return jnp.dot(normed, portion, preferred_element_type=jnp.float32)


def normalise(hidden, norm_gain):
    widened = hidden.astype(jnp.float32)
    return (
        widened * lax.rsqrt(jnp.mean(widened * widened, axis=-1, keepdims=True) + EPS) * norm_gain
    ).astype(jnp.bfloat16)


def gathered_form(
    hidden, norm_gain, q_weight, q_bias, kv_weight, kv_bias, prefix_lens, assignment
):
    tok_rows, features = hidden.shape
    slice_rows = kv_weight.shape[0]
    q_cols = q_weight.shape[1]
    kv_total = kv_weight.shape[2]
    heads_here = q_cols // HD
    tensor_pos = lax.axis_index("tensor")
    kv_cols = kv_total // lax.axis_size("tensor")
    normed = normalise(hidden, norm_gain)
    queries = add_product(normed, lax.all_gather(q_weight, "group", axis=0, tiled=True)) + q_bias
    head_span = max(kv_cols, HD)
    head_base = tensor_pos * kv_cols // head_span * head_span
    local_start = tensor_pos * kv_cols - head_base
    head_rows = lax.dynamic_slice_in_dim(kv_weight, head_base, head_span, 2).reshape(
        slice_rows, 2 * head_span
    )
    projected = add_product(normed, lax.all_gather(head_rows, "group", axis=0, tiled=True))
    projected = projected.reshape(tok_rows, 2, head_span) + lax.dynamic_slice_in_dim(
        kv_bias, head_base, head_span, 1
    )
    kv_here = head_span // HD
    group_size = heads_here // kv_here
    owner_id, offset, places = token_layout(
        prefix_lens, assignment, lax.axis_index("group"), tok_rows
    )
    rotated_queries = rotate(queries.reshape(tok_rows, heads_here, HD), offset).astype(jnp.bfloat16)
    rotated_keys = rotate(projected[:, 0].reshape(tok_rows, kv_here, HD), offset).astype(
        jnp.bfloat16
    )
    value_heads = projected[:, 1].reshape(tok_rows, kv_here, HD).astype(jnp.bfloat16)
    visible = (owner_id[:, None] == owner_id[None, :]) & (places[None, :] <= places[:, None])
    grouped = rotated_queries.reshape(tok_rows, kv_here, group_size, HD)
    scores = jnp.einsum(
        "qgph,kgh->gpqk", grouped, rotated_keys, preferred_element_type=jnp.float32
    ) / math.sqrt(HD)
    scores = jnp.where(visible[None, None], scores, -jnp.inf)
    row_max = jnp.max(scores, axis=-1, keepdims=True)
    exponent = jnp.exp(scores - row_max)
    weights_bf = (exponent / jnp.sum(exponent, axis=-1, keepdims=True)).astype(jnp.bfloat16)
    context = jnp.einsum(
        "gpqk,kgh->qgph", weights_bf, value_heads, preferred_element_type=jnp.float32
    )
    context = context.astype(jnp.bfloat16).reshape(tok_rows, q_cols)
    stacked = jnp.stack(
        [rotated_keys.reshape(tok_rows, head_span), value_heads.reshape(tok_rows, head_span)],
        axis=1,
    )
    kv_cache = lax.dynamic_slice_in_dim(stacked, local_start, kv_cols, 2)
    return (context, kv_cache)


def norm_kernel(part_ref, hidden_ref, gain_ref, out_ref, part_out_ref):
    widened = hidden_ref[...].astype(jnp.float32)
    scale = lax.rsqrt(jnp.mean(widened * widened, axis=-1, keepdims=True) + EPS)
    normed = (widened * scale * gain_ref[...]).astype(jnp.bfloat16)
    depth = out_ref.shape[2]
    for block in range(out_ref.shape[0]):
        out_ref[block] = normed[:, block * depth : (block + 1) * depth]
    count = part_out_ref.shape[0]
    part_out_ref[...] = out_ref[pl.ds(part_ref[0] * count, count)]


def norm(hidden, norm_gain, part, depth, count):
    rows, features = hidden.shape
    blocks = features // depth
    step = 64
    return pl.pallas_call(
        norm_kernel,
        grid_spec=pltpu.PrefetchScalarGridSpec(
            num_scalar_prefetch=1,
            grid=(rows // step,),
            in_specs=[
                pl.BlockSpec((step, features), lambda i, part: (i, 0)),
                pl.BlockSpec((1, features), lambda i, part: (0, 0)),
            ],
            out_specs=[
                pl.BlockSpec((blocks, step, depth), lambda i, part: (0, i, 0)),
                pl.BlockSpec((count, step, depth), lambda i, part: (0, i, 0)),
            ],
        ),
        out_shape=[
            jax.ShapeDtypeStruct((blocks, rows, depth), jnp.bfloat16),
            jax.ShapeDtypeStruct((count, rows, depth), jnp.bfloat16),
        ],
        compiler_params=pltpu.CompilerParams(vmem_limit_bytes=32 * 2**20),
        cost_estimate=pl.CostEstimate(
            flops=4 * rows * features, bytes_accessed=5 * rows * features, transcendentals=rows
        ),
    )(part[None], hidden, norm_gain[None])


TILE = 2 * HD


def turn(value, cosine, sine):
    return (value * cosine + pltpu.roll(value, HD // 2, 1) * sine).astype(jnp.bfloat16)


def attention(queries, keys, values, first_ref, out_ref, skip):
    heads = len(queries)
    rows = out_ref.shape[0]
    scale = math.log2(math.e) / math.sqrt(HD)
    for top in range(0, rows, QROWS):
        low, end = max(0, top - MAXLEN), top + QROWS
        shape = (QROWS, end - low)
        stacked = jnp.concatenate([query[top:end] for query in queries], axis=0)
        scores = lax.dot_general(
            stacked, keys[low:end], (((1,), (1,)), ((), ())), preferred_element_type=jnp.float32
        )
        row = lax.broadcasted_iota(jnp.int32, shape, 0) + top
        col = lax.broadcasted_iota(jnp.int32, shape, 1) + low
        visible = (col <= row) & (col >= first_ref[top:end])
        scores = jnp.where(visible[None], scores.reshape(heads, *shape), -jnp.inf)
        most = jnp.max(scores, axis=-1, keepdims=True)
        exponent = jnp.exp2((scores - most) * scale)
        share = 1.0 / jnp.sum(exponent, axis=-1, keepdims=True)
        weights = (exponent * share).astype(jnp.bfloat16)
        context = jnp.dot(
            weights.reshape(heads * QROWS, end - low),
            values[low:end],
            preferred_element_type=jnp.float32,
        ).astype(jnp.bfloat16)
        for head in range(heads):
            out_ref[top:end, skip + head * HD : skip + (head + 1) * HD] = context[
                head * QROWS : (head + 1) * QROWS
            ]


def heads_kernel(plan, pick_ref, *refs):
    sources, parts, width, with_totals, finish, with_keys = plan
    sets, count = len(sources), len(parts)
    refs = list(refs)

    def take(number):
        taken = refs[:number]
        del refs[:number]
        return taken

    row_refs = [take(number) for number in sources]
    weight_refs = [take(len(part)) for part in parts]
    totals = take(sets) if with_totals else [None] * sets
    if finish:
        (bias_ref,) = take(1)
        tables = [take(3) for _ in range(sets)]
        caches = [None] * sets if with_keys else take(sets)
    outs = take(sets)
    row_buf, weight_buf, *rest = refs
    acc = rest.pop(0) if finish else None
    row_sem, weight_sem = rest

    depth = row_buf.shape[2] // count

    def weight_copies(piece):
        column = 0
        for part, (ref, (lead, skip, wide)) in enumerate(zip(weight_refs[piece], parts[piece])):
            ref = ref if lead is None else ref.at[lead]
            yield pltpu.make_async_copy(
                ref.at[:, skip : skip + wide],
                weight_buf.at[piece * depth : (piece + 1) * depth, column : column + wide],
                weight_sem.at[piece, part],
            )
            column += wide

    def row_copy(which, piece, source):
        return pltpu.make_async_copy(
            row_refs[which][source].at[pick_ref[which, 1, piece]],
            row_buf.at[which, :, piece * depth : (piece + 1) * depth],
            row_sem.at[which, piece],
        )

    half = count // 2
    stages = [(0, 0, half), (0, half, count)] + [(which, 0, count) for which in range(1, sets)]
    if width > 2 * TILE and count > 4:
        stages[:1] = [(0, 0, half // 2), (0, half // 2, half)]

    def start(stage):
        which, low, high = stages[stage]
        for piece in range(low, high):
            if which == 0:
                for copy in weight_copies(piece):
                    copy.start()
            if sources[which] == 1:
                row_copy(which, piece, 0).start()
            else:
                for source in range(sources[which]):

                    @pl.when(pick_ref[which, 0, piece] == source)
                    def _():
                        row_copy(which, piece, source).start()

    start(0)
    for stage, (which, low, high) in enumerate(stages):
        for piece in range(low, high):
            if which == 0:
                for copy in weight_copies(piece):
                    copy.wait()
            row_copy(which, piece, 0).wait()
        if stage + 1 < len(stages):
            start(stage + 1)
        total_ref = acc.at[which] if finish else outs[which]
        for at in range(0, width, TILE):
            cols = slice(at, at + TILE)
            term = jnp.dot(
                row_buf[which, :, low * depth : high * depth],
                weight_buf[low * depth : high * depth, cols],
                preferred_element_type=jnp.float32,
            )
            if low > 0:
                term = total_ref[:, cols] + term
            elif totals[which] is not None:
                term = totals[which][:, cols] + term
            total_ref[:, cols] = term
    if not finish:
        return

    for which in range(sets):
        cos_ref, sin_ref, first_ref = tables[which]
        cosine, sine = cos_ref[...], sin_ref[...]
        out_ref = outs[which]
        skip = TILE if with_keys else 0
        if with_keys:
            out_ref[:, :HD] = turn(acc[which, :, :HD] + bias_ref[:, :HD], cosine, sine)
            out_ref[:, HD:TILE] = (acc[which, :, HD:TILE] + bias_ref[:, HD:TILE]).astype(jnp.bfloat16)
        cache = out_ref if with_keys else caches[which]
        queries = []
        for col in range(skip, out_ref.shape[1], HD):
            cols = slice(col, col + HD)
            queries.append(turn(acc[which, :, cols] + bias_ref[:, cols], cosine, sine))
        attention(queries, cache.at[:, :HD], cache.at[:, HD:TILE], first_ref, out_ref, skip)


def heads_of(row_sets, picks, pieces, width, totals=None, finish=None):
    sets, count = len(row_sets), len(pieces)
    sources = tuple(len(rows) for rows in row_sets)
    tokens, depth = row_sets[0][0].shape[1:]
    operands = [array for rows in row_sets for array in rows]
    operands += [array for piece in pieces for array, *_ in piece]
    in_specs = [pl.BlockSpec(memory_space=pl.ANY)] * len(operands)

    def block(shape, column=0):
        return pl.BlockSpec(shape, functools.partial(lambda at, i, pick: (0, at), column))

    if totals is not None:
        for total, column in totals:
            in_specs.append(block((tokens, width), column))
            operands.append(total)
    with_keys = False
    scratch = [
        pltpu.VMEM((sets, tokens, count * depth), jnp.bfloat16),
        pltpu.VMEM((count * depth, width), jnp.bfloat16),
    ]
    kind = jnp.float32
    if finish is not None:
        bias, tables, caches = finish
        kind = jnp.bfloat16
        in_specs.append(block((1, width)))
        operands.append(bias)
        for table in tables:
            for array in table:
                in_specs.append(block(array.shape))
                operands.append(array)
        with_keys = caches is None
        if not with_keys:
            for cache in caches:
                in_specs.append(block((tokens, TILE)))
                operands.append(cache)
        scratch.append(pltpu.VMEM((sets, tokens, width), jnp.float32))
    scratch += [pltpu.SemaphoreType.DMA((sets, count)), pltpu.SemaphoreType.DMA((count, max(map(len, pieces))))]
    plan = (
        sources,
        tuple(tuple(part[1:] for part in piece) for piece in pieces),
        width,
        totals is not None,
        finish is not None,
        with_keys,
    )
    return pl.pallas_call(
        functools.partial(heads_kernel, plan),
        grid_spec=pltpu.PrefetchScalarGridSpec(
            num_scalar_prefetch=1,
            grid=(1,),
            in_specs=in_specs,
            out_specs=[block((tokens, width))] * sets,
            scratch_shapes=scratch,
        ),
        out_shape=[jax.ShapeDtypeStruct((tokens, width), kind)] * sets,
        compiler_params=pltpu.CompilerParams(vmem_limit_bytes=56 * 2**20),
        cost_estimate=pl.CostEstimate(
            flops=2 * sets * count * tokens * depth * width,
            bytes_accessed=2 * count * depth * (sets * tokens + width) + 8 * sets * tokens * width,
            transcendentals=0,
        ),
    )(jnp.stack(picks), *operands)


def gather_kernel(numbers, flag_ref, *refs):
    ends = [sum(numbers[: i + 1]) for i in range(4)]
    near, beside, back, other = (refs[end - number : end] for end, number in zip(ends, numbers))
    out_ref = refs[-1]
    half = out_ref.shape[1] // 2

    def put(sources, side):
        place = side * half
        for part, source in enumerate(sources):
            value = source[:, TILE if part == 0 else 0 :]
            out_ref[:, place : place + value.shape[1]] = value
            place += value.shape[1]

    for middle, mine, its in ((1, near, beside), (0, back, other)):
        for side in range(2):

            @pl.when((flag_ref[0] == side) & (flag_ref[1] == middle))
            def _():
                put(mine, side)
                put(its, 1 - side)


def gather_context(flags, near, beside, back, other, cols):
    operands = [*near, *beside, *back, *other]
    rows, step = near[0].shape[0], QROWS
    return pl.pallas_call(
        functools.partial(gather_kernel, tuple(map(len, (near, beside, back, other)))),
        grid_spec=pltpu.PrefetchScalarGridSpec(
            num_scalar_prefetch=1,
            grid=(rows // step,),
            in_specs=[
                pl.BlockSpec((step, operand.shape[1]), lambda i, flags: (i, 0))
                for operand in operands
            ],
            out_specs=pl.BlockSpec((step, cols), lambda i, flags: (i, 0)),
        ),
        out_shape=jax.ShapeDtypeStruct((rows, cols), jnp.bfloat16),
        compiler_params=pltpu.CompilerParams(vmem_limit_bytes=24 * 2**20),
        cost_estimate=pl.CostEstimate(flops=0, bytes_accessed=6 * rows * cols, transcendentals=0),
    )(flags, *operands)


MIDDLE = (2, 3, 4, 5)
ENDS = (0, 1, 6, 7)


def after(value, *others):
    return lax.optimization_barrier((value,) + others)[0]


def pairs_from(sources, code):
    return [(s, s ^ code) for s in sources]


def middle_form(hidden, norm_gain, q_weight, q_bias, kv_weight, kv_bias, prefix_lens, assignment):
    tok_rows, features = hidden.shape
    slice_rows, q_cols = q_weight.shape
    half_cols = q_cols // 2
    group = lax.axis_index("group")
    tensor = lax.axis_index("tensor")
    y = group & 1
    is_middle = (group >= 2) & (group < 6)
    barrier = lax.optimization_barrier

    def over_group(value, sources, code):
        return lax.ppermute(value, "group", pairs_from(sources, code))

    def to_middle(value):
        return over_group(value, ENDS, 2)

    def across_middle(value):
        return over_group(value, MIDDLE, 6)

    def over_x(value):
        return lax.ppermute(value, "tensor", pairs_from(range(4), 2))

    def over_core(value):
        return lax.ppermute(value, "tensor", pairs_from(range(4), 1))

    begin, widths = (0, 2 * TILE, 4 * TILE), (2 * TILE, 2 * TILE, TILE)

    def columns(half):
        head = (2 * tensor + half) * HD
        kv_part = lax.dynamic_slice_in_dim(kv_weight, head, HD, 2).reshape(slice_rows, TILE)
        q_part = lax.dynamic_slice_in_dim(q_weight, half * half_cols, half_cols, 1)
        return jnp.concatenate([kv_part, q_part], axis=1)

    def both(one, two, chunk):
        low, high = begin[chunk], begin[chunk] + widths[chunk]
        return jnp.stack([one[:, low:high], two[:, low:high]])

    def pick(code_of_rows, codes):
        block = jnp.stack([group ^ code for code in codes])
        if code_of_rows == 0:
            return jnp.stack([block * 0, block])
        return jnp.stack([(block >> 1) ^ tensor, block & 1])

    def rows_and_picks(sets, codes):
        return [rows_of[c] for c in sets], [pick(c, codes) for c in sets]

    def closed(arriving, others):
        arrived = []
        for value in arriving:
            value, others = barrier((value, others))
            arrived.append(value)
        return barrier((tuple(arrived), others))

    own = columns(y)
    other = columns(1 - y)
    m_own = across_middle(own)
    swap = over_group(other, range(8), 1)
    normed, quarter = norm(hidden, norm_gain, tensor, slice_rows, 2)
    end2 = to_middle(quarter)

    bias = lax.dynamic_slice_in_dim(q_bias, y * half_cols, half_cols, 0)
    kv_bias_here = lax.dynamic_slice_in_dim(kv_bias, (2 * tensor + y) * HD, HD, 1)
    bias = jnp.concatenate([kv_bias_here[0], kv_bias_here[1], bias])[None, :]
    inverse_freq = THETA ** (-2.0 * jnp.arange(HD // 2, dtype=jnp.float32) / HD)
    m_swap = across_middle(after(swap, m_own))
    own, swap, m_own, normed, quarter, end2 = barrier((own, swap, m_own, normed, quarter, end2))

    rows_of = {0: [normed]}
    stack0, end2 = barrier((both(own, swap, 0), end2))
    e0 = to_middle(stack0)
    next1, next2 = both(own, swap, 1), both(own, swap, 2)
    end3 = over_group(end2, MIDDLE, 1)
    across2 = over_x(end2)
    twin2 = over_core(end2)
    tables = []
    for code in range(4):
        _, offset, places = token_layout(prefix_lens, assignment, group ^ code, tok_rows)
        angles = offset.astype(jnp.float32)[:, None] * inverse_freq[None, :]
        cosine, sine = jnp.cos(angles), jnp.sin(angles)
        cosine = jnp.concatenate([cosine, cosine], axis=1)
        sine = jnp.concatenate([-sine, sine], axis=1)
        tables.append((cosine, sine, (places - offset)[:, None]))
    m_e0 = across_middle(after(e0, m_swap))
    (e0, m_swap, end3, across2, twin2), (next1, next2, end2, tables, quarter) = closed(
        (e0, m_swap, end3, across2, twin2), (next1, next2, end2, tables, quarter)
    )

    first_codes, last_codes = (0, 1, 6, 7), (2, 3, 4, 5)
    first_pieces = {0: own, 1: swap, 6: m_own, 7: m_swap}
    last_pieces = {}

    def parts_of(code, chunks):
        low, wide = begin[chunks[0]], sum(widths[chunk] for chunk in chunks)
        if code in first_codes:
            return [(first_pieces[code], None, low, wide)]
        return [(last_pieces[code, chunk], code & 1, 0, widths[chunk]) for chunk in chunks]

    def first_sums(sets):
        rows, picks = rows_and_picks(sets, first_codes)
        pieces = [parts_of(c, (1, 2)) for c in first_codes]
        return heads_of(rows, picks, pieces, sum(widths[1:]))

    outs = {}

    def finished(sets, chunks, totals=None):
        codes = last_codes if totals is not None else first_codes + last_codes
        rows, picks = rows_and_picks(sets, codes)
        low, wide = begin[chunks[0]], sum(widths[chunk] for chunk in chunks)
        if totals is not None:
            totals = [(total, (low - begin[1]) // wide) for total in totals]
        made = heads_of(
            rows,
            picks,
            [parts_of(c, chunks) for c in codes],
            wide,
            totals,
            (
                bias[:, low : low + wide],
                [tables[c] for c in sets],
                None if chunks[0] == 0 else [outs[c, 0] for c in sets],
            ),
        )
        for code, out in zip(sets, made):
            outs[code, chunks[0]] = out

    e1 = to_middle(next1)
    end1 = over_group(quarter, MIDDLE, 1)
    across3 = over_x(end3)
    far2 = over_core(across2)
    rows_of[2] = [end2, twin2, across2, far2]
    sums = dict(zip((0, 2), first_sums((0, 2))))
    m_e1 = across_middle(after(e1, m_e0))
    (m_e0, e1, end1, across3), (next2, e0, end3, far2, sums) = closed(
        (m_e0, e1, end1, across3), (next2, e0, end3, far2, sums)
    )
    rows_of[2] = [end2, twin2, across2, far2]

    e2 = to_middle(next2)
    across1 = over_x(end1)
    twin3 = over_core(end3)
    far3 = over_core(across3)
    rows_of[3] = [end3, twin3, across3, far3]

    def send_back(code, chunk):
        return over_group(outs[code, chunk], MIDDLE, code)

    def arrived(chunk, end, middle):
        for code in last_codes:
            last_pieces[code, chunk] = end if code < 4 else middle

    arrived(0, e0, m_e0)
    finished((2, 3, 0), (0,))
    (sums[3],) = first_sums((3,))
    m_e2 = across_middle(after(e2, m_e1))
    (m_e1, across1, e2), (end1, made, sums) = closed(
        (m_e1, across1, e2), (end1, [outs[c, 0] for c in (2, 3, 0)], sums)
    )
    for code, out in zip((2, 3, 0), made):
        outs[code, 0] = out

    back = {(code, 0): send_back(code, 0) for code in (2, 3)}
    twin1 = over_core(end1)
    far1 = over_core(across1)
    rows_of[1] = [end1, twin1, across1, far1]
    arrived(1, e1, m_e1)
    three = (2, 3, 0)
    finished(three, (1,), [sums[c] for c in three])
    for code in (2, 3):
        back[code, 1] = send_back(code, 1)
    finished((1,), (0, 1))
    back[1, 0] = send_back(1, 0)
    (m_e2, back[2, 0], back[3, 0]), (sums, outs[2, 1], outs[3, 1], outs[1, 0]) = closed(
        (m_e2, back[2, 0], back[3, 0]), (sums, outs[2, 1], outs[3, 1], outs[1, 0])
    )

    arrived(2, e2, m_e2)
    finished(three, (2,), [sums[c] for c in three])
    finished((1,), (2,))
    for code in (3, 2, 1):
        back[code, 2] = send_back(code, 2)

    parts = (0, 1, 2)
    context = gather_context(
        jnp.stack([y, is_middle.astype(jnp.int32)]),
        [outs[0, part] for part in parts],
        [back[1, part] for part in (0, 2)],
        [back[2, part] for part in parts],
        [back[3, part] for part in parts],
        q_cols,
    )

    def cache(part):
        return part[:, :TILE].reshape(tok_rows, 2, HD)

    mine = jnp.where(is_middle, cache(outs[0, 0]), cache(back[2, 0]))
    its = jnp.where(is_middle, cache(back[1, 0]), cache(back[3, 0]))
    kv_cache = jnp.where(
        y == 0,
        jnp.concatenate([mine, its], axis=-1),
        jnp.concatenate([its, mine], axis=-1),
    )
    return (context, kv_cache)


def solution(mesh):
    placed = (
        P("group", None),
        P(),
        P("group", "tensor"),
        P("tensor"),
        P("group", None, None),
        P(),
        P(),
        P(),
    )
    fits = mesh.shape["group"] == 8 and mesh.shape["tensor"] == 4
    return jax.shard_map(
        middle_form if fits else gathered_form,
        mesh=mesh,
        in_specs=placed,
        out_specs=(P("group", "tensor"), P("group", None, "tensor")),
        check_vma=False,
    )
```

```python
import functools
import math

import jax
import jax.numpy as jnp
from jax import lax
from jax.experimental import pallas as pl
from jax.experimental.pallas import tpu as pltpu
from jax.sharding import PartitionSpec as P

HD = 128


EPS = 1e-06
THETA = 1000000.0
QROWS = 128
MAXLEN = 256


def token_layout(prefix_lens, assignment, group_id, tok_rows):
    rollouts = prefix_lens.shape[0]
    member = assignment == group_id
    own_lens = jnp.where(member, prefix_lens, 0)
    starts = jnp.cumsum(own_lens) - own_lens
    places = jnp.arange(tok_rows, dtype=jnp.int32)
    inside = (
        member[None, :]
        & (places[:, None] >= starts[None, :])
        & (places[:, None] < (starts + own_lens)[None, :])
    )
    owner_id = jnp.sum(jnp.where(inside, jnp.arange(rollouts, dtype=jnp.int32)[None, :], 0), axis=1)
    offset = places - jnp.sum(jnp.where(inside, starts[None, :], 0), axis=1)
    return (owner_id, offset, places)


def rotate(values, offset):
    half_dim = values.shape[-1] // 2
    inverse_freq = THETA ** (-2.0 * jnp.arange(half_dim, dtype=jnp.float32) / values.shape[-1])
    angles = offset.astype(jnp.float32)[:, None] * inverse_freq[None, :]
    cosine = jnp.cos(angles)[:, None, :]
    sine_part = jnp.sin(angles)[:, None, :]
    first_half = values[..., :half_dim]
    second_half = values[..., half_dim:]
    return jnp.concatenate(
        [
            first_half * cosine - second_half * sine_part,
            second_half * cosine + first_half * sine_part,
        ],
        axis=-1,
    )


def add_product(normed, portion):
    return jnp.dot(normed, portion, preferred_element_type=jnp.float32)


def normalise(hidden, norm_gain):
    widened = hidden.astype(jnp.float32)
    return (
        widened * lax.rsqrt(jnp.mean(widened * widened, axis=-1, keepdims=True) + EPS) * norm_gain
    ).astype(jnp.bfloat16)


def gathered_form(
    hidden, norm_gain, q_weight, q_bias, kv_weight, kv_bias, prefix_lens, assignment
):
    tok_rows, features = hidden.shape
    slice_rows = kv_weight.shape[0]
    q_cols = q_weight.shape[1]
    kv_total = kv_weight.shape[2]
    heads_here = q_cols // HD
    tensor_pos = lax.axis_index("tensor")
    kv_cols = kv_total // lax.axis_size("tensor")
    normed = normalise(hidden, norm_gain)
    queries = add_product(normed, lax.all_gather(q_weight, "group", axis=0, tiled=True)) + q_bias
    head_span = max(kv_cols, HD)
    head_base = tensor_pos * kv_cols // head_span * head_span
    local_start = tensor_pos * kv_cols - head_base
    head_rows = lax.dynamic_slice_in_dim(kv_weight, head_base, head_span, 2).reshape(
        slice_rows, 2 * head_span
    )
    projected = add_product(normed, lax.all_gather(head_rows, "group", axis=0, tiled=True))
    projected = projected.reshape(tok_rows, 2, head_span) + lax.dynamic_slice_in_dim(
        kv_bias, head_base, head_span, 1
    )
    kv_here = head_span // HD
    group_size = heads_here // kv_here
    owner_id, offset, places = token_layout(
        prefix_lens, assignment, lax.axis_index("group"), tok_rows
    )
    rotated_queries = rotate(queries.reshape(tok_rows, heads_here, HD), offset).astype(jnp.bfloat16)
    rotated_keys = rotate(projected[:, 0].reshape(tok_rows, kv_here, HD), offset).astype(
        jnp.bfloat16
    )
    value_heads = projected[:, 1].reshape(tok_rows, kv_here, HD).astype(jnp.bfloat16)
    visible = (owner_id[:, None] == owner_id[None, :]) & (places[None, :] <= places[:, None])
    grouped = rotated_queries.reshape(tok_rows, kv_here, group_size, HD)
    scores = jnp.einsum(
        "qgph,kgh->gpqk", grouped, rotated_keys, preferred_element_type=jnp.float32
    ) / math.sqrt(HD)
    scores = jnp.where(visible[None, None], scores, -jnp.inf)
    row_max = jnp.max(scores, axis=-1, keepdims=True)
    exponent = jnp.exp(scores - row_max)
    weights_bf = (exponent / jnp.sum(exponent, axis=-1, keepdims=True)).astype(jnp.bfloat16)
    context = jnp.einsum(
        "gpqk,kgh->qgph", weights_bf, value_heads, preferred_element_type=jnp.float32
    )
    context = context.astype(jnp.bfloat16).reshape(tok_rows, q_cols)
    stacked = jnp.stack(
        [rotated_keys.reshape(tok_rows, head_span), value_heads.reshape(tok_rows, head_span)],
        axis=1,
    )
    kv_cache = lax.dynamic_slice_in_dim(stacked, local_start, kv_cols, 2)
    return (context, kv_cache)


def norm_kernel(part_ref, hidden_ref, gain_ref, out_ref, part_out_ref):
    widened = hidden_ref[...].astype(jnp.float32)
    scale = lax.rsqrt(jnp.mean(widened * widened, axis=-1, keepdims=True) + EPS)
    normed = (widened * scale * gain_ref[...]).astype(jnp.bfloat16)
    depth = out_ref.shape[2]
    for block in range(out_ref.shape[0]):
        out_ref[block] = normed[:, block * depth : (block + 1) * depth]
    count = part_out_ref.shape[0]
    part_out_ref[...] = out_ref[pl.ds(part_ref[0] * count, count)]


def norm(hidden, norm_gain, part, depth, count):
    rows, features = hidden.shape
    blocks = features // depth
    step = 64
    return pl.pallas_call(
        norm_kernel,
        grid_spec=pltpu.PrefetchScalarGridSpec(
            num_scalar_prefetch=1,
            grid=(rows // step,),
            in_specs=[
                pl.BlockSpec((step, features), lambda i, part: (i, 0)),
                pl.BlockSpec((1, features), lambda i, part: (0, 0)),
            ],
            out_specs=[
                pl.BlockSpec((blocks, step, depth), lambda i, part: (0, i, 0)),
                pl.BlockSpec((count, step, depth), lambda i, part: (0, i, 0)),
            ],
        ),
        out_shape=[
            jax.ShapeDtypeStruct((blocks, rows, depth), jnp.bfloat16),
            jax.ShapeDtypeStruct((count, rows, depth), jnp.bfloat16),
        ],
        compiler_params=pltpu.CompilerParams(vmem_limit_bytes=32 * 2**20),
        cost_estimate=pl.CostEstimate(
            flops=4 * rows * features, bytes_accessed=5 * rows * features, transcendentals=rows
        ),
    )(part[None], hidden, norm_gain[None])


TILE = 2 * HD


def turn(value, cosine, sine):
    return (value * cosine + pltpu.roll(value, HD // 2, 1) * sine).astype(jnp.bfloat16)


def attention(queries, keys, values, first_ref, out_ref, skip):
    heads = len(queries)
    rows = out_ref.shape[0]
    scale = math.log2(math.e) / math.sqrt(HD)
    for top in range(0, rows, QROWS):
        low, end = max(0, top - MAXLEN), top + QROWS
        shape = (QROWS, end - low)
        stacked = jnp.concatenate([query[top:end] for query in queries], axis=0)
        scores = lax.dot_general(
            stacked, keys[low:end], (((1,), (1,)), ((), ())), preferred_element_type=jnp.float32
        )
        row = lax.broadcasted_iota(jnp.int32, shape, 0) + top
        col = lax.broadcasted_iota(jnp.int32, shape, 1) + low
        visible = (col <= row) & (col >= first_ref[top:end])
        scores = jnp.where(visible[None], scores.reshape(heads, *shape), -jnp.inf)
        most = jnp.max(scores, axis=-1, keepdims=True)
        exponent = jnp.exp2((scores - most) * scale)
        share = 1.0 / jnp.sum(exponent, axis=-1, keepdims=True)
        weights = (exponent * share).astype(jnp.bfloat16)
        context = jnp.dot(
            weights.reshape(heads * QROWS, end - low),
            values[low:end],
            preferred_element_type=jnp.float32,
        ).astype(jnp.bfloat16)
        for head in range(heads):
            out_ref[top:end, skip + head * HD : skip + (head + 1) * HD] = context[
                head * QROWS : (head + 1) * QROWS
            ]


def heads_kernel(plan, pick_ref, *refs):
    sources, parts, width, totals_at, finish, with_keys = plan
    sets, count = len(sources), len(parts)
    refs = list(refs)

    def take(number):
        taken = refs[:number]
        del refs[:number]
        return taken

    row_refs = [take(number) for number in sources]
    weight_refs = [take(len(part)) for part in parts]
    total_refs = take(sets) if totals_at is not None else None
    if finish:
        (bias_ref,) = take(1)
        table_refs, first_refs = take(sets), take(sets)
        cache_refs = None if with_keys else take(sets)
    outs = take(sets)
    row_buf, weight_buf, acc, row_sem, weight_sem, total_sem, out_sem = take(7)
    depth = row_buf.shape[2] // count

    def weight_copies(piece):
        column = 0
        for part, (ref, (lead, skip, wide)) in enumerate(zip(weight_refs[piece], parts[piece])):
            ref = ref if lead is None else ref.at[lead]
            yield pltpu.make_async_copy(
                ref.at[:, skip : skip + wide],
                weight_buf.at[piece * depth : (piece + 1) * depth, column : column + wide],
                weight_sem.at[piece, part],
            )
            column += wide

    def row_copy(which, piece, source):
        return pltpu.make_async_copy(
            row_refs[which][source].at[pick_ref[which, 1, piece]],
            row_buf.at[which, :, piece * depth : (piece + 1) * depth],
            row_sem.at[which, piece],
        )

    def total_copy(which):
        return pltpu.make_async_copy(
            total_refs[which].at[:, totals_at : totals_at + width],
            acc.at[which],
            total_sem.at[which],
        )

    half = count // 2
    stages = [(0, 0, half), (0, half, count)] + [(which, 0, count) for which in range(1, sets)]
    if width > 2 * TILE and count > 4:
        stages[:1] = [(0, 0, half // 2), (0, half // 2, half)]

    def start(stage):
        which, low, high = stages[stage]
        for piece in range(low, high):
            if which == 0:
                for copy in weight_copies(piece):
                    copy.start()
            if sources[which] == 1:
                row_copy(which, piece, 0).start()
            else:
                for source in range(sources[which]):

                    @pl.when(pick_ref[which, 0, piece] == source)
                    def _():
                        row_copy(which, piece, source).start()
        if low == 0 and total_refs is not None:
            total_copy(which).start()

    start(0)
    if finish:
        bias_buf, table_buf, first_buf, *rest = refs[: 3 if with_keys else 4]
        out_buf, side_sem = refs[-2:]
        bias_copy = pltpu.make_async_copy(bias_ref, bias_buf, side_sem.at[sets, 0])
        side_copies = []
        for which in range(sets):
            pairs = [(table_refs[which], table_buf), (first_refs[which], first_buf)]
            if not with_keys:
                pairs.append((cache_refs[which].at[:, :TILE], rest[0]))
            side_copies.append(
                [
                    pltpu.make_async_copy(ref, buf.at[which], side_sem.at[which, number])
                    for number, (ref, buf) in enumerate(pairs)
                ]
            )

    def out_copy(which):
        buf = out_buf if finish else acc
        return pltpu.make_async_copy(buf.at[which], outs[which], out_sem.at[which])

    for stage, (which, low, high) in enumerate(stages):
        for piece in range(low, high):
            if which == 0:
                for copy in weight_copies(piece):
                    copy.wait()
            row_copy(which, piece, 0).wait()
        if low == 0 and total_refs is not None:
            total_copy(which).wait()
        if stage + 1 < len(stages):
            start(stage + 1)
        if stage == 0 and finish:
            bias_copy.start()
            for copies in side_copies:
                for copy in copies:
                    copy.start()
        for at in range(0, width, TILE):
            cols = slice(at, at + TILE)
            term = jnp.dot(
                row_buf[which, :, low * depth : high * depth],
                weight_buf[low * depth : high * depth, cols],
                preferred_element_type=jnp.float32,
            )
            if low > 0 or total_refs is not None:
                term = acc[which, :, cols] + term
            acc[which, :, cols] = term
        if high < count:
            continue
        if finish:
            if which == 0:
                bias_copy.wait()
            for copy in side_copies[which]:
                copy.wait()
            finish_set(
                acc.at[which],
                bias_buf,
                table_buf[which],
                first_buf.at[which],
                None if with_keys else rest[0].at[which],
                out_buf.at[which],
            )
        out_copy(which).start()
    for which in range(sets):
        out_copy(which).wait()


def finish_set(acc, bias, table, first, cache, out):
    swapped = pltpu.roll(table, HD // 2, 1)
    left = lax.broadcasted_iota(jnp.int32, table.shape, 1) < HD // 2
    cosine = jnp.where(left, table, swapped)
    sine = jnp.where(left, -swapped, table)
    skip = 0
    if cache is None:
        cache, skip = out, TILE
        out[:, :HD] = turn(acc[:, :HD] + bias[:, :HD], cosine, sine)
        out[:, HD:TILE] = (acc[:, HD:TILE] + bias[:, HD:TILE]).astype(jnp.bfloat16)
    queries = []
    for col in range(skip, out.shape[1], HD):
        cols = slice(col, col + HD)
        queries.append(turn(acc[:, cols] + bias[:, cols], cosine, sine))
    attention(queries, cache.at[:, :HD], cache.at[:, HD:TILE], first, out, skip)


def heads_of(row_sets, picks, pieces, width, totals=None, finish=None):
    sets, count = len(row_sets), len(pieces)
    sources = tuple(len(rows) for rows in row_sets)
    tokens, depth = row_sets[0][0].shape[1:]
    operands = [array for rows in row_sets for array in rows]
    operands += [array for piece in pieces for array, *_ in piece]
    totals_at = None
    if totals is not None:
        totals, totals_at = totals
        operands += totals
    scratch = [
        pltpu.VMEM((sets, tokens, count * depth), jnp.bfloat16),
        pltpu.VMEM((count * depth, width), jnp.bfloat16),
        pltpu.VMEM((sets, tokens, width), jnp.float32),
        pltpu.SemaphoreType.DMA((sets, count)),
        pltpu.SemaphoreType.DMA((count, max(map(len, pieces)))),
        pltpu.SemaphoreType.DMA((sets,)),
        pltpu.SemaphoreType.DMA((sets,)),
    ]
    with_keys = False
    kind = jnp.float32
    if finish is not None:
        bias, tables, firsts, caches = finish
        kind = jnp.bfloat16
        operands += [bias, *tables, *firsts]
        scratch += [
            pltpu.VMEM((1, width), jnp.float32),
            pltpu.VMEM((sets, tokens, HD), jnp.float32),
            pltpu.VMEM((sets, tokens, 1), jnp.int32),
        ]
        with_keys = caches is None
        if not with_keys:
            operands += caches
            scratch.append(pltpu.VMEM((sets, tokens, TILE), jnp.bfloat16))
        scratch += [
            pltpu.VMEM((sets, tokens, width), jnp.bfloat16),
            pltpu.SemaphoreType.DMA((sets + 1, 3)),
        ]
    plan = (
        sources,
        tuple(tuple(part[1:] for part in piece) for piece in pieces),
        width,
        totals_at,
        finish is not None,
        with_keys,
    )
    anywhere = pl.BlockSpec(memory_space=pl.ANY)
    return pl.pallas_call(
        functools.partial(heads_kernel, plan),
        grid_spec=pltpu.PrefetchScalarGridSpec(
            num_scalar_prefetch=1,
            grid=(1,),
            in_specs=[anywhere] * len(operands),
            out_specs=[anywhere] * sets,
            scratch_shapes=scratch,
        ),
        out_shape=[jax.ShapeDtypeStruct((tokens, width), kind)] * sets,
        compiler_params=pltpu.CompilerParams(vmem_limit_bytes=56 * 2**20),
        cost_estimate=pl.CostEstimate(
            flops=2 * sets * count * tokens * depth * width,
            bytes_accessed=2 * count * depth * (sets * tokens + width) + 8 * sets * tokens * width,
            transcendentals=0,
        ),
    )(jnp.stack(picks), *operands)


def gather_kernel(numbers, flag_ref, *refs):
    ends = [sum(numbers[: i + 1]) for i in range(4)]
    near, beside, back, other = (refs[end - number : end] for end, number in zip(ends, numbers))
    out_ref = refs[-1]
    half = out_ref.shape[1] // 2

    def put(sources, side):
        place = side * half
        for part, source in enumerate(sources):
            value = source[:, TILE if part == 0 else 0 :]
            out_ref[:, place : place + value.shape[1]] = value
            place += value.shape[1]

    for middle, mine, its in ((1, near, beside), (0, back, other)):
        for side in range(2):

            @pl.when((flag_ref[0] == side) & (flag_ref[1] == middle))
            def _():
                put(mine, side)
                put(its, 1 - side)


def gather_context(flags, near, beside, back, other, cols):
    operands = [*near, *beside, *back, *other]
    rows, step = near[0].shape[0], QROWS
    return pl.pallas_call(
        functools.partial(gather_kernel, tuple(map(len, (near, beside, back, other)))),
        grid_spec=pltpu.PrefetchScalarGridSpec(
            num_scalar_prefetch=1,
            grid=(rows // step,),
            in_specs=[
                pl.BlockSpec((step, operand.shape[1]), lambda i, flags: (i, 0))
                for operand in operands
            ],
            out_specs=pl.BlockSpec((step, cols), lambda i, flags: (i, 0)),
        ),
        out_shape=jax.ShapeDtypeStruct((rows, cols), jnp.bfloat16),
        compiler_params=pltpu.CompilerParams(vmem_limit_bytes=24 * 2**20),
        cost_estimate=pl.CostEstimate(flops=0, bytes_accessed=6 * rows * cols, transcendentals=0),
    )(flags, *operands)


MIDDLE = (2, 3, 4, 5)
ENDS = (0, 1, 6, 7)


def after(value, *others):
    return lax.optimization_barrier((value,) + others)[0]


def pairs_from(sources, code):
    return [(s, s ^ code) for s in sources]


def middle_form(hidden, norm_gain, q_weight, q_bias, kv_weight, kv_bias, prefix_lens, assignment):
    tok_rows, features = hidden.shape
    slice_rows, q_cols = q_weight.shape
    half_cols = q_cols // 2
    group = lax.axis_index("group")
    tensor = lax.axis_index("tensor")
    y = group & 1
    is_middle = (group >= 2) & (group < 6)
    barrier = lax.optimization_barrier

    def over_group(value, sources, code):
        return lax.ppermute(value, "group", pairs_from(sources, code))

    def to_middle(value):
        return over_group(value, ENDS, 2)

    def across_middle(value):
        return over_group(value, MIDDLE, 6)

    def over_x(value):
        return lax.ppermute(value, "tensor", pairs_from(range(4), 2))

    def over_core(value):
        return lax.ppermute(value, "tensor", pairs_from(range(4), 1))

    begin, widths = (0, 2 * TILE, 4 * TILE), (2 * TILE, 2 * TILE, TILE)

    def columns(half):
        head = (2 * tensor + half) * HD
        kv_part = lax.dynamic_slice_in_dim(kv_weight, head, HD, 2).reshape(slice_rows, TILE)
        q_part = lax.dynamic_slice_in_dim(q_weight, half * half_cols, half_cols, 1)
        return jnp.concatenate([kv_part, q_part], axis=1)

    def both(one, two, chunk):
        low, high = begin[chunk], begin[chunk] + widths[chunk]
        return jnp.stack([one[:, low:high], two[:, low:high]])

    def pick(code_of_rows, codes):
        block = jnp.stack([group ^ code for code in codes])
        if code_of_rows == 0:
            return jnp.stack([block * 0, block])
        return jnp.stack([(block >> 1) ^ tensor, block & 1])

    def rows_and_picks(sets, codes):
        return [rows_of[c] for c in sets], [pick(c, codes) for c in sets]

    def closed(arriving, others):
        arrived = []
        for value in arriving:
            value, others = barrier((value, others))
            arrived.append(value)
        return barrier((tuple(arrived), others))

    own = columns(y)
    other = columns(1 - y)
    m_own = across_middle(own)
    swap = over_group(other, range(8), 1)
    normed, quarter = norm(hidden, norm_gain, tensor, slice_rows, 2)
    end2 = to_middle(quarter)

    bias = lax.dynamic_slice_in_dim(q_bias, y * half_cols, half_cols, 0)
    kv_bias_here = lax.dynamic_slice_in_dim(kv_bias, (2 * tensor + y) * HD, HD, 1)
    bias = jnp.concatenate([kv_bias_here[0], kv_bias_here[1], bias])[None, :]
    inverse_freq = THETA ** (-2.0 * jnp.arange(HD // 2, dtype=jnp.float32) / HD)
    m_swap = across_middle(after(swap, m_own))
    own, swap, m_own, normed, quarter, end2 = barrier((own, swap, m_own, normed, quarter, end2))

    rows_of = {0: [normed]}
    stack0, end2 = barrier((both(own, swap, 0), end2))
    e0 = to_middle(stack0)
    next1, next2 = both(own, swap, 1), both(own, swap, 2)
    end3 = over_group(end2, MIDDLE, 1)
    across2 = over_x(end2)
    twin2 = over_core(end2)
    tables = []
    for code in range(4):
        _, offset, places = token_layout(prefix_lens, assignment, group ^ code, tok_rows)
        angles = offset.astype(jnp.float32)[:, None] * inverse_freq[None, :]
        table = jnp.concatenate([jnp.cos(angles), jnp.sin(angles)], axis=1)
        tables.append((table, (places - offset)[:, None]))
    m_e0 = across_middle(after(e0, m_swap))
    (e0, m_swap, end3, across2, twin2), (next1, next2, end2, tables, quarter) = closed(
        (e0, m_swap, end3, across2, twin2), (next1, next2, end2, tables, quarter)
    )

    first_codes, last_codes = (0, 1, 6, 7), (2, 3, 4, 5)
    first_pieces = {0: own, 1: swap, 6: m_own, 7: m_swap}
    last_pieces = {}

    def parts_of(code, chunks):
        low, wide = begin[chunks[0]], sum(widths[chunk] for chunk in chunks)
        if code in first_codes:
            return [(first_pieces[code], None, low, wide)]
        return [(last_pieces[code, chunk], code & 1, 0, widths[chunk]) for chunk in chunks]

    def first_sums(sets):
        rows, picks = rows_and_picks(sets, first_codes)
        pieces = [parts_of(c, (1, 2)) for c in first_codes]
        return heads_of(rows, picks, pieces, sum(widths[1:]))

    outs = {}

    def finished(sets, chunks, totals=None):
        codes = last_codes if totals is not None else first_codes + last_codes
        rows, picks = rows_and_picks(sets, codes)
        low, wide = begin[chunks[0]], sum(widths[chunk] for chunk in chunks)
        if totals is not None:
            totals = (totals, low - begin[1])
        made = heads_of(
            rows,
            picks,
            [parts_of(c, chunks) for c in codes],
            wide,
            totals,
            (
                bias[:, low : low + wide],
                [tables[c][0] for c in sets],
                [tables[c][1] for c in sets],
                None if chunks[0] == 0 else [outs[c, 0] for c in sets],
            ),
        )
        for code, out in zip(sets, made):
            outs[code, chunks[0]] = out

    e1 = to_middle(next1)
    end1 = over_group(quarter, MIDDLE, 1)
    across3 = over_x(end3)
    far2 = over_core(across2)
    rows_of[2] = [end2, twin2, across2, far2]
    sums = dict(zip((0, 2), first_sums((0, 2))))
    m_e1 = across_middle(after(e1, m_e0))
    (m_e0, e1, end1, across3), (next2, e0, end3, far2, sums) = closed(
        (m_e0, e1, end1, across3), (next2, e0, end3, far2, sums)
    )
    rows_of[2] = [end2, twin2, across2, far2]

    e2 = to_middle(next2)
    across1 = over_x(end1)
    twin3 = over_core(end3)
    far3 = over_core(across3)
    rows_of[3] = [end3, twin3, across3, far3]

    def send_back(code, chunk):
        return over_group(outs[code, chunk], MIDDLE, code)

    def arrived(chunk, end, middle):
        for code in last_codes:
            last_pieces[code, chunk] = end if code < 4 else middle

    arrived(0, e0, m_e0)
    finished((2, 3, 0), (0,))
    (sums[3],) = first_sums((3,))
    m_e2 = across_middle(after(e2, m_e1))
    (m_e1, across1, e2), (end1, made, sums) = closed(
        (m_e1, across1, e2), (end1, [outs[c, 0] for c in (2, 3, 0)], sums)
    )
    for code, out in zip((2, 3, 0), made):
        outs[code, 0] = out

    back = {(code, 0): send_back(code, 0) for code in (2, 3)}
    twin1 = over_core(end1)
    far1 = over_core(across1)
    arrived(1, e1, m_e1)
    finished((2, 3), (1,), [sums[c] for c in (2, 3)])
    for code in (2, 3):
        back[code, 1] = send_back(code, 1)
    far1, outs[2, 1] = barrier((far1, outs[2, 1]))
    rows_of[1] = [end1, twin1, across1, far1]
    finished((1,), (0, 1))
    back[1, 0] = send_back(1, 0)
    (m_e2, back[2, 0], back[3, 0]), (sums, outs[2, 1], outs[3, 1], outs[1, 0]) = closed(
        (m_e2, back[2, 0], back[3, 0]), (sums, outs[2, 1], outs[3, 1], outs[1, 0])
    )

    arrived(2, e2, m_e2)
    finished((2, 3), (2,), [sums[c] for c in (2, 3)])
    for code in (2, 3):
        back[code, 2] = send_back(code, 2)
    finished((1,), (2,))
    back[1, 2] = send_back(1, 2)
    sums[0], outs[1, 2] = barrier((sums[0], outs[1, 2]))
    finished((0,), (1, 2), [sums[0]])

    parts = (0, 1, 2)
    context = gather_context(
        jnp.stack([y, is_middle.astype(jnp.int32)]),
        [outs[0, part] for part in (0, 1)],
        [back[1, part] for part in (0, 2)],
        [back[2, part] for part in parts],
        [back[3, part] for part in parts],
        q_cols,
    )

    def cache(part):
        return part[:, :TILE].reshape(tok_rows, 2, HD)

    mine = jnp.where(is_middle, cache(outs[0, 0]), cache(back[2, 0]))
    its = jnp.where(is_middle, cache(back[1, 0]), cache(back[3, 0]))
    kv_cache = jnp.where(
        y == 0,
        jnp.concatenate([mine, its], axis=-1),
        jnp.concatenate([its, mine], axis=-1),
    )
    return (context, kv_cache)


def solution(mesh):
    placed = (
        P("group", None),
        P(),
        P("group", "tensor"),
        P("tensor"),
        P("group", None, None),
        P(),
        P(),
        P(),
    )
    fits = mesh.shape["group"] == 8 and mesh.shape["tensor"] == 4
    return jax.shard_map(
        middle_form if fits else gathered_form,
        mesh=mesh,
        in_specs=placed,
        out_specs=(P("group", "tensor"), P("group", None, "tensor")),
        check_vma=False,
    )
```

```python
import functools
import math

import jax
import jax.numpy as jnp
from jax import lax
from jax.experimental import pallas as pl
from jax.experimental.pallas import tpu as pltpu
from jax.sharding import PartitionSpec as P

HD = 128


EPS = 1e-06
THETA = 1000000.0
QROWS = 128
MAXLEN = 256


def token_layout(prefix_lens, assignment, group_id, tok_rows):
    rollouts = prefix_lens.shape[0]
    member = assignment == group_id
    own_lens = jnp.where(member, prefix_lens, 0)
    starts = jnp.cumsum(own_lens) - own_lens
    places = jnp.arange(tok_rows, dtype=jnp.int32)
    inside = (
        member[None, :]
        & (places[:, None] >= starts[None, :])
        & (places[:, None] < (starts + own_lens)[None, :])
    )
    owner_id = jnp.sum(jnp.where(inside, jnp.arange(rollouts, dtype=jnp.int32)[None, :], 0), axis=1)
    offset = places - jnp.sum(jnp.where(inside, starts[None, :], 0), axis=1)
    return (owner_id, offset, places)


def rotate(values, offset):
    half_dim = values.shape[-1] // 2
    inverse_freq = THETA ** (-2.0 * jnp.arange(half_dim, dtype=jnp.float32) / values.shape[-1])
    angles = offset.astype(jnp.float32)[:, None] * inverse_freq[None, :]
    cosine = jnp.cos(angles)[:, None, :]
    sine_part = jnp.sin(angles)[:, None, :]
    first_half = values[..., :half_dim]
    second_half = values[..., half_dim:]
    return jnp.concatenate(
        [
            first_half * cosine - second_half * sine_part,
            second_half * cosine + first_half * sine_part,
        ],
        axis=-1,
    )


def add_product(normed, portion):
    return jnp.dot(normed, portion, preferred_element_type=jnp.float32)


def normalise(hidden, norm_gain):
    widened = hidden.astype(jnp.float32)
    return (
        widened * lax.rsqrt(jnp.mean(widened * widened, axis=-1, keepdims=True) + EPS) * norm_gain
    ).astype(jnp.bfloat16)


def gathered_form(
    hidden, norm_gain, q_weight, q_bias, kv_weight, kv_bias, prefix_lens, assignment
):
    tok_rows, features = hidden.shape
    slice_rows = kv_weight.shape[0]
    q_cols = q_weight.shape[1]
    kv_total = kv_weight.shape[2]
    heads_here = q_cols // HD
    tensor_pos = lax.axis_index("tensor")
    kv_cols = kv_total // lax.axis_size("tensor")
    normed = normalise(hidden, norm_gain)
    queries = add_product(normed, lax.all_gather(q_weight, "group", axis=0, tiled=True)) + q_bias
    head_span = max(kv_cols, HD)
    head_base = tensor_pos * kv_cols // head_span * head_span
    local_start = tensor_pos * kv_cols - head_base
    head_rows = lax.dynamic_slice_in_dim(kv_weight, head_base, head_span, 2).reshape(
        slice_rows, 2 * head_span
    )
    projected = add_product(normed, lax.all_gather(head_rows, "group", axis=0, tiled=True))
    projected = projected.reshape(tok_rows, 2, head_span) + lax.dynamic_slice_in_dim(
        kv_bias, head_base, head_span, 1
    )
    kv_here = head_span // HD
    group_size = heads_here // kv_here
    owner_id, offset, places = token_layout(
        prefix_lens, assignment, lax.axis_index("group"), tok_rows
    )
    rotated_queries = rotate(queries.reshape(tok_rows, heads_here, HD), offset).astype(jnp.bfloat16)
    rotated_keys = rotate(projected[:, 0].reshape(tok_rows, kv_here, HD), offset).astype(
        jnp.bfloat16
    )
    value_heads = projected[:, 1].reshape(tok_rows, kv_here, HD).astype(jnp.bfloat16)
    visible = (owner_id[:, None] == owner_id[None, :]) & (places[None, :] <= places[:, None])
    grouped = rotated_queries.reshape(tok_rows, kv_here, group_size, HD)
    scores = jnp.einsum(
        "qgph,kgh->gpqk", grouped, rotated_keys, preferred_element_type=jnp.float32
    ) / math.sqrt(HD)
    scores = jnp.where(visible[None, None], scores, -jnp.inf)
    row_max = jnp.max(scores, axis=-1, keepdims=True)
    exponent = jnp.exp(scores - row_max)
    weights_bf = (exponent / jnp.sum(exponent, axis=-1, keepdims=True)).astype(jnp.bfloat16)
    context = jnp.einsum(
        "gpqk,kgh->qgph", weights_bf, value_heads, preferred_element_type=jnp.float32
    )
    context = context.astype(jnp.bfloat16).reshape(tok_rows, q_cols)
    stacked = jnp.stack(
        [rotated_keys.reshape(tok_rows, head_span), value_heads.reshape(tok_rows, head_span)],
        axis=1,
    )
    kv_cache = lax.dynamic_slice_in_dim(stacked, local_start, kv_cols, 2)
    return (context, kv_cache)


def norm_kernel(part_ref, hidden_ref, gain_ref, out_ref, part_out_ref):
    widened = hidden_ref[...].astype(jnp.float32)
    scale = lax.rsqrt(jnp.mean(widened * widened, axis=-1, keepdims=True) + EPS)
    normed = (widened * scale * gain_ref[...]).astype(jnp.bfloat16)
    depth = out_ref.shape[2]
    for block in range(out_ref.shape[0]):
        out_ref[block] = normed[:, block * depth : (block + 1) * depth]
    count = part_out_ref.shape[0]
    part_out_ref[...] = out_ref[pl.ds(part_ref[0] * count, count)]


def norm(hidden, norm_gain, part, depth, count):
    rows, features = hidden.shape
    blocks = features // depth
    step = 64
    return pl.pallas_call(
        norm_kernel,
        grid_spec=pltpu.PrefetchScalarGridSpec(
            num_scalar_prefetch=1,
            grid=(rows // step,),
            in_specs=[
                pl.BlockSpec((step, features), lambda i, part: (i, 0)),
                pl.BlockSpec((1, features), lambda i, part: (0, 0)),
            ],
            out_specs=[
                pl.BlockSpec((blocks, step, depth), lambda i, part: (0, i, 0)),
                pl.BlockSpec((count, step, depth), lambda i, part: (0, i, 0)),
            ],
        ),
        out_shape=[
            jax.ShapeDtypeStruct((blocks, rows, depth), jnp.bfloat16),
            jax.ShapeDtypeStruct((count, rows, depth), jnp.bfloat16),
        ],
        compiler_params=pltpu.CompilerParams(vmem_limit_bytes=32 * 2**20),
        cost_estimate=pl.CostEstimate(
            flops=4 * rows * features, bytes_accessed=5 * rows * features, transcendentals=rows
        ),
    )(part[None], hidden, norm_gain[None])


TILE = 2 * HD


def turn(value, cosine, sine):
    return value * cosine + pltpu.roll(value, HD // 2, 1) * sine


def attention(queries, keys, values, first_ref, out_ref, skip):
    heads = len(queries)
    rows = out_ref.shape[0]
    scale = math.log2(math.e) / math.sqrt(HD)
    for top in range(0, rows, QROWS):
        low, end = max(0, top - MAXLEN), top + QROWS
        shape = (QROWS, end - low)
        stacked = jnp.concatenate([query[top:end] for query in queries], axis=0)
        scores = jnp.dot(stacked, keys[:, low:end], preferred_element_type=jnp.float32)
        row = lax.broadcasted_iota(jnp.int32, shape, 0) + top
        col = lax.broadcasted_iota(jnp.int32, shape, 1) + low
        visible = (col <= row) & (col >= first_ref[top:end])
        scores = jnp.where(visible[None], scores.reshape(heads, *shape), -jnp.inf)
        most = jnp.max(scores, axis=-1, keepdims=True)
        exponent = jnp.exp2((scores - most) * scale)
        share = 1.0 / jnp.sum(exponent, axis=-1, keepdims=True)
        weights = (exponent * share).astype(jnp.bfloat16)
        context = jnp.dot(
            weights.reshape(heads * QROWS, end - low),
            values[low:end],
            preferred_element_type=jnp.float32,
        ).astype(jnp.bfloat16)
        for head in range(heads):
            out_ref[top:end, skip + head * HD : skip + (head + 1) * HD] = context[
                head * QROWS : (head + 1) * QROWS
            ]


def heads_kernel(plan, pick_ref, *refs):
    sources, parts, width, closed_width, totals_at, with_keys = plan
    finish = closed_width > 0
    sets, count = len(sources), len(parts)
    refs = list(refs)

    def take(number):
        taken = refs[:number]
        del refs[:number]
        return taken

    row_refs = [take(number) for number in sources]
    weight_refs = [take(len(part)) for part in parts]
    total_refs = take(sets) if totals_at is not None else None
    if finish:
        (bias_ref,) = take(1)
        table_refs, first_refs = take(sets), take(sets)
        key_refs, value_refs = (None, None) if with_keys else (take(sets), take(sets))
    outs = take(sets)
    key_outs = take(sets) if with_keys else None
    sum_outs = take(sets) if finish and closed_width < width else None
    row_buf, weight_buf, acc, row_sem, weight_sem, total_sem, out_sem = take(7)
    depth = row_buf.shape[2] // count

    def weight_copies(piece):
        column = 0
        for part, (ref, (lead, skip, wide)) in enumerate(zip(weight_refs[piece], parts[piece])):
            ref = ref if lead is None else ref.at[lead]
            yield pltpu.make_async_copy(
                ref.at[:, skip : skip + wide],
                weight_buf.at[piece * depth : (piece + 1) * depth, column : column + wide],
                weight_sem.at[piece, part],
            )
            column += wide

    def row_copy(which, piece, source):
        return pltpu.make_async_copy(
            row_refs[which][source].at[pick_ref[which, 1, piece]],
            row_buf.at[which, :, piece * depth : (piece + 1) * depth],
            row_sem.at[which, piece],
        )

    def total_copy(which):
        return pltpu.make_async_copy(
            total_refs[which].at[:, totals_at : totals_at + width],
            acc.at[which],
            total_sem.at[which],
        )

    half = count // 2
    stages = [(0, 0, half), (0, half, count)] + [(which, 0, count) for which in range(1, sets)]
    if width > 2 * TILE and count > 4:
        stages[:1] = [(0, 0, half // 2), (0, half // 2, half)]

    def start(stage):
        which, low, high = stages[stage]
        for piece in range(low, high):
            if which == 0:
                for copy in weight_copies(piece):
                    copy.start()
            if sources[which] == 1:
                row_copy(which, piece, 0).start()
            else:
                for source in range(sources[which]):

                    @pl.when(pick_ref[which, 0, piece] == source)
                    def _():
                        row_copy(which, piece, source).start()
        if low == 0 and total_refs is not None:
            total_copy(which).start()

    start(0)
    if finish:
        bias_buf, table_buf, first_buf, key_buf, value_buf, out_buf, side_sem = refs
        bias_copy = pltpu.make_async_copy(bias_ref, bias_buf, side_sem.at[sets, 0])
        side_copies = []
        for which in range(sets):
            pairs = [(table_refs[which], table_buf), (first_refs[which], first_buf)]
            if not with_keys:
                pairs += [
                    (key_refs[which], key_buf),
                    (value_refs[which].at[:, HD:TILE], value_buf),
                ]
            side_copies.append(
                [
                    pltpu.make_async_copy(ref, buf.at[which], side_sem.at[which, number])
                    for number, (ref, buf) in enumerate(pairs)
                ]
            )

    def out_copies(which):
        pairs = [((out_buf if finish else acc).at[which], outs[which])]
        if key_outs is not None:
            pairs.append((key_buf.at[which], key_outs[which]))
        if sum_outs is not None:
            pairs.append((acc.at[which, :, closed_width:], sum_outs[which]))
        return [
            pltpu.make_async_copy(buf, ref, out_sem.at[which, number])
            for number, (buf, ref) in enumerate(pairs)
        ]

    for stage, (which, low, high) in enumerate(stages):
        for piece in range(low, high):
            if which == 0:
                for copy in weight_copies(piece):
                    copy.wait()
            row_copy(which, piece, 0).wait()
        if low == 0 and total_refs is not None:
            total_copy(which).wait()
        if stage + 1 < len(stages):
            start(stage + 1)
        if stage == 0 and finish:
            bias_copy.start()
            for copies in side_copies:
                for copy in copies:
                    copy.start()
        for at in range(0, width, TILE):
            top = min(high, count - 2) if finish and at >= closed_width else high
            if top <= low:
                continue
            cols = slice(at, at + TILE)
            term = jnp.dot(
                row_buf[which, :, low * depth : top * depth],
                weight_buf[low * depth : top * depth, cols],
                preferred_element_type=jnp.float32,
            )
            if low > 0 or total_refs is not None:
                term = acc[which, :, cols] + term
            acc[which, :, cols] = term
        if high < count:
            continue
        if finish:
            if which == 0:
                bias_copy.wait()
            for copy in side_copies[which]:
                copy.wait()
            finish_set(
                acc.at[which],
                bias_buf,
                table_buf[which],
                first_buf.at[which],
                key_buf.at[which],
                value_buf.at[which],
                out_buf.at[which],
                with_keys,
            )
        for copy in out_copies(which):
            copy.start()
    for which in range(sets):
        for copy in out_copies(which):
            copy.wait()


def finish_set(acc, bias, table, first, keys, values, out, with_keys):
    swapped = pltpu.roll(table, HD // 2, 1)
    left = lax.broadcasted_iota(jnp.int32, table.shape, 1) < HD // 2
    cosine = jnp.where(left, table, swapped)
    sine = jnp.where(left, -swapped, table)
    skip = 0
    if with_keys:
        skip = TILE
        turned = turn(acc[:, :HD] + bias[:, :HD], cosine, sine)
        out[:, :HD] = turned.astype(jnp.bfloat16)
        keys[...] = turned.T.astype(jnp.bfloat16)
        value = (acc[:, HD:TILE] + bias[:, HD:TILE]).astype(jnp.bfloat16)
        out[:, HD:TILE] = value
        values[...] = value
    queries = []
    for col in range(skip, out.shape[1], HD):
        cols = slice(col, col + HD)
        queries.append(turn(acc[:, cols] + bias[:, cols], cosine, sine).astype(jnp.bfloat16))
    attention(queries, keys, values, first, out, skip)


def heads_of(row_sets, picks, pieces, width, totals=None, finish=None):
    sets, count = len(row_sets), len(pieces)
    sources = tuple(len(rows) for rows in row_sets)
    tokens, depth = row_sets[0][0].shape[1:]
    operands = [array for rows in row_sets for array in rows]
    operands += [array for piece in pieces for array, *_ in piece]
    totals_at = None
    if totals is not None:
        totals, totals_at = totals
        operands += totals
    scratch = [
        pltpu.VMEM((sets, tokens, count * depth), jnp.bfloat16),
        pltpu.VMEM((count * depth, width), jnp.bfloat16),
        pltpu.VMEM((sets, tokens, width), jnp.float32),
        pltpu.SemaphoreType.DMA((sets, count)),
        pltpu.SemaphoreType.DMA((count, max(map(len, pieces)))),
        pltpu.SemaphoreType.DMA((sets,)),
        pltpu.SemaphoreType.DMA((sets, 3)),
    ]
    with_keys, closed_width = False, 0
    out_shape = [jax.ShapeDtypeStruct((tokens, width), jnp.float32)] * sets
    if finish is not None:
        closed_width, bias, tables, firsts, caches = finish
        out_shape = [jax.ShapeDtypeStruct((tokens, closed_width), jnp.bfloat16)] * sets
        operands += [bias, *tables, *firsts]
        with_keys = caches is None
        if with_keys:
            out_shape += [jax.ShapeDtypeStruct((HD, tokens), jnp.bfloat16)] * sets
        else:
            operands += [keys for keys, _ in caches] + [values for _, values in caches]
        if closed_width < width:
            out_shape += [jax.ShapeDtypeStruct((tokens, width - closed_width), jnp.float32)] * sets
        scratch += [
            pltpu.VMEM((1, closed_width), jnp.float32),
            pltpu.VMEM((sets, tokens, HD), jnp.float32),
            pltpu.VMEM((sets, tokens, 1), jnp.int32),
            pltpu.VMEM((sets, HD, tokens), jnp.bfloat16),
            pltpu.VMEM((sets, tokens, HD), jnp.bfloat16),
            pltpu.VMEM((sets, tokens, closed_width), jnp.bfloat16),
            pltpu.SemaphoreType.DMA((sets + 1, 4)),
        ]
    plan = (
        sources,
        tuple(tuple(part[1:] for part in piece) for piece in pieces),
        width,
        closed_width,
        totals_at,
        with_keys,
    )
    anywhere = pl.BlockSpec(memory_space=pl.ANY)
    return pl.pallas_call(
        functools.partial(heads_kernel, plan),
        grid_spec=pltpu.PrefetchScalarGridSpec(
            num_scalar_prefetch=1,
            grid=(1,),
            in_specs=[anywhere] * len(operands),
            out_specs=[anywhere] * len(out_shape),
            scratch_shapes=scratch,
        ),
        out_shape=out_shape,
        compiler_params=pltpu.CompilerParams(vmem_limit_bytes=56 * 2**20),
        cost_estimate=pl.CostEstimate(
            flops=2 * sets * count * tokens * depth * width,
            bytes_accessed=2 * count * depth * (sets * tokens + width) + 8 * sets * tokens * width,
            transcendentals=0,
        ),
    )(jnp.stack(picks), *operands)


def gather_kernel(numbers, flag_ref, *refs):
    ends = [sum(numbers[: i + 1]) for i in range(4)]
    near, beside, back, other = (refs[end - number : end] for end, number in zip(ends, numbers))
    out_ref, cache_ref = refs[-2:]
    half = out_ref.shape[1] // 2

    def put(sources, side):
        for at in range(2):
            place = (2 * at + side) * HD
            cache_ref[:, place : place + HD] = sources[0][:, at * HD : (at + 1) * HD]
        place = side * half
        for part, source in enumerate(sources):
            value = source[:, TILE if part == 0 else 0 :]
            out_ref[:, place : place + value.shape[1]] = value
            place += value.shape[1]

    for middle, mine, its in ((1, near, beside), (0, back, other)):
        for side in range(2):

            @pl.when((flag_ref[0] == side) & (flag_ref[1] == middle))
            def _():
                put(mine, side)
                put(its, 1 - side)


def gather_context(flags, near, beside, back, other, cols):
    operands = [*near, *beside, *back, *other]
    rows, step = near[0].shape[0], QROWS
    return pl.pallas_call(
        functools.partial(gather_kernel, tuple(map(len, (near, beside, back, other)))),
        grid_spec=pltpu.PrefetchScalarGridSpec(
            num_scalar_prefetch=1,
            grid=(rows // step,),
            in_specs=[
                pl.BlockSpec((step, operand.shape[1]), lambda i, flags: (i, 0))
                for operand in operands
            ],
            out_specs=[
                pl.BlockSpec((step, cols), lambda i, flags: (i, 0)),
                pl.BlockSpec((step, 2 * TILE), lambda i, flags: (i, 0)),
            ],
        ),
        out_shape=[
            jax.ShapeDtypeStruct((rows, cols), jnp.bfloat16),
            jax.ShapeDtypeStruct((rows, 2 * TILE), jnp.bfloat16),
        ],
        compiler_params=pltpu.CompilerParams(vmem_limit_bytes=24 * 2**20),
        cost_estimate=pl.CostEstimate(flops=0, bytes_accessed=6 * rows * cols, transcendentals=0),
    )(flags, *operands)


MIDDLE = (2, 3, 4, 5)
ENDS = (0, 1, 6, 7)


def after(value, *others):
    return lax.optimization_barrier((value,) + others)[0]


def pairs_from(sources, code):
    return [(s, s ^ code) for s in sources]


def middle_form(hidden, norm_gain, q_weight, q_bias, kv_weight, kv_bias, prefix_lens, assignment):
    tok_rows, features = hidden.shape
    slice_rows, q_cols = q_weight.shape
    half_cols = q_cols // 2
    group = lax.axis_index("group")
    tensor = lax.axis_index("tensor")
    y = group & 1
    is_middle = (group >= 2) & (group < 6)
    barrier = lax.optimization_barrier

    def over_group(value, sources, code):
        return lax.ppermute(value, "group", pairs_from(sources, code))

    def to_middle(value):
        return over_group(value, ENDS, 2)

    def across_middle(value):
        return over_group(value, MIDDLE, 6)

    def over_x(value):
        return lax.ppermute(value, "tensor", pairs_from(range(4), 2))

    def over_core(value):
        return lax.ppermute(value, "tensor", pairs_from(range(4), 1))

    begin, widths = (0, 2 * TILE, 4 * TILE), (2 * TILE, 2 * TILE, TILE)

    def columns(half):
        head = (2 * tensor + half) * HD
        kv_part = lax.dynamic_slice_in_dim(kv_weight, head, HD, 2).reshape(slice_rows, TILE)
        q_part = lax.dynamic_slice_in_dim(q_weight, half * half_cols, half_cols, 1)
        return jnp.concatenate([kv_part, q_part], axis=1)

    def both(one, two, chunk):
        low, high = begin[chunk], begin[chunk] + widths[chunk]
        return jnp.stack([one[:, low:high], two[:, low:high]])

    def pick(code_of_rows, codes):
        block = jnp.stack([group ^ code for code in codes])
        if code_of_rows == 0:
            return jnp.stack([block * 0, block])
        return jnp.stack([(block >> 1) ^ tensor, block & 1])

    def rows_and_picks(sets, codes):
        return [rows_of[c] for c in sets], [pick(c, codes) for c in sets]

    def closed(arriving, others):
        arrived = []
        for value in arriving:
            value, others = barrier((value, others))
            arrived.append(value)
        return barrier((tuple(arrived), others))

    own = columns(y)
    other = columns(1 - y)
    m_own = across_middle(own)
    swap = over_group(other, range(8), 1)
    normed, quarter = norm(hidden, norm_gain, tensor, slice_rows, 2)
    end2 = to_middle(quarter)

    bias = lax.dynamic_slice_in_dim(q_bias, y * half_cols, half_cols, 0)
    kv_bias_here = lax.dynamic_slice_in_dim(kv_bias, (2 * tensor + y) * HD, HD, 1)
    bias = jnp.concatenate([kv_bias_here[0], kv_bias_here[1], bias])[None, :]
    inverse_freq = THETA ** (-2.0 * jnp.arange(HD // 2, dtype=jnp.float32) / HD)
    m_swap = across_middle(after(swap, m_own))
    own, swap, m_own, normed, quarter, end2 = barrier((own, swap, m_own, normed, quarter, end2))

    rows_of = {0: [normed]}
    stack0, end2 = barrier((both(own, swap, 0), end2))
    e0 = to_middle(stack0)
    next1, next2 = both(own, swap, 1), both(own, swap, 2)
    end3 = over_group(end2, MIDDLE, 1)
    across2 = over_x(end2)
    twin2 = over_core(end2)
    tables = []
    for code in range(4):
        _, offset, places = token_layout(prefix_lens, assignment, group ^ code, tok_rows)
        angles = offset.astype(jnp.float32)[:, None] * inverse_freq[None, :]
        table = jnp.concatenate([jnp.cos(angles), jnp.sin(angles)], axis=1)
        tables.append((table, (places - offset)[:, None]))
    m_e0 = across_middle(after(e0, m_swap))
    (e0, m_swap, end3, across2, twin2), (next1, next2, end2, tables, quarter) = closed(
        (e0, m_swap, end3, across2, twin2), (next1, next2, end2, tables, quarter)
    )

    first_codes, last_codes = (0, 1, 6, 7), (2, 3, 4, 5)
    first_pieces = {0: own, 1: swap, 6: m_own, 7: m_swap}
    last_pieces = {}

    def parts_of(code, chunks):
        low, wide = begin[chunks[0]], sum(widths[chunk] for chunk in chunks)
        if code in first_codes:
            return [(first_pieces[code], None, low, wide)]
        return [(last_pieces[code, chunk], code & 1, 0, widths[chunk]) for chunk in chunks]

    every = (0, 1, 2)

    def first_sums(sets):
        rows, picks = rows_and_picks(sets, first_codes)
        pieces = [parts_of(c, every) for c in first_codes]
        return heads_of(rows, picks, pieces, sum(widths))

    def more_sums(sets, chunk, codes, totals):
        rows, picks = rows_and_picks(sets, codes)
        pieces = [parts_of(c, (chunk,)) for c in codes]
        return heads_of(rows, picks, pieces, widths[chunk], (totals, begin[chunk]))

    outs, caches = {}, {}

    def finished(sets, chunks, codes, totals=None, opened=()):
        rows, picks = rows_and_picks(sets, codes)
        low, wide = begin[chunks[0]], sum(widths[chunk] for chunk in chunks)
        made = heads_of(
            rows,
            picks,
            [parts_of(c, chunks + (() if c in codes[-2:] else opened)) for c in codes],
            wide + sum(widths[chunk] for chunk in opened),
            totals,
            (
                wide,
                bias[:, low : low + wide],
                [tables[c][0] for c in sets],
                [tables[c][1] for c in sets],
                None if chunks[0] == 0 else [(caches[c], outs[c, 0]) for c in sets],
            ),
        )
        number = len(sets)
        for at, code in enumerate(sets):
            outs[code, chunks[0]] = made[at]
            if chunks[0] == 0:
                caches[code] = made[number + at]
        return made[-number:]

    e1 = to_middle(next1)
    end1 = over_group(quarter, MIDDLE, 1)
    across3 = over_x(end3)
    far2 = over_core(across2)
    rows_of[2] = [end2, twin2, across2, far2]
    sums = dict(zip((0, 2), first_sums((0, 2))))
    m_e1 = across_middle(after(e1, m_e0))
    (m_e0, e1, end1, across3), (next2, e0, end3, far2, sums) = closed(
        (m_e0, e1, end1, across3), (next2, e0, end3, far2, sums)
    )
    rows_of[2] = [end2, twin2, across2, far2]

    e2 = to_middle(next2)
    across1 = over_x(end1)
    twin3 = over_core(end3)
    far3 = over_core(across3)
    rows_of[3] = [end3, twin3, across3, far3]

    def send_back(code, chunk):
        return over_group(outs[code, chunk], MIDDLE, code)

    def arrived(chunk, end, middle):
        for code in last_codes:
            last_pieces[code, chunk] = end if code < 4 else middle

    arrived(0, e0, m_e0)
    arrived(1, e1, None)
    (sums[3],) = first_sums((3,))
    three = (2, 3, 0)
    finished(three, (0,), last_codes, ([sums[c] for c in three], 0))
    sums1 = dict(zip(three, more_sums(three, 1, last_codes[:2], [sums[c] for c in three])))
    m_e2 = across_middle(after(e2, m_e1))
    (m_e1, across1, e2), (end1, made, caches, sums, sums1) = closed(
        (m_e1, across1, e2), (end1, [outs[c, 0] for c in three], caches, sums, sums1)
    )
    for code, out in zip(three, made):
        outs[code, 0] = out

    back = {(code, 0): send_back(code, 0) for code in (2, 3)}
    twin1 = over_core(end1)
    far1 = over_core(across1)
    arrived(1, e1, m_e1)
    arrived(2, e2, None)
    finished(three, (1,), last_codes[2:], ([sums1[c] for c in three], 0))
    for code in (2, 3):
        back[code, 1] = send_back(code, 1)
    far1, outs[2, 1] = barrier((far1, outs[2, 1]))
    rows_of[1] = [end1, twin1, across1, far1]
    (sums2,) = finished((1,), (0, 1), first_codes + last_codes, opened=(2,))
    back[1, 0] = send_back(1, 0)
    (m_e2, back[2, 0], back[3, 0]), (sums, outs[2, 1], outs[1, 0], sums2) = closed(
        (m_e2, back[2, 0], back[3, 0]), (sums, outs[2, 1], outs[1, 0], sums2)
    )

    arrived(2, e2, m_e2)
    finished((2, 3), (2,), last_codes, ([sums[c] for c in (2, 3)], begin[2]))
    for code in (2, 3):
        back[code, 2] = send_back(code, 2)
    finished((1,), (2,), last_codes[2:], ([sums2], 0))
    back[1, 2] = send_back(1, 2)
    sums[0], outs[1, 2] = barrier((sums[0], outs[1, 2]))
    finished((0,), (2,), last_codes, ([sums[0]], begin[2]))

    context, cache = gather_context(
        jnp.stack([y, is_middle.astype(jnp.int32)]),
        [outs[0, part] for part in every],
        [back[1, part] for part in (0, 2)],
        [back[2, part] for part in every],
        [back[3, part] for part in every],
        q_cols,
    )
    return (context, cache.reshape(tok_rows, 2, TILE))


def solution(mesh):
    placed = (
        P("group", None),
        P(),
        P("group", "tensor"),
        P("tensor"),
        P("group", None, None),
        P(),
        P(),
        P(),
    )
    fits = mesh.shape["group"] == 8 and mesh.shape["tensor"] == 4
    return jax.shard_map(
        middle_form if fits else gathered_form,
        mesh=mesh,
        in_specs=placed,
        out_specs=(P("group", "tensor"), P("group", None, "tensor")),
        check_vma=False,
    )
```

```python
import functools
import math

import jax
import jax.numpy as jnp
from jax import lax
from jax.experimental import pallas as pl
from jax.experimental.pallas import tpu as pltpu
from jax.sharding import PartitionSpec as P

HD = 128


EPS = 1e-06
THETA = 1000000.0
QROWS = 128
MAXLEN = 256


def token_layout(prefix_lens, assignment, group_id, tok_rows):
    rollouts = prefix_lens.shape[0]
    member = assignment == group_id
    own_lens = jnp.where(member, prefix_lens, 0)
    starts = jnp.cumsum(own_lens) - own_lens
    places = jnp.arange(tok_rows, dtype=jnp.int32)
    inside = (
        member[None, :]
        & (places[:, None] >= starts[None, :])
        & (places[:, None] < (starts + own_lens)[None, :])
    )
    owner_id = jnp.sum(jnp.where(inside, jnp.arange(rollouts, dtype=jnp.int32)[None, :], 0), axis=1)
    offset = places - jnp.sum(jnp.where(inside, starts[None, :], 0), axis=1)
    return (owner_id, offset, places)


def rotate(values, offset):
    half_dim = values.shape[-1] // 2
    inverse_freq = THETA ** (-2.0 * jnp.arange(half_dim, dtype=jnp.float32) / values.shape[-1])
    angles = offset.astype(jnp.float32)[:, None] * inverse_freq[None, :]
    cosine = jnp.cos(angles)[:, None, :]
    sine_part = jnp.sin(angles)[:, None, :]
    first_half = values[..., :half_dim]
    second_half = values[..., half_dim:]
    return jnp.concatenate(
        [
            first_half * cosine - second_half * sine_part,
            second_half * cosine + first_half * sine_part,
        ],
        axis=-1,
    )


def add_product(normed, portion):
    return jnp.dot(normed, portion, preferred_element_type=jnp.float32)


def normalise(hidden, norm_gain):
    widened = hidden.astype(jnp.float32)
    return (
        widened * lax.rsqrt(jnp.mean(widened * widened, axis=-1, keepdims=True) + EPS) * norm_gain
    ).astype(jnp.bfloat16)


def gathered_form(
    hidden, norm_gain, q_weight, q_bias, kv_weight, kv_bias, prefix_lens, assignment
):
    tok_rows, features = hidden.shape
    slice_rows = kv_weight.shape[0]
    q_cols = q_weight.shape[1]
    kv_total = kv_weight.shape[2]
    heads_here = q_cols // HD
    tensor_pos = lax.axis_index("tensor")
    kv_cols = kv_total // lax.axis_size("tensor")
    normed = normalise(hidden, norm_gain)
    queries = add_product(normed, lax.all_gather(q_weight, "group", axis=0, tiled=True)) + q_bias
    head_span = max(kv_cols, HD)
    head_base = tensor_pos * kv_cols // head_span * head_span
    local_start = tensor_pos * kv_cols - head_base
    head_rows = lax.dynamic_slice_in_dim(kv_weight, head_base, head_span, 2).reshape(
        slice_rows, 2 * head_span
    )
    projected = add_product(normed, lax.all_gather(head_rows, "group", axis=0, tiled=True))
    projected = projected.reshape(tok_rows, 2, head_span) + lax.dynamic_slice_in_dim(
        kv_bias, head_base, head_span, 1
    )
    kv_here = head_span // HD
    group_size = heads_here // kv_here
    owner_id, offset, places = token_layout(
        prefix_lens, assignment, lax.axis_index("group"), tok_rows
    )
    rotated_queries = rotate(queries.reshape(tok_rows, heads_here, HD), offset).astype(jnp.bfloat16)
    rotated_keys = rotate(projected[:, 0].reshape(tok_rows, kv_here, HD), offset).astype(
        jnp.bfloat16
    )
    value_heads = projected[:, 1].reshape(tok_rows, kv_here, HD).astype(jnp.bfloat16)
    visible = (owner_id[:, None] == owner_id[None, :]) & (places[None, :] <= places[:, None])
    grouped = rotated_queries.reshape(tok_rows, kv_here, group_size, HD)
    scores = jnp.einsum(
        "qgph,kgh->gpqk", grouped, rotated_keys, preferred_element_type=jnp.float32
    ) / math.sqrt(HD)
    scores = jnp.where(visible[None, None], scores, -jnp.inf)
    row_max = jnp.max(scores, axis=-1, keepdims=True)
    exponent = jnp.exp(scores - row_max)
    weights_bf = (exponent / jnp.sum(exponent, axis=-1, keepdims=True)).astype(jnp.bfloat16)
    context = jnp.einsum(
        "gpqk,kgh->qgph", weights_bf, value_heads, preferred_element_type=jnp.float32
    )
    context = context.astype(jnp.bfloat16).reshape(tok_rows, q_cols)
    stacked = jnp.stack(
        [rotated_keys.reshape(tok_rows, head_span), value_heads.reshape(tok_rows, head_span)],
        axis=1,
    )
    kv_cache = lax.dynamic_slice_in_dim(stacked, local_start, kv_cols, 2)
    return (context, kv_cache)


def norm_kernel(part_ref, hidden_ref, gain_ref, out_ref, part_out_ref):
    widened = hidden_ref[...].astype(jnp.float32)
    scale = lax.rsqrt(jnp.mean(widened * widened, axis=-1, keepdims=True) + EPS)
    normed = (widened * scale * gain_ref[...]).astype(jnp.bfloat16)
    depth = out_ref.shape[2]
    for block in range(out_ref.shape[0]):
        out_ref[block] = normed[:, block * depth : (block + 1) * depth]
    count = part_out_ref.shape[0]
    part_out_ref[...] = out_ref[pl.ds(part_ref[0] * count, count)]


def norm(hidden, norm_gain, part, depth, count):
    rows, features = hidden.shape
    blocks = features // depth
    step = 64
    return pl.pallas_call(
        norm_kernel,
        grid_spec=pltpu.PrefetchScalarGridSpec(
            num_scalar_prefetch=1,
            grid=(rows // step,),
            in_specs=[
                pl.BlockSpec((step, features), lambda i, part: (i, 0)),
                pl.BlockSpec((1, features), lambda i, part: (0, 0)),
            ],
            out_specs=[
                pl.BlockSpec((blocks, step, depth), lambda i, part: (0, i, 0)),
                pl.BlockSpec((count, step, depth), lambda i, part: (0, i, 0)),
            ],
        ),
        out_shape=[
            jax.ShapeDtypeStruct((blocks, rows, depth), jnp.bfloat16),
            jax.ShapeDtypeStruct((count, rows, depth), jnp.bfloat16),
        ],
        compiler_params=pltpu.CompilerParams(vmem_limit_bytes=32 * 2**20),
        cost_estimate=pl.CostEstimate(
            flops=4 * rows * features, bytes_accessed=5 * rows * features, transcendentals=rows
        ),
    )(part[None], hidden, norm_gain[None])


TILE = 2 * HD


def turn(value, cosine, sine):
    return value * cosine + pltpu.roll(value, HD // 2, 1) * sine


def heads_kernel(plan, pick_ref, *refs):
    sources, skips, parts, width, closed_width, totals_at, with_keys = plan
    finish = closed_width > 0
    sets, count = len(sources), len(parts)
    refs = list(refs)

    def take(number):
        taken = refs[:number]
        del refs[:number]
        return taken

    row_refs = [take(number) for number in sources]
    weight_refs = [take(len(part)) for part in parts]
    total_refs = take(sets) if totals_at is not None else None
    if finish:
        (bias_ref,) = take(1)
        table_refs = take(sets)
    outs = take(sets)
    sum_outs = take(sets) if finish and closed_width < width else None
    row_buf, weight_buf, acc, row_sem, weight_sem, total_sem, out_sem = take(7)
    depth = row_buf.shape[2] // count

    def weight_copies(piece):
        column = 0
        for part, (ref, (lead, skip, wide)) in enumerate(zip(weight_refs[piece], parts[piece])):
            ref = ref if lead is None else ref.at[lead]
            yield pltpu.make_async_copy(
                ref.at[:, skip : skip + wide],
                weight_buf.at[piece * depth : (piece + 1) * depth, column : column + wide],
                weight_sem.at[piece, part],
            )
            column += wide

    def row_copy(which, piece, source):
        return pltpu.make_async_copy(
            row_refs[which][source].at[pick_ref[which, 1, piece]],
            row_buf.at[which, :, piece * depth : (piece + 1) * depth],
            row_sem.at[which, piece],
        )

    def total_copy(which):
        return pltpu.make_async_copy(
            total_refs[which].at[:, totals_at[which] : totals_at[which] + width],
            acc.at[which],
            total_sem.at[which],
        )

    stages = [(0, low, min(low + 2, count)) for low in range(0, count, 2)]
    stages += [(which, skips[which], count) for which in range(1, sets)]

    def start(stage):
        which, low, high = stages[stage]
        for piece in range(low, high):
            if which == 0:
                for copy in weight_copies(piece):
                    copy.start()
            if sources[which] == 1:
                row_copy(which, piece, 0).start()
            else:
                for source in range(sources[which]):

                    @pl.when(pick_ref[which, 0, piece] == source)
                    def _():
                        row_copy(which, piece, source).start()
        if low == skips[which] and total_refs is not None:
            total_copy(which).start()

    start(0)
    if len(stages) > 1:
        start(1)
    if finish:
        bias_buf, table_buf, out_buf, side_sem = refs
        side_copies = [pltpu.make_async_copy(bias_ref, bias_buf, side_sem.at[sets])]
        side_copies += [
            pltpu.make_async_copy(table_refs[which], table_buf.at[which], side_sem.at[which])
            for which in range(sets)
        ]

    def out_copies(which):
        pairs = [((out_buf if finish else acc).at[which], outs[which])]
        if sum_outs is not None:
            pairs.append((acc.at[which, :, closed_width:], sum_outs[which]))
        return [
            pltpu.make_async_copy(buf, ref, out_sem.at[which, number])
            for number, (buf, ref) in enumerate(pairs)
        ]

    for stage, (which, low, high) in enumerate(stages):
        for piece in range(low, high):
            if which == 0:
                for copy in weight_copies(piece):
                    copy.wait()
            row_copy(which, piece, 0).wait()
        if low == skips[which] and total_refs is not None:
            total_copy(which).wait()
        if stage + 2 < len(stages):
            start(stage + 2)
        if stage == 0 and finish:
            for copy in side_copies:
                copy.start()
        for at in range(0, width, TILE):
            top = min(high, count - 2) if finish and at >= closed_width else high
            if top <= low:
                continue
            cols = slice(at, at + TILE)
            term = jnp.dot(
                row_buf[which, :, low * depth : top * depth],
                weight_buf[low * depth : top * depth, cols],
                preferred_element_type=jnp.float32,
            )
            if low > skips[which] or total_refs is not None:
                term = acc[which, :, cols] + term
            acc[which, :, cols] = term
        if high < count:
            continue
        if finish:
            if which == 0:
                side_copies[0].wait()
            side_copies[1 + which].wait()
            finish_set(acc.at[which], bias_buf, table_buf[which], out_buf.at[which], with_keys)
        for copy in out_copies(which):
            copy.start()
    for which in range(sets):
        for copy in out_copies(which):
            copy.wait()


def finish_set(acc, bias, table, out, with_keys):
    swapped = pltpu.roll(table, HD // 2, 1)
    left = lax.broadcasted_iota(jnp.int32, table.shape, 1) < HD // 2
    cosine = jnp.where(left, table, swapped)
    sine = jnp.where(left, -swapped, table)
    for col in range(0, out.shape[1], HD):
        cols = slice(col, col + HD)
        value = acc[:, cols] + bias[:, cols]
        if not (with_keys and col == HD):
            value = turn(value, cosine, sine)
        out[:, cols] = value.astype(jnp.bfloat16)


def heads_of(row_sets, picks, pieces, width, totals=None, finish=None, skips=None):
    sets, count = len(row_sets), len(pieces)
    skips = skips or (0,) * sets
    sources = tuple(len(rows) for rows in row_sets)
    tokens, depth = row_sets[0][0].shape[1:]
    operands = [array for rows in row_sets for array in rows]
    operands += [array for piece in pieces for array, *_ in piece]
    totals_at = None
    if totals is not None:
        totals, totals_at = totals
        operands += totals
    scratch = [
        pltpu.VMEM((sets, tokens, count * depth), jnp.bfloat16),
        pltpu.VMEM((count * depth, width), jnp.bfloat16),
        pltpu.VMEM((sets, tokens, width), jnp.float32),
        pltpu.SemaphoreType.DMA((sets, count)),
        pltpu.SemaphoreType.DMA((count, max(map(len, pieces)))),
        pltpu.SemaphoreType.DMA((sets,)),
        pltpu.SemaphoreType.DMA((sets, 3)),
    ]
    with_keys, closed_width = False, 0
    out_shape = [jax.ShapeDtypeStruct((tokens, width), jnp.float32)] * sets
    if finish is not None:
        closed_width, bias, tables, with_keys = finish
        out_shape = [jax.ShapeDtypeStruct((tokens, closed_width), jnp.bfloat16)] * sets
        operands += [bias, *tables]
        if closed_width < width:
            out_shape += [jax.ShapeDtypeStruct((tokens, width - closed_width), jnp.float32)] * sets
        scratch += [
            pltpu.VMEM((1, closed_width), jnp.float32),
            pltpu.VMEM((sets, tokens, HD), jnp.float32),
            pltpu.VMEM((sets, tokens, closed_width), jnp.bfloat16),
            pltpu.SemaphoreType.DMA((sets + 1,)),
        ]
    plan = (
        sources,
        skips,
        tuple(tuple(part[1:] for part in piece) for piece in pieces),
        width,
        closed_width,
        totals_at,
        with_keys,
    )
    anywhere = pl.BlockSpec(memory_space=pl.ANY)
    return pl.pallas_call(
        functools.partial(heads_kernel, plan),
        grid_spec=pltpu.PrefetchScalarGridSpec(
            num_scalar_prefetch=1,
            grid=(1,),
            in_specs=[anywhere] * len(operands),
            out_specs=[anywhere] * len(out_shape),
            scratch_shapes=scratch,
        ),
        out_shape=out_shape,
        compiler_params=pltpu.CompilerParams(vmem_limit_bytes=56 * 2**20),
        cost_estimate=pl.CostEstimate(
            flops=2 * sets * count * tokens * depth * width,
            bytes_accessed=2 * count * depth * (sets * tokens + width) + 8 * sets * tokens * width,
            transcendentals=0,
        ),
    )(jnp.stack(picks), *operands)


def attention(queries, keys, values, first_ref, out_ref):
    rows, cols = out_ref.shape
    heads = cols // HD
    scale = math.log2(math.e) / math.sqrt(HD)
    for top in range(0, rows, QROWS):
        low, end = max(0, top - MAXLEN), top + QROWS
        shape = (QROWS, end - low)
        stacked = jnp.concatenate(
            [queries[top:end, col : col + HD] for col in range(0, cols, HD)], axis=0
        )
        scores = jnp.dot(stacked, keys[:, low:end], preferred_element_type=jnp.float32)
        row = lax.broadcasted_iota(jnp.int32, shape, 0) + top
        col = lax.broadcasted_iota(jnp.int32, shape, 1) + low
        visible = (col <= row) & (col >= first_ref[top:end])
        scores = jnp.where(visible[None], scores.reshape(heads, *shape), -jnp.inf)
        most = jnp.max(scores, axis=-1, keepdims=True)
        exponent = jnp.exp2((scores - most) * scale)
        share = 1.0 / jnp.sum(exponent, axis=-1, keepdims=True)
        weights = (exponent * share).astype(jnp.bfloat16)
        context = jnp.dot(
            weights.reshape(heads * QROWS, end - low),
            values[low:end],
            preferred_element_type=jnp.float32,
        ).astype(jnp.bfloat16)
        for head in range(heads):
            out_ref[top:end, head * HD : (head + 1) * HD] = context[
                head * QROWS : (head + 1) * QROWS
            ]


def attend_kernel(numbers, flag_ref, *refs):
    ends = [sum(numbers[: i + 1]) for i in range(4)]
    near, beside, back, other = (refs[end - number : end] for end, number in zip(ends, numbers))
    first_ref, out_ref, cache_ref, part_buf, out_buf, in_sem, out_sem = refs[ends[-1] :]
    half = out_buf.shape[2]

    def copies(side, sources):
        column = 0
        for part, source in enumerate(sources):
            wide = source.shape[1]
            yield pltpu.make_async_copy(
                source, part_buf.at[side, :, column : column + wide], in_sem.at[side, part]
            )
            column += wide

    def on_parts(act):
        for middle, sides in ((1, (near, beside)), (0, (back, other))):

            @pl.when(flag_ref[1] == middle)
            def _():
                for side, sources in enumerate(sides):
                    for copy in copies(side, sources):
                        act(copy)

    on_parts(lambda copy: copy.start())
    on_parts(lambda copy: copy.wait())
    sent = []
    for side in range(2):
        at = flag_ref[0] if side == 0 else 1 - flag_ref[0]
        part = part_buf.at[side]
        for number in range(2):
            sent.append(
                pltpu.make_async_copy(
                    part.at[:, number * HD : (number + 1) * HD],
                    cache_ref.at[:, pl.ds(pl.multiple_of((2 * number + at) * HD, HD), HD)],
                    out_sem.at[side, number],
                )
            )
            sent[-1].start()
        keys = part[:, :HD].astype(jnp.float32).T.astype(jnp.bfloat16)
        attention(part.at[:, TILE:], keys, part.at[:, HD:TILE], first_ref, out_buf.at[side])
        sent.append(
            pltpu.make_async_copy(
                out_buf.at[side],
                out_ref.at[:, pl.ds(pl.multiple_of(at * half, half), half)],
                out_sem.at[side, 2],
            )
        )
        sent[-1].start()
    for copy in sent:
        copy.wait()


def attend_all(flags, near, beside, back, other, first, cols):
    operands = [*near, *beside, *back, *other]
    rows = near[0].shape[0]
    anywhere = pl.BlockSpec(memory_space=pl.ANY)
    return pl.pallas_call(
        functools.partial(attend_kernel, tuple(map(len, (near, beside, back, other)))),
        grid_spec=pltpu.PrefetchScalarGridSpec(
            num_scalar_prefetch=1,
            grid=(1,),
            in_specs=[anywhere] * len(operands) + [pl.BlockSpec((rows, 1), lambda i, flags: (0, 0))],
            out_specs=[anywhere] * 2,
            scratch_shapes=[
                pltpu.VMEM((2, rows, TILE + cols // 2), jnp.bfloat16),
                pltpu.VMEM((2, rows, cols // 2), jnp.bfloat16),
                pltpu.SemaphoreType.DMA((2, 3)),
                pltpu.SemaphoreType.DMA((2, 3)),
            ],
        ),
        out_shape=[
            jax.ShapeDtypeStruct((rows, cols), jnp.bfloat16),
            jax.ShapeDtypeStruct((rows, 2 * TILE), jnp.bfloat16),
        ],
        compiler_params=pltpu.CompilerParams(vmem_limit_bytes=40 * 2**20),
        cost_estimate=pl.CostEstimate(
            flops=4 * cols * rows * 3 * QROWS,
            bytes_accessed=6 * rows * cols,
            transcendentals=cols // HD * rows * 3 * QROWS,
        ),
    )(flags, *operands, first)


MIDDLE = (2, 3, 4, 5)
ENDS = (0, 1, 6, 7)


def after(value, *others):
    return lax.optimization_barrier((value,) + others)[0]


def pairs_from(sources, code):
    return [(s, s ^ code) for s in sources]


def middle_form(hidden, norm_gain, q_weight, q_bias, kv_weight, kv_bias, prefix_lens, assignment):
    tok_rows, features = hidden.shape
    slice_rows, q_cols = q_weight.shape
    half_cols = q_cols // 2
    group = lax.axis_index("group")
    tensor = lax.axis_index("tensor")
    y = group & 1
    is_middle = (group >= 2) & (group < 6)
    barrier = lax.optimization_barrier

    def over_group(value, sources, code):
        return lax.ppermute(value, "group", pairs_from(sources, code))

    def to_middle(value):
        return over_group(value, ENDS, 2)

    def across_middle(value):
        return over_group(value, MIDDLE, 6)

    def over_x(value):
        return lax.ppermute(value, "tensor", pairs_from(range(4), 2))

    def over_core(value):
        return lax.ppermute(value, "tensor", pairs_from(range(4), 1))

    begin, widths = (0, 2 * TILE, 4 * TILE), (2 * TILE, 2 * TILE, TILE)

    def columns(half):
        head = (2 * tensor + half) * HD
        kv_part = lax.dynamic_slice_in_dim(kv_weight, head, HD, 2).reshape(slice_rows, TILE)
        q_part = lax.dynamic_slice_in_dim(q_weight, half * half_cols, half_cols, 1)
        return jnp.concatenate([kv_part, q_part], axis=1)

    def both(one, two, chunk):
        low, high = begin[chunk], begin[chunk] + widths[chunk]
        return jnp.stack([one[:, low:high], two[:, low:high]])

    def pick(code_of_rows, codes):
        block = jnp.stack([group ^ code for code in codes])
        if code_of_rows == 0:
            return jnp.stack([block * 0, block])
        return jnp.stack([(block >> 1) ^ tensor, block & 1])

    def rows_and_picks(sets, codes):
        return [rows_of[c] for c in sets], [pick(c, codes) for c in sets]

    def closed(arriving, others):
        arrived = []
        for value in arriving:
            value, others = barrier((value, others))
            arrived.append(value)
        return barrier((tuple(arrived), others))

    own = columns(y)
    other = columns(1 - y)
    m_own = across_middle(own)
    swap = over_group(other, range(8), 1)
    normed, quarter = norm(hidden, norm_gain, tensor, slice_rows, 2)
    end2 = to_middle(quarter)

    bias = lax.dynamic_slice_in_dim(q_bias, y * half_cols, half_cols, 0)
    kv_bias_here = lax.dynamic_slice_in_dim(kv_bias, (2 * tensor + y) * HD, HD, 1)
    bias = jnp.concatenate([kv_bias_here[0], kv_bias_here[1], bias])[None, :]
    inverse_freq = THETA ** (-2.0 * jnp.arange(HD // 2, dtype=jnp.float32) / HD)
    m_swap = across_middle(after(swap, m_own))
    own, swap, m_own, normed, quarter, end2 = barrier((own, swap, m_own, normed, quarter, end2))

    rows_of = {0: [normed]}
    stack0, end2 = barrier((both(own, swap, 0), end2))
    e0 = to_middle(stack0)
    next1, next2 = both(own, swap, 1), both(own, swap, 2)
    end3 = over_group(end2, MIDDLE, 1)
    across2 = over_x(end2)
    twin2 = over_core(end2)
    tables = []
    for code in range(4):
        _, offset, places = token_layout(prefix_lens, assignment, group ^ code, tok_rows)
        angles = offset.astype(jnp.float32)[:, None] * inverse_freq[None, :]
        table = jnp.concatenate([jnp.cos(angles), jnp.sin(angles)], axis=1)
        tables.append((table, (places - offset)[:, None]))
    m_e0 = across_middle(after(e0, m_swap))
    (e0, m_swap, end3, across2, twin2), (next1, next2, end2, tables, quarter) = closed(
        (e0, m_swap, end3, across2, twin2), (next1, next2, end2, tables, quarter)
    )

    first_codes, last_codes = (0, 1, 6, 7), (2, 3, 4, 5)
    first_pieces = {0: own, 1: swap, 6: m_own, 7: m_swap}
    last_pieces = {}

    def parts_of(code, chunks):
        low, wide = begin[chunks[0]], sum(widths[chunk] for chunk in chunks)
        if code in first_codes:
            return [(first_pieces[code], None, low, wide)]
        return [(last_pieces[code, chunk], code & 1, 0, widths[chunk]) for chunk in chunks]

    every = (0, 1, 2)

    def first_sums(sets):
        rows, picks = rows_and_picks(sets, first_codes)
        pieces = [parts_of(c, every) for c in first_codes]
        return heads_of(rows, picks, pieces, sum(widths))

    outs = {}

    def finished(sets, chunks, codes, totals=None, opened=(), skips=None):
        rows, picks = rows_and_picks(sets, codes)
        low, wide = begin[chunks[0]], sum(widths[chunk] for chunk in chunks)
        made = heads_of(
            rows,
            picks,
            [parts_of(c, chunks + (() if c in codes[-2:] else opened)) for c in codes],
            wide + sum(widths[chunk] for chunk in opened),
            totals,
            (wide, bias[:, low : low + wide], [tables[c][0] for c in sets], chunks[0] == 0),
            skips,
        )
        for code, out in zip(sets, made):
            outs[code, chunks[0]] = out
        return made[-1]

    e1 = to_middle(next1)
    end1 = over_group(quarter, MIDDLE, 1)
    across3 = over_x(end3)
    far2 = over_core(across2)
    rows_of[2] = [end2, twin2, across2, far2]
    sums = dict(zip((0, 2), first_sums((0, 2))))
    m_e1 = across_middle(after(e1, m_e0))
    (m_e0, e1, end1, across3), (next2, e0, end3, far2, sums) = closed(
        (m_e0, e1, end1, across3), (next2, e0, end3, far2, sums)
    )
    rows_of[2] = [end2, twin2, across2, far2]

    e2 = to_middle(next2)
    across1 = over_x(end1)
    twin3 = over_core(end3)
    far3 = over_core(across3)
    rows_of[3] = [end3, twin3, across3, far3]

    def send_back(code, chunk):
        return over_group(outs[code, chunk], MIDDLE, code)

    def arrived(chunk, end, middle):
        for code in last_codes:
            last_pieces[code, chunk] = end if code < 4 else middle

    arrived(0, e0, m_e0)
    (sums[3],) = first_sums((3,))
    three = (2, 3, 0)
    finished(three, (0,), last_codes, ([sums[c] for c in three], (0, 0, 0)))
    m_e2 = across_middle(after(e2, m_e1))
    (m_e1, across1, e2), (end1, made, sums) = closed(
        (m_e1, across1, e2), (end1, [outs[c, 0] for c in three], sums)
    )
    for code, out in zip(three, made):
        outs[code, 0] = out

    back = {(code, 0): send_back(code, 0) for code in (2, 3)}
    twin1 = over_core(end1)
    far1 = over_core(across1)
    arrived(1, e1, m_e1)
    arrived(2, e2, None)
    finished(three, (1,), last_codes, ([sums[c] for c in three], (begin[1],) * 3))
    for code in (2, 3):
        back[code, 1] = send_back(code, 1)
    far1, outs[2, 1] = barrier((far1, outs[2, 1]))
    rows_of[1] = [end1, twin1, across1, far1]
    sums[1] = finished((1,), (0, 1), first_codes + last_codes, opened=(2,))
    back[1, 0] = send_back(1, 0)
    (m_e2,), (sums, outs[2, 1], outs[1, 0]) = closed((m_e2,), (sums, outs[2, 1], outs[1, 0]))

    arrived(2, e2, m_e2)
    three = (2, 3, 1)
    finished(
        three,
        (2,),
        last_codes,
        ([sums[c] for c in three], (begin[2], begin[2], 0)),
        skips=(0, 0, 2),
    )
    for code in three:
        back[code, 2] = send_back(code, 2)
    sums[0], outs[1, 2] = barrier((sums[0], outs[1, 2]))
    finished((0,), (2,), last_codes, ([sums[0]], (begin[2],)))

    context, cache = attend_all(
        jnp.stack([y, is_middle.astype(jnp.int32)]),
        [outs[0, part] for part in every],
        [back[1, part] for part in (0, 2)],
        [back[2, part] for part in every],
        [back[3, part] for part in every],
        tables[0][1],
        q_cols,
    )
    return (context, cache.reshape(tok_rows, 2, TILE))


def solution(mesh):
    placed = (
        P("group", None),
        P(),
        P("group", "tensor"),
        P("tensor"),
        P("group", None, None),
        P(),
        P(),
        P(),
    )
    fits = mesh.shape["group"] == 8 and mesh.shape["tensor"] == 4
    return jax.shard_map(
        middle_form if fits else gathered_form,
        mesh=mesh,
        in_specs=placed,
        out_specs=(P("group", "tensor"), P("group", None, "tensor")),
        check_vma=False,
    )
```

```python
import functools
import math

import jax
import jax.numpy as jnp
from jax import lax
from jax.experimental import pallas as pl
from jax.experimental.pallas import tpu as pltpu
from jax.sharding import PartitionSpec as P

HD = 128


EPS = 1e-06
THETA = 1000000.0
QROWS = 128
MAXLEN = 256


def token_layout(prefix_lens, assignment, group_id, tok_rows):
    rollouts = prefix_lens.shape[0]
    member = assignment == group_id
    own_lens = jnp.where(member, prefix_lens, 0)
    starts = jnp.cumsum(own_lens) - own_lens
    places = jnp.arange(tok_rows, dtype=jnp.int32)
    inside = (
        member[None, :]
        & (places[:, None] >= starts[None, :])
        & (places[:, None] < (starts + own_lens)[None, :])
    )
    owner_id = jnp.sum(jnp.where(inside, jnp.arange(rollouts, dtype=jnp.int32)[None, :], 0), axis=1)
    offset = places - jnp.sum(jnp.where(inside, starts[None, :], 0), axis=1)
    return (owner_id, offset, places)


def rotate(values, offset):
    half_dim = values.shape[-1] // 2
    inverse_freq = THETA ** (-2.0 * jnp.arange(half_dim, dtype=jnp.float32) / values.shape[-1])
    angles = offset.astype(jnp.float32)[:, None] * inverse_freq[None, :]
    cosine = jnp.cos(angles)[:, None, :]
    sine_part = jnp.sin(angles)[:, None, :]
    first_half = values[..., :half_dim]
    second_half = values[..., half_dim:]
    return jnp.concatenate(
        [
            first_half * cosine - second_half * sine_part,
            second_half * cosine + first_half * sine_part,
        ],
        axis=-1,
    )


def add_product(normed, portion):
    return jnp.dot(normed, portion, preferred_element_type=jnp.float32)


def normalise(hidden, norm_gain):
    widened = hidden.astype(jnp.float32)
    return (
        widened * lax.rsqrt(jnp.mean(widened * widened, axis=-1, keepdims=True) + EPS) * norm_gain
    ).astype(jnp.bfloat16)


def gathered_form(
    hidden, norm_gain, q_weight, q_bias, kv_weight, kv_bias, prefix_lens, assignment
):
    tok_rows, features = hidden.shape
    slice_rows = kv_weight.shape[0]
    q_cols = q_weight.shape[1]
    kv_total = kv_weight.shape[2]
    heads_here = q_cols // HD
    tensor_pos = lax.axis_index("tensor")
    kv_cols = kv_total // lax.axis_size("tensor")
    normed = normalise(hidden, norm_gain)
    queries = add_product(normed, lax.all_gather(q_weight, "group", axis=0, tiled=True)) + q_bias
    head_span = max(kv_cols, HD)
    head_base = tensor_pos * kv_cols // head_span * head_span
    local_start = tensor_pos * kv_cols - head_base
    head_rows = lax.dynamic_slice_in_dim(kv_weight, head_base, head_span, 2).reshape(
        slice_rows, 2 * head_span
    )
    projected = add_product(normed, lax.all_gather(head_rows, "group", axis=0, tiled=True))
    projected = projected.reshape(tok_rows, 2, head_span) + lax.dynamic_slice_in_dim(
        kv_bias, head_base, head_span, 1
    )
    kv_here = head_span // HD
    group_size = heads_here // kv_here
    owner_id, offset, places = token_layout(
        prefix_lens, assignment, lax.axis_index("group"), tok_rows
    )
    rotated_queries = rotate(queries.reshape(tok_rows, heads_here, HD), offset).astype(jnp.bfloat16)
    rotated_keys = rotate(projected[:, 0].reshape(tok_rows, kv_here, HD), offset).astype(
        jnp.bfloat16
    )
    value_heads = projected[:, 1].reshape(tok_rows, kv_here, HD).astype(jnp.bfloat16)
    visible = (owner_id[:, None] == owner_id[None, :]) & (places[None, :] <= places[:, None])
    grouped = rotated_queries.reshape(tok_rows, kv_here, group_size, HD)
    scores = jnp.einsum(
        "qgph,kgh->gpqk", grouped, rotated_keys, preferred_element_type=jnp.float32
    ) / math.sqrt(HD)
    scores = jnp.where(visible[None, None], scores, -jnp.inf)
    row_max = jnp.max(scores, axis=-1, keepdims=True)
    exponent = jnp.exp(scores - row_max)
    weights_bf = (exponent / jnp.sum(exponent, axis=-1, keepdims=True)).astype(jnp.bfloat16)
    context = jnp.einsum(
        "gpqk,kgh->qgph", weights_bf, value_heads, preferred_element_type=jnp.float32
    )
    context = context.astype(jnp.bfloat16).reshape(tok_rows, q_cols)
    stacked = jnp.stack(
        [rotated_keys.reshape(tok_rows, head_span), value_heads.reshape(tok_rows, head_span)],
        axis=1,
    )
    kv_cache = lax.dynamic_slice_in_dim(stacked, local_start, kv_cols, 2)
    return (context, kv_cache)


def norm_kernel(part_ref, hidden_ref, gain_ref, out_ref, part_out_ref):
    widened = hidden_ref[...].astype(jnp.float32)
    scale = lax.rsqrt(jnp.mean(widened * widened, axis=-1, keepdims=True) + EPS)
    normed = (widened * scale * gain_ref[...]).astype(jnp.bfloat16)
    depth = out_ref.shape[2]
    for block in range(out_ref.shape[0]):
        out_ref[block] = normed[:, block * depth : (block + 1) * depth]
    count = part_out_ref.shape[0]
    part_out_ref[...] = out_ref[pl.ds(part_ref[0] * count, count)]


def norm(hidden, norm_gain, part, depth, count):
    rows, features = hidden.shape
    blocks = features // depth
    step = 64
    return pl.pallas_call(
        norm_kernel,
        grid_spec=pltpu.PrefetchScalarGridSpec(
            num_scalar_prefetch=1,
            grid=(rows // step,),
            in_specs=[
                pl.BlockSpec((step, features), lambda i, part: (i, 0)),
                pl.BlockSpec((1, features), lambda i, part: (0, 0)),
            ],
            out_specs=[
                pl.BlockSpec((blocks, step, depth), lambda i, part: (0, i, 0)),
                pl.BlockSpec((count, step, depth), lambda i, part: (0, i, 0)),
            ],
        ),
        out_shape=[
            pltpu.HBM((blocks, rows, depth), jnp.bfloat16),
            pltpu.HBM((count, rows, depth), jnp.bfloat16),
        ],
        compiler_params=pltpu.CompilerParams(vmem_limit_bytes=32 * 2**20),
        cost_estimate=pl.CostEstimate(
            flops=4 * rows * features, bytes_accessed=5 * rows * features, transcendentals=rows
        ),
    )(part[None], hidden, norm_gain[None])


TILE = 2 * HD


def turn(value, cosine, sine):
    return value * cosine + pltpu.roll(value, HD // 2, 1) * sine


def heads_kernel(plan, pick_ref, *refs):
    sources, skips, parts, width, closed_width, totals_at, with_keys = plan
    finish = closed_width > 0
    sets, count = len(sources), len(parts)
    refs = list(refs)

    def take(number):
        taken = refs[:number]
        del refs[:number]
        return taken

    row_refs = [take(number) for number in sources]
    weight_refs = [take(len(part)) for part in parts]
    total_refs = take(sets) if totals_at is not None else None
    if finish:
        (bias_ref,) = take(1)
        table_refs = take(sets)
    outs = take(sets)
    sum_outs = take(sets) if finish and closed_width < width else None
    row_buf, weight_buf, acc, row_sem, weight_sem, total_sem, out_sem = take(7)
    depth = row_buf.shape[2] // count

    def weight_copies(piece):
        column = 0
        for part, (ref, (lead, skip, wide)) in enumerate(zip(weight_refs[piece], parts[piece])):
            ref = ref if lead is None else ref.at[lead]
            yield pltpu.make_async_copy(
                ref.at[:, skip : skip + wide],
                weight_buf.at[piece * depth : (piece + 1) * depth, column : column + wide],
                weight_sem.at[piece, part],
            )
            column += wide

    def row_copy(which, piece, source):
        return pltpu.make_async_copy(
            row_refs[which][source].at[pick_ref[which, 1, piece]],
            row_buf.at[which, :, piece * depth : (piece + 1) * depth],
            row_sem.at[which, piece],
        )

    def total_copy(which):
        return pltpu.make_async_copy(
            total_refs[which].at[:, totals_at[which] : totals_at[which] + width],
            acc.at[which],
            total_sem.at[which],
        )

    stages = [(0, low, min(low + 2, count)) for low in range(0, count, 2)]
    stages += [(which, skips[which], count) for which in range(1, sets)]

    def start(stage):
        which, low, high = stages[stage]
        for piece in range(low, high):
            if which == 0:
                for copy in weight_copies(piece):
                    copy.start()
            if sources[which] == 1:
                row_copy(which, piece, 0).start()
            else:
                for source in range(sources[which]):

                    @pl.when(pick_ref[which, 0, piece] == source)
                    def _():
                        row_copy(which, piece, source).start()
        if low == skips[which] and total_refs is not None:
            total_copy(which).start()

    start(0)
    if len(stages) > 1:
        start(1)
    if finish:
        bias_buf, table_buf, out_buf, side_sem = refs
        side_copies = [pltpu.make_async_copy(bias_ref, bias_buf, side_sem.at[sets])]
        side_copies += [
            pltpu.make_async_copy(table_refs[which], table_buf.at[which], side_sem.at[which])
            for which in range(sets)
        ]

    def out_copies(which):
        pairs = [((out_buf if finish else acc).at[which], outs[which])]
        if sum_outs is not None:
            pairs.append((acc.at[which, :, closed_width:], sum_outs[which]))
        return [
            pltpu.make_async_copy(buf, ref, out_sem.at[which, number])
            for number, (buf, ref) in enumerate(pairs)
        ]

    for stage, (which, low, high) in enumerate(stages):
        for piece in range(low, high):
            if which == 0:
                for copy in weight_copies(piece):
                    copy.wait()
            row_copy(which, piece, 0).wait()
        if low == skips[which] and total_refs is not None:
            total_copy(which).wait()
        if stage + 2 < len(stages):
            start(stage + 2)
        if stage == 0 and finish:
            for copy in side_copies:
                copy.start()
        for at in range(0, width, TILE):
            top = min(high, count - 2) if finish and at >= closed_width else high
            if top <= low:
                continue
            cols = slice(at, at + TILE)
            term = jnp.dot(
                row_buf[which, :, low * depth : top * depth],
                weight_buf[low * depth : top * depth, cols],
                preferred_element_type=jnp.float32,
            )
            if low > skips[which] or total_refs is not None:
                term = acc[which, :, cols] + term
            acc[which, :, cols] = term
        if high < count:
            continue
        if finish:
            if which == 0:
                side_copies[0].wait()
            side_copies[1 + which].wait()
            finish_set(acc.at[which], bias_buf, table_buf[which], out_buf.at[which], with_keys)
        for copy in out_copies(which):
            copy.start()
    for which in range(sets):
        for copy in out_copies(which):
            copy.wait()


def finish_set(acc, bias, table, out, with_keys):
    swapped = pltpu.roll(table, HD // 2, 1)
    left = lax.broadcasted_iota(jnp.int32, table.shape, 1) < HD // 2
    cosine = jnp.where(left, table, swapped)
    sine = jnp.where(left, -swapped, table)
    for col in range(0, out.shape[1], HD):
        cols = slice(col, col + HD)
        value = acc[:, cols] + bias[:, cols]
        if not (with_keys and col == HD):
            value = turn(value, cosine, sine)
        out[:, cols] = value.astype(jnp.bfloat16)


def heads_of(row_sets, picks, pieces, width, totals=None, finish=None, skips=None):
    sets, count = len(row_sets), len(pieces)
    skips = skips or (0,) * sets
    sources = tuple(len(rows) for rows in row_sets)
    tokens, depth = row_sets[0][0].shape[1:]
    operands = [array for rows in row_sets for array in rows]
    operands += [array for piece in pieces for array, *_ in piece]
    totals_at = None
    if totals is not None:
        totals, totals_at = totals
        operands += totals
    scratch = [
        pltpu.VMEM((sets, tokens, count * depth), jnp.bfloat16),
        pltpu.VMEM((count * depth, width), jnp.bfloat16),
        pltpu.VMEM((sets, tokens, width), jnp.float32),
        pltpu.SemaphoreType.DMA((sets, count)),
        pltpu.SemaphoreType.DMA((count, max(map(len, pieces)))),
        pltpu.SemaphoreType.DMA((sets,)),
        pltpu.SemaphoreType.DMA((sets, 3)),
    ]
    with_keys, closed_width = False, 0
    out_shape = [jax.ShapeDtypeStruct((tokens, width), jnp.float32)] * sets
    if finish is not None:
        closed_width, bias, tables, with_keys = finish
        out_shape = [jax.ShapeDtypeStruct((tokens, closed_width), jnp.bfloat16)] * sets
        operands += [bias, *tables]
        if closed_width < width:
            out_shape += [jax.ShapeDtypeStruct((tokens, width - closed_width), jnp.float32)] * sets
        scratch += [
            pltpu.VMEM((1, closed_width), jnp.float32),
            pltpu.VMEM((sets, tokens, HD), jnp.float32),
            pltpu.VMEM((sets, tokens, closed_width), jnp.bfloat16),
            pltpu.SemaphoreType.DMA((sets + 1,)),
        ]
    plan = (
        sources,
        skips,
        tuple(tuple(part[1:] for part in piece) for piece in pieces),
        width,
        closed_width,
        totals_at,
        with_keys,
    )
    anywhere = pl.BlockSpec(memory_space=pl.ANY)
    return pl.pallas_call(
        functools.partial(heads_kernel, plan),
        grid_spec=pltpu.PrefetchScalarGridSpec(
            num_scalar_prefetch=1,
            grid=(1,),
            in_specs=[anywhere] * len(operands),
            out_specs=[pl.BlockSpec(memory_space=pltpu.HBM)] * len(out_shape),
            scratch_shapes=scratch,
        ),
        out_shape=out_shape,
        compiler_params=pltpu.CompilerParams(vmem_limit_bytes=56 * 2**20),
        cost_estimate=pl.CostEstimate(
            flops=2 * sets * count * tokens * depth * width,
            bytes_accessed=2 * count * depth * (sets * tokens + width) + 8 * sets * tokens * width,
            transcendentals=0,
        ),
    )(jnp.stack(picks), *operands)


def attention(queries, keys, values, first_ref, out_ref):
    rows, cols = out_ref.shape
    heads = cols // HD
    scale = math.log2(math.e) / math.sqrt(HD)
    for top in range(0, rows, QROWS):
        low, end = max(0, top - MAXLEN), top + QROWS
        shape = (QROWS, end - low)
        stacked = jnp.concatenate(
            [queries[top:end, col : col + HD] for col in range(0, cols, HD)], axis=0
        )
        scores = jnp.dot(stacked, keys[:, low:end], preferred_element_type=jnp.float32)
        row = lax.broadcasted_iota(jnp.int32, shape, 0) + top
        col = lax.broadcasted_iota(jnp.int32, shape, 1) + low
        visible = (col <= row) & (col >= first_ref[top:end])
        scores = jnp.where(visible[None], scores.reshape(heads, *shape), -jnp.inf)
        most = jnp.max(scores, axis=-1, keepdims=True)
        exponent = jnp.exp2((scores - most) * scale)
        share = 1.0 / jnp.sum(exponent, axis=-1, keepdims=True)
        weights = (exponent * share).astype(jnp.bfloat16)
        context = jnp.dot(
            weights.reshape(heads * QROWS, end - low),
            values[low:end],
            preferred_element_type=jnp.float32,
        ).astype(jnp.bfloat16)
        for head in range(heads):
            out_ref[top:end, head * HD : (head + 1) * HD] = context[
                head * QROWS : (head + 1) * QROWS
            ]


def attend_kernel(numbers, flag_ref, *refs):
    ends = [sum(numbers[: i + 1]) for i in range(4)]
    near, beside, back, other = (refs[end - number : end] for end, number in zip(ends, numbers))
    first_ref, out_ref, cache_ref, part_buf, out_buf, in_sem, out_sem = refs[ends[-1] :]
    half = out_buf.shape[2]

    def copies(side, sources):
        column = 0
        for part, source in enumerate(sources):
            wide = source.shape[1]
            yield pltpu.make_async_copy(
                source, part_buf.at[side, :, column : column + wide], in_sem.at[side, part]
            )
            column += wide

    def on_parts(act):
        for middle, sides in ((1, (near, beside)), (0, (back, other))):

            @pl.when(flag_ref[1] == middle)
            def _():
                for side, sources in enumerate(sides):
                    for copy in copies(side, sources):
                        act(copy)

    on_parts(lambda copy: copy.start())
    on_parts(lambda copy: copy.wait())
    sent = []
    for side in range(2):
        at = flag_ref[0] if side == 0 else 1 - flag_ref[0]
        part = part_buf.at[side]
        for number in range(2):
            sent.append(
                pltpu.make_async_copy(
                    part.at[:, number * HD : (number + 1) * HD],
                    cache_ref.at[:, pl.ds(pl.multiple_of((2 * number + at) * HD, HD), HD)],
                    out_sem.at[side, number],
                )
            )
            sent[-1].start()
        keys = part[:, :HD].astype(jnp.float32).T.astype(jnp.bfloat16)
        attention(part.at[:, TILE:], keys, part.at[:, HD:TILE], first_ref, out_buf.at[side])
        sent.append(
            pltpu.make_async_copy(
                out_buf.at[side],
                out_ref.at[:, pl.ds(pl.multiple_of(at * half, half), half)],
                out_sem.at[side, 2],
            )
        )
        sent[-1].start()
    for copy in sent:
        copy.wait()


def attend_all(flags, near, beside, back, other, first, cols):
    operands = [*near, *beside, *back, *other]
    rows = near[0].shape[0]
    in_hbm = pl.BlockSpec(memory_space=pltpu.HBM)
    return pl.pallas_call(
        functools.partial(attend_kernel, tuple(map(len, (near, beside, back, other)))),
        grid_spec=pltpu.PrefetchScalarGridSpec(
            num_scalar_prefetch=1,
            grid=(1,),
            in_specs=[in_hbm] * len(operands) + [pl.BlockSpec((rows, 1), lambda i, flags: (0, 0))],
            out_specs=[in_hbm] * 2,
            scratch_shapes=[
                pltpu.VMEM((2, rows, TILE + cols // 2), jnp.bfloat16),
                pltpu.VMEM((2, rows, cols // 2), jnp.bfloat16),
                pltpu.SemaphoreType.DMA((2, 3)),
                pltpu.SemaphoreType.DMA((2, 3)),
            ],
        ),
        out_shape=[
            jax.ShapeDtypeStruct((rows, cols), jnp.bfloat16),
            jax.ShapeDtypeStruct((rows, 2 * TILE), jnp.bfloat16),
        ],
        compiler_params=pltpu.CompilerParams(vmem_limit_bytes=40 * 2**20),
        cost_estimate=pl.CostEstimate(
            flops=4 * cols * rows * 3 * QROWS,
            bytes_accessed=6 * rows * cols,
            transcendentals=cols // HD * rows * 3 * QROWS,
        ),
    )(flags, *operands, first)


MIDDLE = (2, 3, 4, 5)
ENDS = (0, 1, 6, 7)


def after(value, *others):
    return lax.optimization_barrier((value,) + others)[0]


def pairs_from(sources, code):
    return [(s, s ^ code) for s in sources]


def middle_form(hidden, norm_gain, q_weight, q_bias, kv_weight, kv_bias, prefix_lens, assignment):
    tok_rows, features = hidden.shape
    slice_rows, q_cols = q_weight.shape
    half_cols = q_cols // 2
    group = lax.axis_index("group")
    tensor = lax.axis_index("tensor")
    y = group & 1
    is_middle = (group >= 2) & (group < 6)
    barrier = lax.optimization_barrier

    def over_group(value, sources, code):
        return lax.ppermute(value, "group", pairs_from(sources, code))

    def to_middle(value):
        return over_group(value, ENDS, 2)

    def across_middle(value):
        return over_group(value, MIDDLE, 6)

    def over_x(value):
        return lax.ppermute(value, "tensor", pairs_from(range(4), 2))

    def over_core(value):
        return lax.ppermute(value, "tensor", pairs_from(range(4), 1))

    begin, widths = (0, 2 * TILE, 4 * TILE), (2 * TILE, 2 * TILE, TILE)

    def columns(half):
        head = (2 * tensor + half) * HD
        kv_part = lax.dynamic_slice_in_dim(kv_weight, head, HD, 2).reshape(slice_rows, TILE)
        q_part = lax.dynamic_slice_in_dim(q_weight, half * half_cols, half_cols, 1)
        return jnp.concatenate([kv_part, q_part], axis=1)

    def both(one, two, chunk):
        low, high = begin[chunk], begin[chunk] + widths[chunk]
        return jnp.stack([one[:, low:high], two[:, low:high]])

    def pick(code_of_rows, codes):
        block = jnp.stack([group ^ code for code in codes])
        if code_of_rows == 0:
            return jnp.stack([block * 0, block])
        return jnp.stack([(block >> 1) ^ tensor, block & 1])

    def rows_and_picks(sets, codes):
        return [rows_of[c] for c in sets], [pick(c, codes) for c in sets]

    def closed(arriving, others):
        arrived = []
        for value in arriving:
            value, others = barrier((value, others))
            arrived.append(value)
        return barrier((tuple(arrived), others))

    own = columns(y)
    other = columns(1 - y)
    m_own = across_middle(own)
    swap = over_group(other, range(8), 1)
    normed, quarter = norm(hidden, norm_gain, tensor, slice_rows, 2)
    end2 = to_middle(quarter)

    bias = lax.dynamic_slice_in_dim(q_bias, y * half_cols, half_cols, 0)
    kv_bias_here = lax.dynamic_slice_in_dim(kv_bias, (2 * tensor + y) * HD, HD, 1)
    bias = jnp.concatenate([kv_bias_here[0], kv_bias_here[1], bias])[None, :]
    inverse_freq = THETA ** (-2.0 * jnp.arange(HD // 2, dtype=jnp.float32) / HD)
    m_swap = across_middle(after(swap, m_own))
    own, swap, m_own, normed, quarter, end2 = barrier((own, swap, m_own, normed, quarter, end2))

    rows_of = {0: [normed]}
    stack0, end2 = barrier((both(own, swap, 0), end2))
    e0 = to_middle(stack0)
    next1, next2 = both(own, swap, 1), both(own, swap, 2)
    end3 = over_group(end2, MIDDLE, 1)
    across2 = over_x(end2)
    twin2 = over_core(end2)
    tables = []
    for code in range(4):
        _, offset, places = token_layout(prefix_lens, assignment, group ^ code, tok_rows)
        angles = offset.astype(jnp.float32)[:, None] * inverse_freq[None, :]
        table = jnp.concatenate([jnp.cos(angles), jnp.sin(angles)], axis=1)
        tables.append((table, (places - offset)[:, None]))
    m_e0 = across_middle(after(e0, m_swap))
    (e0, m_swap, end3, across2, twin2), (next1, next2, end2, tables, quarter) = closed(
        (e0, m_swap, end3, across2, twin2), (next1, next2, end2, tables, quarter)
    )

    first_codes, last_codes = (0, 1, 6, 7), (2, 3, 4, 5)
    first_pieces = {0: own, 1: swap, 6: m_own, 7: m_swap}
    last_pieces = {}

    def parts_of(code, chunks):
        low, wide = begin[chunks[0]], sum(widths[chunk] for chunk in chunks)
        if code in first_codes:
            return [(first_pieces[code], None, low, wide)]
        return [(last_pieces[code, chunk], code & 1, 0, widths[chunk]) for chunk in chunks]

    every = (0, 1, 2)

    def first_sums(sets):
        rows, picks = rows_and_picks(sets, first_codes)
        pieces = [parts_of(c, every) for c in first_codes]
        return heads_of(rows, picks, pieces, sum(widths))

    outs = {}

    def finished(sets, chunks, codes, totals=None, opened=(), skips=None):
        rows, picks = rows_and_picks(sets, codes)
        low, wide = begin[chunks[0]], sum(widths[chunk] for chunk in chunks)
        made = heads_of(
            rows,
            picks,
            [parts_of(c, chunks + (() if c in codes[-2:] else opened)) for c in codes],
            wide + sum(widths[chunk] for chunk in opened),
            totals,
            (wide, bias[:, low : low + wide], [tables[c][0] for c in sets], chunks[0] == 0),
            skips,
        )
        for code, out in zip(sets, made):
            outs[code, chunks[0]] = out
        return made[-1]

    e1 = to_middle(next1)
    end1 = over_group(quarter, MIDDLE, 1)
    across3 = over_x(end3)
    far2 = over_core(across2)
    rows_of[2] = [end2, twin2, across2, far2]
    sums = dict(zip((0, 2), first_sums((0, 2))))
    m_e1 = across_middle(after(e1, m_e0))
    (m_e0, e1, end1, across3), (next2, e0, end3, far2, sums) = closed(
        (m_e0, e1, end1, across3), (next2, e0, end3, far2, sums)
    )
    rows_of[2] = [end2, twin2, across2, far2]

    e2 = to_middle(next2)
    across1 = over_x(end1)
    twin3 = over_core(end3)
    far3 = over_core(across3)
    rows_of[3] = [end3, twin3, across3, far3]

    def send_back(code, chunk):
        return over_group(outs[code, chunk], MIDDLE, code)

    def arrived(chunk, end, middle):
        for code in last_codes:
            last_pieces[code, chunk] = end if code < 4 else middle

    arrived(0, e0, m_e0)
    (sums[3],) = first_sums((3,))
    three = (2, 3, 0)
    finished(three, (0,), last_codes, ([sums[c] for c in three], (0, 0, 0)))
    m_e2 = across_middle(after(e2, m_e1))
    back = {(code, 0): send_back(code, 0) for code in (2, 3)}
    (m_e1, across1, e2), (end1, made, sums) = closed(
        (m_e1, across1, e2), (end1, [outs[c, 0] for c in three], sums)
    )
    for code, out in zip(three, made):
        outs[code, 0] = out

    twin1 = over_core(end1)
    far1 = over_core(across1)
    arrived(1, e1, m_e1)
    arrived(2, e2, None)
    finished((2, 3), (1,), last_codes, ([sums[c] for c in (2, 3)], (begin[1],) * 2))
    for code in (2, 3):
        back[code, 1] = send_back(code, 1)
    far1, outs[2, 1] = barrier((far1, outs[2, 1]))
    rows_of[1] = [end1, twin1, across1, far1]
    sums[1] = finished((1,), (0, 1), first_codes + last_codes, opened=(2,))
    back[1, 0] = send_back(1, 0)
    (m_e2, back[2, 0], back[3, 0], back[2, 1]), (sums, outs[1, 0]) = closed(
        (m_e2, back[2, 0], back[3, 0], back[2, 1]), (sums, outs[1, 0])
    )

    arrived(2, e2, m_e2)
    three = (2, 3, 1)
    finished(
        three,
        (2,),
        last_codes,
        ([sums[c] for c in three], (begin[2], begin[2], 0)),
        skips=(0, 0, 2),
    )
    for code in three:
        back[code, 2] = send_back(code, 2)
    sums[0], outs[1, 2], back[3, 1] = barrier((sums[0], outs[1, 2], back[3, 1]))
    finished((0,), (1, 2), last_codes, ([sums[0]], (begin[1],)))

    context, cache = attend_all(
        jnp.stack([y, is_middle.astype(jnp.int32)]),
        [outs[0, part] for part in (0, 1)],
        [back[1, part] for part in (0, 2)],
        [back[2, part] for part in every],
        [back[3, part] for part in every],
        tables[0][1],
        q_cols,
    )
    return (context, cache.reshape(tok_rows, 2, TILE))


def solution(mesh):
    placed = (
        P("group", None),
        P(),
        P("group", "tensor"),
        P("tensor"),
        P("group", None, None),
        P(),
        P(),
        P(),
    )
    fits = mesh.shape["group"] == 8 and mesh.shape["tensor"] == 4
    return jax.shard_map(
        middle_form if fits else gathered_form,
        mesh=mesh,
        in_specs=placed,
        out_specs=(P("group", "tensor"), P("group", None, "tensor")),
        check_vma=False,
    )
```

```python
import functools
import math

import jax
import jax.numpy as jnp
from jax import lax
from jax.experimental import pallas as pl
from jax.experimental.pallas import tpu as pltpu
from jax.sharding import PartitionSpec as P

HD = 128


EPS = 1e-06
THETA = 1000000.0
QROWS = 128
MAXLEN = 256


def token_layout(prefix_lens, assignment, group_id, tok_rows):
    rollouts = prefix_lens.shape[0]
    member = assignment == group_id
    own_lens = jnp.where(member, prefix_lens, 0)
    starts = jnp.cumsum(own_lens) - own_lens
    places = jnp.arange(tok_rows, dtype=jnp.int32)
    inside = (
        member[None, :]
        & (places[:, None] >= starts[None, :])
        & (places[:, None] < (starts + own_lens)[None, :])
    )
    owner_id = jnp.sum(jnp.where(inside, jnp.arange(rollouts, dtype=jnp.int32)[None, :], 0), axis=1)
    offset = places - jnp.sum(jnp.where(inside, starts[None, :], 0), axis=1)
    return (owner_id, offset, places)


def rotate(values, offset):
    half_dim = values.shape[-1] // 2
    inverse_freq = THETA ** (-2.0 * jnp.arange(half_dim, dtype=jnp.float32) / values.shape[-1])
    angles = offset.astype(jnp.float32)[:, None] * inverse_freq[None, :]
    cosine = jnp.cos(angles)[:, None, :]
    sine_part = jnp.sin(angles)[:, None, :]
    first_half = values[..., :half_dim]
    second_half = values[..., half_dim:]
    return jnp.concatenate(
        [
            first_half * cosine - second_half * sine_part,
            second_half * cosine + first_half * sine_part,
        ],
        axis=-1,
    )


def add_product(normed, portion):
    return jnp.dot(normed, portion, preferred_element_type=jnp.float32)


def normalise(hidden, norm_gain):
    widened = hidden.astype(jnp.float32)
    return (
        widened * lax.rsqrt(jnp.mean(widened * widened, axis=-1, keepdims=True) + EPS) * norm_gain
    ).astype(jnp.bfloat16)


def gathered_form(
    hidden, norm_gain, q_weight, q_bias, kv_weight, kv_bias, prefix_lens, assignment
):
    tok_rows, features = hidden.shape
    slice_rows = kv_weight.shape[0]
    q_cols = q_weight.shape[1]
    kv_total = kv_weight.shape[2]
    heads_here = q_cols // HD
    tensor_pos = lax.axis_index("tensor")
    kv_cols = kv_total // lax.axis_size("tensor")
    normed = normalise(hidden, norm_gain)
    queries = add_product(normed, lax.all_gather(q_weight, "group", axis=0, tiled=True)) + q_bias
    head_span = max(kv_cols, HD)
    head_base = tensor_pos * kv_cols // head_span * head_span
    local_start = tensor_pos * kv_cols - head_base
    head_rows = lax.dynamic_slice_in_dim(kv_weight, head_base, head_span, 2).reshape(
        slice_rows, 2 * head_span
    )
    projected = add_product(normed, lax.all_gather(head_rows, "group", axis=0, tiled=True))
    projected = projected.reshape(tok_rows, 2, head_span) + lax.dynamic_slice_in_dim(
        kv_bias, head_base, head_span, 1
    )
    kv_here = head_span // HD
    group_size = heads_here // kv_here
    owner_id, offset, places = token_layout(
        prefix_lens, assignment, lax.axis_index("group"), tok_rows
    )
    rotated_queries = rotate(queries.reshape(tok_rows, heads_here, HD), offset).astype(jnp.bfloat16)
    rotated_keys = rotate(projected[:, 0].reshape(tok_rows, kv_here, HD), offset).astype(
        jnp.bfloat16
    )
    value_heads = projected[:, 1].reshape(tok_rows, kv_here, HD).astype(jnp.bfloat16)
    visible = (owner_id[:, None] == owner_id[None, :]) & (places[None, :] <= places[:, None])
    grouped = rotated_queries.reshape(tok_rows, kv_here, group_size, HD)
    scores = jnp.einsum(
        "qgph,kgh->gpqk", grouped, rotated_keys, preferred_element_type=jnp.float32
    ) / math.sqrt(HD)
    scores = jnp.where(visible[None, None], scores, -jnp.inf)
    row_max = jnp.max(scores, axis=-1, keepdims=True)
    exponent = jnp.exp(scores - row_max)
    weights_bf = (exponent / jnp.sum(exponent, axis=-1, keepdims=True)).astype(jnp.bfloat16)
    context = jnp.einsum(
        "gpqk,kgh->qgph", weights_bf, value_heads, preferred_element_type=jnp.float32
    )
    context = context.astype(jnp.bfloat16).reshape(tok_rows, q_cols)
    stacked = jnp.stack(
        [rotated_keys.reshape(tok_rows, head_span), value_heads.reshape(tok_rows, head_span)],
        axis=1,
    )
    kv_cache = lax.dynamic_slice_in_dim(stacked, local_start, kv_cols, 2)
    return (context, kv_cache)


def norm_kernel(part_ref, hidden_ref, gain_ref, out_ref):
    widened = hidden_ref[...].astype(jnp.float32)
    scale = lax.rsqrt(jnp.mean(widened * widened, axis=-1, keepdims=True) + EPS)
    count, _, depth = out_ref.shape
    for block in range(count):
        at = pl.multiple_of((part_ref[0] * count + block) * depth, depth)
        taken = hidden_ref[:, pl.ds(at, depth)].astype(jnp.float32)
        out_ref[block] = (taken * scale * gain_ref[:, pl.ds(at, depth)]).astype(jnp.bfloat16)


def norm(hidden, norm_gain, part, depth, count):
    rows, features = hidden.shape
    step = 64
    return pl.pallas_call(
        norm_kernel,
        grid_spec=pltpu.PrefetchScalarGridSpec(
            num_scalar_prefetch=1,
            grid=(rows // step,),
            in_specs=[
                pl.BlockSpec((step, features), lambda i, part: (i, 0)),
                pl.BlockSpec((1, features), lambda i, part: (0, 0)),
            ],
            out_specs=pl.BlockSpec((count, step, depth), lambda i, part: (0, i, 0)),
        ),
        out_shape=pltpu.HBM((count, rows, depth), jnp.bfloat16),
        compiler_params=pltpu.CompilerParams(vmem_limit_bytes=32 * 2**20),
        cost_estimate=pl.CostEstimate(
            flops=4 * rows * features,
            bytes_accessed=2 * rows * (features + count * depth),
            transcendentals=rows,
        ),
    )(part[None], hidden, norm_gain[None])


TILE = 2 * HD


def turn(value, cosine, sine):
    return value * cosine + pltpu.roll(value, HD // 2, 1) * sine


def heads_kernel(plan, pick_ref, *refs):
    sources, skips, parts, width, closed_width, totals_at, with_keys = plan
    finish = closed_width > 0
    sets, count = len(sources), len(parts)
    refs = list(refs)

    def take(number):
        taken = refs[:number]
        del refs[:number]
        return taken

    row_refs = [take(number) for number in sources]
    weight_refs = [take(len(part)) for part in parts]
    total_refs = take(sets) if totals_at is not None else None
    if finish:
        (bias_ref,) = take(1)
        table_refs = take(sets)
    outs = take(sets)
    sum_outs = take(sets) if finish and closed_width < width else None
    row_buf, weight_buf, acc, row_sem, weight_sem, total_sem, out_sem = take(7)
    depth = row_buf.shape[2] // count

    def weight_copies(piece):
        column = 0
        for part, (ref, (lead, skip, wide)) in enumerate(zip(weight_refs[piece], parts[piece])):
            ref = ref if lead is None else ref.at[lead]
            yield pltpu.make_async_copy(
                ref.at[:, skip : skip + wide],
                weight_buf.at[piece * depth : (piece + 1) * depth, column : column + wide],
                weight_sem.at[piece, part],
            )
            column += wide

    def row_copy(which, piece, source):
        return pltpu.make_async_copy(
            row_refs[which][source].at[pick_ref[which, 1, piece]],
            row_buf.at[which, :, piece * depth : (piece + 1) * depth],
            row_sem.at[which, piece],
        )

    def total_copy(which):
        return pltpu.make_async_copy(
            total_refs[which].at[:, totals_at[which] : totals_at[which] + width],
            acc.at[which],
            total_sem.at[which],
        )

    stages = [(0, low, min(low + 2, count)) for low in range(0, count, 2)]
    stages += [(which, skips[which], count) for which in range(1, sets)]

    def start(stage):
        which, low, high = stages[stage]
        for piece in range(low, high):
            if which == 0:
                for copy in weight_copies(piece):
                    copy.start()
            if sources[which] == 1:
                row_copy(which, piece, 0).start()
            else:
                for source in range(sources[which]):

                    @pl.when(pick_ref[which, 0, piece] == source)
                    def _():
                        row_copy(which, piece, source).start()
        if low == skips[which] and total_refs is not None:
            total_copy(which).start()

    start(0)
    if len(stages) > 1:
        start(1)
    if finish:
        bias_buf, table_buf, out_buf, side_sem = refs
        side_copies = [pltpu.make_async_copy(bias_ref, bias_buf, side_sem.at[sets])]
        side_copies += [
            pltpu.make_async_copy(table_refs[which], table_buf.at[which], side_sem.at[which])
            for which in range(sets)
        ]

    def out_copies(which):
        pairs = [((out_buf if finish else acc).at[which], outs[which])]
        if sum_outs is not None:
            pairs.append((acc.at[which, :, closed_width:], sum_outs[which]))
        return [
            pltpu.make_async_copy(buf, ref, out_sem.at[which, number])
            for number, (buf, ref) in enumerate(pairs)
        ]

    for stage, (which, low, high) in enumerate(stages):
        for piece in range(low, high):
            if which == 0:
                for copy in weight_copies(piece):
                    copy.wait()
            row_copy(which, piece, 0).wait()
        if low == skips[which] and total_refs is not None:
            total_copy(which).wait()
        if stage + 2 < len(stages):
            start(stage + 2)
        if stage == 0 and finish:
            for copy in side_copies:
                copy.start()
        for at in range(0, width, TILE):
            top = min(high, count - 2) if finish and at >= closed_width else high
            if top <= low:
                continue
            cols = slice(at, at + TILE)
            term = jnp.dot(
                row_buf[which, :, low * depth : top * depth],
                weight_buf[low * depth : top * depth, cols],
                preferred_element_type=jnp.float32,
            )
            if low > skips[which] or total_refs is not None:
                term = acc[which, :, cols] + term
            acc[which, :, cols] = term
        if high < count:
            continue
        if finish:
            if which == 0:
                side_copies[0].wait()
            side_copies[1 + which].wait()
            finish_set(acc.at[which], bias_buf, table_buf[which], out_buf.at[which], with_keys)
        for copy in out_copies(which):
            copy.start()
    for which in range(sets):
        for copy in out_copies(which):
            copy.wait()


def finish_set(acc, bias, table, out, with_keys):
    swapped = pltpu.roll(table, HD // 2, 1)
    left = lax.broadcasted_iota(jnp.int32, table.shape, 1) < HD // 2
    cosine = jnp.where(left, table, swapped)
    sine = jnp.where(left, -swapped, table)
    for col in range(0, out.shape[1], HD):
        cols = slice(col, col + HD)
        value = acc[:, cols] + bias[:, cols]
        if not (with_keys and col == HD):
            value = turn(value, cosine, sine)
        out[:, cols] = value.astype(jnp.bfloat16)


def heads_of(row_sets, picks, pieces, width, totals=None, finish=None, skips=None):
    sets, count = len(row_sets), len(pieces)
    skips = skips or (0,) * sets
    sources = tuple(len(rows) for rows in row_sets)
    tokens, depth = row_sets[0][0].shape[1:]
    operands = [array for rows in row_sets for array in rows]
    operands += [array for piece in pieces for array, *_ in piece]
    totals_at = None
    if totals is not None:
        totals, totals_at = totals
        operands += totals
    scratch = [
        pltpu.VMEM((sets, tokens, count * depth), jnp.bfloat16),
        pltpu.VMEM((count * depth, width), jnp.bfloat16),
        pltpu.VMEM((sets, tokens, width), jnp.float32),
        pltpu.SemaphoreType.DMA((sets, count)),
        pltpu.SemaphoreType.DMA((count, max(map(len, pieces)))),
        pltpu.SemaphoreType.DMA((sets,)),
        pltpu.SemaphoreType.DMA((sets, 3)),
    ]
    with_keys, closed_width = False, 0
    out_shape = [jax.ShapeDtypeStruct((tokens, width), jnp.float32)] * sets
    if finish is not None:
        closed_width, bias, tables, with_keys = finish
        out_shape = [jax.ShapeDtypeStruct((tokens, closed_width), jnp.bfloat16)] * sets
        operands += [bias, *tables]
        if closed_width < width:
            out_shape += [jax.ShapeDtypeStruct((tokens, width - closed_width), jnp.float32)] * sets
        scratch += [
            pltpu.VMEM((1, closed_width), jnp.float32),
            pltpu.VMEM((sets, tokens, HD), jnp.float32),
            pltpu.VMEM((sets, tokens, closed_width), jnp.bfloat16),
            pltpu.SemaphoreType.DMA((sets + 1,)),
        ]
    plan = (
        sources,
        skips,
        tuple(tuple(part[1:] for part in piece) for piece in pieces),
        width,
        closed_width,
        totals_at,
        with_keys,
    )
    anywhere = pl.BlockSpec(memory_space=pl.ANY)
    return pl.pallas_call(
        functools.partial(heads_kernel, plan),
        grid_spec=pltpu.PrefetchScalarGridSpec(
            num_scalar_prefetch=1,
            grid=(1,),
            in_specs=[anywhere] * len(operands),
            out_specs=[pl.BlockSpec(memory_space=pltpu.HBM)] * len(out_shape),
            scratch_shapes=scratch,
        ),
        out_shape=out_shape,
        compiler_params=pltpu.CompilerParams(vmem_limit_bytes=56 * 2**20),
        cost_estimate=pl.CostEstimate(
            flops=2 * sets * count * tokens * depth * width,
            bytes_accessed=2 * count * depth * (sets * tokens + width) + 8 * sets * tokens * width,
            transcendentals=0,
        ),
    )(jnp.stack(picks), *operands)


def attention(queries, keys, values, first_ref, out_ref):
    rows, cols = out_ref.shape
    heads = cols // HD
    scale = math.log2(math.e) / math.sqrt(HD)
    for top in range(0, rows, QROWS):
        low, end = max(0, top - MAXLEN), top + QROWS
        shape = (QROWS, end - low)
        stacked = jnp.concatenate(
            [queries[top:end, col : col + HD] for col in range(0, cols, HD)], axis=0
        )
        scores = jnp.dot(stacked, keys[:, low:end], preferred_element_type=jnp.float32)
        row = lax.broadcasted_iota(jnp.int32, shape, 0) + top
        col = lax.broadcasted_iota(jnp.int32, shape, 1) + low
        visible = (col <= row) & (col >= first_ref[top:end])
        scores = jnp.where(visible[None], scores.reshape(heads, *shape), -jnp.inf)
        most = jnp.max(scores, axis=-1, keepdims=True)
        exponent = jnp.exp2((scores - most) * scale)
        share = 1.0 / jnp.sum(exponent, axis=-1, keepdims=True)
        weights = (exponent * share).astype(jnp.bfloat16)
        context = jnp.dot(
            weights.reshape(heads * QROWS, end - low),
            values[low:end],
            preferred_element_type=jnp.float32,
        ).astype(jnp.bfloat16)
        for head in range(heads):
            out_ref[top:end, head * HD : (head + 1) * HD] = context[
                head * QROWS : (head + 1) * QROWS
            ]


def attend_kernel(numbers, flag_ref, *refs):
    ends = [sum(numbers[: i + 1]) for i in range(4)]
    near, beside, back, other = (refs[end - number : end] for end, number in zip(ends, numbers))
    first_ref, out_ref, cache_ref, part_buf, out_buf, in_sem, out_sem = refs[ends[-1] :]
    half = out_buf.shape[2]

    def copies(side, sources):
        column = 0
        for part, source in enumerate(sources):
            wide = source.shape[1]
            yield pltpu.make_async_copy(
                source, part_buf.at[side, :, column : column + wide], in_sem.at[side, part]
            )
            column += wide

    def on_parts(act):
        for middle, sides in ((1, (near, beside)), (0, (back, other))):

            @pl.when(flag_ref[1] == middle)
            def _():
                for side, sources in enumerate(sides):
                    for copy in copies(side, sources):
                        act(copy)

    on_parts(lambda copy: copy.start())
    on_parts(lambda copy: copy.wait())
    sent = []
    for side in range(2):
        at = flag_ref[0] if side == 0 else 1 - flag_ref[0]
        part = part_buf.at[side]
        for number in range(2):
            sent.append(
                pltpu.make_async_copy(
                    part.at[:, number * HD : (number + 1) * HD],
                    cache_ref.at[:, pl.ds(pl.multiple_of((2 * number + at) * HD, HD), HD)],
                    out_sem.at[side, number],
                )
            )
            sent[-1].start()
        keys = part[:, :HD].astype(jnp.float32).T.astype(jnp.bfloat16)
        attention(part.at[:, TILE:], keys, part.at[:, HD:TILE], first_ref, out_buf.at[side])
        sent.append(
            pltpu.make_async_copy(
                out_buf.at[side],
                out_ref.at[:, pl.ds(pl.multiple_of(at * half, half), half)],
                out_sem.at[side, 2],
            )
        )
        sent[-1].start()
    for copy in sent:
        copy.wait()


def attend_all(flags, near, beside, back, other, first, cols):
    operands = [*near, *beside, *back, *other]
    rows = near[0].shape[0]
    in_hbm = pl.BlockSpec(memory_space=pltpu.HBM)
    return pl.pallas_call(
        functools.partial(attend_kernel, tuple(map(len, (near, beside, back, other)))),
        grid_spec=pltpu.PrefetchScalarGridSpec(
            num_scalar_prefetch=1,
            grid=(1,),
            in_specs=[in_hbm] * len(operands) + [pl.BlockSpec((rows, 1), lambda i, flags: (0, 0))],
            out_specs=[in_hbm] * 2,
            scratch_shapes=[
                pltpu.VMEM((2, rows, TILE + cols // 2), jnp.bfloat16),
                pltpu.VMEM((2, rows, cols // 2), jnp.bfloat16),
                pltpu.SemaphoreType.DMA((2, 3)),
                pltpu.SemaphoreType.DMA((2, 3)),
            ],
        ),
        out_shape=[
            jax.ShapeDtypeStruct((rows, cols), jnp.bfloat16),
            jax.ShapeDtypeStruct((rows, 2 * TILE), jnp.bfloat16),
        ],
        compiler_params=pltpu.CompilerParams(vmem_limit_bytes=40 * 2**20),
        cost_estimate=pl.CostEstimate(
            flops=4 * cols * rows * 3 * QROWS,
            bytes_accessed=6 * rows * cols,
            transcendentals=cols // HD * rows * 3 * QROWS,
        ),
    )(flags, *operands, first)


MIDDLE = (2, 3, 4, 5)
ENDS = (0, 1, 6, 7)


def after(value, *others):
    return lax.optimization_barrier((value,) + others)[0]


def pairs_from(sources, code):
    return [(s, s ^ code) for s in sources]


def middle_form(hidden, norm_gain, q_weight, q_bias, kv_weight, kv_bias, prefix_lens, assignment):
    tok_rows, features = hidden.shape
    slice_rows, q_cols = q_weight.shape
    half_cols = q_cols // 2
    group = lax.axis_index("group")
    tensor = lax.axis_index("tensor")
    y = group & 1
    is_middle = (group >= 2) & (group < 6)
    barrier = lax.optimization_barrier

    def over_group(value, sources, code):
        return lax.ppermute(value, "group", pairs_from(sources, code))

    def to_middle(value):
        return over_group(value, ENDS, 2)

    def across_middle(value):
        return over_group(value, MIDDLE, 6)

    def over_x(value):
        return lax.ppermute(value, "tensor", pairs_from(range(4), 2))

    def over_core(value):
        return lax.ppermute(value, "tensor", pairs_from(range(4), 1))

    begin, widths = (0, 2 * TILE, 4 * TILE), (2 * TILE, 2 * TILE, TILE)

    def columns(half):
        head = (2 * tensor + half) * HD
        kv_part = lax.dynamic_slice_in_dim(kv_weight, head, HD, 2).reshape(slice_rows, TILE)
        q_part = lax.dynamic_slice_in_dim(q_weight, half * half_cols, half_cols, 1)
        return jnp.concatenate([kv_part, q_part], axis=1)

    def both(one, two, chunk):
        low, high = begin[chunk], begin[chunk] + widths[chunk]
        return jnp.stack([one[:, low:high], two[:, low:high]])

    def pick(code_of_rows, codes):
        block = jnp.stack([group ^ code for code in codes])
        if code_of_rows == 0:
            return jnp.stack([block * 0, block])
        return jnp.stack([(block >> 1) ^ tensor, block & 1])

    def rows_and_picks(sets, codes):
        return [rows_of[c] for c in sets], [pick(c, codes) for c in sets]

    def closed(arriving, others):
        arrived = []
        for value in arriving:
            value, others = barrier((value, others))
            arrived.append(value)
        return barrier((tuple(arrived), others))

    own = columns(y)
    other = columns(1 - y)
    m_own = across_middle(own)
    swap = over_group(other, range(8), 1)
    quarter = norm(hidden, norm_gain, tensor, slice_rows, 2)
    end2 = to_middle(quarter)
    normed = norm(after(hidden, quarter), norm_gain, tensor * 0, slice_rows, features // slice_rows)

    bias = lax.dynamic_slice_in_dim(q_bias, y * half_cols, half_cols, 0)
    kv_bias_here = lax.dynamic_slice_in_dim(kv_bias, (2 * tensor + y) * HD, HD, 1)
    bias = jnp.concatenate([kv_bias_here[0], kv_bias_here[1], bias])[None, :]
    inverse_freq = THETA ** (-2.0 * jnp.arange(HD // 2, dtype=jnp.float32) / HD)
    m_swap = across_middle(after(swap, m_own))
    own, swap, m_own, normed, quarter, end2 = barrier((own, swap, m_own, normed, quarter, end2))

    rows_of = {0: [normed]}
    stack0, end2 = barrier((both(own, swap, 0), end2))
    e0 = to_middle(stack0)
    next1, next2 = both(own, swap, 1), both(own, swap, 2)
    end3 = over_group(end2, MIDDLE, 1)
    across2 = over_x(end2)
    twin2 = over_core(end2)
    tables = []
    for code in range(4):
        _, offset, places = token_layout(prefix_lens, assignment, group ^ code, tok_rows)
        angles = offset.astype(jnp.float32)[:, None] * inverse_freq[None, :]
        table = jnp.concatenate([jnp.cos(angles), jnp.sin(angles)], axis=1)
        tables.append((table, (places - offset)[:, None]))
    m_e0 = across_middle(after(e0, m_swap))
    (e0, m_swap, end3, across2, twin2), (next1, next2, end2, tables, quarter) = closed(
        (e0, m_swap, end3, across2, twin2), (next1, next2, end2, tables, quarter)
    )

    first_codes, last_codes = (0, 1, 6, 7), (2, 3, 4, 5)
    first_pieces = {0: own, 1: swap, 6: m_own, 7: m_swap}
    last_pieces = {}

    def parts_of(code, chunks):
        low, wide = begin[chunks[0]], sum(widths[chunk] for chunk in chunks)
        if code in first_codes:
            return [(first_pieces[code], None, low, wide)]
        return [(last_pieces[code, chunk], code & 1, 0, widths[chunk]) for chunk in chunks]

    every = (0, 1, 2)

    def first_sums(sets):
        rows, picks = rows_and_picks(sets, first_codes)
        pieces = [parts_of(c, every) for c in first_codes]
        return heads_of(rows, picks, pieces, sum(widths))

    def more_sums(sets, chunk, codes, totals):
        rows, picks = rows_and_picks(sets, codes)
        pieces = [parts_of(c, (chunk,)) for c in codes]
        return heads_of(rows, picks, pieces, widths[chunk], (totals, (begin[chunk],) * len(sets)))

    outs = {}

    def finished(sets, chunks, codes, totals=None, opened=(), skips=None):
        rows, picks = rows_and_picks(sets, codes)
        low, wide = begin[chunks[0]], sum(widths[chunk] for chunk in chunks)
        made = heads_of(
            rows,
            picks,
            [parts_of(c, chunks + (() if c in codes[-2:] else opened)) for c in codes],
            wide + sum(widths[chunk] for chunk in opened),
            totals,
            (wide, bias[:, low : low + wide], [tables[c][0] for c in sets], chunks[0] == 0),
            skips,
        )
        for code, out in zip(sets, made):
            outs[code, chunks[0]] = out
        return made[-1]

    e1 = to_middle(next1)
    end1 = over_group(quarter, MIDDLE, 1)
    across3 = over_x(end3)
    far2 = over_core(across2)
    rows_of[2] = [end2, twin2, across2, far2]
    sums = dict(zip((0, 2), first_sums((0, 2))))
    m_e1 = across_middle(after(e1, m_e0))
    (m_e0, e1, end1, across3), (next2, e0, end3, far2, sums) = closed(
        (m_e0, e1, end1, across3), (next2, e0, end3, far2, sums)
    )
    rows_of[2] = [end2, twin2, across2, far2]

    e2 = to_middle(next2)
    across1 = over_x(end1)
    twin3 = over_core(end3)
    far3 = over_core(across3)
    rows_of[3] = [end3, twin3, across3, far3]

    def send_back(code, chunk):
        return over_group(outs[code, chunk], MIDDLE, code)

    def arrived(chunk, end, middle):
        for code in last_codes:
            last_pieces[code, chunk] = end if code < 4 else middle

    arrived(0, e0, m_e0)
    arrived(1, e1, None)
    (sums[3],) = first_sums((3,))
    three = (2, 3, 0)
    finished(three, (0,), last_codes, ([sums[c] for c in three], (0, 0, 0)))
    m_e2 = across_middle(after(e2, m_e1))
    back = {(2, 0): send_back(2, 0)}
    sums1 = more_sums(three, 1, last_codes[:2], [sums[c] for c in three])
    (m_e1, across1, e2, back[2, 0]), (end1, made, sums, sums1) = closed(
        (m_e1, across1, e2, back[2, 0]), (end1, [outs[c, 0] for c in three], sums, sums1)
    )
    for code, out in zip(three, made):
        outs[code, 0] = out

    twin1 = over_core(end1)
    far1 = over_core(across1)
    arrived(1, e1, m_e1)
    arrived(2, e2, None)
    back[3, 0] = send_back(3, 0)
    finished(three, (1,), last_codes[2:], (sums1, (0, 0, 0)))
    for code in (2, 3):
        back[code, 1] = send_back(code, 1)
    far1, outs[2, 1] = barrier((far1, outs[2, 1]))
    rows_of[1] = [end1, twin1, across1, far1]
    sums[1] = finished((1,), (0, 1), first_codes + last_codes, opened=(2,))
    back[1, 0] = send_back(1, 0)
    (m_e2, back[3, 0], back[2, 1]), (sums, outs[1, 0]) = closed(
        (m_e2, back[3, 0], back[2, 1]), (sums, outs[1, 0])
    )

    arrived(2, e2, m_e2)
    three = (2, 3, 1)
    finished(
        three,
        (2,),
        last_codes,
        ([sums[c] for c in three], (begin[2], begin[2], 0)),
        skips=(0, 0, 2),
    )
    for code in three:
        back[code, 2] = send_back(code, 2)
    sums[0], outs[1, 2], back[3, 1] = barrier((sums[0], outs[1, 2], back[3, 1]))
    finished((0,), (2,), last_codes, ([sums[0]], (begin[2],)))

    context, cache = attend_all(
        jnp.stack([y, is_middle.astype(jnp.int32)]),
        [outs[0, part] for part in every],
        [back[1, part] for part in (0, 2)],
        [back[2, part] for part in every],
        [back[3, part] for part in every],
        tables[0][1],
        q_cols,
    )
    return (context, cache.reshape(tok_rows, 2, TILE))


def solution(mesh):
    placed = (
        P("group", None),
        P(),
        P("group", "tensor"),
        P("tensor"),
        P("group", None, None),
        P(),
        P(),
        P(),
    )
    fits = mesh.shape["group"] == 8 and mesh.shape["tensor"] == 4
    return jax.shard_map(
        middle_form if fits else gathered_form,
        mesh=mesh,
        in_specs=placed,
        out_specs=(P("group", "tensor"), P("group", None, "tensor")),
        check_vma=False,
    )
```

```python
import functools
import math

import jax
import jax.numpy as jnp
from jax import lax
from jax.experimental import pallas as pl
from jax.experimental.pallas import tpu as pltpu
from jax.sharding import PartitionSpec as P

HD = 128


EPS = 1e-06
THETA = 1000000.0
QROWS = 128
MAXLEN = 256


def token_layout(prefix_lens, assignment, group_id, tok_rows):
    rollouts = prefix_lens.shape[0]
    member = assignment == group_id
    own_lens = jnp.where(member, prefix_lens, 0)
    starts = jnp.cumsum(own_lens) - own_lens
    places = jnp.arange(tok_rows, dtype=jnp.int32)
    inside = (
        member[None, :]
        & (places[:, None] >= starts[None, :])
        & (places[:, None] < (starts + own_lens)[None, :])
    )
    owner_id = jnp.sum(jnp.where(inside, jnp.arange(rollouts, dtype=jnp.int32)[None, :], 0), axis=1)
    offset = places - jnp.sum(jnp.where(inside, starts[None, :], 0), axis=1)
    return (owner_id, offset, places)


def rotate(values, offset):
    half_dim = values.shape[-1] // 2
    inverse_freq = THETA ** (-2.0 * jnp.arange(half_dim, dtype=jnp.float32) / values.shape[-1])
    angles = offset.astype(jnp.float32)[:, None] * inverse_freq[None, :]
    cosine = jnp.cos(angles)[:, None, :]
    sine_part = jnp.sin(angles)[:, None, :]
    first_half = values[..., :half_dim]
    second_half = values[..., half_dim:]
    return jnp.concatenate(
        [
            first_half * cosine - second_half * sine_part,
            second_half * cosine + first_half * sine_part,
        ],
        axis=-1,
    )


def add_product(normed, portion):
    return jnp.dot(normed, portion, preferred_element_type=jnp.float32)


def normalise(hidden, norm_gain):
    widened = hidden.astype(jnp.float32)
    return (
        widened * lax.rsqrt(jnp.mean(widened * widened, axis=-1, keepdims=True) + EPS) * norm_gain
    ).astype(jnp.bfloat16)


def gathered_form(
    hidden, norm_gain, q_weight, q_bias, kv_weight, kv_bias, prefix_lens, assignment
):
    tok_rows, features = hidden.shape
    slice_rows = kv_weight.shape[0]
    q_cols = q_weight.shape[1]
    kv_total = kv_weight.shape[2]
    heads_here = q_cols // HD
    tensor_pos = lax.axis_index("tensor")
    kv_cols = kv_total // lax.axis_size("tensor")
    normed = normalise(hidden, norm_gain)
    queries = add_product(normed, lax.all_gather(q_weight, "group", axis=0, tiled=True)) + q_bias
    head_span = max(kv_cols, HD)
    head_base = tensor_pos * kv_cols // head_span * head_span
    local_start = tensor_pos * kv_cols - head_base
    head_rows = lax.dynamic_slice_in_dim(kv_weight, head_base, head_span, 2).reshape(
        slice_rows, 2 * head_span
    )
    projected = add_product(normed, lax.all_gather(head_rows, "group", axis=0, tiled=True))
    projected = projected.reshape(tok_rows, 2, head_span) + lax.dynamic_slice_in_dim(
        kv_bias, head_base, head_span, 1
    )
    kv_here = head_span // HD
    group_size = heads_here // kv_here
    owner_id, offset, places = token_layout(
        prefix_lens, assignment, lax.axis_index("group"), tok_rows
    )
    rotated_queries = rotate(queries.reshape(tok_rows, heads_here, HD), offset).astype(jnp.bfloat16)
    rotated_keys = rotate(projected[:, 0].reshape(tok_rows, kv_here, HD), offset).astype(
        jnp.bfloat16
    )
    value_heads = projected[:, 1].reshape(tok_rows, kv_here, HD).astype(jnp.bfloat16)
    visible = (owner_id[:, None] == owner_id[None, :]) & (places[None, :] <= places[:, None])
    grouped = rotated_queries.reshape(tok_rows, kv_here, group_size, HD)
    scores = jnp.einsum(
        "qgph,kgh->gpqk", grouped, rotated_keys, preferred_element_type=jnp.float32
    ) / math.sqrt(HD)
    scores = jnp.where(visible[None, None], scores, -jnp.inf)
    row_max = jnp.max(scores, axis=-1, keepdims=True)
    exponent = jnp.exp(scores - row_max)
    weights_bf = (exponent / jnp.sum(exponent, axis=-1, keepdims=True)).astype(jnp.bfloat16)
    context = jnp.einsum(
        "gpqk,kgh->qgph", weights_bf, value_heads, preferred_element_type=jnp.float32
    )
    context = context.astype(jnp.bfloat16).reshape(tok_rows, q_cols)
    stacked = jnp.stack(
        [rotated_keys.reshape(tok_rows, head_span), value_heads.reshape(tok_rows, head_span)],
        axis=1,
    )
    kv_cache = lax.dynamic_slice_in_dim(stacked, local_start, kv_cols, 2)
    return (context, kv_cache)


def norm_kernel(part_ref, hidden_ref, gain_ref, out_ref):
    widened = hidden_ref[...].astype(jnp.float32)
    scale = lax.rsqrt(jnp.mean(widened * widened, axis=-1, keepdims=True) + EPS)
    count, _, depth = out_ref.shape
    for block in range(count):
        at = pl.multiple_of((part_ref[0] * count + block) * depth, depth)
        taken = hidden_ref[:, pl.ds(at, depth)].astype(jnp.float32)
        out_ref[block] = (taken * scale * gain_ref[:, pl.ds(at, depth)]).astype(jnp.bfloat16)


def norm(hidden, norm_gain, part, depth, count):
    rows, features = hidden.shape
    step = 64
    return pl.pallas_call(
        norm_kernel,
        grid_spec=pltpu.PrefetchScalarGridSpec(
            num_scalar_prefetch=1,
            grid=(rows // step,),
            in_specs=[
                pl.BlockSpec((step, features), lambda i, part: (i, 0)),
                pl.BlockSpec((1, features), lambda i, part: (0, 0)),
            ],
            out_specs=pl.BlockSpec((count, step, depth), lambda i, part: (0, i, 0)),
        ),
        out_shape=pltpu.HBM((count, rows, depth), jnp.bfloat16),
        compiler_params=pltpu.CompilerParams(vmem_limit_bytes=32 * 2**20),
        cost_estimate=pl.CostEstimate(
            flops=4 * rows * features,
            bytes_accessed=2 * rows * (features + count * depth),
            transcendentals=rows,
        ),
    )(part[None], hidden, norm_gain[None])


TILE = 2 * HD


def turn(value, cosine, sine):
    return value * cosine + pltpu.roll(value, HD // 2, 1) * sine


def heads_kernel(plan, pick_ref, *refs):
    sources, skips, parts, limits, width, closed_width, totals_at, with_keys = plan
    finish = closed_width > 0
    sets, count = len(sources), len(parts)
    refs = list(refs)

    def take(number):
        taken = refs[:number]
        del refs[:number]
        return taken

    row_refs = [take(number) for number in sources]
    weight_refs = [take(len(part)) for part in parts]
    total_refs = take(sets) if totals_at is not None else None
    if finish:
        (bias_ref,) = take(1)
        table_refs = take(sets)
    outs = take(sets)
    sum_outs = take(sets) if finish and closed_width < width else None
    row_buf, weight_buf, acc, row_sem, weight_sem, total_sem, out_sem = take(7)
    depth = row_buf.shape[2] // count

    def weight_copies(piece):
        column = 0
        for part, (ref, (lead, skip, wide)) in enumerate(zip(weight_refs[piece], parts[piece])):
            ref = ref if lead is None else ref.at[lead]
            yield pltpu.make_async_copy(
                ref.at[:, skip : skip + wide],
                weight_buf.at[piece * depth : (piece + 1) * depth, column : column + wide],
                weight_sem.at[piece, part],
            )
            column += wide

    def row_copy(which, piece, source):
        return pltpu.make_async_copy(
            row_refs[which][source].at[pick_ref[which, 1, piece]],
            row_buf.at[which, :, piece * depth : (piece + 1) * depth],
            row_sem.at[which, piece],
        )

    def total_copy(which):
        return pltpu.make_async_copy(
            total_refs[which].at[:, totals_at[which] : totals_at[which] + width],
            acc.at[which],
            total_sem.at[which],
        )

    stages = [(0, low, min(low + 2, count)) for low in range(0, count, 2)]
    stages += [(which, skips[which], count) for which in range(1, sets)]

    def start(stage):
        which, low, high = stages[stage]
        for piece in range(low, high):
            if which == 0:
                for copy in weight_copies(piece):
                    copy.start()
            if sources[which] == 1:
                row_copy(which, piece, 0).start()
            else:
                for source in range(sources[which]):

                    @pl.when(pick_ref[which, 0, piece] == source)
                    def _():
                        row_copy(which, piece, source).start()
        if low == skips[which] and total_refs is not None:
            total_copy(which).start()

    start(0)
    if len(stages) > 1:
        start(1)
    if finish:
        bias_buf, table_buf, out_buf, side_sem = refs
        side_copies = [pltpu.make_async_copy(bias_ref, bias_buf, side_sem.at[sets])]
        side_copies += [
            pltpu.make_async_copy(table_refs[which], table_buf.at[which], side_sem.at[which])
            for which in range(sets)
        ]

    def out_copies(which):
        pairs = [((out_buf if finish else acc).at[which], outs[which])]
        if sum_outs is not None:
            pairs.append((acc.at[which, :, closed_width:], sum_outs[which]))
        return [
            pltpu.make_async_copy(buf, ref, out_sem.at[which, number])
            for number, (buf, ref) in enumerate(pairs)
        ]

    for stage, (which, low, high) in enumerate(stages):
        for piece in range(low, high):
            if which == 0:
                for copy in weight_copies(piece):
                    copy.wait()
            row_copy(which, piece, 0).wait()
        if low == skips[which] and total_refs is not None:
            total_copy(which).wait()
        if stage + 2 < len(stages):
            start(stage + 2)
        if stage == 0 and finish:
            for copy in side_copies:
                copy.start()
        for at in range(0, width, TILE):
            top = min(high, limits[at // TILE])
            if top <= low:
                continue
            cols = slice(at, at + TILE)
            term = jnp.dot(
                row_buf[which, :, low * depth : top * depth],
                weight_buf[low * depth : top * depth, cols],
                preferred_element_type=jnp.float32,
            )
            if low > skips[which] or total_refs is not None:
                term = acc[which, :, cols] + term
            acc[which, :, cols] = term
        if high < count:
            continue
        if finish:
            if which == 0:
                side_copies[0].wait()
            side_copies[1 + which].wait()
            finish_set(acc.at[which], bias_buf, table_buf[which], out_buf.at[which], with_keys)
        for copy in out_copies(which):
            copy.start()
    for which in range(sets):
        for copy in out_copies(which):
            copy.wait()


def finish_set(acc, bias, table, out, with_keys):
    swapped = pltpu.roll(table, HD // 2, 1)
    left = lax.broadcasted_iota(jnp.int32, table.shape, 1) < HD // 2
    cosine = jnp.where(left, table, swapped)
    sine = jnp.where(left, -swapped, table)
    for col in range(0, out.shape[1], HD):
        cols = slice(col, col + HD)
        value = acc[:, cols] + bias[:, cols]
        if not (with_keys and col == HD):
            value = turn(value, cosine, sine)
        out[:, cols] = value.astype(jnp.bfloat16)


def heads_of(row_sets, picks, pieces, limits, totals=None, finish=None, skips=None):
    sets, count = len(row_sets), len(pieces)
    skips = skips or (0,) * sets
    width = len(limits) * TILE
    sources = tuple(len(rows) for rows in row_sets)
    tokens, depth = row_sets[0][0].shape[1:]
    operands = [array for rows in row_sets for array in rows]
    operands += [array for piece in pieces for array, *_ in piece]
    totals_at = None
    if totals is not None:
        totals, totals_at = totals
        operands += totals
    scratch = [
        pltpu.VMEM((sets, tokens, count * depth), jnp.bfloat16),
        pltpu.VMEM((count * depth, width), jnp.bfloat16),
        pltpu.VMEM((sets, tokens, width), jnp.float32),
        pltpu.SemaphoreType.DMA((sets, count)),
        pltpu.SemaphoreType.DMA((count, max(map(len, pieces)))),
        pltpu.SemaphoreType.DMA((sets,)),
        pltpu.SemaphoreType.DMA((sets, 3)),
    ]
    with_keys, closed_width = False, 0
    out_shape = [jax.ShapeDtypeStruct((tokens, width), jnp.float32)] * sets
    if finish is not None:
        closed_width, bias, tables, with_keys = finish
        out_shape = [jax.ShapeDtypeStruct((tokens, closed_width), jnp.bfloat16)] * sets
        operands += [bias, *tables]
        if closed_width < width:
            out_shape += [jax.ShapeDtypeStruct((tokens, width - closed_width), jnp.float32)] * sets
        scratch += [
            pltpu.VMEM((1, closed_width), jnp.float32),
            pltpu.VMEM((sets, tokens, HD), jnp.float32),
            pltpu.VMEM((sets, tokens, closed_width), jnp.bfloat16),
            pltpu.SemaphoreType.DMA((sets + 1,)),
        ]
    plan = (
        sources,
        skips,
        tuple(tuple(part[1:] for part in piece) for piece in pieces),
        limits,
        width,
        closed_width,
        totals_at,
        with_keys,
    )
    anywhere = pl.BlockSpec(memory_space=pl.ANY)
    return pl.pallas_call(
        functools.partial(heads_kernel, plan),
        grid_spec=pltpu.PrefetchScalarGridSpec(
            num_scalar_prefetch=1,
            grid=(1,),
            in_specs=[anywhere] * len(operands),
            out_specs=[pl.BlockSpec(memory_space=pltpu.HBM)] * len(out_shape),
            scratch_shapes=scratch,
        ),
        out_shape=out_shape,
        compiler_params=pltpu.CompilerParams(vmem_limit_bytes=56 * 2**20),
        cost_estimate=pl.CostEstimate(
            flops=2 * sets * count * tokens * depth * width,
            bytes_accessed=2 * count * depth * (sets * tokens + width) + 8 * sets * tokens * width,
            transcendentals=0,
        ),
    )(jnp.stack(picks), *operands)


def attention(queries, keys, values, first_ref, out_ref):
    rows, cols = out_ref.shape
    heads = cols // HD
    scale = math.log2(math.e) / math.sqrt(HD)
    for top in range(0, rows, QROWS):
        low, end = max(0, top - MAXLEN), top + QROWS
        shape = (QROWS, end - low)
        stacked = jnp.concatenate(
            [queries[top:end, col : col + HD] for col in range(0, cols, HD)], axis=0
        )
        scores = jnp.dot(stacked, keys[:, low:end], preferred_element_type=jnp.float32)
        row = lax.broadcasted_iota(jnp.int32, shape, 0) + top
        col = lax.broadcasted_iota(jnp.int32, shape, 1) + low
        visible = (col <= row) & (col >= first_ref[top:end])
        scores = jnp.where(visible[None], scores.reshape(heads, *shape), -jnp.inf)
        most = jnp.max(scores, axis=-1, keepdims=True)
        exponent = jnp.exp2((scores - most) * scale)
        share = 1.0 / jnp.sum(exponent, axis=-1, keepdims=True)
        weights = (exponent * share).astype(jnp.bfloat16)
        context = jnp.dot(
            weights.reshape(heads * QROWS, end - low),
            values[low:end],
            preferred_element_type=jnp.float32,
        ).astype(jnp.bfloat16)
        for head in range(heads):
            out_ref[top:end, head * HD : (head + 1) * HD] = context[
                head * QROWS : (head + 1) * QROWS
            ]


def attend_kernel(numbers, flag_ref, *refs):
    ends = [sum(numbers[: i + 1]) for i in range(4)]
    near, beside, back, other = (refs[end - number : end] for end, number in zip(ends, numbers))
    first_ref, out_ref, cache_ref, part_buf, out_buf, in_sem, out_sem = refs[ends[-1] :]
    half = out_buf.shape[2]

    def copies(side, sources):
        column = 0
        for part, source in enumerate(sources):
            wide = source.shape[1]
            yield pltpu.make_async_copy(
                source, part_buf.at[side, :, column : column + wide], in_sem.at[side, part]
            )
            column += wide

    def on_parts(act):
        for middle, sides in ((1, (near, beside)), (0, (back, other))):

            @pl.when(flag_ref[1] == middle)
            def _():
                for side, sources in enumerate(sides):
                    for copy in copies(side, sources):
                        act(copy)

    on_parts(lambda copy: copy.start())
    on_parts(lambda copy: copy.wait())
    sent = []
    for side in range(2):
        at = flag_ref[0] if side == 0 else 1 - flag_ref[0]
        part = part_buf.at[side]
        for number in range(2):
            sent.append(
                pltpu.make_async_copy(
                    part.at[:, number * HD : (number + 1) * HD],
                    cache_ref.at[:, pl.ds(pl.multiple_of((2 * number + at) * HD, HD), HD)],
                    out_sem.at[side, number],
                )
            )
            sent[-1].start()
        keys = part[:, :HD].astype(jnp.float32).T.astype(jnp.bfloat16)
        attention(part.at[:, TILE:], keys, part.at[:, HD:TILE], first_ref, out_buf.at[side])
        sent.append(
            pltpu.make_async_copy(
                out_buf.at[side],
                out_ref.at[:, pl.ds(pl.multiple_of(at * half, half), half)],
                out_sem.at[side, 2],
            )
        )
        sent[-1].start()
    for copy in sent:
        copy.wait()


def attend_all(flags, near, beside, back, other, first, cols):
    operands = [*near, *beside, *back, *other]
    rows = near[0].shape[0]
    in_hbm = pl.BlockSpec(memory_space=pltpu.HBM)
    return pl.pallas_call(
        functools.partial(attend_kernel, tuple(map(len, (near, beside, back, other)))),
        grid_spec=pltpu.PrefetchScalarGridSpec(
            num_scalar_prefetch=1,
            grid=(1,),
            in_specs=[in_hbm] * len(operands) + [pl.BlockSpec((rows, 1), lambda i, flags: (0, 0))],
            out_specs=[in_hbm] * 2,
            scratch_shapes=[
                pltpu.VMEM((2, rows, TILE + cols // 2), jnp.bfloat16),
                pltpu.VMEM((2, rows, cols // 2), jnp.bfloat16),
                pltpu.SemaphoreType.DMA((2, 3)),
                pltpu.SemaphoreType.DMA((2, 3)),
            ],
        ),
        out_shape=[
            jax.ShapeDtypeStruct((rows, cols), jnp.bfloat16),
            jax.ShapeDtypeStruct((rows, 2 * TILE), jnp.bfloat16),
        ],
        compiler_params=pltpu.CompilerParams(vmem_limit_bytes=40 * 2**20),
        cost_estimate=pl.CostEstimate(
            flops=4 * cols * rows * 3 * QROWS,
            bytes_accessed=6 * rows * cols,
            transcendentals=cols // HD * rows * 3 * QROWS,
        ),
    )(flags, *operands, first)


MIDDLE = (2, 3, 4, 5)
ENDS = (0, 1, 6, 7)


def after(value, *others):
    return lax.optimization_barrier((value,) + others)[0]


def pairs_from(sources, code):
    return [(s, s ^ code) for s in sources]


def middle_form(hidden, norm_gain, q_weight, q_bias, kv_weight, kv_bias, prefix_lens, assignment):
    tok_rows, features = hidden.shape
    slice_rows, q_cols = q_weight.shape
    half_cols = q_cols // 2
    group = lax.axis_index("group")
    tensor = lax.axis_index("tensor")
    y = group & 1
    is_middle = (group >= 2) & (group < 6)
    barrier = lax.optimization_barrier

    def over_group(value, sources, code):
        return lax.ppermute(value, "group", pairs_from(sources, code))

    def to_middle(value):
        return over_group(value, ENDS, 2)

    def across_middle(value):
        return over_group(value, MIDDLE, 6)

    def over_x(value):
        return lax.ppermute(value, "tensor", pairs_from(range(4), 2))

    def over_core(value):
        return lax.ppermute(value, "tensor", pairs_from(range(4), 1))

    begin, widths = (0, 2 * TILE, 4 * TILE), (2 * TILE, 2 * TILE, TILE)

    def columns(half, cuts):
        head = (2 * tensor + half) * HD
        kv_part = lax.dynamic_slice_in_dim(kv_weight, head, HD, 2).reshape(slice_rows, TILE)
        taken, low = [], half * half_cols
        for number, wide in enumerate(cuts):
            wide = wide - (TILE if number == 0 else 0)
            part = lax.dynamic_slice_in_dim(q_weight, low, wide, 1)
            low = low + wide
            taken.append(jnp.concatenate([kv_part, part], axis=1) if number == 0 else part)
        return taken

    def both(one, two, chunk):
        low, high = begin[chunk], begin[chunk] + widths[chunk]
        return jnp.stack([one[:, low:high], two[:, low:high]])

    def pick(code_of_rows, codes):
        block = jnp.stack([group ^ code for code in codes])
        if code_of_rows == 0:
            return jnp.stack([block * 0, block])
        return jnp.stack([(block >> 1) ^ tensor, block & 1])

    def rows_and_picks(sets, codes):
        return [rows_of[c] for c in sets], [pick(c, codes) for c in sets]

    def closed(arriving, others):
        arrived = []
        for value in arriving:
            value, others = barrier((value, others))
            arrived.append(value)
        return barrier((tuple(arrived), others))

    (own,) = columns(y, (sum(widths),))
    other, other2 = columns(1 - y, (begin[2], widths[2]))
    m_own = across_middle(own)
    swap = over_group(other, range(8), 1)
    swap2 = over_group(other2, range(8), 1)
    quarter = norm(hidden, norm_gain, tensor, slice_rows, 2)
    end2 = to_middle(quarter)
    normed = norm(after(hidden, quarter), norm_gain, tensor * 0, slice_rows, features // slice_rows)

    bias = lax.dynamic_slice_in_dim(q_bias, y * half_cols, half_cols, 0)
    kv_bias_here = lax.dynamic_slice_in_dim(kv_bias, (2 * tensor + y) * HD, HD, 1)
    bias = jnp.concatenate([kv_bias_here[0], kv_bias_here[1], bias])[None, :]
    inverse_freq = THETA ** (-2.0 * jnp.arange(HD // 2, dtype=jnp.float32) / HD)
    m_swap = across_middle(after(swap, m_own))
    own, swap, m_own, normed, quarter, end2 = barrier((own, swap, m_own, normed, quarter, end2))

    rows_of = {0: [normed]}
    stack0, end2 = barrier((both(own, swap, 0), end2))
    e0 = to_middle(stack0)
    next1, next2 = both(own, swap, 1), jnp.stack([own[:, begin[2] :], swap2])
    end3 = over_group(end2, MIDDLE, 1)
    across2 = over_x(end2)
    twin2 = over_core(end2)
    tables = []
    for code in range(4):
        _, offset, places = token_layout(prefix_lens, assignment, group ^ code, tok_rows)
        angles = offset.astype(jnp.float32)[:, None] * inverse_freq[None, :]
        table = jnp.concatenate([jnp.cos(angles), jnp.sin(angles)], axis=1)
        tables.append((table, (places - offset)[:, None]))
    m_e0 = across_middle(after(e0, m_swap))
    (e0, m_swap, end3, across2, twin2), (next1, next2, end2, tables, quarter) = closed(
        (e0, m_swap, end3, across2, twin2), (next1, next2, end2, tables, quarter)
    )

    places = {}

    def arrived(chunk, **codes):
        for code, (array, lead, skip) in codes.items():
            places[int(code[1:]), chunk] = (array, lead, skip)

    for chunk, low in enumerate(begin):
        arrived(chunk, c0=(own, None, low), c6=(m_own, None, low))
        if chunk < 2:
            arrived(chunk, c1=(swap, None, low), c7=(m_swap, None, low))
    arrived(2, c1=(swap2, None, 0))
    arrived(0, c2=(e0, 0, 0), c3=(e0, 1, 0))

    def call(sets, codes, chunks, totals=None, finish=None, skips=None):
        rows, picks = rows_and_picks(sets, codes)
        pieces, limits = [], []
        for code in codes:
            there = [chunk for chunk in chunks if (code, chunk) in places]
            pieces.append([places[code, chunk] + (widths[chunk],) for chunk in there])
        for chunk in chunks:
            there = [(code, chunk) in places for code in codes]
            limits += [sum(there)] * (widths[chunk] // TILE)
            assert all(there[: sum(there)])
        return heads_of(rows, picks, pieces, tuple(limits), totals, finish, skips)

    outs, every = {}, (0, 1, 2)

    def first_sums(sets):
        return call(sets, (0, 1, 6, 7, 2, 3), every)

    def finished(sets, chunks, codes, totals=None, opened=(), skips=None):
        low, wide = begin[chunks[0]], sum(widths[chunk] for chunk in chunks)
        finish = (wide, bias[:, low : low + wide], [tables[c][0] for c in sets], chunks[0] == 0)
        made = call(sets, codes, chunks + opened, totals, finish, skips)
        for code, out in zip(sets, made):
            outs[code, chunks[0]] = out
        return made[-1]

    e1 = to_middle(next1)
    end1 = over_group(quarter, MIDDLE, 1)
    across3 = over_x(end3)
    far2 = over_core(across2)
    rows_of[2] = [end2, twin2, across2, far2]
    sums = dict(zip((0, 2), first_sums((0, 2))))
    m_e1 = across_middle(after(e1, m_e0))
    (m_e0, e1, end1, across3), (next2, e0, end3, far2, sums) = closed(
        (m_e0, e1, end1, across3), (next2, e0, end3, far2, sums)
    )
    rows_of[2] = [end2, twin2, across2, far2]

    e2 = to_middle(next2)
    across1 = over_x(end1)
    twin3 = over_core(end3)
    far3 = over_core(across3)
    rows_of[3] = [end3, twin3, across3, far3]

    def send_back(code, chunk):
        return over_group(outs[code, chunk], MIDDLE, code)

    arrived(1, c2=(e1, 0, 0), c3=(e1, 1, 0))
    (sums[3],) = first_sums((3,))
    arrived(0, c4=(m_e0, 0, 0), c5=(m_e0, 1, 0))
    three = (2, 3, 0)
    finished(three, (0,), (4, 5), ([sums[c] for c in three], (0, 0, 0)))
    back = {(2, 0): send_back(2, 0)}
    m_last = across_middle(after(jnp.concatenate([swap2[None], e2]), m_e1))
    (m_e1, across1, e2, back[2, 0]), (end1, made, sums) = closed(
        (m_e1, across1, e2, back[2, 0]), (end1, [outs[c, 0] for c in three], sums)
    )
    for code, out in zip(three, made):
        outs[code, 0] = out

    twin1 = over_core(end1)
    far1 = over_core(across1)
    arrived(1, c4=(m_e1, 0, 0), c5=(m_e1, 1, 0))
    arrived(2, c2=(e2, 0, 0), c3=(e2, 1, 0))
    back[3, 0] = send_back(3, 0)
    three = (2, 0, 3)
    finished(
        three,
        (1,),
        (2, 3, 4, 5),
        ([sums[c] for c in three], (begin[1],) * 3),
        skips=(0, 0, 2),
    )
    for code in (2, 3):
        back[code, 1] = send_back(code, 1)
    far1, outs[2, 1] = barrier((far1, outs[2, 1]))
    rows_of[1] = [end1, twin1, across1, far1]
    sums[1] = finished((1,), (0, 1), (0, 1, 6, 2, 3, 7, 4, 5), opened=(2,))
    back[1, 0] = send_back(1, 0)
    (m_last, back[3, 0], back[2, 1]), (sums, outs[1, 0]) = closed(
        (m_last, back[3, 0], back[2, 1]), (sums, outs[1, 0])
    )

    arrived(2, c7=(m_last, 0, 0), c4=(m_last, 1, 0), c5=(m_last, 2, 0))
    three = (2, 3, 1)
    finished(
        three,
        (2,),
        (2, 3, 7, 4, 5),
        ([sums[c] for c in three], (begin[2], begin[2], 0)),
        skips=(0, 0, 2),
    )
    for code in (2, 3):
        back[code, 2] = send_back(code, 2)
    back[1, 2] = send_back(1, 2)
    sums[0], outs[1, 2], back[3, 1] = barrier((sums[0], outs[1, 2], back[3, 1]))
    finished((0,), (2,), (2, 3, 7, 4, 5), ([sums[0]], (begin[2],)))

    context, cache = attend_all(
        jnp.stack([y, is_middle.astype(jnp.int32)]),
        [outs[0, part] for part in every],
        [back[1, part] for part in (0, 2)],
        [back[2, part] for part in every],
        [back[3, part] for part in every],
        tables[0][1],
        q_cols,
    )
    return (context, cache.reshape(tok_rows, 2, TILE))


def solution(mesh):
    placed = (
        P("group", None),
        P(),
        P("group", "tensor"),
        P("tensor"),
        P("group", None, None),
        P(),
        P(),
        P(),
    )
    fits = mesh.shape["group"] == 8 and mesh.shape["tensor"] == 4
    return jax.shard_map(
        middle_form if fits else gathered_form,
        mesh=mesh,
        in_specs=placed,
        out_specs=(P("group", "tensor"), P("group", None, "tensor")),
        check_vma=False,
    )
```

```python
import functools
import math

import jax
import jax.numpy as jnp
from jax import lax
from jax.experimental import pallas as pl
from jax.experimental.pallas import tpu as pltpu
from jax.sharding import PartitionSpec as P

HD = 128


EPS = 1e-06
THETA = 1000000.0
QROWS = 128
MAXLEN = 256


def token_layout(prefix_lens, assignment, group_id, tok_rows):
    rollouts = prefix_lens.shape[0]
    member = assignment == group_id
    own_lens = jnp.where(member, prefix_lens, 0)
    starts = jnp.cumsum(own_lens) - own_lens
    places = jnp.arange(tok_rows, dtype=jnp.int32)
    inside = (
        member[None, :]
        & (places[:, None] >= starts[None, :])
        & (places[:, None] < (starts + own_lens)[None, :])
    )
    owner_id = jnp.sum(jnp.where(inside, jnp.arange(rollouts, dtype=jnp.int32)[None, :], 0), axis=1)
    offset = places - jnp.sum(jnp.where(inside, starts[None, :], 0), axis=1)
    return (owner_id, offset, places)


def rotate(values, offset):
    half_dim = values.shape[-1] // 2
    inverse_freq = THETA ** (-2.0 * jnp.arange(half_dim, dtype=jnp.float32) / values.shape[-1])
    angles = offset.astype(jnp.float32)[:, None] * inverse_freq[None, :]
    cosine = jnp.cos(angles)[:, None, :]
    sine_part = jnp.sin(angles)[:, None, :]
    first_half = values[..., :half_dim]
    second_half = values[..., half_dim:]
    return jnp.concatenate(
        [
            first_half * cosine - second_half * sine_part,
            second_half * cosine + first_half * sine_part,
        ],
        axis=-1,
    )


def add_product(normed, portion):
    return jnp.dot(normed, portion, preferred_element_type=jnp.float32)


def normalise(hidden, norm_gain):
    widened = hidden.astype(jnp.float32)
    return (
        widened * lax.rsqrt(jnp.mean(widened * widened, axis=-1, keepdims=True) + EPS) * norm_gain
    ).astype(jnp.bfloat16)


def gathered_form(
    hidden, norm_gain, q_weight, q_bias, kv_weight, kv_bias, prefix_lens, assignment
):
    tok_rows, features = hidden.shape
    slice_rows = kv_weight.shape[0]
    q_cols = q_weight.shape[1]
    kv_total = kv_weight.shape[2]
    heads_here = q_cols // HD
    tensor_pos = lax.axis_index("tensor")
    kv_cols = kv_total // lax.axis_size("tensor")
    normed = normalise(hidden, norm_gain)
    queries = add_product(normed, lax.all_gather(q_weight, "group", axis=0, tiled=True)) + q_bias
    head_span = max(kv_cols, HD)
    head_base = tensor_pos * kv_cols // head_span * head_span
    local_start = tensor_pos * kv_cols - head_base
    head_rows = lax.dynamic_slice_in_dim(kv_weight, head_base, head_span, 2).reshape(
        slice_rows, 2 * head_span
    )
    projected = add_product(normed, lax.all_gather(head_rows, "group", axis=0, tiled=True))
    projected = projected.reshape(tok_rows, 2, head_span) + lax.dynamic_slice_in_dim(
        kv_bias, head_base, head_span, 1
    )
    kv_here = head_span // HD
    group_size = heads_here // kv_here
    owner_id, offset, places = token_layout(
        prefix_lens, assignment, lax.axis_index("group"), tok_rows
    )
    rotated_queries = rotate(queries.reshape(tok_rows, heads_here, HD), offset).astype(jnp.bfloat16)
    rotated_keys = rotate(projected[:, 0].reshape(tok_rows, kv_here, HD), offset).astype(
        jnp.bfloat16
    )
    value_heads = projected[:, 1].reshape(tok_rows, kv_here, HD).astype(jnp.bfloat16)
    visible = (owner_id[:, None] == owner_id[None, :]) & (places[None, :] <= places[:, None])
    grouped = rotated_queries.reshape(tok_rows, kv_here, group_size, HD)
    scores = jnp.einsum(
        "qgph,kgh->gpqk", grouped, rotated_keys, preferred_element_type=jnp.float32
    ) / math.sqrt(HD)
    scores = jnp.where(visible[None, None], scores, -jnp.inf)
    row_max = jnp.max(scores, axis=-1, keepdims=True)
    exponent = jnp.exp(scores - row_max)
    weights_bf = (exponent / jnp.sum(exponent, axis=-1, keepdims=True)).astype(jnp.bfloat16)
    context = jnp.einsum(
        "gpqk,kgh->qgph", weights_bf, value_heads, preferred_element_type=jnp.float32
    )
    context = context.astype(jnp.bfloat16).reshape(tok_rows, q_cols)
    stacked = jnp.stack(
        [rotated_keys.reshape(tok_rows, head_span), value_heads.reshape(tok_rows, head_span)],
        axis=1,
    )
    kv_cache = lax.dynamic_slice_in_dim(stacked, local_start, kv_cols, 2)
    return (context, kv_cache)


def norm_kernel(part_ref, hidden_ref, gain_ref, out_ref):
    widened = hidden_ref[...].astype(jnp.float32)
    scale = lax.rsqrt(jnp.mean(widened * widened, axis=-1, keepdims=True) + EPS)
    count, _, depth = out_ref.shape
    for block in range(count):
        at = pl.multiple_of((part_ref[0] * count + block) * depth, depth)
        taken = hidden_ref[:, pl.ds(at, depth)].astype(jnp.float32)
        out_ref[block] = (taken * scale * gain_ref[:, pl.ds(at, depth)]).astype(jnp.bfloat16)


def norm(hidden, norm_gain, part, depth, count):
    rows, features = hidden.shape
    step = 64
    return pl.pallas_call(
        norm_kernel,
        grid_spec=pltpu.PrefetchScalarGridSpec(
            num_scalar_prefetch=1,
            grid=(rows // step,),
            in_specs=[
                pl.BlockSpec((step, features), lambda i, part: (i, 0)),
                pl.BlockSpec((1, features), lambda i, part: (0, 0)),
            ],
            out_specs=pl.BlockSpec((count, step, depth), lambda i, part: (0, i, 0)),
        ),
        out_shape=pltpu.HBM((count, rows, depth), jnp.bfloat16),
        compiler_params=pltpu.CompilerParams(vmem_limit_bytes=60 * 2**20),
        cost_estimate=pl.CostEstimate(
            flops=4 * rows * features,
            bytes_accessed=2 * rows * (features + count * depth),
            transcendentals=rows,
        ),
    )(part[None], hidden, norm_gain[None])


TILE = 2 * HD


def turn(value, cosine, sine):
    return value * cosine + pltpu.roll(value, HD // 2, 1) * sine


def heads_kernel(plan, pick_ref, *refs):
    sources, skips, parts, limits, width, closed_width, totals_at, with_keys = plan
    finish = closed_width > 0
    sets, count = len(sources), len(parts)
    refs = list(refs)

    def take(number):
        taken = refs[:number]
        del refs[:number]
        return taken

    row_refs = [take(number) for number in sources]
    weight_refs = [take(len(part)) for part in parts]
    total_refs = take(sets) if totals_at is not None else None
    if finish:
        (bias_ref,) = take(1)
        table_refs = take(sets)
    outs = take(sets)
    sum_outs = take(sets) if finish and closed_width < width else None
    row_buf, weight_buf, acc, row_sem, weight_sem, total_sem, out_sem = take(7)
    depth = row_buf.shape[2] // count

    def weight_copies(piece):
        column = 0
        for part, (ref, (lead, skip, wide)) in enumerate(zip(weight_refs[piece], parts[piece])):
            ref = ref if lead is None else ref.at[lead]
            yield pltpu.make_async_copy(
                ref.at[:, skip : skip + wide],
                weight_buf.at[piece * depth : (piece + 1) * depth, column : column + wide],
                weight_sem.at[piece, part],
            )
            column += wide

    def row_copy(which, piece, source):
        return pltpu.make_async_copy(
            row_refs[which][source].at[pick_ref[which, 1, piece]],
            row_buf.at[which, :, piece * depth : (piece + 1) * depth],
            row_sem.at[which, piece],
        )

    def total_copy(which):
        return pltpu.make_async_copy(
            total_refs[which].at[:, totals_at[which] : totals_at[which] + width],
            acc.at[which],
            total_sem.at[which],
        )

    stages = [(0, low, min(low + 2, count)) for low in range(0, count, 2)]
    stages += [(which, skips[which], count) for which in range(1, sets)]

    def start(stage):
        which, low, high = stages[stage]
        for piece in range(low, high):
            if which == 0:
                for copy in weight_copies(piece):
                    copy.start()
            if sources[which] == 1:
                row_copy(which, piece, 0).start()
            else:
                for source in range(sources[which]):

                    @pl.when(pick_ref[which, 0, piece] == source)
                    def _():
                        row_copy(which, piece, source).start()
        if low == skips[which] and total_refs is not None:
            total_copy(which).start()

    start(0)
    if len(stages) > 1:
        start(1)
    if finish:
        bias_buf, table_buf, out_buf, side_sem = refs
        side_copies = [pltpu.make_async_copy(bias_ref, bias_buf, side_sem.at[sets])]
        side_copies += [
            pltpu.make_async_copy(table_refs[which], table_buf.at[which], side_sem.at[which])
            for which in range(sets)
        ]

    def out_copies(which):
        pairs = [((out_buf if finish else acc).at[which], outs[which])]
        if sum_outs is not None:
            pairs.append((acc.at[which, :, closed_width:], sum_outs[which]))
        return [
            pltpu.make_async_copy(buf, ref, out_sem.at[which, number])
            for number, (buf, ref) in enumerate(pairs)
        ]

    for stage, (which, low, high) in enumerate(stages):
        for piece in range(low, high):
            if which == 0:
                for copy in weight_copies(piece):
                    copy.wait()
            row_copy(which, piece, 0).wait()
        if low == skips[which] and total_refs is not None:
            total_copy(which).wait()
        if stage + 2 < len(stages):
            start(stage + 2)
        if stage == 0 and finish:
            for copy in side_copies:
                copy.start()
        for at in range(0, width, TILE):
            top = min(high, limits[at // TILE])
            if top <= low:
                continue
            cols = slice(at, at + TILE)
            term = jnp.dot(
                row_buf[which, :, low * depth : top * depth],
                weight_buf[low * depth : top * depth, cols],
                preferred_element_type=jnp.float32,
            )
            if low > skips[which] or total_refs is not None:
                term = acc[which, :, cols] + term
            acc[which, :, cols] = term
        if high < count:
            continue
        if finish:
            if which == 0:
                side_copies[0].wait()
            side_copies[1 + which].wait()
            finish_set(acc.at[which], bias_buf, table_buf[which], out_buf.at[which], with_keys)
        for copy in out_copies(which):
            copy.start()
    for which in range(sets):
        for copy in out_copies(which):
            copy.wait()


def finish_set(acc, bias, table, out, with_keys):
    swapped = pltpu.roll(table, HD // 2, 1)
    left = lax.broadcasted_iota(jnp.int32, table.shape, 1) < HD // 2
    cosine = jnp.where(left, table, swapped)
    sine = jnp.where(left, -swapped, table)
    for col in range(0, out.shape[1], HD):
        cols = slice(col, col + HD)
        value = acc[:, cols] + bias[:, cols]
        if not (with_keys and col == HD):
            value = turn(value, cosine, sine)
        out[:, cols] = value.astype(jnp.bfloat16)


def heads_of(row_sets, picks, pieces, limits, totals=None, finish=None, skips=None):
    sets, count = len(row_sets), len(pieces)
    skips = skips or (0,) * sets
    width = len(limits) * TILE
    sources = tuple(len(rows) for rows in row_sets)
    tokens, depth = row_sets[0][0].shape[1:]
    operands = [array for rows in row_sets for array in rows]
    operands += [array for piece in pieces for array, *_ in piece]
    totals_at = None
    if totals is not None:
        totals, totals_at = totals
        operands += totals
    scratch = [
        pltpu.VMEM((sets, tokens, count * depth), jnp.bfloat16),
        pltpu.VMEM((count * depth, width), jnp.bfloat16),
        pltpu.VMEM((sets, tokens, width), jnp.float32),
        pltpu.SemaphoreType.DMA((sets, count)),
        pltpu.SemaphoreType.DMA((count, max(map(len, pieces)))),
        pltpu.SemaphoreType.DMA((sets,)),
        pltpu.SemaphoreType.DMA((sets, 3)),
    ]
    with_keys, closed_width = False, 0
    out_shape = [jax.ShapeDtypeStruct((tokens, width), jnp.float32)] * sets
    if finish is not None:
        closed_width, bias, tables, with_keys = finish
        out_shape = [jax.ShapeDtypeStruct((tokens, closed_width), jnp.bfloat16)] * sets
        operands += [bias, *tables]
        if closed_width < width:
            out_shape += [jax.ShapeDtypeStruct((tokens, width - closed_width), jnp.float32)] * sets
        scratch += [
            pltpu.VMEM((1, closed_width), jnp.float32),
            pltpu.VMEM((sets, tokens, HD), jnp.float32),
            pltpu.VMEM((sets, tokens, closed_width), jnp.bfloat16),
            pltpu.SemaphoreType.DMA((sets + 1,)),
        ]
    plan = (
        sources,
        skips,
        tuple(tuple(part[1:] for part in piece) for piece in pieces),
        limits,
        width,
        closed_width,
        totals_at,
        with_keys,
    )
    anywhere = pl.BlockSpec(memory_space=pl.ANY)
    return pl.pallas_call(
        functools.partial(heads_kernel, plan),
        grid_spec=pltpu.PrefetchScalarGridSpec(
            num_scalar_prefetch=1,
            grid=(1,),
            in_specs=[anywhere] * len(operands),
            out_specs=[pl.BlockSpec(memory_space=pltpu.HBM)] * len(out_shape),
            scratch_shapes=scratch,
        ),
        out_shape=out_shape,
        compiler_params=pltpu.CompilerParams(vmem_limit_bytes=56 * 2**20),
        cost_estimate=pl.CostEstimate(
            flops=2 * sets * count * tokens * depth * width,
            bytes_accessed=2 * count * depth * (sets * tokens + width) + 8 * sets * tokens * width,
            transcendentals=0,
        ),
    )(jnp.stack(picks), *operands)


def attention(queries, keys, values, first_ref, out_ref):
    rows, cols = out_ref.shape
    heads = cols // HD
    scale = math.log2(math.e) / math.sqrt(HD)
    for top in range(0, rows, QROWS):
        low, end = max(0, top - MAXLEN), top + QROWS
        shape = (QROWS, end - low)
        stacked = jnp.concatenate(
            [queries[top:end, col : col + HD] for col in range(0, cols, HD)], axis=0
        )
        scores = jnp.dot(stacked, keys[:, low:end], preferred_element_type=jnp.float32)
        row = lax.broadcasted_iota(jnp.int32, shape, 0) + top
        col = lax.broadcasted_iota(jnp.int32, shape, 1) + low
        visible = (col <= row) & (col >= first_ref[top:end])
        scores = jnp.where(visible[None], scores.reshape(heads, *shape), -jnp.inf)
        most = jnp.max(scores, axis=-1, keepdims=True)
        exponent = jnp.exp2((scores - most) * scale)
        share = 1.0 / jnp.sum(exponent, axis=-1, keepdims=True)
        weights = (exponent * share).astype(jnp.bfloat16)
        context = jnp.dot(
            weights.reshape(heads * QROWS, end - low),
            values[low:end],
            preferred_element_type=jnp.float32,
        ).astype(jnp.bfloat16)
        for head in range(heads):
            out_ref[top:end, head * HD : (head + 1) * HD] = context[
                head * QROWS : (head + 1) * QROWS
            ]


def attend_kernel(numbers, flag_ref, *refs):
    ends = [sum(numbers[: i + 1]) for i in range(4)]
    near, beside, back, other = (refs[end - number : end] for end, number in zip(ends, numbers))
    first_ref, out_ref, cache_ref, part_buf, out_buf, in_sem, out_sem = refs[ends[-1] :]
    half = out_buf.shape[2]

    def copies(side, sources):
        column = 0
        for part, source in enumerate(sources):
            wide = source.shape[1]
            yield pltpu.make_async_copy(
                source, part_buf.at[side, :, column : column + wide], in_sem.at[side, part]
            )
            column += wide

    def on_parts(act):
        for middle, sides in ((1, (near, beside)), (0, (back, other))):

            @pl.when(flag_ref[1] == middle)
            def _():
                for side, sources in enumerate(sides):
                    for copy in copies(side, sources):
                        act(copy)

    on_parts(lambda copy: copy.start())
    on_parts(lambda copy: copy.wait())
    sent = []
    for side in range(2):
        at = flag_ref[0] if side == 0 else 1 - flag_ref[0]
        part = part_buf.at[side]
        for number in range(2):
            sent.append(
                pltpu.make_async_copy(
                    part.at[:, number * HD : (number + 1) * HD],
                    cache_ref.at[:, pl.ds(pl.multiple_of((2 * number + at) * HD, HD), HD)],
                    out_sem.at[side, number],
                )
            )
            sent[-1].start()
        keys = part[:, :HD].astype(jnp.float32).T.astype(jnp.bfloat16)
        attention(part.at[:, TILE:], keys, part.at[:, HD:TILE], first_ref, out_buf.at[side])
        sent.append(
            pltpu.make_async_copy(
                out_buf.at[side],
                out_ref.at[:, pl.ds(pl.multiple_of(at * half, half), half)],
                out_sem.at[side, 2],
            )
        )
        sent[-1].start()
    for copy in sent:
        copy.wait()


def attend_all(flags, near, beside, back, other, first, cols):
    operands = [*near, *beside, *back, *other]
    rows = near[0].shape[0]
    in_hbm = pl.BlockSpec(memory_space=pltpu.HBM)
    return pl.pallas_call(
        functools.partial(attend_kernel, tuple(map(len, (near, beside, back, other)))),
        grid_spec=pltpu.PrefetchScalarGridSpec(
            num_scalar_prefetch=1,
            grid=(1,),
            in_specs=[in_hbm] * len(operands) + [pl.BlockSpec((rows, 1), lambda i, flags: (0, 0))],
            out_specs=[in_hbm] * 2,
            scratch_shapes=[
                pltpu.VMEM((2, rows, TILE + cols // 2), jnp.bfloat16),
                pltpu.VMEM((2, rows, cols // 2), jnp.bfloat16),
                pltpu.SemaphoreType.DMA((2, 3)),
                pltpu.SemaphoreType.DMA((2, 3)),
            ],
        ),
        out_shape=[
            jax.ShapeDtypeStruct((rows, cols), jnp.bfloat16),
            jax.ShapeDtypeStruct((rows, 2 * TILE), jnp.bfloat16),
        ],
        compiler_params=pltpu.CompilerParams(vmem_limit_bytes=40 * 2**20),
        cost_estimate=pl.CostEstimate(
            flops=4 * cols * rows * 3 * QROWS,
            bytes_accessed=6 * rows * cols,
            transcendentals=cols // HD * rows * 3 * QROWS,
        ),
    )(flags, *operands, first)


MIDDLE = (2, 3, 4, 5)
ENDS = (0, 1, 6, 7)


def after(value, *others):
    return lax.optimization_barrier((value,) + others)[0]


def pairs_from(sources, code):
    return [(s, s ^ code) for s in sources]


def middle_form(hidden, norm_gain, q_weight, q_bias, kv_weight, kv_bias, prefix_lens, assignment):
    tok_rows, features = hidden.shape
    slice_rows, q_cols = q_weight.shape
    half_cols = q_cols // 2
    group = lax.axis_index("group")
    tensor = lax.axis_index("tensor")
    y = group & 1
    is_middle = (group >= 2) & (group < 6)
    barrier = lax.optimization_barrier

    def over_group(value, sources, code):
        return lax.ppermute(value, "group", pairs_from(sources, code))

    def to_middle(value):
        return over_group(value, ENDS, 2)

    def across_middle(value):
        return over_group(value, MIDDLE, 6)

    def over_x(value):
        return lax.ppermute(value, "tensor", pairs_from(range(4), 2))

    def over_core(value):
        return lax.ppermute(value, "tensor", pairs_from(range(4), 1))

    begin, widths = (0, 2 * TILE, 4 * TILE), (2 * TILE, 2 * TILE, TILE)

    def columns(half, cuts):
        head = (2 * tensor + half) * HD
        kv_part = lax.dynamic_slice_in_dim(kv_weight, head, HD, 2).reshape(slice_rows, TILE)
        taken, low = [], half * half_cols
        for number, wide in enumerate(cuts):
            wide = wide - (TILE if number == 0 else 0)
            part = lax.dynamic_slice_in_dim(q_weight, low, wide, 1)
            low = low + wide
            taken.append(jnp.concatenate([kv_part, part], axis=1) if number == 0 else part)
        return taken

    def both(one, two, chunk):
        low, high = begin[chunk], begin[chunk] + widths[chunk]
        return jnp.stack([one[:, low:high], two[:, low:high]])

    def pick(code_of_rows, codes):
        block = jnp.stack([group ^ code for code in codes])
        if code_of_rows == 0:
            return jnp.stack([block * 0, block])
        return jnp.stack([(block >> 1) ^ tensor, block & 1])

    def rows_and_picks(sets, codes):
        return [rows_of[c] for c in sets], [pick(c, codes) for c in sets]

    def closed(arriving, others):
        arrived = []
        for value in arriving:
            value, others = barrier((value, others))
            arrived.append(value)
        return barrier((tuple(arrived), others))

    (own,) = columns(y, (sum(widths),))
    other, other2 = columns(1 - y, (begin[2], widths[2]))
    m_own = across_middle(own)
    swap = over_group(other, range(8), 1)
    swap2 = over_group(other2, range(8), 1)
    quarter = norm(hidden, norm_gain, tensor, slice_rows, 2)
    end2 = to_middle(quarter)
    normed = norm(after(hidden, quarter), norm_gain, tensor * 0, slice_rows, features // slice_rows)

    bias = lax.dynamic_slice_in_dim(q_bias, y * half_cols, half_cols, 0)
    kv_bias_here = lax.dynamic_slice_in_dim(kv_bias, (2 * tensor + y) * HD, HD, 1)
    bias = jnp.concatenate([kv_bias_here[0], kv_bias_here[1], bias])[None, :]
    inverse_freq = THETA ** (-2.0 * jnp.arange(HD // 2, dtype=jnp.float32) / HD)
    m_swap = across_middle(after(swap, m_own))
    own, swap, m_own, normed, quarter, end2 = barrier((own, swap, m_own, normed, quarter, end2))

    rows_of = {0: [normed]}
    stack0, end2 = barrier((both(own, swap, 0), end2))
    e0 = to_middle(stack0)
    next1, next2 = both(own, swap, 1), jnp.stack([own[:, begin[2] :], swap2])
    end3 = over_group(end2, MIDDLE, 1)
    across2 = over_x(end2)
    twin2 = over_core(end2)
    tables = []
    for code in range(4):
        _, offset, places = token_layout(prefix_lens, assignment, group ^ code, tok_rows)
        angles = offset.astype(jnp.float32)[:, None] * inverse_freq[None, :]
        table = jnp.concatenate([jnp.cos(angles), jnp.sin(angles)], axis=1)
        tables.append((table, (places - offset)[:, None]))
    m_e0 = across_middle(after(e0, m_swap))
    (e0, m_swap, end3, across2, twin2), (next1, next2, end2, tables, quarter) = closed(
        (e0, m_swap, end3, across2, twin2), (next1, next2, end2, tables, quarter)
    )

    places = {}

    def arrived(chunk, **codes):
        for code, (array, lead, skip) in codes.items():
            places[int(code[1:]), chunk] = (array, lead, skip)

    for chunk, low in enumerate(begin):
        arrived(chunk, c0=(own, None, low), c6=(m_own, None, low))
        if chunk < 2:
            arrived(chunk, c1=(swap, None, low), c7=(m_swap, None, low))
    arrived(2, c1=(swap2, None, 0))
    arrived(0, c2=(e0, 0, 0), c3=(e0, 1, 0))

    def call(sets, codes, chunks, totals=None, finish=None, skips=None):
        rows, picks = rows_and_picks(sets, codes)
        pieces, limits = [], []
        for code in codes:
            there = [chunk for chunk in chunks if (code, chunk) in places]
            pieces.append([places[code, chunk] + (widths[chunk],) for chunk in there])
        for chunk in chunks:
            there = [(code, chunk) in places for code in codes]
            limits += [sum(there)] * (widths[chunk] // TILE)
            assert all(there[: sum(there)])
        return heads_of(rows, picks, pieces, tuple(limits), totals, finish, skips)

    outs, every = {}, (0, 1, 2)

    def first_sums(sets):
        return call(sets, (0, 1, 6, 7, 2, 3), every)

    def finished(sets, chunks, codes, totals=None, opened=(), skips=None):
        low, wide = begin[chunks[0]], sum(widths[chunk] for chunk in chunks)
        finish = (wide, bias[:, low : low + wide], [tables[c][0] for c in sets], chunks[0] == 0)
        made = call(sets, codes, chunks + opened, totals, finish, skips)
        for code, out in zip(sets, made):
            outs[code, chunks[0]] = out
        return made[-1]

    e1 = to_middle(next1)
    end1 = over_group(quarter, MIDDLE, 1)
    across3 = over_x(end3)
    far2 = over_core(across2)
    rows_of[2] = [end2, twin2, across2, far2]
    sums = dict(zip((0, 2), first_sums((0, 2))))
    m_e1 = across_middle(after(e1, m_e0))
    (m_e0, e1, end1, across3), (next2, e0, end3, far2, sums) = closed(
        (m_e0, e1, end1, across3), (next2, e0, end3, far2, sums)
    )
    rows_of[2] = [end2, twin2, across2, far2]

    e2 = to_middle(next2)
    across1 = over_x(end1)
    twin3 = over_core(end3)
    far3 = over_core(across3)
    rows_of[3] = [end3, twin3, across3, far3]

    def send_back(code, chunk):
        return over_group(outs[code, chunk], MIDDLE, code)

    arrived(1, c2=(e1, 0, 0), c3=(e1, 1, 0))
    (sums[3],) = first_sums((3,))
    arrived(0, c4=(m_e0, 0, 0), c5=(m_e0, 1, 0))
    three = (2, 3, 0)
    finished(three, (0,), (4, 5), ([sums[c] for c in three], (0, 0, 0)))
    back = {(2, 0): send_back(2, 0)}
    last = jnp.concatenate([swap2[None], e2])
    m_last = across_middle(after(last, m_e1))
    (last, m_e1, across1, back[2, 0]), (end1, made, sums) = closed(
        (last, m_e1, across1, back[2, 0]), (end1, [outs[c, 0] for c in three], sums)
    )
    for code, out in zip(three, made):
        outs[code, 0] = out

    twin1 = over_core(end1)
    far1 = over_core(across1)
    arrived(1, c4=(m_e1, 0, 0), c5=(m_e1, 1, 0))
    arrived(2, c2=(last, 1, 0), c3=(last, 2, 0))
    back[3, 0] = send_back(3, 0)
    three = (2, 0, 3)
    finished(
        three,
        (1,),
        (2, 3, 4, 5),
        ([sums[c] for c in three], (begin[1],) * 3),
        skips=(0, 0, 2),
    )
    for code in (2, 3):
        back[code, 1] = send_back(code, 1)
    far1, outs[2, 1] = barrier((far1, outs[2, 1]))
    rows_of[1] = [end1, twin1, across1, far1]
    sums[1] = finished((1,), (0, 1), (0, 1, 6, 2, 3, 7, 4, 5), opened=(2,))
    back[1, 0] = send_back(1, 0)
    (m_last, back[3, 0], back[2, 1]), (sums, outs[1, 0]) = closed(
        (m_last, back[3, 0], back[2, 1]), (sums, outs[1, 0])
    )

    arrived(2, c7=(m_last, 0, 0), c4=(m_last, 1, 0), c5=(m_last, 2, 0))
    three = (2, 3, 1)
    finished(
        three,
        (2,),
        (2, 3, 7, 4, 5),
        ([sums[c] for c in three], (begin[2], begin[2], 0)),
        skips=(0, 0, 2),
    )
    for code in (2, 3):
        back[code, 2] = send_back(code, 2)
    back[1, 2] = send_back(1, 2)
    sums[0], outs[1, 2], back[3, 1] = barrier((sums[0], outs[1, 2], back[3, 1]))
    finished((0,), (2,), (2, 3, 7, 4, 5), ([sums[0]], (begin[2],)))

    (back[2, 2], back[3, 2], back[1, 2]), _ = closed((back[2, 2], back[3, 2], back[1, 2]), ())
    context, cache = attend_all(
        jnp.stack([y, is_middle.astype(jnp.int32)]),
        [outs[0, part] for part in every],
        [back[1, part] for part in (0, 2)],
        [back[2, part] for part in every],
        [back[3, part] for part in every],
        tables[0][1],
        q_cols,
    )
    return (context, cache.reshape(tok_rows, 2, TILE))


def solution(mesh):
    placed = (
        P("group", None),
        P(),
        P("group", "tensor"),
        P("tensor"),
        P("group", None, None),
        P(),
        P(),
        P(),
    )
    fits = mesh.shape["group"] == 8 and mesh.shape["tensor"] == 4
    return jax.shard_map(
        middle_form if fits else gathered_form,
        mesh=mesh,
        in_specs=placed,
        out_specs=(P("group", "tensor"), P("group", None, "tensor")),
        check_vma=False,
    )
```

```python
import functools
import math

import jax
import jax.numpy as jnp
from jax import lax
from jax.experimental import pallas as pl
from jax.experimental.pallas import tpu as pltpu
from jax.sharding import PartitionSpec as P

HD = 128


EPS = 1e-06
THETA = 1000000.0
QROWS = 128
MAXLEN = 256


def token_layout(prefix_lens, assignment, group_id, tok_rows):
    rollouts = prefix_lens.shape[0]
    member = assignment == group_id
    own_lens = jnp.where(member, prefix_lens, 0)
    starts = jnp.cumsum(own_lens) - own_lens
    places = jnp.arange(tok_rows, dtype=jnp.int32)
    inside = (
        member[None, :]
        & (places[:, None] >= starts[None, :])
        & (places[:, None] < (starts + own_lens)[None, :])
    )
    owner_id = jnp.sum(jnp.where(inside, jnp.arange(rollouts, dtype=jnp.int32)[None, :], 0), axis=1)
    offset = places - jnp.sum(jnp.where(inside, starts[None, :], 0), axis=1)
    return (owner_id, offset, places)


def rotate(values, offset):
    half_dim = values.shape[-1] // 2
    inverse_freq = THETA ** (-2.0 * jnp.arange(half_dim, dtype=jnp.float32) / values.shape[-1])
    angles = offset.astype(jnp.float32)[:, None] * inverse_freq[None, :]
    cosine = jnp.cos(angles)[:, None, :]
    sine_part = jnp.sin(angles)[:, None, :]
    first_half = values[..., :half_dim]
    second_half = values[..., half_dim:]
    return jnp.concatenate(
        [
            first_half * cosine - second_half * sine_part,
            second_half * cosine + first_half * sine_part,
        ],
        axis=-1,
    )


def add_product(normed, portion):
    return jnp.dot(normed, portion, preferred_element_type=jnp.float32)


def normalise(hidden, norm_gain):
    widened = hidden.astype(jnp.float32)
    return (
        widened * lax.rsqrt(jnp.mean(widened * widened, axis=-1, keepdims=True) + EPS) * norm_gain
    ).astype(jnp.bfloat16)


def gathered_form(
    hidden, norm_gain, q_weight, q_bias, kv_weight, kv_bias, prefix_lens, assignment
):
    tok_rows, features = hidden.shape
    slice_rows = kv_weight.shape[0]
    q_cols = q_weight.shape[1]
    kv_total = kv_weight.shape[2]
    heads_here = q_cols // HD
    tensor_pos = lax.axis_index("tensor")
    kv_cols = kv_total // lax.axis_size("tensor")
    normed = normalise(hidden, norm_gain)
    queries = add_product(normed, lax.all_gather(q_weight, "group", axis=0, tiled=True)) + q_bias
    head_span = max(kv_cols, HD)
    head_base = tensor_pos * kv_cols // head_span * head_span
    local_start = tensor_pos * kv_cols - head_base
    head_rows = lax.dynamic_slice_in_dim(kv_weight, head_base, head_span, 2).reshape(
        slice_rows, 2 * head_span
    )
    projected = add_product(normed, lax.all_gather(head_rows, "group", axis=0, tiled=True))
    projected = projected.reshape(tok_rows, 2, head_span) + lax.dynamic_slice_in_dim(
        kv_bias, head_base, head_span, 1
    )
    kv_here = head_span // HD
    group_size = heads_here // kv_here
    owner_id, offset, places = token_layout(
        prefix_lens, assignment, lax.axis_index("group"), tok_rows
    )
    rotated_queries = rotate(queries.reshape(tok_rows, heads_here, HD), offset).astype(jnp.bfloat16)
    rotated_keys = rotate(projected[:, 0].reshape(tok_rows, kv_here, HD), offset).astype(
        jnp.bfloat16
    )
    value_heads = projected[:, 1].reshape(tok_rows, kv_here, HD).astype(jnp.bfloat16)
    visible = (owner_id[:, None] == owner_id[None, :]) & (places[None, :] <= places[:, None])
    grouped = rotated_queries.reshape(tok_rows, kv_here, group_size, HD)
    scores = jnp.einsum(
        "qgph,kgh->gpqk", grouped, rotated_keys, preferred_element_type=jnp.float32
    ) / math.sqrt(HD)
    scores = jnp.where(visible[None, None], scores, -jnp.inf)
    row_max = jnp.max(scores, axis=-1, keepdims=True)
    exponent = jnp.exp(scores - row_max)
    weights_bf = (exponent / jnp.sum(exponent, axis=-1, keepdims=True)).astype(jnp.bfloat16)
    context = jnp.einsum(
        "gpqk,kgh->qgph", weights_bf, value_heads, preferred_element_type=jnp.float32
    )
    context = context.astype(jnp.bfloat16).reshape(tok_rows, q_cols)
    stacked = jnp.stack(
        [rotated_keys.reshape(tok_rows, head_span), value_heads.reshape(tok_rows, head_span)],
        axis=1,
    )
    kv_cache = lax.dynamic_slice_in_dim(stacked, local_start, kv_cols, 2)
    return (context, kv_cache)


def norm_kernel(part_ref, hidden_ref, gain_ref, out_ref):
    widened = hidden_ref[...].astype(jnp.float32)
    scale = lax.rsqrt(jnp.mean(widened * widened, axis=-1, keepdims=True) + EPS)
    count, _, depth = out_ref.shape
    for block in range(count):
        at = pl.multiple_of((part_ref[0] * count + block) * depth, depth)
        taken = hidden_ref[:, pl.ds(at, depth)].astype(jnp.float32)
        out_ref[block] = (taken * scale * gain_ref[:, pl.ds(at, depth)]).astype(jnp.bfloat16)


def norm(hidden, norm_gain, part, depth, count):
    rows, features = hidden.shape
    step = QROWS
    return pl.pallas_call(
        norm_kernel,
        grid_spec=pltpu.PrefetchScalarGridSpec(
            num_scalar_prefetch=1,
            grid=(rows // step,),
            in_specs=[
                pl.BlockSpec((step, features), lambda i, part: (i, 0)),
                pl.BlockSpec((1, features), lambda i, part: (0, 0)),
            ],
            out_specs=pl.BlockSpec((count, step, depth), lambda i, part: (0, i, 0)),
        ),
        out_shape=pltpu.HBM((count, rows, depth), jnp.bfloat16),
        compiler_params=pltpu.CompilerParams(vmem_limit_bytes=60 * 2**20),
        cost_estimate=pl.CostEstimate(
            flops=4 * rows * features,
            bytes_accessed=2 * rows * (features + count * depth),
            transcendentals=rows,
        ),
    )(part[None], hidden, norm_gain[None])


TILE = 2 * HD


def turn(value, cosine, sine):
    return value * cosine + pltpu.roll(value, HD // 2, 1) * sine


def heads_kernel(plan, pick_ref, *refs):
    sources, skips, parts, limits, width, closed_width, totals_at, with_keys = plan
    finish = closed_width > 0
    sets, count = len(sources), len(parts)
    refs = list(refs)

    def take(number):
        taken = refs[:number]
        del refs[:number]
        return taken

    row_refs = [take(number) for number in sources]
    weight_refs = [take(len(part)) for part in parts]
    total_refs = take(sets) if totals_at is not None else None
    if finish:
        (bias_ref,) = take(1)
        table_refs = take(sets)
    outs = take(sets)
    sum_outs = take(sets) if finish and closed_width < width else None
    row_buf, weight_buf, acc, row_sem, weight_sem, total_sem, out_sem = take(7)
    depth = row_buf.shape[2] // count

    def weight_copies(piece):
        column = 0
        for part, (ref, (lead, skip, wide)) in enumerate(zip(weight_refs[piece], parts[piece])):
            ref = ref if lead is None else ref.at[lead]
            yield pltpu.make_async_copy(
                ref.at[:, skip : skip + wide],
                weight_buf.at[piece * depth : (piece + 1) * depth, column : column + wide],
                weight_sem.at[piece, part],
            )
            column += wide

    def row_copy(which, piece, source):
        return pltpu.make_async_copy(
            row_refs[which][source].at[pick_ref[which, 1, piece]],
            row_buf.at[which, :, piece * depth : (piece + 1) * depth],
            row_sem.at[which, piece],
        )

    def total_copy(which):
        return pltpu.make_async_copy(
            total_refs[which].at[:, totals_at[which] : totals_at[which] + width],
            acc.at[which],
            total_sem.at[which],
        )

    stages = [(0, low, min(low + 2, count)) for low in range(0, count, 2)]
    stages += [(which, skips[which], count) for which in range(1, sets)]

    def start(stage):
        which, low, high = stages[stage]
        for piece in range(low, high):
            if which == 0:
                for copy in weight_copies(piece):
                    copy.start()
            if sources[which] == 1:
                row_copy(which, piece, 0).start()
            else:
                for source in range(sources[which]):

                    @pl.when(pick_ref[which, 0, piece] == source)
                    def _():
                        row_copy(which, piece, source).start()
        if low == skips[which] and total_refs is not None:
            total_copy(which).start()

    start(0)
    if len(stages) > 1:
        start(1)
    if finish:
        bias_buf, table_buf, out_buf, side_sem = refs
        side_copies = [pltpu.make_async_copy(bias_ref, bias_buf, side_sem.at[sets])]
        side_copies += [
            pltpu.make_async_copy(table_refs[which], table_buf.at[which], side_sem.at[which])
            for which in range(sets)
        ]

    def out_copies(which):
        pairs = [((out_buf if finish else acc).at[which], outs[which])]
        if sum_outs is not None:
            pairs.append((acc.at[which, :, closed_width:], sum_outs[which]))
        return [
            pltpu.make_async_copy(buf, ref, out_sem.at[which, number])
            for number, (buf, ref) in enumerate(pairs)
        ]

    for stage, (which, low, high) in enumerate(stages):
        for piece in range(low, high):
            if which == 0:
                for copy in weight_copies(piece):
                    copy.wait()
            row_copy(which, piece, 0).wait()
        if low == skips[which] and total_refs is not None:
            total_copy(which).wait()
        if stage + 2 < len(stages):
            start(stage + 2)
        if stage == 0 and finish:
            for copy in side_copies:
                copy.start()
        for at in range(0, width, TILE):
            top = min(high, limits[at // TILE])
            if top <= low:
                continue
            cols = slice(at, at + TILE)
            term = jnp.dot(
                row_buf[which, :, low * depth : top * depth],
                weight_buf[low * depth : top * depth, cols],
                preferred_element_type=jnp.float32,
            )
            if low > skips[which] or total_refs is not None:
                term = acc[which, :, cols] + term
            acc[which, :, cols] = term
        if high < count:
            continue
        if finish:
            if which == 0:
                side_copies[0].wait()
            side_copies[1 + which].wait()
            finish_set(acc.at[which], bias_buf, table_buf[which], out_buf.at[which], with_keys)
        for copy in out_copies(which):
            copy.start()
    for which in range(sets):
        for copy in out_copies(which):
            copy.wait()


def finish_set(acc, bias, table, out, with_keys):
    swapped = pltpu.roll(table, HD // 2, 1)
    left = lax.broadcasted_iota(jnp.int32, table.shape, 1) < HD // 2
    cosine = jnp.where(left, table, swapped)
    sine = jnp.where(left, -swapped, table)
    for col in range(0, out.shape[1], HD):
        cols = slice(col, col + HD)
        value = acc[:, cols] + bias[:, cols]
        if not (with_keys and col == HD):
            value = turn(value, cosine, sine)
        out[:, cols] = value.astype(jnp.bfloat16)


def heads_of(row_sets, picks, pieces, limits, totals=None, finish=None, skips=None):
    sets, count = len(row_sets), len(pieces)
    skips = skips or (0,) * sets
    width = len(limits) * TILE
    sources = tuple(len(rows) for rows in row_sets)
    tokens, depth = row_sets[0][0].shape[1:]
    operands = [array for rows in row_sets for array in rows]
    operands += [array for piece in pieces for array, *_ in piece]
    totals_at = None
    if totals is not None:
        totals, totals_at = totals
        operands += totals
    scratch = [
        pltpu.VMEM((sets, tokens, count * depth), jnp.bfloat16),
        pltpu.VMEM((count * depth, width), jnp.bfloat16),
        pltpu.VMEM((sets, tokens, width), jnp.float32),
        pltpu.SemaphoreType.DMA((sets, count)),
        pltpu.SemaphoreType.DMA((count, max(map(len, pieces)))),
        pltpu.SemaphoreType.DMA((sets,)),
        pltpu.SemaphoreType.DMA((sets, 3)),
    ]
    with_keys, closed_width = False, 0
    out_shape = [jax.ShapeDtypeStruct((tokens, width), jnp.float32)] * sets
    if finish is not None:
        closed_width, bias, tables, with_keys = finish
        out_shape = [jax.ShapeDtypeStruct((tokens, closed_width), jnp.bfloat16)] * sets
        operands += [bias, *tables]
        if closed_width < width:
            out_shape += [jax.ShapeDtypeStruct((tokens, width - closed_width), jnp.float32)] * sets
        scratch += [
            pltpu.VMEM((1, closed_width), jnp.float32),
            pltpu.VMEM((sets, tokens, HD), jnp.float32),
            pltpu.VMEM((sets, tokens, closed_width), jnp.bfloat16),
            pltpu.SemaphoreType.DMA((sets + 1,)),
        ]
    plan = (
        sources,
        skips,
        tuple(tuple(part[1:] for part in piece) for piece in pieces),
        limits,
        width,
        closed_width,
        totals_at,
        with_keys,
    )
    anywhere = pl.BlockSpec(memory_space=pl.ANY)
    return pl.pallas_call(
        functools.partial(heads_kernel, plan),
        grid_spec=pltpu.PrefetchScalarGridSpec(
            num_scalar_prefetch=1,
            grid=(1,),
            in_specs=[anywhere] * len(operands),
            out_specs=[pl.BlockSpec(memory_space=pltpu.HBM)] * len(out_shape),
            scratch_shapes=scratch,
        ),
        out_shape=out_shape,
        compiler_params=pltpu.CompilerParams(vmem_limit_bytes=56 * 2**20),
        cost_estimate=pl.CostEstimate(
            flops=2 * sets * count * tokens * depth * width,
            bytes_accessed=2 * count * depth * (sets * tokens + width) + 8 * sets * tokens * width,
            transcendentals=0,
        ),
    )(picks, *operands)


def attention(queries, keys, values, first_ref, out_ref):
    rows, cols = out_ref.shape
    heads = cols // HD
    scale = math.log2(math.e) / math.sqrt(HD)
    for top in range(0, rows, QROWS):
        low, end = max(0, top - MAXLEN), top + QROWS
        shape = (QROWS, end - low)
        stacked = jnp.concatenate(
            [queries[top:end, col : col + HD] for col in range(0, cols, HD)], axis=0
        )
        scores = jnp.dot(stacked, keys[:, low:end], preferred_element_type=jnp.float32)
        row = lax.broadcasted_iota(jnp.int32, shape, 0) + top
        col = lax.broadcasted_iota(jnp.int32, shape, 1) + low
        visible = (col <= row) & (col >= first_ref[top:end])
        scores = jnp.where(visible[None], scores.reshape(heads, *shape), -jnp.inf)
        most = jnp.max(scores, axis=-1, keepdims=True)
        exponent = jnp.exp2((scores - most) * scale)
        share = 1.0 / jnp.sum(exponent, axis=-1, keepdims=True)
        weights = (exponent * share).astype(jnp.bfloat16)
        context = jnp.dot(
            weights.reshape(heads * QROWS, end - low),
            values[low:end],
            preferred_element_type=jnp.float32,
        ).astype(jnp.bfloat16)
        for head in range(heads):
            out_ref[top:end, head * HD : (head + 1) * HD] = context[
                head * QROWS : (head + 1) * QROWS
            ]


def attend_kernel(numbers, flag_ref, *refs):
    ends = [sum(numbers[: i + 1]) for i in range(4)]
    near, beside, back, other = (refs[end - number : end] for end, number in zip(ends, numbers))
    first_ref, out_ref, cache_ref, part_buf, out_buf, in_sem, out_sem = refs[ends[-1] :]
    half = out_buf.shape[2]

    def copies(side, sources):
        column = 0
        for part, source in enumerate(sources):
            wide = source.shape[1]
            yield pltpu.make_async_copy(
                source, part_buf.at[side, :, column : column + wide], in_sem.at[side, part]
            )
            column += wide

    def on_parts(act):
        for middle, sides in ((1, (near, beside)), (0, (back, other))):

            @pl.when(flag_ref[1] == middle)
            def _():
                for side, sources in enumerate(sides):
                    for copy in copies(side, sources):
                        act(copy)

    on_parts(lambda copy: copy.start())
    on_parts(lambda copy: copy.wait())
    sent = []
    for side in range(2):
        at = flag_ref[0] if side == 0 else 1 - flag_ref[0]
        part = part_buf.at[side]
        for number in range(2):
            sent.append(
                pltpu.make_async_copy(
                    part.at[:, number * HD : (number + 1) * HD],
                    cache_ref.at[:, pl.ds(pl.multiple_of((2 * number + at) * HD, HD), HD)],
                    out_sem.at[side, number],
                )
            )
            sent[-1].start()
        keys = part[:, :HD].astype(jnp.float32).T.astype(jnp.bfloat16)
        attention(part.at[:, TILE:], keys, part.at[:, HD:TILE], first_ref, out_buf.at[side])
        sent.append(
            pltpu.make_async_copy(
                out_buf.at[side],
                out_ref.at[:, pl.ds(pl.multiple_of(at * half, half), half)],
                out_sem.at[side, 2],
            )
        )
        sent[-1].start()
    for copy in sent:
        copy.wait()


def attend_all(flags, near, beside, back, other, first, cols):
    operands = [*near, *beside, *back, *other]
    rows = near[0].shape[0]
    in_hbm = pl.BlockSpec(memory_space=pltpu.HBM)
    return pl.pallas_call(
        functools.partial(attend_kernel, tuple(map(len, (near, beside, back, other)))),
        grid_spec=pltpu.PrefetchScalarGridSpec(
            num_scalar_prefetch=1,
            grid=(1,),
            in_specs=[in_hbm] * len(operands) + [pl.BlockSpec((rows, 1), lambda i, flags: (0, 0))],
            out_specs=[in_hbm] * 2,
            scratch_shapes=[
                pltpu.VMEM((2, rows, TILE + cols // 2), jnp.bfloat16),
                pltpu.VMEM((2, rows, cols // 2), jnp.bfloat16),
                pltpu.SemaphoreType.DMA((2, 3)),
                pltpu.SemaphoreType.DMA((2, 3)),
            ],
        ),
        out_shape=[
            jax.ShapeDtypeStruct((rows, cols), jnp.bfloat16),
            jax.ShapeDtypeStruct((rows, 2 * TILE), jnp.bfloat16),
        ],
        compiler_params=pltpu.CompilerParams(vmem_limit_bytes=40 * 2**20),
        cost_estimate=pl.CostEstimate(
            flops=4 * cols * rows * 3 * QROWS,
            bytes_accessed=6 * rows * cols,
            transcendentals=cols // HD * rows * 3 * QROWS,
        ),
    )(flags, *operands, first)


MIDDLE = (2, 3, 4, 5)
ENDS = (0, 1, 6, 7)


def after(value, *others):
    return lax.optimization_barrier((value,) + others)[0]


def pairs_from(sources, code):
    return [(s, s ^ code) for s in sources]


def middle_form(hidden, norm_gain, q_weight, q_bias, kv_weight, kv_bias, prefix_lens, assignment):
    tok_rows, features = hidden.shape
    slice_rows, q_cols = q_weight.shape
    half_cols = q_cols // 2
    group = lax.axis_index("group")
    tensor = lax.axis_index("tensor")
    y = group & 1
    is_middle = (group >= 2) & (group < 6)
    barrier = lax.optimization_barrier

    def over_group(value, sources, code):
        return lax.ppermute(value, "group", pairs_from(sources, code))

    def to_middle(value):
        return over_group(value, ENDS, 2)

    def across_middle(value):
        return over_group(value, MIDDLE, 6)

    def over_x(value):
        return lax.ppermute(value, "tensor", pairs_from(range(4), 2))

    def over_core(value):
        return lax.ppermute(value, "tensor", pairs_from(range(4), 1))

    begin, widths = (0, 2 * TILE, 4 * TILE), (2 * TILE, 2 * TILE, TILE)

    def columns(half, cuts):
        head = (2 * tensor + half) * HD
        kv_part = lax.dynamic_slice_in_dim(kv_weight, head, HD, 2).reshape(slice_rows, TILE)
        taken, low = [], half * half_cols
        for number, wide in enumerate(cuts):
            wide = wide - (TILE if number == 0 else 0)
            part = lax.dynamic_slice_in_dim(q_weight, low, wide, 1)
            low = low + wide
            taken.append(jnp.concatenate([kv_part, part], axis=1) if number == 0 else part)
        return taken

    def both(one, two, chunk):
        low, high = begin[chunk], begin[chunk] + widths[chunk]
        return jnp.stack([one[:, low:high], two[:, low:high]])

    def pick(code_of_rows, codes):
        block = jnp.stack([group ^ code for code in codes])
        if code_of_rows == 0:
            return jnp.stack([block * 0, block])
        return jnp.stack([(block >> 1) ^ tensor, block & 1])

    first_codes, last_codes, beside_codes = (0, 1, 6, 7, 2, 3), (2, 3, 7, 4, 5), (0, 1, 6, 2, 3, 7, 4, 5)
    picks = {
        (sets, codes): jnp.stack([pick(c, codes) for c in sets])
        for sets, codes in (
            ((0, 2), first_codes),
            ((3,), first_codes),
            ((2, 3, 0), (4, 5)),
            ((2, 0, 3), (2, 3, 4, 5)),
            ((1,), beside_codes),
            ((2, 3, 1), last_codes),
            ((0,), last_codes),
        )
    }
    flags = jnp.stack([y, is_middle.astype(jnp.int32)])

    def closed(arriving, others):
        arrived = []
        for value in arriving:
            value, others = barrier((value, others))
            arrived.append(value)
        return barrier((tuple(arrived), others))

    (own,) = columns(y, (sum(widths),))
    other, other2 = columns(1 - y, (begin[2], widths[2]))
    m_own = across_middle(own)
    swap = over_group(other, range(8), 1)
    swap2 = over_group(other2, range(8), 1)
    quarter = norm(hidden, norm_gain, tensor, slice_rows, 2)
    end2 = to_middle(quarter)
    normed = norm(after(hidden, quarter), norm_gain, tensor * 0, slice_rows, features // slice_rows)

    bias = lax.dynamic_slice_in_dim(q_bias, y * half_cols, half_cols, 0)
    kv_bias_here = lax.dynamic_slice_in_dim(kv_bias, (2 * tensor + y) * HD, HD, 1)
    bias = jnp.concatenate([kv_bias_here[0], kv_bias_here[1], bias])[None, :]
    inverse_freq = THETA ** (-2.0 * jnp.arange(HD // 2, dtype=jnp.float32) / HD)
    m_swap = across_middle(after(swap, m_own))
    own, swap, m_own, normed, quarter, end2 = barrier((own, swap, m_own, normed, quarter, end2))

    rows_of = {0: [normed]}
    stack0, end2 = barrier((both(own, swap, 0), end2))
    e0 = to_middle(stack0)
    next1, next2 = both(own, swap, 1), jnp.stack([own[:, begin[2] :], swap2])
    end3 = over_group(end2, MIDDLE, 1)
    across2 = over_x(end2)
    twin2 = over_core(end2)
    tables = []
    for code in range(4):
        _, offset, places = token_layout(prefix_lens, assignment, group ^ code, tok_rows)
        angles = offset.astype(jnp.float32)[:, None] * inverse_freq[None, :]
        table = jnp.concatenate([jnp.cos(angles), jnp.sin(angles)], axis=1)
        tables.append((table, (places - offset)[:, None]))
    m_e0 = across_middle(after(e0, m_swap))
    biases = {
        chunks: bias[:, begin[chunks[0]] : begin[chunks[0]] + sum(widths[c] for c in chunks)]
        for chunks in ((0,), (1,), (2,), (0, 1))
    }
    (e0, m_swap, end3, across2, twin2), ready = closed(
        (e0, m_swap, end3, across2, twin2),
        (next1, next2, end2, tables, quarter, picks, biases, flags),
    )
    next1, next2, end2, tables, quarter, picks, biases, flags = ready

    places = {}

    def arrived(chunk, **codes):
        for code, (array, lead, skip) in codes.items():
            places[int(code[1:]), chunk] = (array, lead, skip)

    for chunk, low in enumerate(begin):
        arrived(chunk, c0=(own, None, low), c6=(m_own, None, low))
        if chunk < 2:
            arrived(chunk, c1=(swap, None, low), c7=(m_swap, None, low))
    arrived(2, c1=(swap2, None, 0))
    arrived(0, c2=(e0, 0, 0), c3=(e0, 1, 0))

    def call(sets, codes, chunks, totals=None, finish=None, skips=None):
        rows = [rows_of[c] for c in sets]
        pieces, limits = [], []
        for code in codes:
            there = [chunk for chunk in chunks if (code, chunk) in places]
            pieces.append([places[code, chunk] + (widths[chunk],) for chunk in there])
        for chunk in chunks:
            there = [(code, chunk) in places for code in codes]
            limits += [sum(there)] * (widths[chunk] // TILE)
            assert all(there[: sum(there)])
        return heads_of(rows, picks[sets, codes], pieces, tuple(limits), totals, finish, skips)

    outs, every = {}, (0, 1, 2)

    def first_sums(sets):
        return call(sets, first_codes, every)

    def finished(sets, chunks, codes, totals=None, opened=(), skips=None):
        wide = sum(widths[chunk] for chunk in chunks)
        finish = (wide, biases[chunks], [tables[c][0] for c in sets], chunks[0] == 0)
        made = call(sets, codes, chunks + opened, totals, finish, skips)
        for code, out in zip(sets, made):
            outs[code, chunks[0]] = out
        return made[-1]

    e1 = to_middle(next1)
    end1 = over_group(quarter, MIDDLE, 1)
    across3 = over_x(end3)
    far2 = over_core(across2)
    rows_of[2] = [end2, twin2, across2, far2]
    sums = dict(zip((0, 2), first_sums((0, 2))))
    m_e1 = across_middle(after(e1, m_e0))
    (m_e0, e1, end1, across3), (next2, e0, end3, far2, sums) = closed(
        (m_e0, e1, end1, across3), (next2, e0, end3, far2, sums)
    )
    rows_of[2] = [end2, twin2, across2, far2]

    e2 = to_middle(next2)
    across1 = over_x(end1)
    twin3 = over_core(end3)
    far3 = over_core(across3)
    rows_of[3] = [end3, twin3, across3, far3]

    def send_back(code, chunk):
        return over_group(outs[code, chunk], MIDDLE, code)

    arrived(1, c2=(e1, 0, 0), c3=(e1, 1, 0))
    (sums[3],) = first_sums((3,))
    arrived(0, c4=(m_e0, 0, 0), c5=(m_e0, 1, 0))
    three = (2, 3, 0)
    finished(three, (0,), (4, 5), ([sums[c] for c in three], (0, 0, 0)))
    back = {(2, 0): send_back(2, 0)}
    last = jnp.concatenate([swap2[None], e2])
    m_last = across_middle(after(last, m_e1))
    (last, m_e1, across1, back[2, 0]), (end1, made, sums) = closed(
        (last, m_e1, across1, back[2, 0]), (end1, [outs[c, 0] for c in three], sums)
    )
    for code, out in zip(three, made):
        outs[code, 0] = out

    twin1 = over_core(end1)
    far1 = over_core(across1)
    arrived(1, c4=(m_e1, 0, 0), c5=(m_e1, 1, 0))
    arrived(2, c2=(last, 1, 0), c3=(last, 2, 0))
    back[3, 0] = send_back(3, 0)
    three = (2, 0, 3)
    finished(
        three,
        (1,),
        (2, 3, 4, 5),
        ([sums[c] for c in three], (begin[1],) * 3),
        skips=(0, 0, 2),
    )
    for code in (2, 3):
        back[code, 1] = send_back(code, 1)
    far1, outs[2, 1] = barrier((far1, outs[2, 1]))
    rows_of[1] = [end1, twin1, across1, far1]
    sums[1] = finished((1,), (0, 1), beside_codes, opened=(2,))
    back[1, 0] = send_back(1, 0)
    (m_last, back[3, 0], back[2, 1]), (sums, outs[1, 0]) = closed(
        (m_last, back[3, 0], back[2, 1]), (sums, outs[1, 0])
    )

    arrived(2, c7=(m_last, 0, 0), c4=(m_last, 1, 0), c5=(m_last, 2, 0))
    three = (2, 3, 1)
    finished(
        three,
        (2,),
        last_codes,
        ([sums[c] for c in three], (begin[2], begin[2], 0)),
        skips=(0, 0, 2),
    )
    for code in (2, 3):
        back[code, 2] = send_back(code, 2)
    back[1, 2] = send_back(1, 2)
    sums[0], outs[1, 2], back[3, 1] = barrier((sums[0], outs[1, 2], back[3, 1]))
    finished((0,), (2,), last_codes, ([sums[0]], (begin[2],)))

    (back[2, 2], back[3, 2], back[1, 2]), _ = closed((back[2, 2], back[3, 2], back[1, 2]), ())
    context, cache = attend_all(
        flags,
        [outs[0, part] for part in every],
        [back[1, part] for part in (0, 2)],
        [back[2, part] for part in every],
        [back[3, part] for part in every],
        tables[0][1],
        q_cols,
    )
    return (context, cache.reshape(tok_rows, 2, TILE))


def solution(mesh):
    placed = (
        P("group", None),
        P(),
        P("group", "tensor"),
        P("tensor"),
        P("group", None, None),
        P(),
        P(),
        P(),
    )
    fits = mesh.shape["group"] == 8 and mesh.shape["tensor"] == 4
    return jax.shard_map(
        middle_form if fits else gathered_form,
        mesh=mesh,
        in_specs=placed,
        out_specs=(P("group", "tensor"), P("group", None, "tensor")),
        check_vma=False,
    )
```

```python
import functools
import math

import jax
import jax.numpy as jnp
from jax import lax
from jax.experimental import pallas as pl
from jax.experimental.pallas import tpu as pltpu
from jax.sharding import PartitionSpec as P

HD = 128


EPS = 1e-06
THETA = 1000000.0
QROWS = 128
MAXLEN = 256


def token_layout(prefix_lens, assignment, group_id, tok_rows):
    rollouts = prefix_lens.shape[0]
    member = assignment == group_id
    own_lens = jnp.where(member, prefix_lens, 0)
    starts = jnp.cumsum(own_lens) - own_lens
    places = jnp.arange(tok_rows, dtype=jnp.int32)
    inside = (
        member[None, :]
        & (places[:, None] >= starts[None, :])
        & (places[:, None] < (starts + own_lens)[None, :])
    )
    owner_id = jnp.sum(jnp.where(inside, jnp.arange(rollouts, dtype=jnp.int32)[None, :], 0), axis=1)
    offset = places - jnp.sum(jnp.where(inside, starts[None, :], 0), axis=1)
    return (owner_id, offset, places)


def rotate(values, offset):
    half_dim = values.shape[-1] // 2
    inverse_freq = THETA ** (-2.0 * jnp.arange(half_dim, dtype=jnp.float32) / values.shape[-1])
    angles = offset.astype(jnp.float32)[:, None] * inverse_freq[None, :]
    cosine = jnp.cos(angles)[:, None, :]
    sine_part = jnp.sin(angles)[:, None, :]
    first_half = values[..., :half_dim]
    second_half = values[..., half_dim:]
    return jnp.concatenate(
        [
            first_half * cosine - second_half * sine_part,
            second_half * cosine + first_half * sine_part,
        ],
        axis=-1,
    )


def add_product(normed, portion):
    return jnp.dot(normed, portion, preferred_element_type=jnp.float32)


def normalise(hidden, norm_gain):
    widened = hidden.astype(jnp.float32)
    return (
        widened * lax.rsqrt(jnp.mean(widened * widened, axis=-1, keepdims=True) + EPS) * norm_gain
    ).astype(jnp.bfloat16)


def gathered_form(
    hidden, norm_gain, q_weight, q_bias, kv_weight, kv_bias, prefix_lens, assignment
):
    tok_rows, features = hidden.shape
    slice_rows = kv_weight.shape[0]
    q_cols = q_weight.shape[1]
    kv_total = kv_weight.shape[2]
    heads_here = q_cols // HD
    tensor_pos = lax.axis_index("tensor")
    kv_cols = kv_total // lax.axis_size("tensor")
    normed = normalise(hidden, norm_gain)
    queries = add_product(normed, lax.all_gather(q_weight, "group", axis=0, tiled=True)) + q_bias
    head_span = max(kv_cols, HD)
    head_base = tensor_pos * kv_cols // head_span * head_span
    local_start = tensor_pos * kv_cols - head_base
    head_rows = lax.dynamic_slice_in_dim(kv_weight, head_base, head_span, 2).reshape(
        slice_rows, 2 * head_span
    )
    projected = add_product(normed, lax.all_gather(head_rows, "group", axis=0, tiled=True))
    projected = projected.reshape(tok_rows, 2, head_span) + lax.dynamic_slice_in_dim(
        kv_bias, head_base, head_span, 1
    )
    kv_here = head_span // HD
    group_size = heads_here // kv_here
    owner_id, offset, places = token_layout(
        prefix_lens, assignment, lax.axis_index("group"), tok_rows
    )
    rotated_queries = rotate(queries.reshape(tok_rows, heads_here, HD), offset).astype(jnp.bfloat16)
    rotated_keys = rotate(projected[:, 0].reshape(tok_rows, kv_here, HD), offset).astype(
        jnp.bfloat16
    )
    value_heads = projected[:, 1].reshape(tok_rows, kv_here, HD).astype(jnp.bfloat16)
    visible = (owner_id[:, None] == owner_id[None, :]) & (places[None, :] <= places[:, None])
    grouped = rotated_queries.reshape(tok_rows, kv_here, group_size, HD)
    scores = jnp.einsum(
        "qgph,kgh->gpqk", grouped, rotated_keys, preferred_element_type=jnp.float32
    ) / math.sqrt(HD)
    scores = jnp.where(visible[None, None], scores, -jnp.inf)
    row_max = jnp.max(scores, axis=-1, keepdims=True)
    exponent = jnp.exp(scores - row_max)
    weights_bf = (exponent / jnp.sum(exponent, axis=-1, keepdims=True)).astype(jnp.bfloat16)
    context = jnp.einsum(
        "gpqk,kgh->qgph", weights_bf, value_heads, preferred_element_type=jnp.float32
    )
    context = context.astype(jnp.bfloat16).reshape(tok_rows, q_cols)
    stacked = jnp.stack(
        [rotated_keys.reshape(tok_rows, head_span), value_heads.reshape(tok_rows, head_span)],
        axis=1,
    )
    kv_cache = lax.dynamic_slice_in_dim(stacked, local_start, kv_cols, 2)
    return (context, kv_cache)


def norm_kernel(part_ref, hidden_ref, gain_ref, out_ref):
    widened = hidden_ref[...].astype(jnp.float32)
    scale = lax.rsqrt(jnp.mean(widened * widened, axis=-1, keepdims=True) + EPS)
    count, _, depth = out_ref.shape
    for block in range(count):
        at = pl.multiple_of((part_ref[0] * count + block) * depth, depth)
        taken = hidden_ref[:, pl.ds(at, depth)].astype(jnp.float32)
        out_ref[block] = (taken * scale * gain_ref[:, pl.ds(at, depth)]).astype(jnp.bfloat16)


def norm(hidden, norm_gain, part, depth, count):
    rows, features = hidden.shape
    step = QROWS
    return pl.pallas_call(
        norm_kernel,
        grid_spec=pltpu.PrefetchScalarGridSpec(
            num_scalar_prefetch=1,
            grid=(rows // step,),
            in_specs=[
                pl.BlockSpec((step, features), lambda i, part: (i, 0)),
                pl.BlockSpec((1, features), lambda i, part: (0, 0)),
            ],
            out_specs=pl.BlockSpec((count, step, depth), lambda i, part: (0, i, 0)),
        ),
        out_shape=pltpu.HBM((count, rows, depth), jnp.bfloat16),
        compiler_params=pltpu.CompilerParams(vmem_limit_bytes=60 * 2**20),
        cost_estimate=pl.CostEstimate(
            flops=4 * rows * features,
            bytes_accessed=2 * rows * (features + count * depth),
            transcendentals=rows,
        ),
    )(part[None], hidden, norm_gain[None])


TILE = 2 * HD


def turn(value, cosine, sine):
    return value * cosine + pltpu.roll(value, HD // 2, 1) * sine


def heads_kernel(plan, pick_ref, *refs):
    sources, skips, parts, limits, width, closed_width, totals_at, with_keys = plan
    finish = closed_width > 0
    sets, count = len(sources), len(parts)
    refs = list(refs)

    def take(number):
        taken = refs[:number]
        del refs[:number]
        return taken

    row_refs = [take(number) for number in sources]
    weight_refs = [take(len(part)) for part in parts]
    total_refs = take(sets) if totals_at is not None else None
    if finish:
        (bias_ref,) = take(1)
        table_refs = take(sets)
    outs = take(sets)
    sum_outs = take(sets) if finish and closed_width < width else None
    row_buf, weight_buf, acc, row_sem, weight_sem, total_sem, out_sem = take(7)
    depth = row_buf.shape[2] // count

    def weight_copies(piece):
        column = 0
        for part, (ref, (lead, skip, wide)) in enumerate(zip(weight_refs[piece], parts[piece])):
            ref = ref if lead is None else ref.at[lead]
            yield pltpu.make_async_copy(
                ref.at[:, skip : skip + wide],
                weight_buf.at[piece * depth : (piece + 1) * depth, column : column + wide],
                weight_sem.at[piece, part],
            )
            column += wide

    def row_copy(which, piece, source):
        return pltpu.make_async_copy(
            row_refs[which][source].at[pick_ref[which, 1, piece]],
            row_buf.at[which, :, piece * depth : (piece + 1) * depth],
            row_sem.at[which, piece],
        )

    def total_copy(which):
        return pltpu.make_async_copy(
            total_refs[which].at[:, totals_at[which] : totals_at[which] + width],
            acc.at[which],
            total_sem.at[which],
        )

    stages = [(0, low, min(low + 2, count)) for low in range(0, count, 2)]
    stages += [(which, skips[which], count) for which in range(1, sets)]

    def start(stage):
        which, low, high = stages[stage]
        for piece in range(low, high):
            if which == 0:
                for copy in weight_copies(piece):
                    copy.start()
            if sources[which] == 1:
                row_copy(which, piece, 0).start()
            else:
                for source in range(sources[which]):

                    @pl.when(pick_ref[which, 0, piece] == source)
                    def _():
                        row_copy(which, piece, source).start()
        if low == skips[which] and total_refs is not None:
            total_copy(which).start()

    start(0)
    if len(stages) > 1:
        start(1)
    if finish:
        bias_buf, table_buf, out_buf, side_sem = refs
        side_copies = [pltpu.make_async_copy(bias_ref, bias_buf, side_sem.at[sets])]
        side_copies += [
            pltpu.make_async_copy(table_refs[which], table_buf.at[which], side_sem.at[which])
            for which in range(sets)
        ]

    def out_copies(which):
        pairs = [((out_buf if finish else acc).at[which], outs[which])]
        if sum_outs is not None:
            pairs.append((acc.at[which, :, closed_width:], sum_outs[which]))
        return [
            pltpu.make_async_copy(buf, ref, out_sem.at[which, number])
            for number, (buf, ref) in enumerate(pairs)
        ]

    for stage, (which, low, high) in enumerate(stages):
        for piece in range(low, high):
            if which == 0:
                for copy in weight_copies(piece):
                    copy.wait()
            row_copy(which, piece, 0).wait()
        if low == skips[which] and total_refs is not None:
            total_copy(which).wait()
        if stage + 2 < len(stages):
            start(stage + 2)
        if stage == 0 and finish:
            for copy in side_copies:
                copy.start()
        for at in range(0, width, TILE):
            top = min(high, limits[at // TILE])
            if top <= low:
                continue
            cols = slice(at, at + TILE)
            term = jnp.dot(
                row_buf[which, :, low * depth : top * depth],
                weight_buf[low * depth : top * depth, cols],
                preferred_element_type=jnp.float32,
            )
            if low > skips[which] or total_refs is not None:
                term = acc[which, :, cols] + term
            acc[which, :, cols] = term
        if high < count:
            continue
        if finish:
            if which == 0:
                side_copies[0].wait()
            side_copies[1 + which].wait()
            finish_set(acc.at[which], bias_buf, table_buf[which], out_buf.at[which], with_keys)
        for copy in out_copies(which):
            copy.start()
    for which in range(sets):
        for copy in out_copies(which):
            copy.wait()


def finish_set(acc, bias, table, out, with_keys):
    swapped = pltpu.roll(table, HD // 2, 1)
    left = lax.broadcasted_iota(jnp.int32, table.shape, 1) < HD // 2
    cosine = jnp.where(left, table, swapped)
    sine = jnp.where(left, -swapped, table)
    for col in range(0, out.shape[1], HD):
        cols = slice(col, col + HD)
        value = acc[:, cols] + bias[:, cols]
        if not (with_keys and col == HD):
            value = turn(value, cosine, sine)
        out[:, cols] = value.astype(jnp.bfloat16)


def heads_of(row_sets, picks, pieces, limits, totals=None, finish=None, skips=None):
    sets, count = len(row_sets), len(pieces)
    skips = skips or (0,) * sets
    width = len(limits) * TILE
    sources = tuple(len(rows) for rows in row_sets)
    tokens, depth = row_sets[0][0].shape[1:]
    operands = [array for rows in row_sets for array in rows]
    operands += [array for piece in pieces for array, *_ in piece]
    totals_at = None
    if totals is not None:
        totals, totals_at = totals
        operands += totals
    scratch = [
        pltpu.VMEM((sets, tokens, count * depth), jnp.bfloat16),
        pltpu.VMEM((count * depth, width), jnp.bfloat16),
        pltpu.VMEM((sets, tokens, width), jnp.float32),
        pltpu.SemaphoreType.DMA((sets, count)),
        pltpu.SemaphoreType.DMA((count, max(map(len, pieces)))),
        pltpu.SemaphoreType.DMA((sets,)),
        pltpu.SemaphoreType.DMA((sets, 3)),
    ]
    with_keys, closed_width = False, 0
    out_shape = [jax.ShapeDtypeStruct((tokens, width), jnp.float32)] * sets
    if finish is not None:
        closed_width, bias, tables, with_keys = finish
        out_shape = [jax.ShapeDtypeStruct((tokens, closed_width), jnp.bfloat16)] * sets
        operands += [bias, *tables]
        if closed_width < width:
            out_shape += [jax.ShapeDtypeStruct((tokens, width - closed_width), jnp.float32)] * sets
        scratch += [
            pltpu.VMEM((1, closed_width), jnp.float32),
            pltpu.VMEM((sets, tokens, HD), jnp.float32),
            pltpu.VMEM((sets, tokens, closed_width), jnp.bfloat16),
            pltpu.SemaphoreType.DMA((sets + 1,)),
        ]
    plan = (
        sources,
        skips,
        tuple(tuple(part[1:] for part in piece) for piece in pieces),
        limits,
        width,
        closed_width,
        totals_at,
        with_keys,
    )
    anywhere = pl.BlockSpec(memory_space=pl.ANY)
    return pl.pallas_call(
        functools.partial(heads_kernel, plan),
        grid_spec=pltpu.PrefetchScalarGridSpec(
            num_scalar_prefetch=1,
            grid=(1,),
            in_specs=[anywhere] * len(operands),
            out_specs=[pl.BlockSpec(memory_space=pltpu.HBM)] * len(out_shape),
            scratch_shapes=scratch,
        ),
        out_shape=out_shape,
        compiler_params=pltpu.CompilerParams(vmem_limit_bytes=56 * 2**20),
        cost_estimate=pl.CostEstimate(
            flops=2 * sets * count * tokens * depth * width,
            bytes_accessed=2 * count * depth * (sets * tokens + width) + 8 * sets * tokens * width,
            transcendentals=0,
        ),
    )(picks, *operands)


def attention(queries, keys, values, first_ref, out_ref):
    rows, cols = out_ref.shape
    heads = cols // HD
    scale = math.log2(math.e) / math.sqrt(HD)
    for top in range(0, rows, QROWS):
        low, end = max(0, top - MAXLEN), top + QROWS
        shape = (QROWS, end - low)
        stacked = jnp.concatenate(
            [queries[top:end, col : col + HD] for col in range(0, cols, HD)], axis=0
        )
        scores = jnp.dot(stacked, keys[:, low:end], preferred_element_type=jnp.float32)
        row = lax.broadcasted_iota(jnp.int32, shape, 0) + top
        col = lax.broadcasted_iota(jnp.int32, shape, 1) + low
        visible = (col <= row) & (col >= first_ref[top:end])
        scores = jnp.where(visible[None], scores.reshape(heads, *shape), -jnp.inf)
        most = jnp.max(scores, axis=-1, keepdims=True)
        exponent = jnp.exp2((scores - most) * scale)
        share = 1.0 / jnp.sum(exponent, axis=-1, keepdims=True)
        weights = (exponent * share).astype(jnp.bfloat16)
        context = jnp.dot(
            weights.reshape(heads * QROWS, end - low),
            values[low:end],
            preferred_element_type=jnp.float32,
        ).astype(jnp.bfloat16)
        for head in range(heads):
            out_ref[top:end, head * HD : (head + 1) * HD] = context[
                head * QROWS : (head + 1) * QROWS
            ]


def attend_kernel(numbers, flag_ref, *refs):
    ends = [sum(numbers[: i + 1]) for i in range(4)]
    near, beside, back, other = (refs[end - number : end] for end, number in zip(ends, numbers))
    first_ref, out_ref, cache_ref, part_buf, out_buf, in_sem, out_sem = refs[ends[-1] :]
    half = out_buf.shape[2]

    def copies(side, sources):
        column = 0
        for part, source in enumerate(sources):
            wide = source.shape[1]
            yield pltpu.make_async_copy(
                source, part_buf.at[side, :, column : column + wide], in_sem.at[side, part]
            )
            column += wide

    def on_parts(act):
        for middle, sides in ((1, (near, beside)), (0, (back, other))):

            @pl.when(flag_ref[1] == middle)
            def _():
                for side, sources in enumerate(sides):
                    for copy in copies(side, sources):
                        act(copy)

    on_parts(lambda copy: copy.start())
    on_parts(lambda copy: copy.wait())
    sent = []
    for side in range(2):
        at = flag_ref[0] if side == 0 else 1 - flag_ref[0]
        part = part_buf.at[side]
        for number in range(2):
            sent.append(
                pltpu.make_async_copy(
                    part.at[:, number * HD : (number + 1) * HD],
                    cache_ref.at[:, pl.ds(pl.multiple_of((2 * number + at) * HD, HD), HD)],
                    out_sem.at[side, number],
                )
            )
            sent[-1].start()
        keys = part[:, :HD].astype(jnp.float32).T.astype(jnp.bfloat16)
        attention(part.at[:, TILE:], keys, part.at[:, HD:TILE], first_ref, out_buf.at[side])
        sent.append(
            pltpu.make_async_copy(
                out_buf.at[side],
                out_ref.at[:, pl.ds(pl.multiple_of(at * half, half), half)],
                out_sem.at[side, 2],
            )
        )
        sent[-1].start()
    for copy in sent:
        copy.wait()


def attend_all(flags, near, beside, back, other, first, cols):
    operands = [*near, *beside, *back, *other]
    rows = near[0].shape[0]
    in_hbm = pl.BlockSpec(memory_space=pltpu.HBM)
    return pl.pallas_call(
        functools.partial(attend_kernel, tuple(map(len, (near, beside, back, other)))),
        grid_spec=pltpu.PrefetchScalarGridSpec(
            num_scalar_prefetch=1,
            grid=(1,),
            in_specs=[in_hbm] * len(operands) + [pl.BlockSpec((rows, 1), lambda i, flags: (0, 0))],
            out_specs=[in_hbm] * 2,
            scratch_shapes=[
                pltpu.VMEM((2, rows, TILE + cols // 2), jnp.bfloat16),
                pltpu.VMEM((2, rows, cols // 2), jnp.bfloat16),
                pltpu.SemaphoreType.DMA((2, 3)),
                pltpu.SemaphoreType.DMA((2, 3)),
            ],
        ),
        out_shape=[
            jax.ShapeDtypeStruct((rows, cols), jnp.bfloat16),
            jax.ShapeDtypeStruct((rows, 2 * TILE), jnp.bfloat16),
        ],
        compiler_params=pltpu.CompilerParams(vmem_limit_bytes=40 * 2**20),
        cost_estimate=pl.CostEstimate(
            flops=4 * cols * rows * 3 * QROWS,
            bytes_accessed=6 * rows * cols,
            transcendentals=cols // HD * rows * 3 * QROWS,
        ),
    )(flags, *operands, first)


MIDDLE = (2, 3, 4, 5)
ENDS = (0, 1, 6, 7)


def after(value, *others):
    return lax.optimization_barrier((value,) + others)[0]


def pairs_from(sources, code):
    return [(s, s ^ code) for s in sources]


def middle_form(hidden, norm_gain, q_weight, q_bias, kv_weight, kv_bias, prefix_lens, assignment):
    tok_rows, features = hidden.shape
    slice_rows, q_cols = q_weight.shape
    half_cols = q_cols // 2
    group = lax.axis_index("group")
    tensor = lax.axis_index("tensor")
    y = group & 1
    is_middle = (group >= 2) & (group < 6)
    barrier = lax.optimization_barrier

    def over_group(value, sources, code):
        return lax.ppermute(value, "group", pairs_from(sources, code))

    def to_middle(value):
        return over_group(value, ENDS, 2)

    def across_middle(value):
        return over_group(value, MIDDLE, 6)

    def over_x(value):
        return lax.ppermute(value, "tensor", pairs_from(range(4), 2))

    def over_core(value):
        return lax.ppermute(value, "tensor", pairs_from(range(4), 1))

    begin, widths = (0, 2 * TILE, 4 * TILE), (2 * TILE, 2 * TILE, TILE)

    def columns(half, cuts, q_weight, kv_weight):
        head = (2 * tensor + half) * HD
        kv_part = lax.dynamic_slice_in_dim(kv_weight, head, HD, 2).reshape(slice_rows, TILE)
        taken, low = [], half * half_cols
        for number, wide in enumerate(cuts):
            wide = wide - (TILE if number == 0 else 0)
            part = lax.dynamic_slice_in_dim(q_weight, low, wide, 1)
            low = low + wide
            taken.append(jnp.concatenate([kv_part, part], axis=1) if number == 0 else part)
        return taken

    def both(one, two, chunk):
        low, high = begin[chunk], begin[chunk] + widths[chunk]
        return jnp.stack([one[:, low:high], two[:, low:high]])

    def pick(code_of_rows, codes):
        block = jnp.stack([group ^ code for code in codes])
        if code_of_rows == 0:
            return jnp.stack([block * 0, block])
        return jnp.stack([(block >> 1) ^ tensor, block & 1])

    first_codes, last_codes, beside_codes = (0, 1, 6, 7, 2, 3), (2, 3, 7, 4, 5), (0, 1, 6, 2, 3, 7, 4, 5)
    picks = {
        (sets, codes): jnp.stack([pick(c, codes) for c in sets])
        for sets, codes in (
            ((0, 2), first_codes),
            ((3,), first_codes),
            ((2, 3, 0), (4, 5)),
            ((2, 0, 3), (2, 3, 4, 5)),
            ((1,), beside_codes),
            ((2, 3, 1), last_codes),
            ((0,), last_codes),
        )
    }
    flags = jnp.stack([y, is_middle.astype(jnp.int32)])

    def closed(arriving, others):
        arrived = []
        for value in arriving:
            value, others = barrier((value, others))
            arrived.append(value)
        return barrier((tuple(arrived), others))

    (own,) = columns(y, (sum(widths),), q_weight, kv_weight)
    own, *later = barrier((own, q_weight, kv_weight))
    other, other2 = columns(1 - y, (begin[2], widths[2]), *later)
    m_own = across_middle(own)
    swap = over_group(other, range(8), 1)
    swap2 = over_group(other2, range(8), 1)
    quarter = norm(hidden, norm_gain, tensor, slice_rows, 2)
    end2 = to_middle(quarter)
    normed = norm(after(hidden, quarter), norm_gain, tensor * 0, slice_rows, features // slice_rows)

    bias = lax.dynamic_slice_in_dim(q_bias, y * half_cols, half_cols, 0)
    kv_bias_here = lax.dynamic_slice_in_dim(kv_bias, (2 * tensor + y) * HD, HD, 1)
    bias = jnp.concatenate([kv_bias_here[0], kv_bias_here[1], bias])[None, :]
    inverse_freq = THETA ** (-2.0 * jnp.arange(HD // 2, dtype=jnp.float32) / HD)
    m_swap = across_middle(after(swap, m_own))
    own, swap, m_own, normed, quarter, end2 = barrier((own, swap, m_own, normed, quarter, end2))

    rows_of = {0: [normed]}
    stack0, end2 = barrier((both(own, swap, 0), end2))
    e0 = to_middle(stack0)
    next1, next2 = both(own, swap, 1), jnp.stack([own[:, begin[2] :], swap2])
    end3 = over_group(end2, MIDDLE, 1)
    across2 = over_x(end2)
    twin2 = over_core(end2)
    tables = []
    for code in range(4):
        _, offset, places = token_layout(prefix_lens, assignment, group ^ code, tok_rows)
        angles = offset.astype(jnp.float32)[:, None] * inverse_freq[None, :]
        table = jnp.concatenate([jnp.cos(angles), jnp.sin(angles)], axis=1)
        tables.append((table, (places - offset)[:, None]))
    m_e0 = across_middle(after(e0, m_swap))
    biases = {
        chunks: bias[:, begin[chunks[0]] : begin[chunks[0]] + sum(widths[c] for c in chunks)]
        for chunks in ((0,), (1,), (2,), (0, 1))
    }
    (e0, m_swap, end3, across2, twin2), ready = closed(
        (e0, m_swap, end3, across2, twin2),
        (next1, next2, end2, tables, quarter, picks, biases, flags),
    )
    next1, next2, end2, tables, quarter, picks, biases, flags = ready

    places = {}

    def arrived(chunk, **codes):
        for code, (array, lead, skip) in codes.items():
            places[int(code[1:]), chunk] = (array, lead, skip)

    for chunk, low in enumerate(begin):
        arrived(chunk, c0=(own, None, low), c6=(m_own, None, low))
        if chunk < 2:
            arrived(chunk, c1=(swap, None, low), c7=(m_swap, None, low))
    arrived(2, c1=(swap2, None, 0))
    arrived(0, c2=(e0, 0, 0), c3=(e0, 1, 0))

    def call(sets, codes, chunks, totals=None, finish=None, skips=None):
        rows = [rows_of[c] for c in sets]
        pieces, limits = [], []
        for code in codes:
            there = [chunk for chunk in chunks if (code, chunk) in places]
            pieces.append([places[code, chunk] + (widths[chunk],) for chunk in there])
        for chunk in chunks:
            there = [(code, chunk) in places for code in codes]
            limits += [sum(there)] * (widths[chunk] // TILE)
            assert all(there[: sum(there)])
        return heads_of(rows, picks[sets, codes], pieces, tuple(limits), totals, finish, skips)

    outs, every = {}, (0, 1, 2)

    def first_sums(sets):
        return call(sets, first_codes, every)

    def finished(sets, chunks, codes, totals=None, opened=(), skips=None):
        wide = sum(widths[chunk] for chunk in chunks)
        finish = (wide, biases[chunks], [tables[c][0] for c in sets], chunks[0] == 0)
        made = call(sets, codes, chunks + opened, totals, finish, skips)
        for code, out in zip(sets, made):
            outs[code, chunks[0]] = out
        return made[-1]

    e1 = to_middle(next1)
    end1 = over_group(quarter, MIDDLE, 1)
    across3 = over_x(end3)
    far2 = over_core(across2)
    rows_of[2] = [end2, twin2, across2, far2]
    sums = dict(zip((0, 2), first_sums((0, 2))))
    m_e1 = across_middle(after(e1, m_e0))
    (m_e0, e1, end1, across3), (next2, e0, end3, far2, sums) = closed(
        (m_e0, e1, end1, across3), (next2, e0, end3, far2, sums)
    )
    rows_of[2] = [end2, twin2, across2, far2]

    e2 = to_middle(next2)
    across1 = over_x(end1)
    twin3 = over_core(end3)
    far3 = over_core(across3)
    rows_of[3] = [end3, twin3, across3, far3]

    def send_back(code, chunk):
        return over_group(outs[code, chunk], MIDDLE, code)

    arrived(1, c2=(e1, 0, 0), c3=(e1, 1, 0))
    (sums[3],) = first_sums((3,))
    arrived(0, c4=(m_e0, 0, 0), c5=(m_e0, 1, 0))
    three = (2, 3, 0)
    finished(three, (0,), (4, 5), ([sums[c] for c in three], (0, 0, 0)))
    back = {(2, 0): send_back(2, 0)}
    last = jnp.concatenate([swap2[None], e2])
    m_last = across_middle(after(last, m_e1))
    (last, m_e1, across1, back[2, 0]), (end1, made, sums) = closed(
        (last, m_e1, across1, back[2, 0]), (end1, [outs[c, 0] for c in three], sums)
    )
    for code, out in zip(three, made):
        outs[code, 0] = out

    twin1 = over_core(end1)
    far1 = over_core(across1)
    arrived(1, c4=(m_e1, 0, 0), c5=(m_e1, 1, 0))
    arrived(2, c2=(last, 1, 0), c3=(last, 2, 0))
    back[3, 0] = send_back(3, 0)
    three = (2, 0, 3)
    finished(
        three,
        (1,),
        (2, 3, 4, 5),
        ([sums[c] for c in three], (begin[1],) * 3),
        skips=(0, 0, 2),
    )
    for code in (2, 3):
        back[code, 1] = send_back(code, 1)
    far1, outs[2, 1] = barrier((far1, outs[2, 1]))
    rows_of[1] = [end1, twin1, across1, far1]
    sums[1] = finished((1,), (0, 1), beside_codes, opened=(2,))
    back[1, 0] = send_back(1, 0)
    (m_last, back[3, 0], back[2, 1]), (sums, outs[1, 0]) = closed(
        (m_last, back[3, 0], back[2, 1]), (sums, outs[1, 0])
    )

    arrived(2, c7=(m_last, 0, 0), c4=(m_last, 1, 0), c5=(m_last, 2, 0))
    three = (2, 3, 1)
    finished(
        three,
        (2,),
        last_codes,
        ([sums[c] for c in three], (begin[2], begin[2], 0)),
        skips=(0, 0, 2),
    )
    for code in (2, 3):
        back[code, 2] = send_back(code, 2)
    back[1, 2] = send_back(1, 2)
    sums[0], outs[1, 2], back[3, 1] = barrier((sums[0], outs[1, 2], back[3, 1]))
    finished((0,), (2,), last_codes, ([sums[0]], (begin[2],)))

    (back[2, 2], back[3, 2], back[1, 2]), _ = closed((back[2, 2], back[3, 2], back[1, 2]), ())
    context, cache = attend_all(
        flags,
        [outs[0, part] for part in every],
        [back[1, part] for part in (0, 2)],
        [back[2, part] for part in every],
        [back[3, part] for part in every],
        tables[0][1],
        q_cols,
    )
    return (context, cache.reshape(tok_rows, 2, TILE))


def solution(mesh):
    placed = (
        P("group", None),
        P(),
        P("group", "tensor"),
        P("tensor"),
        P("group", None, None),
        P(),
        P(),
        P(),
    )
    fits = mesh.shape["group"] == 8 and mesh.shape["tensor"] == 4
    return jax.shard_map(
        middle_form if fits else gathered_form,
        mesh=mesh,
        in_specs=placed,
        out_specs=(P("group", "tensor"), P("group", None, "tensor")),
        check_vma=False,
    )
```

```python
import functools
import math

import jax
import jax.numpy as jnp
from jax import lax
from jax.experimental import pallas as pl
from jax.experimental.pallas import tpu as pltpu
from jax.sharding import PartitionSpec as P

HD = 128


EPS = 1e-06
THETA = 1000000.0
QROWS = 128
MAXLEN = 256


def token_layout(prefix_lens, assignment, group_id, tok_rows):
    rollouts = prefix_lens.shape[0]
    member = assignment == group_id
    own_lens = jnp.where(member, prefix_lens, 0)
    starts = jnp.cumsum(own_lens) - own_lens
    places = jnp.arange(tok_rows, dtype=jnp.int32)
    inside = (
        member[None, :]
        & (places[:, None] >= starts[None, :])
        & (places[:, None] < (starts + own_lens)[None, :])
    )
    owner_id = jnp.sum(jnp.where(inside, jnp.arange(rollouts, dtype=jnp.int32)[None, :], 0), axis=1)
    offset = places - jnp.sum(jnp.where(inside, starts[None, :], 0), axis=1)
    return (owner_id, offset, places)


def rotate(values, offset):
    half_dim = values.shape[-1] // 2
    inverse_freq = THETA ** (-2.0 * jnp.arange(half_dim, dtype=jnp.float32) / values.shape[-1])
    angles = offset.astype(jnp.float32)[:, None] * inverse_freq[None, :]
    cosine = jnp.cos(angles)[:, None, :]
    sine_part = jnp.sin(angles)[:, None, :]
    first_half = values[..., :half_dim]
    second_half = values[..., half_dim:]
    return jnp.concatenate(
        [
            first_half * cosine - second_half * sine_part,
            second_half * cosine + first_half * sine_part,
        ],
        axis=-1,
    )


def add_product(normed, portion):
    return jnp.dot(normed, portion, preferred_element_type=jnp.float32)


def normalise(hidden, norm_gain):
    widened = hidden.astype(jnp.float32)
    return (
        widened * lax.rsqrt(jnp.mean(widened * widened, axis=-1, keepdims=True) + EPS) * norm_gain
    ).astype(jnp.bfloat16)


def gathered_form(
    hidden, norm_gain, q_weight, q_bias, kv_weight, kv_bias, prefix_lens, assignment
):
    tok_rows, features = hidden.shape
    slice_rows = kv_weight.shape[0]
    q_cols = q_weight.shape[1]
    kv_total = kv_weight.shape[2]
    heads_here = q_cols // HD
    tensor_pos = lax.axis_index("tensor")
    kv_cols = kv_total // lax.axis_size("tensor")
    normed = normalise(hidden, norm_gain)
    queries = add_product(normed, lax.all_gather(q_weight, "group", axis=0, tiled=True)) + q_bias
    head_span = max(kv_cols, HD)
    head_base = tensor_pos * kv_cols // head_span * head_span
    local_start = tensor_pos * kv_cols - head_base
    head_rows = lax.dynamic_slice_in_dim(kv_weight, head_base, head_span, 2).reshape(
        slice_rows, 2 * head_span
    )
    projected = add_product(normed, lax.all_gather(head_rows, "group", axis=0, tiled=True))
    projected = projected.reshape(tok_rows, 2, head_span) + lax.dynamic_slice_in_dim(
        kv_bias, head_base, head_span, 1
    )
    kv_here = head_span // HD
    group_size = heads_here // kv_here
    owner_id, offset, places = token_layout(
        prefix_lens, assignment, lax.axis_index("group"), tok_rows
    )
    rotated_queries = rotate(queries.reshape(tok_rows, heads_here, HD), offset).astype(jnp.bfloat16)
    rotated_keys = rotate(projected[:, 0].reshape(tok_rows, kv_here, HD), offset).astype(
        jnp.bfloat16
    )
    value_heads = projected[:, 1].reshape(tok_rows, kv_here, HD).astype(jnp.bfloat16)
    visible = (owner_id[:, None] == owner_id[None, :]) & (places[None, :] <= places[:, None])
    grouped = rotated_queries.reshape(tok_rows, kv_here, group_size, HD)
    scores = jnp.einsum(
        "qgph,kgh->gpqk", grouped, rotated_keys, preferred_element_type=jnp.float32
    ) / math.sqrt(HD)
    scores = jnp.where(visible[None, None], scores, -jnp.inf)
    row_max = jnp.max(scores, axis=-1, keepdims=True)
    exponent = jnp.exp(scores - row_max)
    weights_bf = (exponent / jnp.sum(exponent, axis=-1, keepdims=True)).astype(jnp.bfloat16)
    context = jnp.einsum(
        "gpqk,kgh->qgph", weights_bf, value_heads, preferred_element_type=jnp.float32
    )
    context = context.astype(jnp.bfloat16).reshape(tok_rows, q_cols)
    stacked = jnp.stack(
        [rotated_keys.reshape(tok_rows, head_span), value_heads.reshape(tok_rows, head_span)],
        axis=1,
    )
    kv_cache = lax.dynamic_slice_in_dim(stacked, local_start, kv_cols, 2)
    return (context, kv_cache)


def norm_kernel(part_ref, hidden_ref, gain_ref, out_ref):
    widened = hidden_ref[...].astype(jnp.float32)
    scale = lax.rsqrt(jnp.mean(widened * widened, axis=-1, keepdims=True) + EPS)
    count, _, depth = out_ref.shape
    for block in range(count):
        at = pl.multiple_of((part_ref[0] * count + block) * depth, depth)
        taken = hidden_ref[:, pl.ds(at, depth)].astype(jnp.float32)
        out_ref[block] = (taken * scale * gain_ref[:, pl.ds(at, depth)]).astype(jnp.bfloat16)


def norm(hidden, norm_gain, part, depth, count):
    rows, features = hidden.shape
    step = QROWS
    return pl.pallas_call(
        norm_kernel,
        grid_spec=pltpu.PrefetchScalarGridSpec(
            num_scalar_prefetch=1,
            grid=(rows // step,),
            in_specs=[
                pl.BlockSpec((step, features), lambda i, part: (i, 0)),
                pl.BlockSpec((1, features), lambda i, part: (0, 0)),
            ],
            out_specs=pl.BlockSpec((count, step, depth), lambda i, part: (0, i, 0)),
        ),
        out_shape=pltpu.HBM((count, rows, depth), jnp.bfloat16),
        compiler_params=pltpu.CompilerParams(vmem_limit_bytes=60 * 2**20),
        cost_estimate=pl.CostEstimate(
            flops=4 * rows * features,
            bytes_accessed=2 * rows * (features + count * depth),
            transcendentals=rows,
        ),
    )(part[None], hidden, norm_gain[None])


TILE = 2 * HD


def turn(value, cosine, sine):
    return value * cosine + pltpu.roll(value, HD // 2, 1) * sine


def heads_kernel(plan, pick_ref, *refs):
    sources, skips, parts, limits, width, closed_width, totals_at, with_keys = plan
    finish = closed_width > 0
    sets, count = len(sources), len(parts)
    refs = list(refs)

    def take(number):
        taken = refs[:number]
        del refs[:number]
        return taken

    row_refs = [take(number) for number in sources]
    weight_refs = [take(len(part)) for part in parts]
    total_refs = take(sets) if totals_at is not None else None
    if finish:
        (bias_ref,) = take(1)
        table_refs = take(sets)
    outs = take(sets)
    sum_outs = take(sets) if finish and closed_width < width else None
    row_buf, weight_buf, acc, row_sem, weight_sem, total_sem, out_sem = take(7)
    depth = row_buf.shape[2] // count

    def weight_copies(piece):
        column = 0
        for part, (ref, (lead, skip, wide)) in enumerate(zip(weight_refs[piece], parts[piece])):
            ref = ref if lead is None else ref.at[lead]
            yield pltpu.make_async_copy(
                ref.at[:, skip : skip + wide],
                weight_buf.at[piece * depth : (piece + 1) * depth, column : column + wide],
                weight_sem.at[piece, part],
            )
            column += wide

    def row_copy(which, piece, source):
        return pltpu.make_async_copy(
            row_refs[which][source].at[pick_ref[which, 1, piece]],
            row_buf.at[which, :, piece * depth : (piece + 1) * depth],
            row_sem.at[which, piece],
        )

    def total_copy(which):
        return pltpu.make_async_copy(
            total_refs[which].at[:, totals_at[which] : totals_at[which] + width],
            acc.at[which],
            total_sem.at[which],
        )

    stages = [(0, low, min(low + 2, count)) for low in range(0, count, 2)]
    stages += [(which, skips[which], count) for which in range(1, sets)]

    def start(stage):
        which, low, high = stages[stage]
        for piece in range(low, high):
            if which == 0:
                for copy in weight_copies(piece):
                    copy.start()
            if sources[which] == 1:
                row_copy(which, piece, 0).start()
            else:
                for source in range(sources[which]):

                    @pl.when(pick_ref[which, 0, piece] == source)
                    def _():
                        row_copy(which, piece, source).start()
        if low == skips[which] and total_refs is not None:
            total_copy(which).start()

    start(0)
    if len(stages) > 1:
        start(1)
    if finish:
        bias_buf, table_buf, out_buf, side_sem = refs
        side_copies = [pltpu.make_async_copy(bias_ref, bias_buf, side_sem.at[sets])]
        side_copies += [
            pltpu.make_async_copy(table_refs[which], table_buf.at[which], side_sem.at[which])
            for which in range(sets)
        ]

    def out_copies(which):
        pairs = [((out_buf if finish else acc).at[which], outs[which])]
        if sum_outs is not None:
            pairs.append((acc.at[which, :, closed_width:], sum_outs[which]))
        return [
            pltpu.make_async_copy(buf, ref, out_sem.at[which, number])
            for number, (buf, ref) in enumerate(pairs)
        ]

    for stage, (which, low, high) in enumerate(stages):
        for piece in range(low, high):
            if which == 0:
                for copy in weight_copies(piece):
                    copy.wait()
            row_copy(which, piece, 0).wait()
        if low == skips[which] and total_refs is not None:
            total_copy(which).wait()
        if stage + 2 < len(stages):
            start(stage + 2)
        if stage == 0 and finish:
            for copy in side_copies:
                copy.start()
        for at in range(0, width, TILE):
            top = min(high, limits[at // TILE])
            if top <= low:
                continue
            cols = slice(at, at + TILE)
            term = jnp.dot(
                row_buf[which, :, low * depth : top * depth],
                weight_buf[low * depth : top * depth, cols],
                preferred_element_type=jnp.float32,
            )
            if low > skips[which] or total_refs is not None:
                term = acc[which, :, cols] + term
            acc[which, :, cols] = term
        if high < count:
            continue
        if finish:
            if which == 0:
                side_copies[0].wait()
            side_copies[1 + which].wait()
            finish_set(acc.at[which], bias_buf, table_buf[which], out_buf.at[which], with_keys)
        for copy in out_copies(which):
            copy.start()
    for which in range(sets):
        for copy in out_copies(which):
            copy.wait()


def finish_set(acc, bias, table, out, with_keys):
    swapped = pltpu.roll(table, HD // 2, 1)
    left = lax.broadcasted_iota(jnp.int32, table.shape, 1) < HD // 2
    cosine = jnp.where(left, table, swapped)
    sine = jnp.where(left, -swapped, table)
    for col in range(0, out.shape[1], HD):
        cols = slice(col, col + HD)
        value = acc[:, cols] + bias[:, cols]
        if not (with_keys and col == HD):
            value = turn(value, cosine, sine)
        out[:, cols] = value.astype(jnp.bfloat16)


def heads_of(row_sets, picks, pieces, limits, totals=None, finish=None, skips=None):
    sets, count = len(row_sets), len(pieces)
    skips = skips or (0,) * sets
    width = len(limits) * TILE
    sources = tuple(len(rows) for rows in row_sets)
    tokens, depth = row_sets[0][0].shape[1:]
    operands = [array for rows in row_sets for array in rows]
    operands += [array for piece in pieces for array, *_ in piece]
    totals_at = None
    if totals is not None:
        totals, totals_at = totals
        operands += totals
    scratch = [
        pltpu.VMEM((sets, tokens, count * depth), jnp.bfloat16),
        pltpu.VMEM((count * depth, width), jnp.bfloat16),
        pltpu.VMEM((sets, tokens, width), jnp.float32),
        pltpu.SemaphoreType.DMA((sets, count)),
        pltpu.SemaphoreType.DMA((count, max(map(len, pieces)))),
        pltpu.SemaphoreType.DMA((sets,)),
        pltpu.SemaphoreType.DMA((sets, 3)),
    ]
    with_keys, closed_width = False, 0
    out_shape = [jax.ShapeDtypeStruct((tokens, width), jnp.float32)] * sets
    if finish is not None:
        closed_width, bias, tables, with_keys = finish
        out_shape = [jax.ShapeDtypeStruct((tokens, closed_width), jnp.bfloat16)] * sets
        operands += [bias, *tables]
        if closed_width < width:
            out_shape += [jax.ShapeDtypeStruct((tokens, width - closed_width), jnp.float32)] * sets
        scratch += [
            pltpu.VMEM((1, closed_width), jnp.float32),
            pltpu.VMEM((sets, tokens, HD), jnp.float32),
            pltpu.VMEM((sets, tokens, closed_width), jnp.bfloat16),
            pltpu.SemaphoreType.DMA((sets + 1,)),
        ]
    plan = (
        sources,
        skips,
        tuple(tuple(part[1:] for part in piece) for piece in pieces),
        limits,
        width,
        closed_width,
        totals_at,
        with_keys,
    )
    anywhere = pl.BlockSpec(memory_space=pl.ANY)
    return pl.pallas_call(
        functools.partial(heads_kernel, plan),
        grid_spec=pltpu.PrefetchScalarGridSpec(
            num_scalar_prefetch=1,
            grid=(1,),
            in_specs=[anywhere] * len(operands),
            out_specs=[pl.BlockSpec(memory_space=pltpu.HBM)] * len(out_shape),
            scratch_shapes=scratch,
        ),
        out_shape=out_shape,
        compiler_params=pltpu.CompilerParams(vmem_limit_bytes=56 * 2**20),
        cost_estimate=pl.CostEstimate(
            flops=2 * sets * count * tokens * depth * width,
            bytes_accessed=2 * count * depth * (sets * tokens + width) + 8 * sets * tokens * width,
            transcendentals=0,
        ),
    )(picks, *operands)


def attention(queries, keys, values, first_ref, out_ref):
    rows, cols = out_ref.shape
    heads = cols // HD
    scale = math.log2(math.e) / math.sqrt(HD)
    for top in range(0, rows, QROWS):
        low, end = max(0, top - MAXLEN), top + QROWS
        shape = (QROWS, end - low)
        stacked = jnp.concatenate(
            [queries[top:end, col : col + HD] for col in range(0, cols, HD)], axis=0
        )
        scores = jnp.dot(stacked, keys[:, low:end], preferred_element_type=jnp.float32)
        row = lax.broadcasted_iota(jnp.int32, shape, 0) + top
        col = lax.broadcasted_iota(jnp.int32, shape, 1) + low
        visible = (col <= row) & (col >= first_ref[top:end])
        scores = jnp.where(visible[None], scores.reshape(heads, *shape), -jnp.inf)
        most = jnp.max(scores, axis=-1, keepdims=True)
        exponent = jnp.exp2((scores - most) * scale)
        share = 1.0 / jnp.sum(exponent, axis=-1, keepdims=True)
        weights = (exponent * share).astype(jnp.bfloat16)
        context = jnp.dot(
            weights.reshape(heads * QROWS, end - low),
            values[low:end],
            preferred_element_type=jnp.float32,
        ).astype(jnp.bfloat16)
        for head in range(heads):
            out_ref[top:end, head * HD : (head + 1) * HD] = context[
                head * QROWS : (head + 1) * QROWS
            ]


def attend_kernel(numbers, flag_ref, *refs):
    ends = [sum(numbers[: i + 1]) for i in range(4)]
    near, beside, back, other = (refs[end - number : end] for end, number in zip(ends, numbers))
    first_ref, out_ref, cache_ref, part_buf, out_buf, in_sem, out_sem = refs[ends[-1] :]
    half = out_buf.shape[2]

    def copies(side, sources):
        column = 0
        for part, source in enumerate(sources):
            wide = source.shape[1]
            yield pltpu.make_async_copy(
                source, part_buf.at[side, :, column : column + wide], in_sem.at[side, part]
            )
            column += wide

    def on_parts(act):
        for middle, sides in ((1, (near, beside)), (0, (back, other))):

            @pl.when(flag_ref[1] == middle)
            def _():
                for side, sources in enumerate(sides):
                    for copy in copies(side, sources):
                        act(copy)

    on_parts(lambda copy: copy.start())
    on_parts(lambda copy: copy.wait())
    sent = []
    for side in range(2):
        at = flag_ref[0] if side == 0 else 1 - flag_ref[0]
        part = part_buf.at[side]
        for number in range(2):
            sent.append(
                pltpu.make_async_copy(
                    part.at[:, number * HD : (number + 1) * HD],
                    cache_ref.at[:, pl.ds(pl.multiple_of((2 * number + at) * HD, HD), HD)],
                    out_sem.at[side, number],
                )
            )
            sent[-1].start()
        keys = part[:, :HD].astype(jnp.float32).T.astype(jnp.bfloat16)
        attention(part.at[:, TILE:], keys, part.at[:, HD:TILE], first_ref, out_buf.at[side])
        sent.append(
            pltpu.make_async_copy(
                out_buf.at[side],
                out_ref.at[:, pl.ds(pl.multiple_of(at * half, half), half)],
                out_sem.at[side, 2],
            )
        )
        sent[-1].start()
    for copy in sent:
        copy.wait()


def attend_all(flags, near, beside, back, other, first, cols):
    operands = [*near, *beside, *back, *other]
    rows = near[0].shape[0]
    in_hbm = pl.BlockSpec(memory_space=pltpu.HBM)
    return pl.pallas_call(
        functools.partial(attend_kernel, tuple(map(len, (near, beside, back, other)))),
        grid_spec=pltpu.PrefetchScalarGridSpec(
            num_scalar_prefetch=1,
            grid=(1,),
            in_specs=[in_hbm] * len(operands) + [pl.BlockSpec((rows, 1), lambda i, flags: (0, 0))],
            out_specs=[in_hbm] * 2,
            scratch_shapes=[
                pltpu.VMEM((2, rows, TILE + cols // 2), jnp.bfloat16),
                pltpu.VMEM((2, rows, cols // 2), jnp.bfloat16),
                pltpu.SemaphoreType.DMA((2, 3)),
                pltpu.SemaphoreType.DMA((2, 3)),
            ],
        ),
        out_shape=[
            jax.ShapeDtypeStruct((rows, cols), jnp.bfloat16),
            jax.ShapeDtypeStruct((rows, 2 * TILE), jnp.bfloat16),
        ],
        compiler_params=pltpu.CompilerParams(vmem_limit_bytes=40 * 2**20),
        cost_estimate=pl.CostEstimate(
            flops=4 * cols * rows * 3 * QROWS,
            bytes_accessed=6 * rows * cols,
            transcendentals=cols // HD * rows * 3 * QROWS,
        ),
    )(flags, *operands, first)


MIDDLE = (2, 3, 4, 5)
ENDS = (0, 1, 6, 7)


def after(value, *others):
    return lax.optimization_barrier((value,) + others)[0]


def pairs_from(sources, code):
    return [(s, s ^ code) for s in sources]


def middle_form(hidden, norm_gain, q_weight, q_bias, kv_weight, kv_bias, prefix_lens, assignment):
    tok_rows, features = hidden.shape
    slice_rows, q_cols = q_weight.shape
    half_cols = q_cols // 2
    group = lax.axis_index("group")
    tensor = lax.axis_index("tensor")
    y = group & 1
    is_middle = (group >= 2) & (group < 6)
    barrier = lax.optimization_barrier

    def over_group(value, sources, code):
        return lax.ppermute(value, "group", pairs_from(sources, code))

    def to_middle(value):
        return over_group(value, ENDS, 2)

    def across_middle(value):
        return over_group(value, MIDDLE, 6)

    def over_x(value):
        return lax.ppermute(value, "tensor", pairs_from(range(4), 2))

    def over_core(value):
        return lax.ppermute(value, "tensor", pairs_from(range(4), 1))

    begin, widths = (0, 2 * TILE, 4 * TILE), (2 * TILE, 2 * TILE, TILE)

    def columns(half, cuts):
        head = (2 * tensor + half) * HD
        kv_part = lax.dynamic_slice_in_dim(kv_weight, head, HD, 2).reshape(slice_rows, TILE)
        taken, low = [], half * half_cols
        for number, wide in enumerate(cuts):
            wide = wide - (TILE if number == 0 else 0)
            part = lax.dynamic_slice_in_dim(q_weight, low, wide, 1)
            low = low + wide
            taken.append(jnp.concatenate([kv_part, part], axis=1) if number == 0 else part)
        return taken

    def both(one, two, chunk):
        low, high = begin[chunk], begin[chunk] + widths[chunk]
        return jnp.stack([one[:, low:high], two[:, low:high]])

    def pick(code_of_rows, codes):
        block = jnp.stack([group ^ code for code in codes])
        if code_of_rows == 0:
            return jnp.stack([block * 0, block])
        return jnp.stack([(block >> 1) ^ tensor, block & 1])

    first_codes, last_codes, beside_codes = (0, 1, 6, 7, 2, 3), (2, 3, 7, 4, 5), (0, 1, 6, 2, 3, 7, 4, 5)
    picks = {
        (sets, codes): jnp.stack([pick(c, codes) for c in sets])
        for sets, codes in (
            ((0, 2), first_codes),
            ((3,), first_codes),
            ((2, 3, 0), (4, 5)),
            ((2, 0, 3), (2, 3, 4, 5)),
            ((1,), beside_codes),
            ((2, 3, 1), last_codes),
            ((0,), last_codes),
        )
    }
    flags = jnp.stack([y, is_middle.astype(jnp.int32)])

    def closed(arriving, others):
        arrived = []
        for value in arriving:
            value, others = barrier((value, others))
            arrived.append(value)
        return barrier((tuple(arrived), others))

    (own,) = columns(y, (sum(widths),))
    other, other2 = columns(1 - y, (begin[2], widths[2]))
    m_own = across_middle(own)
    swap = over_group(other, range(8), 1)
    swap2 = over_group(other2, range(8), 1)
    quarter = norm(hidden, norm_gain, tensor, slice_rows, 2)
    end2 = to_middle(quarter)
    normed = norm(after(hidden, quarter), norm_gain, tensor * 0, slice_rows, features // slice_rows)

    bias = lax.dynamic_slice_in_dim(q_bias, y * half_cols, half_cols, 0)
    kv_bias_here = lax.dynamic_slice_in_dim(kv_bias, (2 * tensor + y) * HD, HD, 1)
    bias = jnp.concatenate([kv_bias_here[0], kv_bias_here[1], bias])[None, :]
    inverse_freq = THETA ** (-2.0 * jnp.arange(HD // 2, dtype=jnp.float32) / HD)
    m_swap = across_middle(after(swap, m_own))
    own, swap, m_own, normed, quarter, end2 = barrier((own, swap, m_own, normed, quarter, end2))

    rows_of = {0: [normed]}
    stack0, end2 = barrier((both(own, swap, 0), end2))
    e0 = to_middle(stack0)
    next1, next2 = both(own, swap, 1), jnp.stack([own[:, begin[2] :], swap2])
    end3 = over_group(end2, MIDDLE, 1)
    across2 = over_x(end2)
    twin2 = over_core(end2)
    tables = []
    for code in range(4):
        _, offset, places = token_layout(prefix_lens, assignment, group ^ code, tok_rows)
        angles = offset.astype(jnp.float32)[:, None] * inverse_freq[None, :]
        table = jnp.concatenate([jnp.cos(angles), jnp.sin(angles)], axis=1)
        tables.append((table, (places - offset)[:, None]))
    m_e0 = across_middle(after(e0, m_swap))
    biases = {
        chunks: bias[:, begin[chunks[0]] : begin[chunks[0]] + sum(widths[c] for c in chunks)]
        for chunks in ((0,), (1,), (2,), (0, 1))
    }
    (e0, m_swap, end3, across2, twin2), ready = closed(
        (e0, m_swap, end3, across2, twin2),
        (next1, next2, end2, tables, quarter),
    )
    next1, next2, end2, tables, quarter = ready

    places = {}

    def arrived(chunk, **codes):
        for code, (array, lead, skip) in codes.items():
            places[int(code[1:]), chunk] = (array, lead, skip)

    for chunk, low in enumerate(begin):
        arrived(chunk, c0=(own, None, low), c6=(m_own, None, low))
        if chunk < 2:
            arrived(chunk, c1=(swap, None, low), c7=(m_swap, None, low))
    arrived(2, c1=(swap2, None, 0))
    arrived(0, c2=(e0, 0, 0), c3=(e0, 1, 0))

    def call(sets, codes, chunks, totals=None, finish=None, skips=None):
        rows = [rows_of[c] for c in sets]
        pieces, limits = [], []
        for code in codes:
            there = [chunk for chunk in chunks if (code, chunk) in places]
            pieces.append([places[code, chunk] + (widths[chunk],) for chunk in there])
        for chunk in chunks:
            there = [(code, chunk) in places for code in codes]
            limits += [sum(there)] * (widths[chunk] // TILE)
            assert all(there[: sum(there)])
        return heads_of(rows, picks[sets, codes], pieces, tuple(limits), totals, finish, skips)

    outs, every = {}, (0, 1, 2)

    def first_sums(sets):
        return call(sets, first_codes, every)

    def finished(sets, chunks, codes, totals=None, opened=(), skips=None):
        wide = sum(widths[chunk] for chunk in chunks)
        finish = (wide, biases[chunks], [tables[c][0] for c in sets], chunks[0] == 0)
        made = call(sets, codes, chunks + opened, totals, finish, skips)
        for code, out in zip(sets, made):
            outs[code, chunks[0]] = out
        return made[-1]

    e1 = to_middle(next1)
    end1 = over_group(quarter, MIDDLE, 1)
    across3 = over_x(end3)
    far2 = over_core(across2)
    rows_of[2] = [end2, twin2, across2, far2]
    sums = dict(zip((0, 2), first_sums((0, 2))))
    m_e1 = across_middle(after(e1, m_e0))
    (m_e0, e1, end1, across3), ready = closed(
        (m_e0, e1, end1, across3), (next2, e0, end3, far2, sums, picks, biases, flags)
    )
    next2, e0, end3, far2, sums, picks, biases, flags = ready
    rows_of[2] = [end2, twin2, across2, far2]

    e2 = to_middle(next2)
    across1 = over_x(end1)
    twin3 = over_core(end3)
    far3 = over_core(across3)
    rows_of[3] = [end3, twin3, across3, far3]

    def send_back(code, chunk):
        return over_group(outs[code, chunk], MIDDLE, code)

    arrived(1, c2=(e1, 0, 0), c3=(e1, 1, 0))
    (sums[3],) = first_sums((3,))
    arrived(0, c4=(m_e0, 0, 0), c5=(m_e0, 1, 0))
    three = (2, 3, 0)
    finished(three, (0,), (4, 5), ([sums[c] for c in three], (0, 0, 0)))
    back = {(2, 0): send_back(2, 0)}
    last = jnp.concatenate([swap2[None], e2])
    m_last = across_middle(after(last, m_e1))
    (last, m_e1, across1, back[2, 0]), (end1, made, sums) = closed(
        (last, m_e1, across1, back[2, 0]), (end1, [outs[c, 0] for c in three], sums)
    )
    for code, out in zip(three, made):
        outs[code, 0] = out

    twin1 = over_core(end1)
    far1 = over_core(across1)
    arrived(1, c4=(m_e1, 0, 0), c5=(m_e1, 1, 0))
    arrived(2, c2=(last, 1, 0), c3=(last, 2, 0))
    back[3, 0] = send_back(3, 0)
    three = (2, 0, 3)
    finished(
        three,
        (1,),
        (2, 3, 4, 5),
        ([sums[c] for c in three], (begin[1],) * 3),
        skips=(0, 0, 2),
    )
    for code in (2, 3):
        back[code, 1] = send_back(code, 1)
    far1, outs[2, 1] = barrier((far1, outs[2, 1]))
    rows_of[1] = [end1, twin1, across1, far1]
    sums[1] = finished((1,), (0, 1), beside_codes, opened=(2,))
    back[1, 0] = send_back(1, 0)
    (m_last, back[3, 0], back[2, 1]), (sums, outs[1, 0]) = closed(
        (m_last, back[3, 0], back[2, 1]), (sums, outs[1, 0])
    )

    arrived(2, c7=(m_last, 0, 0), c4=(m_last, 1, 0), c5=(m_last, 2, 0))
    three = (2, 3, 1)
    finished(
        three,
        (2,),
        last_codes,
        ([sums[c] for c in three], (begin[2], begin[2], 0)),
        skips=(0, 0, 2),
    )
    for code in (2, 3):
        back[code, 2] = send_back(code, 2)
    back[1, 2] = send_back(1, 2)
    sums[0], outs[1, 2], back[3, 1] = barrier((sums[0], outs[1, 2], back[3, 1]))
    finished((0,), (2,), last_codes, ([sums[0]], (begin[2],)))

    (back[2, 2], back[3, 2], back[1, 2]), _ = closed((back[2, 2], back[3, 2], back[1, 2]), ())
    context, cache = attend_all(
        flags,
        [outs[0, part] for part in every],
        [back[1, part] for part in (0, 2)],
        [back[2, part] for part in every],
        [back[3, part] for part in every],
        tables[0][1],
        q_cols,
    )
    return (context, cache.reshape(tok_rows, 2, TILE))


def solution(mesh):
    placed = (
        P("group", None),
        P(),
        P("group", "tensor"),
        P("tensor"),
        P("group", None, None),
        P(),
        P(),
        P(),
    )
    fits = mesh.shape["group"] == 8 and mesh.shape["tensor"] == 4
    return jax.shard_map(
        middle_form if fits else gathered_form,
        mesh=mesh,
        in_specs=placed,
        out_specs=(P("group", "tensor"), P("group", None, "tensor")),
        check_vma=False,
    )
```

```python
import functools
import math

import jax
import jax.numpy as jnp
from jax import lax
from jax.experimental import pallas as pl
from jax.experimental.pallas import tpu as pltpu
from jax.sharding import PartitionSpec as P

HD = 128


EPS = 1e-06
THETA = 1000000.0
QROWS = 128
MAXLEN = 256


def token_layout(prefix_lens, assignment, group_id, tok_rows):
    rollouts = prefix_lens.shape[0]
    member = assignment == group_id
    own_lens = jnp.where(member, prefix_lens, 0)
    starts = jnp.cumsum(own_lens) - own_lens
    places = jnp.arange(tok_rows, dtype=jnp.int32)
    inside = (
        member[None, :]
        & (places[:, None] >= starts[None, :])
        & (places[:, None] < (starts + own_lens)[None, :])
    )
    owner_id = jnp.sum(jnp.where(inside, jnp.arange(rollouts, dtype=jnp.int32)[None, :], 0), axis=1)
    offset = places - jnp.sum(jnp.where(inside, starts[None, :], 0), axis=1)
    return (owner_id, offset, places)


def rotate(values, offset):
    half_dim = values.shape[-1] // 2
    inverse_freq = THETA ** (-2.0 * jnp.arange(half_dim, dtype=jnp.float32) / values.shape[-1])
    angles = offset.astype(jnp.float32)[:, None] * inverse_freq[None, :]
    cosine = jnp.cos(angles)[:, None, :]
    sine_part = jnp.sin(angles)[:, None, :]
    first_half = values[..., :half_dim]
    second_half = values[..., half_dim:]
    return jnp.concatenate(
        [
            first_half * cosine - second_half * sine_part,
            second_half * cosine + first_half * sine_part,
        ],
        axis=-1,
    )


def add_product(normed, portion):
    return jnp.dot(normed, portion, preferred_element_type=jnp.float32)


def normalise(hidden, norm_gain):
    widened = hidden.astype(jnp.float32)
    return (
        widened * lax.rsqrt(jnp.mean(widened * widened, axis=-1, keepdims=True) + EPS) * norm_gain
    ).astype(jnp.bfloat16)


def gathered_form(
    hidden, norm_gain, q_weight, q_bias, kv_weight, kv_bias, prefix_lens, assignment
):
    tok_rows, features = hidden.shape
    slice_rows = kv_weight.shape[0]
    q_cols = q_weight.shape[1]
    kv_total = kv_weight.shape[2]
    heads_here = q_cols // HD
    tensor_pos = lax.axis_index("tensor")
    kv_cols = kv_total // lax.axis_size("tensor")
    normed = normalise(hidden, norm_gain)
    queries = add_product(normed, lax.all_gather(q_weight, "group", axis=0, tiled=True)) + q_bias
    head_span = max(kv_cols, HD)
    head_base = tensor_pos * kv_cols // head_span * head_span
    local_start = tensor_pos * kv_cols - head_base
    head_rows = lax.dynamic_slice_in_dim(kv_weight, head_base, head_span, 2).reshape(
        slice_rows, 2 * head_span
    )
    projected = add_product(normed, lax.all_gather(head_rows, "group", axis=0, tiled=True))
    projected = projected.reshape(tok_rows, 2, head_span) + lax.dynamic_slice_in_dim(
        kv_bias, head_base, head_span, 1
    )
    kv_here = head_span // HD
    group_size = heads_here // kv_here
    owner_id, offset, places = token_layout(
        prefix_lens, assignment, lax.axis_index("group"), tok_rows
    )
    rotated_queries = rotate(queries.reshape(tok_rows, heads_here, HD), offset).astype(jnp.bfloat16)
    rotated_keys = rotate(projected[:, 0].reshape(tok_rows, kv_here, HD), offset).astype(
        jnp.bfloat16
    )
    value_heads = projected[:, 1].reshape(tok_rows, kv_here, HD).astype(jnp.bfloat16)
    visible = (owner_id[:, None] == owner_id[None, :]) & (places[None, :] <= places[:, None])
    grouped = rotated_queries.reshape(tok_rows, kv_here, group_size, HD)
    scores = jnp.einsum(
        "qgph,kgh->gpqk", grouped, rotated_keys, preferred_element_type=jnp.float32
    ) / math.sqrt(HD)
    scores = jnp.where(visible[None, None], scores, -jnp.inf)
    row_max = jnp.max(scores, axis=-1, keepdims=True)
    exponent = jnp.exp(scores - row_max)
    weights_bf = (exponent / jnp.sum(exponent, axis=-1, keepdims=True)).astype(jnp.bfloat16)
    context = jnp.einsum(
        "gpqk,kgh->qgph", weights_bf, value_heads, preferred_element_type=jnp.float32
    )
    context = context.astype(jnp.bfloat16).reshape(tok_rows, q_cols)
    stacked = jnp.stack(
        [rotated_keys.reshape(tok_rows, head_span), value_heads.reshape(tok_rows, head_span)],
        axis=1,
    )
    kv_cache = lax.dynamic_slice_in_dim(stacked, local_start, kv_cols, 2)
    return (context, kv_cache)


def norm_kernel(part_ref, hidden_ref, gain_ref, out_ref):
    widened = hidden_ref[...].astype(jnp.float32)
    scale = lax.rsqrt(jnp.mean(widened * widened, axis=-1, keepdims=True) + EPS)
    count, _, depth = out_ref.shape
    for block in range(count):
        at = pl.multiple_of((part_ref[0] * count + block) * depth, depth)
        taken = hidden_ref[:, pl.ds(at, depth)].astype(jnp.float32)
        out_ref[block] = (taken * scale * gain_ref[:, pl.ds(at, depth)]).astype(jnp.bfloat16)


def norm(hidden, norm_gain, part, depth, count):
    rows, features = hidden.shape
    step = QROWS
    return pl.pallas_call(
        norm_kernel,
        grid_spec=pltpu.PrefetchScalarGridSpec(
            num_scalar_prefetch=1,
            grid=(rows // step,),
            in_specs=[
                pl.BlockSpec((step, features), lambda i, part: (i, 0)),
                pl.BlockSpec((1, features), lambda i, part: (0, 0)),
            ],
            out_specs=pl.BlockSpec((count, step, depth), lambda i, part: (0, i, 0)),
        ),
        out_shape=pltpu.HBM((count, rows, depth), jnp.bfloat16),
        compiler_params=pltpu.CompilerParams(vmem_limit_bytes=60 * 2**20),
        cost_estimate=pl.CostEstimate(
            flops=4 * rows * features,
            bytes_accessed=2 * rows * (features + count * depth),
            transcendentals=rows,
        ),
    )(part[None], hidden, norm_gain[None])


TILE = 2 * HD


def turn(value, cosine, sine):
    return value * cosine + pltpu.roll(value, HD // 2, 1) * sine


def heads_kernel(plan, pick_ref, *refs):
    sources, skips, parts, limits, width, closed_width, totals_at, with_keys = plan
    finish = closed_width > 0
    sets, count = len(sources), len(parts)
    refs = list(refs)

    def take(number):
        taken = refs[:number]
        del refs[:number]
        return taken

    row_refs = [take(number) for number in sources]
    weight_refs = [take(len(part)) for part in parts]
    total_refs = take(sets) if totals_at is not None else None
    if finish:
        (bias_ref,) = take(1)
        table_refs = take(sets)
    outs = take(sets)
    sum_outs = take(sets) if finish and closed_width < width else None
    row_buf, weight_buf, acc, row_sem, weight_sem, total_sem, out_sem = take(7)
    depth = row_buf.shape[2] // count

    def weight_copies(piece):
        column = 0
        for part, (ref, (lead, skip, wide)) in enumerate(zip(weight_refs[piece], parts[piece])):
            ref = ref if lead is None else ref.at[lead]
            yield pltpu.make_async_copy(
                ref.at[:, skip : skip + wide],
                weight_buf.at[piece * depth : (piece + 1) * depth, column : column + wide],
                weight_sem.at[piece, part],
            )
            column += wide

    def row_copy(which, piece, source):
        return pltpu.make_async_copy(
            row_refs[which][source].at[pick_ref[which, 1, piece]],
            row_buf.at[which, :, piece * depth : (piece + 1) * depth],
            row_sem.at[which, piece],
        )

    def total_copy(which):
        return pltpu.make_async_copy(
            total_refs[which].at[:, totals_at[which] : totals_at[which] + width],
            acc.at[which],
            total_sem.at[which],
        )

    stages = [(0, low, min(low + 2, count)) for low in range(0, count, 2)]
    stages += [(which, skips[which], count) for which in range(1, sets)]

    def start(stage):
        which, low, high = stages[stage]
        for piece in range(low, high):
            if which == 0:
                for copy in weight_copies(piece):
                    copy.start()
            if sources[which] == 1:
                row_copy(which, piece, 0).start()
            else:
                for source in range(sources[which]):

                    @pl.when(pick_ref[which, 0, piece] == source)
                    def _():
                        row_copy(which, piece, source).start()
        if low == skips[which] and total_refs is not None:
            total_copy(which).start()

    start(0)
    if len(stages) > 1:
        start(1)
    if finish:
        bias_buf, table_buf, out_buf, side_sem = refs
        side_copies = [pltpu.make_async_copy(bias_ref, bias_buf, side_sem.at[sets])]
        side_copies += [
            pltpu.make_async_copy(table_refs[which], table_buf.at[which], side_sem.at[which])
            for which in range(sets)
        ]

    def out_copies(which):
        pairs = [((out_buf if finish else acc).at[which], outs[which])]
        if sum_outs is not None:
            pairs.append((acc.at[which, :, closed_width:], sum_outs[which]))
        return [
            pltpu.make_async_copy(buf, ref, out_sem.at[which, number])
            for number, (buf, ref) in enumerate(pairs)
        ]

    for stage, (which, low, high) in enumerate(stages):
        for piece in range(low, high):
            if which == 0:
                for copy in weight_copies(piece):
                    copy.wait()
            row_copy(which, piece, 0).wait()
        if low == skips[which] and total_refs is not None:
            total_copy(which).wait()
        if stage + 2 < len(stages):
            start(stage + 2)
        if stage == 0 and finish:
            for copy in side_copies:
                copy.start()
        for at in range(0, width, TILE):
            top = min(high, limits[at // TILE])
            if top <= low:
                continue
            cols = slice(at, at + TILE)
            term = jnp.dot(
                row_buf[which, :, low * depth : top * depth],
                weight_buf[low * depth : top * depth, cols],
                preferred_element_type=jnp.float32,
            )
            if low > skips[which] or total_refs is not None:
                term = acc[which, :, cols] + term
            acc[which, :, cols] = term
        if high < count:
            continue
        if finish:
            if which == 0:
                side_copies[0].wait()
            side_copies[1 + which].wait()
            finish_set(acc.at[which], bias_buf, table_buf[which], out_buf.at[which], with_keys)
        for copy in out_copies(which):
            copy.start()
    for which in range(sets):
        for copy in out_copies(which):
            copy.wait()


def finish_set(acc, bias, table, out, with_keys):
    swapped = pltpu.roll(table, HD // 2, 1)
    left = lax.broadcasted_iota(jnp.int32, table.shape, 1) < HD // 2
    cosine = jnp.where(left, table, swapped)
    sine = jnp.where(left, -swapped, table)
    for col in range(0, out.shape[1], HD):
        cols = slice(col, col + HD)
        value = acc[:, cols] + bias[:, cols]
        if not (with_keys and col == HD):
            value = turn(value, cosine, sine)
        out[:, cols] = value.astype(jnp.bfloat16)


def heads_of(row_sets, picks, pieces, limits, totals=None, finish=None, skips=None):
    sets, count = len(row_sets), len(pieces)
    skips = skips or (0,) * sets
    width = len(limits) * TILE
    sources = tuple(len(rows) for rows in row_sets)
    tokens, depth = row_sets[0][0].shape[1:]
    operands = [array for rows in row_sets for array in rows]
    operands += [array for piece in pieces for array, *_ in piece]
    totals_at = None
    if totals is not None:
        totals, totals_at = totals
        operands += totals
    scratch = [
        pltpu.VMEM((sets, tokens, count * depth), jnp.bfloat16),
        pltpu.VMEM((count * depth, width), jnp.bfloat16),
        pltpu.VMEM((sets, tokens, width), jnp.float32),
        pltpu.SemaphoreType.DMA((sets, count)),
        pltpu.SemaphoreType.DMA((count, max(map(len, pieces)))),
        pltpu.SemaphoreType.DMA((sets,)),
        pltpu.SemaphoreType.DMA((sets, 3)),
    ]
    with_keys, closed_width = False, 0
    out_shape = [jax.ShapeDtypeStruct((tokens, width), jnp.float32)] * sets
    if finish is not None:
        closed_width, bias, tables, with_keys = finish
        out_shape = [jax.ShapeDtypeStruct((tokens, closed_width), jnp.bfloat16)] * sets
        operands += [bias, *tables]
        if closed_width < width:
            out_shape += [jax.ShapeDtypeStruct((tokens, width - closed_width), jnp.float32)] * sets
        scratch += [
            pltpu.VMEM((1, closed_width), jnp.float32),
            pltpu.VMEM((sets, tokens, HD), jnp.float32),
            pltpu.VMEM((sets, tokens, closed_width), jnp.bfloat16),
            pltpu.SemaphoreType.DMA((sets + 1,)),
        ]
    plan = (
        sources,
        skips,
        tuple(tuple(part[1:] for part in piece) for piece in pieces),
        limits,
        width,
        closed_width,
        totals_at,
        with_keys,
    )
    anywhere = pl.BlockSpec(memory_space=pl.ANY)
    return pl.pallas_call(
        functools.partial(heads_kernel, plan),
        grid_spec=pltpu.PrefetchScalarGridSpec(
            num_scalar_prefetch=1,
            grid=(1,),
            in_specs=[anywhere] * len(operands),
            out_specs=[pl.BlockSpec(memory_space=pltpu.HBM)] * len(out_shape),
            scratch_shapes=scratch,
        ),
        out_shape=out_shape,
        compiler_params=pltpu.CompilerParams(vmem_limit_bytes=56 * 2**20),
        cost_estimate=pl.CostEstimate(
            flops=2 * sets * count * tokens * depth * width,
            bytes_accessed=2 * count * depth * (sets * tokens + width) + 8 * sets * tokens * width,
            transcendentals=0,
        ),
    )(jnp.stack(picks), *operands)


def attention(queries, keys, values, first_ref, out_ref):
    rows, cols = out_ref.shape
    heads = cols // HD
    scale = math.log2(math.e) / math.sqrt(HD)
    for top in range(0, rows, QROWS):
        low, end = max(0, top - MAXLEN), top + QROWS
        shape = (QROWS, end - low)
        stacked = jnp.concatenate(
            [queries[top:end, col : col + HD] for col in range(0, cols, HD)], axis=0
        )
        scores = jnp.dot(stacked, keys[:, low:end], preferred_element_type=jnp.float32)
        row = lax.broadcasted_iota(jnp.int32, shape, 0) + top
        col = lax.broadcasted_iota(jnp.int32, shape, 1) + low
        visible = (col <= row) & (col >= first_ref[top:end])
        scores = jnp.where(visible[None], scores.reshape(heads, *shape), -jnp.inf)
        most = jnp.max(scores, axis=-1, keepdims=True)
        exponent = jnp.exp2((scores - most) * scale)
        share = 1.0 / jnp.sum(exponent, axis=-1, keepdims=True)
        weights = (exponent * share).astype(jnp.bfloat16)
        context = jnp.dot(
            weights.reshape(heads * QROWS, end - low),
            values[low:end],
            preferred_element_type=jnp.float32,
        ).astype(jnp.bfloat16)
        for head in range(heads):
            out_ref[top:end, head * HD : (head + 1) * HD] = context[
                head * QROWS : (head + 1) * QROWS
            ]


def attend_kernel(numbers, flag_ref, *refs):
    ends = [sum(numbers[: i + 1]) for i in range(4)]
    near, beside, back, other = (refs[end - number : end] for end, number in zip(ends, numbers))
    first_ref, out_ref, cache_ref, part_buf, out_buf, in_sem, out_sem = refs[ends[-1] :]
    half = out_buf.shape[2]

    def copies(side, sources):
        column = 0
        for part, source in enumerate(sources):
            wide = source.shape[1]
            yield pltpu.make_async_copy(
                source, part_buf.at[side, :, column : column + wide], in_sem.at[side, part]
            )
            column += wide

    def on_parts(act):
        for middle, sides in ((1, (near, beside)), (0, (back, other))):

            @pl.when(flag_ref[1] == middle)
            def _():
                for side, sources in enumerate(sides):
                    for copy in copies(side, sources):
                        act(copy)

    on_parts(lambda copy: copy.start())
    on_parts(lambda copy: copy.wait())
    sent = []
    for side in range(2):
        at = flag_ref[0] if side == 0 else 1 - flag_ref[0]
        part = part_buf.at[side]
        for number in range(2):
            sent.append(
                pltpu.make_async_copy(
                    part.at[:, number * HD : (number + 1) * HD],
                    cache_ref.at[:, pl.ds(pl.multiple_of((2 * number + at) * HD, HD), HD)],
                    out_sem.at[side, number],
                )
            )
            sent[-1].start()
        keys = part[:, :HD].astype(jnp.float32).T.astype(jnp.bfloat16)
        attention(part.at[:, TILE:], keys, part.at[:, HD:TILE], first_ref, out_buf.at[side])
        sent.append(
            pltpu.make_async_copy(
                out_buf.at[side],
                out_ref.at[:, pl.ds(pl.multiple_of(at * half, half), half)],
                out_sem.at[side, 2],
            )
        )
        sent[-1].start()
    for copy in sent:
        copy.wait()


def attend_all(flags, near, beside, back, other, first, cols):
    operands = [*near, *beside, *back, *other]
    rows = near[0].shape[0]
    in_hbm = pl.BlockSpec(memory_space=pltpu.HBM)
    return pl.pallas_call(
        functools.partial(attend_kernel, tuple(map(len, (near, beside, back, other)))),
        grid_spec=pltpu.PrefetchScalarGridSpec(
            num_scalar_prefetch=1,
            grid=(1,),
            in_specs=[in_hbm] * len(operands) + [pl.BlockSpec((rows, 1), lambda i, flags: (0, 0))],
            out_specs=[in_hbm] * 2,
            scratch_shapes=[
                pltpu.VMEM((2, rows, TILE + cols // 2), jnp.bfloat16),
                pltpu.VMEM((2, rows, cols // 2), jnp.bfloat16),
                pltpu.SemaphoreType.DMA((2, 3)),
                pltpu.SemaphoreType.DMA((2, 3)),
            ],
        ),
        out_shape=[
            jax.ShapeDtypeStruct((rows, cols), jnp.bfloat16),
            jax.ShapeDtypeStruct((rows, 2 * TILE), jnp.bfloat16),
        ],
        compiler_params=pltpu.CompilerParams(vmem_limit_bytes=40 * 2**20),
        cost_estimate=pl.CostEstimate(
            flops=4 * cols * rows * 3 * QROWS,
            bytes_accessed=6 * rows * cols,
            transcendentals=cols // HD * rows * 3 * QROWS,
        ),
    )(flags, *operands, first)


MIDDLE = (2, 3, 4, 5)
ENDS = (0, 1, 6, 7)


def after(value, *others):
    return lax.optimization_barrier((value,) + others)[0]


def pairs_from(sources, code):
    return [(s, s ^ code) for s in sources]


def middle_form(hidden, norm_gain, q_weight, q_bias, kv_weight, kv_bias, prefix_lens, assignment):
    tok_rows, features = hidden.shape
    slice_rows, q_cols = q_weight.shape
    half_cols = q_cols // 2
    group = lax.axis_index("group")
    tensor = lax.axis_index("tensor")
    y = group & 1
    is_middle = (group >= 2) & (group < 6)
    barrier = lax.optimization_barrier

    def over_group(value, sources, code):
        return lax.ppermute(value, "group", pairs_from(sources, code))

    def to_middle(value):
        return over_group(value, ENDS, 2)

    def across_middle(value):
        return over_group(value, MIDDLE, 6)

    def over_x(value):
        return lax.ppermute(value, "tensor", pairs_from(range(4), 2))

    def over_core(value):
        return lax.ppermute(value, "tensor", pairs_from(range(4), 1))

    begin, widths = (0, 2 * TILE, 4 * TILE), (2 * TILE, 2 * TILE, TILE)

    def columns(half, cuts):
        head = (2 * tensor + half) * HD
        kv_part = lax.dynamic_slice_in_dim(kv_weight, head, HD, 2).reshape(slice_rows, TILE)
        taken, low = [], half * half_cols
        for number, wide in enumerate(cuts):
            wide = wide - (TILE if number == 0 else 0)
            part = lax.dynamic_slice_in_dim(q_weight, low, wide, 1)
            low = low + wide
            taken.append(jnp.concatenate([kv_part, part], axis=1) if number == 0 else part)
        return taken

    def both(one, two, chunk):
        low, high = begin[chunk], begin[chunk] + widths[chunk]
        return jnp.stack([one[:, low:high], two[:, low:high]])

    def pick(code_of_rows, codes):
        block = jnp.stack([group ^ code for code in codes])
        if code_of_rows == 0:
            return jnp.stack([block * 0, block])
        return jnp.stack([(block >> 1) ^ tensor, block & 1])

    def rows_and_picks(sets, codes):
        return [rows_of[c] for c in sets], [pick(c, codes) for c in sets]

    def closed(arriving, others):
        arrived = []
        for value in arriving:
            value, others = barrier((value, others))
            arrived.append(value)
        return barrier((tuple(arrived), others))

    (own,) = columns(y, (sum(widths),))
    other, other2 = columns(1 - y, (begin[2], widths[2]))
    m_own = across_middle(own)
    swap = over_group(other, range(8), 1)
    swap2 = over_group(other2, range(8), 1)
    quarter = norm(hidden, norm_gain, tensor, slice_rows, 2)
    end2 = to_middle(quarter)
    normed = norm(after(hidden, quarter), norm_gain, tensor * 0, slice_rows, features // slice_rows)

    bias = lax.dynamic_slice_in_dim(q_bias, y * half_cols, half_cols, 0)
    kv_bias_here = lax.dynamic_slice_in_dim(kv_bias, (2 * tensor + y) * HD, HD, 1)
    bias = jnp.concatenate([kv_bias_here[0], kv_bias_here[1], bias])[None, :]
    inverse_freq = THETA ** (-2.0 * jnp.arange(HD // 2, dtype=jnp.float32) / HD)
    m_swap = across_middle(after(swap, m_own))
    own, swap, m_own, normed, quarter, end2 = barrier((own, swap, m_own, normed, quarter, end2))

    rows_of = {0: [normed]}
    stack0, end2 = barrier((both(own, swap, 0), end2))
    e0 = to_middle(stack0)
    next1, next2 = both(own, swap, 1), jnp.stack([own[:, begin[2] :], swap2])
    end3 = over_group(end2, MIDDLE, 1)
    across2 = over_x(end2)
    twin2 = over_core(end2)
    tables = []
    for code in range(4):
        _, offset, places = token_layout(prefix_lens, assignment, group ^ code, tok_rows)
        angles = offset.astype(jnp.float32)[:, None] * inverse_freq[None, :]
        table = jnp.concatenate([jnp.cos(angles), jnp.sin(angles)], axis=1)
        tables.append((table, (places - offset)[:, None]))
    m_e0 = across_middle(after(e0, m_swap))
    (e0, m_swap, end3, across2, twin2), (next1, next2, end2, tables, quarter) = closed(
        (e0, m_swap, end3, across2, twin2), (next1, next2, end2, tables, quarter)
    )

    places = {}

    def arrived(chunk, **codes):
        for code, (array, lead, skip) in codes.items():
            places[int(code[1:]), chunk] = (array, lead, skip)

    for chunk, low in enumerate(begin):
        arrived(chunk, c0=(own, None, low), c6=(m_own, None, low))
        if chunk < 2:
            arrived(chunk, c1=(swap, None, low), c7=(m_swap, None, low))
    arrived(2, c1=(swap2, None, 0))
    arrived(0, c2=(e0, 0, 0), c3=(e0, 1, 0))

    def call(sets, codes, chunks, totals=None, finish=None, skips=None):
        rows, picks = rows_and_picks(sets, codes)
        pieces, limits = [], []
        for code in codes:
            there = [chunk for chunk in chunks if (code, chunk) in places]
            pieces.append([places[code, chunk] + (widths[chunk],) for chunk in there])
        for chunk in chunks:
            there = [(code, chunk) in places for code in codes]
            limits += [sum(there)] * (widths[chunk] // TILE)
            assert all(there[: sum(there)])
        return heads_of(rows, picks, pieces, tuple(limits), totals, finish, skips)

    outs, every = {}, (0, 1, 2)

    def first_sums(sets):
        return call(sets, (0, 1, 6, 7, 2, 3), every)

    def finished(sets, chunks, codes, totals=None, opened=(), skips=None):
        low, wide = begin[chunks[0]], sum(widths[chunk] for chunk in chunks)
        finish = (wide, bias[:, low : low + wide], [tables[c][0] for c in sets], chunks[0] == 0)
        made = call(sets, codes, chunks + opened, totals, finish, skips)
        for code, out in zip(sets, made):
            outs[code, chunks[0]] = out
        return made[-1]

    e1 = to_middle(next1)
    end1 = over_group(quarter, MIDDLE, 1)
    across3 = over_x(end3)
    far2 = over_core(across2)
    rows_of[2] = [end2, twin2, across2, far2]
    sums = dict(zip((0, 2), first_sums((0, 2))))
    m_e1 = across_middle(after(e1, m_e0))
    (m_e0, e1, end1, across3), (next2, e0, end3, far2, sums) = closed(
        (m_e0, e1, end1, across3), (next2, e0, end3, far2, sums)
    )
    rows_of[2] = [end2, twin2, across2, far2]

    e2 = to_middle(next2)
    across1 = over_x(end1)
    twin3 = over_core(end3)
    far3 = over_core(across3)
    rows_of[3] = [end3, twin3, across3, far3]

    def send_back(code, chunk):
        return over_group(outs[code, chunk], MIDDLE, code)

    arrived(1, c2=(e1, 0, 0), c3=(e1, 1, 0))
    (sums[3],) = first_sums((3,))
    arrived(0, c4=(m_e0, 0, 0), c5=(m_e0, 1, 0))
    three = (2, 3, 0)
    finished(three, (0,), (4, 5), ([sums[c] for c in three], (0, 0, 0)))
    back = {(2, 0): send_back(2, 0)}
    last = jnp.concatenate([swap2[None], e2])
    m_last = across_middle(after(last, m_e1))
    (last, m_e1, across1, back[2, 0]), (end1, made, sums) = closed(
        (last, m_e1, across1, back[2, 0]), (end1, [outs[c, 0] for c in three], sums)
    )
    for code, out in zip(three, made):
        outs[code, 0] = out

    twin1 = over_core(end1)
    far1 = over_core(across1)
    arrived(1, c4=(m_e1, 0, 0), c5=(m_e1, 1, 0))
    arrived(2, c2=(last, 1, 0), c3=(last, 2, 0))
    back[3, 0] = send_back(3, 0)
    three = (2, 0, 3)
    finished(
        three,
        (1,),
        (2, 3, 4, 5),
        ([sums[c] for c in three], (begin[1],) * 3),
        skips=(0, 0, 2),
    )
    for code in (2, 3):
        back[code, 1] = send_back(code, 1)
    far1, outs[2, 1] = barrier((far1, outs[2, 1]))
    rows_of[1] = [end1, twin1, across1, far1]
    sums[1] = finished((1,), (0, 1), (0, 1, 6, 2, 3, 7, 4, 5), opened=(2,))
    back[1, 0] = send_back(1, 0)
    (m_last, back[3, 0], back[2, 1]), (sums, outs[1, 0]) = closed(
        (m_last, back[3, 0], back[2, 1]), (sums, outs[1, 0])
    )

    arrived(2, c7=(m_last, 0, 0), c4=(m_last, 1, 0), c5=(m_last, 2, 0))
    three = (2, 3, 1)
    finished(
        three,
        (2,),
        (2, 3, 7, 4, 5),
        ([sums[c] for c in three], (begin[2], begin[2], 0)),
        skips=(0, 0, 2),
    )
    for code in (2, 3):
        back[code, 2] = send_back(code, 2)
    back[1, 2] = send_back(1, 2)
    sums[0], outs[1, 2], back[3, 1] = barrier((sums[0], outs[1, 2], back[3, 1]))
    finished((0,), (2,), (2, 3, 7, 4, 5), ([sums[0]], (begin[2],)))

    (back[2, 2], back[3, 2], back[1, 2]), _ = closed((back[2, 2], back[3, 2], back[1, 2]), ())
    context, cache = attend_all(
        jnp.stack([y, is_middle.astype(jnp.int32)]),
        [outs[0, part] for part in every],
        [back[1, part] for part in (0, 2)],
        [back[2, part] for part in every],
        [back[3, part] for part in every],
        tables[0][1],
        q_cols,
    )
    return (context, cache.reshape(tok_rows, 2, TILE))


def solution(mesh):
    placed = (
        P("group", None),
        P(),
        P("group", "tensor"),
        P("tensor"),
        P("group", None, None),
        P(),
        P(),
        P(),
    )
    fits = mesh.shape["group"] == 8 and mesh.shape["tensor"] == 4
    return jax.shard_map(
        middle_form if fits else gathered_form,
        mesh=mesh,
        in_specs=placed,
        out_specs=(P("group", "tensor"), P("group", None, "tensor")),
        check_vma=False,
    )
```
